512 devices in a mesh: bra: 16 (over y, z_hi), ket: 32 (over x, z_lo, core).
Axes of the slice: x: 4, y: 8, z: 8 (z_hi: 2, z_lo: 4; z = z_hi * 4 + z_lo), core: 2. Of those that a mesh axis runs over, the one named last changes fastest.
Arguments:
- basis_centers: float32 [3, 8192], replicated, may hold values from -30 to 30
- bra_pairs: int32 [512], P('bra'), may hold values from 0 to 63, as said below
- ket_pairs: int32 [1024], P('ket'), may hold values from 0 to 63, as said below
- quartets: int32 [16, 32, 2, 2048], P('bra', 'ket'), may hold values from 0 to 31
- quartet_counts: int32 [16, 32], P('bra', 'ket'), may hold values from 512 to 2048
- density_owner: int32 [32, 64], P('ket'), may hold values from 0 to 63, each once within a row
- density_store: bfloat16 [64, 4096, 128], P('bra', 'ket'), may hold values from -0.29882812 to 0.29882812
Outputs:
- exchange: bfloat16 [2048, 8192], P('bra', 'ket')
The draws below stay inside these ranges and needn't reach their ends.
Inputs may be any that keep to these rules, and one draw needn't show every extreme that they name: `bra_pairs`: screened by block distance: the blocks of row r's pairs are distinct and lie within 16 blocks of i_r, counted cyclically over the 64 blocks. `ket_pairs`: the blocks of column c's pairs are distinct.
All inputs are finite; a program needn't handle non-finite values.
Results may differ from the reference program's by a relative error of at most 0.007.
Values may be sent and summed in bfloat16 or wider, within the bound.
A program may use at most 64 MiB of HBM per device.

```python
import math
import jax
import jax.numpy as jnp
from jax import lax

BLOCK = 128
QUARTETS = 2048
NBLK = 64
PAIRS = 32
N_BRA = 16
N_KET = 32


def cycle_centers(key, cycle_radius, jitter_size, offset_scale):
    first_key = jax.random.fold_in(key, 0)
    third_key = jax.random.fold_in(key, 2)
    fourth_key = jax.random.fold_in(key, 3)
    order = jax.random.permutation(third_key, NBLK).astype(jnp.float32)
    angle = 2.0 * math.pi / NBLK * order
    cycle = jnp.stack([cycle_radius * jnp.cos(angle), cycle_radius * jnp.sin(angle), jnp.zeros((NBLK,), jnp.float32)])
    jitter = jax.random.uniform(first_key, (3, NBLK, 1), jnp.float32, -jitter_size, jitter_size)
    bell_part = 0.5 * jax.random.truncated_normal(fourth_key, -2.0, 2.0, (3, NBLK, BLOCK), jnp.float32)
    offset = offset_scale * bell_part
    return (cycle[:, :, None] + jitter + offset).reshape(3, NBLK * BLOCK)


def draw_basis_centers(key, part):
    key = jax.random.fold_in(key, 11)
    return cycle_centers(key, 4.0, 0.5, 6.0)


def distinct_offsets(keys, choices_total):

    def single(one_key):
        return jax.random.permutation(one_key, choices_total)[:PAIRS]
    return jax.vmap(single)(keys).astype(jnp.int32)


def draw_bra_pairs(key, part):
    key = jax.random.fold_in(key, 23)
    pair_reach = NBLK // 4
    keys = jax.random.split(key, N_BRA)
    offsets = distinct_offsets(keys, 2 * pair_reach + 1) - pair_reach
    home = (jnp.arange(N_BRA, dtype=jnp.int32) * (NBLK // N_BRA))[:, None]
    return ((home + offsets + NBLK) % NBLK).reshape(N_BRA * PAIRS).astype(jnp.int32)


def draw_ket_pairs(key, part):
    key = jax.random.fold_in(key, 37)
    keys = jax.random.split(key, N_KET)
    offsets = distinct_offsets(keys, NBLK)
    home = (jnp.arange(N_KET, dtype=jnp.int32) * (NBLK // N_KET))[:, None]
    return ((home + offsets) % NBLK).reshape(N_KET * PAIRS).astype(jnp.int32)


def plant(result, rng, low, top_value):
    extent = result.shape
    place = [jax.random.randint(jax.random.fold_in(rng, axis), (), 0, extent[axis]) for axis in range(len(extent))]
    result = result.at[tuple(place)].set(low)
    longest = extent.index(max(extent))
    place[longest] = (place[longest] + 1) % extent[longest]
    return result.at[tuple(place)].set(top_value)


def levels(key, extent, shards, low, high):
    loudness, own = 1.0, jax.random.fold_in(key, 6)
    for position, blocks in shards:
        draws = jnp.exp(jax.random.uniform(jax.random.fold_in(own, position), (blocks,), jnp.float32, low / len(shards), high / len(shards)))
        loudness = loudness * jnp.repeat(draws, extent[position] // blocks).reshape([-1 if axis == position else 1 for axis in range(len(extent))])
    return loudness


def normal_values(rng, extent, scale, bound, cuts=(), kind=jnp.bfloat16):
    result = jax.random.normal(rng, extent, jnp.float32) * scale
    if len(cuts) > 0:
        result = levels(rng, extent, cuts, -0.22, 0.18) * result
    return jnp.clip(result, min=-bound, max=bound).astype(kind)


def setup_inputs(seed: int = 0) -> dict:
    splits = jax.random.split(jax.random.key(seed), 8)
    basis_centers = draw_basis_centers(jax.random.fold_in(splits[7], 71), 0)
    bra_pairs = draw_bra_pairs(jax.random.fold_in(splits[7], 71), 0)
    ket_pairs = draw_ket_pairs(jax.random.fold_in(splits[7], 71), 0)
    quartets = plant(jax.random.randint(splits[3], (N_BRA, N_KET, 2, QUARTETS), 0, PAIRS), jax.random.fold_in(splits[3], 1), 0, PAIRS - 1).astype(jnp.int32)
    quartet_counts = plant(jax.random.randint(splits[4], (N_BRA, N_KET), QUARTETS // 4, QUARTETS + 1), jax.random.fold_in(splits[4], 1), QUARTETS // 4, QUARTETS).astype(jnp.int32)
    density_owner = jax.vmap(lambda own: jax.random.permutation(own, NBLK))(jax.random.split(splits[5], N_KET)).reshape((N_KET, NBLK)).astype(jnp.int32)
    density_store = normal_values(splits[6], (NBLK, N_KET * BLOCK, BLOCK), 0.05, 0.29882812, ((0, 16), (1, 32)))
    return {"basis_centers": basis_centers, "bra_pairs": bra_pairs, "ket_pairs": ket_pairs, "quartets": quartets, "quartet_counts": quartet_counts, "density_owner": density_owner, "density_store": density_store}


OMEGA = 0.11
SOFTEN = 0.25

def kernel_tiles(centers_left, centers_right):
    squared = jnp.zeros((centers_left.shape[1], centers_left.shape[2], centers_right.shape[2]), jnp.float32)
    for coord_axis in range(3):
        difference = centers_left[coord_axis][:, :, None] - centers_right[coord_axis][:, None, :]
        squared = squared + difference * difference
    radius = jnp.sqrt(squared + SOFTEN)
    return (lax.erfc(OMEGA * radius) / radius).astype(jnp.bfloat16)

def pair_weights(quartet_list, quartet_count, pair_total):
    capacity = quartet_list.shape[1]
    active = (jnp.arange(capacity) < quartet_count).astype(jnp.float32)
    slots = jnp.arange(pair_total)
    ket_onehot = (quartet_list[1][:, None] == slots[None, :]).astype(jnp.bfloat16)
    bra_onehot = ((quartet_list[0][:, None] == slots[None, :]).astype(jnp.float32) * active[:, None]).astype(jnp.bfloat16)
    return jnp.dot(ket_onehot.T, bra_onehot, preferred_element_type=jnp.float32).astype(jnp.bfloat16)

def reference(basis_centers, bra_pairs, ket_pairs, quartets, quartet_counts, density_owner, density_store):
    basis_grid = basis_centers.reshape(3, NBLK, BLOCK)
    bra_table = bra_pairs.reshape(N_BRA, PAIRS)
    ket_table = ket_pairs.reshape(N_KET, PAIRS)
    store_grid = density_store.reshape(NBLK, N_KET, BLOCK, BLOCK)
    stride = NBLK // N_BRA
    column_stride = NBLK // N_KET

    def row_term(row_index):
        bra_blocks = bra_table[row_index]
        row_centers = lax.dynamic_slice_in_dim(basis_grid, (row_index * stride).astype(jnp.int32), 1, 1)
        bra_tiles = kernel_tiles(jnp.broadcast_to(row_centers, (3, PAIRS, BLOCK)), jnp.take(basis_grid, bra_blocks, axis=1))

        def column_term(total, column_index):
            column = store_grid[:, column_index]
            owner_row = density_owner[column_index]
            picked = jnp.take(column, jnp.take(owner_row, bra_blocks), axis=0)
            product = jnp.einsum('pab,pbc->pac', bra_tiles.astype(jnp.float32), picked.astype(jnp.float32)).astype(jnp.bfloat16)
            weights = pair_weights(quartets[row_index, column_index], quartet_counts[row_index, column_index], PAIRS)
            summed = jnp.dot(weights, product.reshape(PAIRS, BLOCK * BLOCK), preferred_element_type=jnp.float32)
            summed = summed.astype(jnp.bfloat16).reshape(PAIRS, BLOCK, BLOCK)
            ket_blocks = ket_table[column_index]
            own_center = lax.dynamic_slice_in_dim(basis_grid, (column_index * column_stride).astype(jnp.int32), 1, 1)
            ket_tiles = kernel_tiles(jnp.take(basis_grid, ket_blocks, axis=1), jnp.broadcast_to(own_center, (3, PAIRS, BLOCK)))
            image = jnp.einsum('qab,qcb->qac', summed.astype(jnp.float32), ket_tiles.astype(jnp.float32))
            return (total + jax.ops.segment_sum(image, ket_blocks, num_segments=NBLK), None)
        total, _ = lax.scan(column_term, jnp.zeros((NBLK, BLOCK, BLOCK), jnp.float32), jnp.arange(N_KET, dtype=jnp.int32))
        return total.transpose(1, 0, 2).reshape(BLOCK, NBLK * BLOCK)
    rows_all = lax.map(row_term, jnp.arange(N_BRA, dtype=jnp.int32))
    return rows_all.reshape(N_BRA * BLOCK, NBLK * BLOCK).astype(jnp.bfloat16)
```

```python
import jax
import jax.numpy as jnp
from jax import lax
from jax.experimental import pallas as pl
from jax.experimental.pallas import tpu as pltpu
from jax.sharding import PartitionSpec as P

OMEGA = 0.11
SOFTEN = 0.25
BLOCK = 128
NBLK = 64
PAIRS = 32
RING = 8
DEEP = 2
SIDE = 4
OWN = 4
GROUP = 8
MESH = pl.DeviceIdType.MESH
F32 = jnp.float32
BF16 = jnp.bfloat16

ERFC = (
    -1.26551223,
    1.00002368,
    0.37409196,
    0.09678418,
    -0.18628806,
    0.27886807,
    -1.13520398,
    1.48851587,
    -0.82215223,
    0.17087277,
)


def kernel_value(squared):
    inverse = lax.rsqrt(squared)
    x = OMEGA * (squared * inverse)
    t = 1.0 / (1.0 + 0.5 * x)
    poly = jnp.full_like(t, ERFC[-1])
    for c in ERFC[-2::-1]:
        poly = poly * t + c
    return t * jnp.exp(poly - x * x) * inverse


def body(
    centers,
    bra_pairs,
    ket_pairs,
    quartets,
    count,
    owner,
    density,
    out,
    gathered,
    lines,
    columns,
    bra_tiles,
    ket_tiles,
    spread,
    product,
    weighted,
    keep,
    sib_out,
    sib_in,
    x_out,
    rel_in,
    x_in,
    z_out,
    z_in,
    part_send,
    part_recv,
    ring_send,
    ring_recv,
    sib_send,
    sib_recv,
    rel_send,
    rel_recv,
    x_send,
    x_recv,
    z_send,
    z_recv,
):
    row = lax.axis_index("bra")
    col = lax.axis_index("ket")
    y, deep = row // DEEP, row % DEEP
    core = col % 2
    zl = (col // 2) % SIDE
    xx = col // (2 * SIDE)

    def at_row(yy, dd):
        return lax.rem(yy + 2 * RING, RING) * DEEP + dd

    def at_col(x_at, z_at, core_at):
        return (lax.rem(x_at + SIDE, SIDE) * SIDE + z_at) * 2 + core_at

    up, down = at_row(y + 1, deep), at_row(y - 1, deep)
    partner = at_row(y, 1 - deep)
    sibling = at_col(xx, zl, 1 - core)
    x_up, x_down = at_col(xx + 1, zl, core), at_col(xx - 1, zl, core)

    def z_at(step):
        return lax.rem(zl + step, SIDE)

    peers = [(up, col), (down, col), (partner, col), (row, sibling), (row, x_up), (row, x_down)]
    peers += [(row, at_col(xx, z_at(step), core)) for step in range(1, SIDE)]
    barrier = pltpu.get_barrier_semaphore()
    for peer in peers:
        pl.semaphore_signal(barrier, inc=1, device_id=peer, device_id_type=MESH)
    gathered[pl.ds(row * OWN, OWN)] = density[...]
    pl.semaphore_wait(barrier, len(peers))

    def remote(src, dst, send, recv, device):
        return pltpu.make_async_remote_copy(
            src_ref=src,
            dst_ref=dst,
            send_sem=send,
            recv_sem=recv,
            device_id=device,
            device_id_type=MESH,
        )

    own_slots = gathered.at[pl.ds(row * OWN, OWN)]
    to_partner = remote(own_slots, own_slots, part_send, part_recv, (partner, col))
    to_partner.start()

    def hop(family, way, m, arriving):
        sign = 1 - 2 * way
        dd = deep if family == 0 else 1 - deep
        back = m // OWN + arriving
        slot = at_row(y - sign * back, dd) * OWN + lax.rem(m + 2 * way, OWN)
        ref = gathered.at[pl.ds(slot, 1)]
        device = (up, col) if way == 0 else (down, col)
        return remote(
            ref, ref, ring_send.at[family, way, m], ring_recv.at[family, way, m], device
        )

    last = 3 * OWN + OWN // 2

    def first_sends(family):
        for m in range(OWN):
            for way in range(2):
                hop(family, way, m, 0).start()

    def forward(family, m):
        for way in range(2):
            hop(family, way, m - OWN, 1).wait_recv()
            hop(family, way, m, 0).start()

    first_sends(0)

    for block in range(NBLK):
        lines[block, 0:3] = centers[:, block * BLOCK : (block + 1) * BLOCK]
    for side, start in ((0, row * (NBLK // 16)), (1, col * (NBLK // 32))):
        line = lines[start]
        for axis in range(3):
            wide = jnp.broadcast_to(line[axis : axis + 1], (BLOCK, BLOCK))
            columns[side, axis] = wide.T

    def tile(side, block, ref, place):
        line = lines[block]
        rows = 32
        for part in range(BLOCK // rows):
            squared = jnp.full((rows, BLOCK), SOFTEN, F32)
            for axis in range(3):
                difference = columns[side, axis, pl.ds(part * rows, rows)] - line[axis : axis + 1]
                squared = squared + difference * difference
            ref[place, pl.ds(part * rows, rows)] = kernel_value(squared).astype(BF16)

    def ket_tile(j):
        tile(1, j, ket_tiles, j)

    def bra_tile(p):
        tile(0, bra_pairs[p], bra_tiles, p)

    entry = lax.broadcasted_iota(jnp.int32, (PAIRS, quartets.shape[3]), 1)
    slot = lax.broadcasted_iota(jnp.int32, (PAIRS, quartets.shape[3]), 0)
    one, zero = jnp.float32(1.0), jnp.float32(0.0)
    bra_hot = jnp.where(
        (quartets[0, 0, 0:1] == slot) & (entry < count[0, 0]), one, zero
    ).astype(BF16)
    ket_hot = jnp.where(quartets[0, 0, 1:2] == slot, one, zero).astype(BF16)
    counts = lax.dot_general(
        ket_hot, bra_hot, (((1,), (1,)), ((), ())), preferred_element_type=F32
    ).astype(BF16)
    tall = lax.broadcasted_iota(jnp.int32, (NBLK * GROUP, PAIRS), 0) // GROUP
    pick = jnp.where(ket_pairs[...] == tall, one, zero).astype(BF16)
    by_block = jnp.dot(pick, counts, preferred_element_type=F32).astype(BF16)
    wide_shape = (PAIRS, PAIRS * GROUP)
    wide_hot = jnp.where(
        lax.broadcasted_iota(jnp.int32, wide_shape, 1) // GROUP
        == lax.broadcasted_iota(jnp.int32, wide_shape, 0),
        one,
        zero,
    ).astype(BF16)
    spread_shape = (NBLK * GROUP, PAIRS * GROUP)
    same = (
        lax.broadcasted_iota(jnp.int32, spread_shape, 0) % GROUP
        == lax.broadcasted_iota(jnp.int32, spread_shape, 1) % GROUP
    )
    spread[...] = jnp.where(
        same, jnp.dot(by_block, wide_hot, preferred_element_type=F32), zero
    ).astype(BF16)

    @pl.loop(OWN, last)
    def _(m):
        forward(0, m)
        for extra in range(4):
            ket_tile((m - OWN) * 4 + extra)

    to_partner.wait()
    first_sends(1)

    @pl.loop(0, 4)
    def _(n):
        ket_tile(40 + n)
        for extra in range(3):
            bra_tile(n * 3 + extra)

    @pl.loop(OWN, last)
    def _(m):
        forward(1, m)
        for extra in range(2):
            ket_tile(44 + (m - OWN) * 2 + extra)
            bra_tile(12 + (m - OWN) * 2 + extra)

    @pl.loop(last - OWN, last)
    def _(m):
        for family in range(2):
            for way in range(2):
                hop(family, way, m, 1).wait_recv()

    @pl.loop(0, PAIRS // 4)
    def _(n):
        for extra in range(4):
            p = n * 4 + extra
            block = gathered[owner[0, bra_pairs[p]]]
            z = jnp.dot(bra_tiles[p], block, preferred_element_type=F32)
            product[p] = z.astype(BF16).astype(F32)

    @pl.loop(0, BLOCK // GROUP // 2)
    def _(n):
        base = pl.multiple_of(n * 2 * GROUP, 2 * GROUP)
        halves = [
            product[:, pl.ds(base + half * GROUP, GROUP), :]
            .reshape(PAIRS * GROUP, BLOCK)
            .astype(BF16)
            for half in range(2)
        ]
        both = jnp.dot(
            spread[...], jnp.concatenate(halves, axis=1), preferred_element_type=F32
        )
        for half in range(2):
            weighted[:, pl.ds(base + half * GROUP, GROUP), :] = both[
                :, half * BLOCK : (half + 1) * BLOCK
            ].reshape(NBLK, GROUP, BLOCK)

    def image(j):
        return jnp.dot(weighted[j].astype(BF16), ket_tiles[j], preferred_element_type=F32)

    def to_sibling(d):
        return remote(
            sib_out.at[d], sib_in.at[d], sib_send.at[d], sib_recv.at[d], (row, sibling)
        )

    def images(d):
        base = lax.rem(xx + d, SIDE) * 4 * SIDE

        @pl.loop(0, SIDE)
        def _(zz):
            for jj in range(2):
                sib_out[d, jj, zz] = image(base + zz * 4 + (1 - core) * 2 + jj).astype(BF16)

        to_sibling(d).start()

        @pl.loop(0, SIDE)
        def _(zz):
            for jj in range(2):
                keep[d, jj, zz] = image(base + zz * 4 + core * 2 + jj)

    def chip_sum(d, jj):
        return keep[d, jj] + sib_in[d, jj].astype(F32)

    def relay(way):
        device = (row, x_up) if way == 0 else (row, x_down)
        return remote(
            x_out.at[2, way], rel_in.at[way], rel_send.at[way], rel_recv.at[way], device
        )

    def to_x(way, jj):
        device = (row, x_up) if way == 0 else (row, x_down)
        return remote(
            x_out.at[way, jj], x_in.at[way, jj], x_send.at[way, jj], x_recv.at[way, jj], device
        )

    images(2)
    images(1)
    to_sibling(2).wait_recv()
    for way in range(2):
        x_out[2, way] = chip_sum(2, way).astype(BF16)
        relay(way).start()
    images(3)
    to_sibling(1).wait_recv()
    x_out[0, 1] = chip_sum(1, 1).astype(BF16)
    to_x(0, 1).start()
    images(0)
    to_sibling(3).wait_recv()
    x_out[1, 0] = chip_sum(3, 0).astype(BF16)
    to_x(1, 0).start()
    relay(0).wait_recv()
    x_out[0, 0] = (chip_sum(1, 0) + rel_in[0].astype(F32)).astype(BF16)
    to_x(0, 0).start()
    relay(1).wait_recv()
    x_out[1, 1] = (chip_sum(3, 1) + rel_in[1].astype(F32)).astype(BF16)
    to_x(1, 1).start()
    to_sibling(0).wait_recv()
    for jj in range(2):
        keep[0, jj] = chip_sum(0, jj)
    for way, jj in ((0, 1), (1, 0), (0, 0), (1, 1)):
        to_x(way, jj).wait_recv()
        keep[0, jj] = keep[0, jj] + x_in[way, jj].astype(F32)

    def to_z(step):
        return remote(
            z_out.at[step - 1],
            z_in.at[step - 1],
            z_send.at[step - 1],
            z_recv.at[step - 1],
            (row, at_col(xx, z_at(step), core)),
        )

    for step in (2, 3, 1):
        for jj in range(2):
            z_out[step - 1, jj] = keep[0, jj, z_at(step)].astype(BF16)
        to_z(step).start()

    @pl.loop(0, last)
    def _(m):
        for family in range(2):
            for way in range(2):
                hop(family, way, m, 0).wait_send()

    for d in range(SIDE):
        to_sibling(d).wait_send()
    for way in range(2):
        relay(way).wait_send()
        for jj in range(2):
            to_x(way, jj).wait_send()
    for step in (1, 2, 3):
        to_z(step).wait()
    for jj in range(2):
        total = keep[0, jj, zl]
        for step in range(1, SIDE):
            total = total + z_in[step - 1, jj].astype(F32)
        out[:, jj * BLOCK : (jj + 1) * BLOCK] = total.astype(BF16)


def local(
    basis_centers, bra_pairs, ket_pairs, quartets, quartet_counts, density_owner, density_store
):
    vmem = pl.BlockSpec(memory_space=pltpu.VMEM)
    smem = pl.BlockSpec(memory_space=pltpu.SMEM)
    block = (BLOCK, BLOCK)
    dma = pltpu.SemaphoreType.DMA
    hops = 3 * OWN + OWN // 2
    return pl.pallas_call(
        body,
        out_shape=jax.ShapeDtypeStruct((BLOCK, 2 * BLOCK), BF16),
        in_specs=[vmem, smem, vmem, vmem, smem, smem, vmem],
        out_specs=vmem,
        scratch_shapes=[
            pltpu.VMEM((NBLK,) + block, BF16),
            pltpu.VMEM((NBLK, 8, BLOCK), F32),
            pltpu.VMEM((2, 3) + block, F32),
            pltpu.VMEM((PAIRS,) + block, BF16),
            pltpu.VMEM((NBLK,) + block, BF16),
            pltpu.VMEM((NBLK * GROUP, PAIRS * GROUP), BF16),
            pltpu.VMEM((PAIRS,) + block, F32),
            pltpu.VMEM((NBLK,) + block, F32),
            pltpu.VMEM((SIDE, 2, SIDE) + block, F32),
            pltpu.VMEM((SIDE, 2, SIDE) + block, BF16),
            pltpu.VMEM((SIDE, 2, SIDE) + block, BF16),
            pltpu.VMEM((3, 2, SIDE) + block, BF16),
            pltpu.VMEM((2, SIDE) + block, BF16),
            pltpu.VMEM((2, 2, SIDE) + block, BF16),
            pltpu.VMEM((3, 2) + block, BF16),
            pltpu.VMEM((3, 2) + block, BF16),
            dma,
            dma,
            dma((2, 2, hops)),
            dma((2, 2, hops)),
            dma((SIDE,)),
            dma((SIDE,)),
            dma((2,)),
            dma((2,)),
            dma((2, 2)),
            dma((2, 2)),
            dma((3,)),
            dma((3,)),
        ],
        compiler_params=pltpu.CompilerParams(
            collective_id=0, has_side_effects=True, vmem_limit_bytes=40 * 2**20
        ),
        cost_estimate=pl.CostEstimate(
            flops=2 * 10**9, bytes_accessed=4 * 2**20, transcendentals=4 * 10**6
        ),
    )(
        basis_centers,
        bra_pairs,
        ket_pairs.reshape(1, PAIRS),
        quartets,
        quartet_counts,
        density_owner,
        density_store,
    )


def solution(mesh):
    return jax.shard_map(
        local,
        mesh=mesh,
        in_specs=(
            P(),
            P("bra"),
            P("ket"),
            P("bra", "ket", None, None),
            P("bra", "ket"),
            P("ket", None),
            P("bra", "ket", None),
        ),
        out_specs=P("bra", "ket"),
        check_vma=False,
    )
```

```python
import jax
import jax.numpy as jnp
from jax import lax
from jax.experimental import pallas as pl
from jax.experimental.pallas import tpu as pltpu
from jax.sharding import PartitionSpec as P

OMEGA = 0.11
SOFTEN = 0.25
BLOCK = 128
NBLK = 64
PAIRS = 32
RING = 8
DEEP = 2
SIDE = 4
OWN = 4
HALF = 64
GROUP = 8
MESH = pl.DeviceIdType.MESH
F32 = jnp.float32
BF16 = jnp.bfloat16

SLOPE = 0.6 * OMEGA
DECAY = -OMEGA * OMEGA * 1.4426950408889634
ERFC = (
    0.33856715,
    0.33711259,
    0.29264139,
    0.06933287,
    0.29272546,
    -0.65555156,
    0.41918066,
    -0.09400974,
)


def kernel_value(squared):
    inverse = lax.rsqrt(squared)
    divisor = 1.0 + SLOPE * (squared * inverse)
    t = pl.reciprocal(divisor, approx=True)
    t = t * (2.0 - divisor * t)
    poly = ERFC[-1] * t + ERFC[-2]
    for c in ERFC[-3::-1]:
        poly = poly * t + c
    return jnp.exp2(DECAY * squared) * (t * inverse) * poly


def body(
    centers_hbm,
    bra_hbm,
    ket_hbm,
    quartets_hbm,
    count,
    owner_hbm,
    density_hbm,
    out,
    centers,
    bra_pairs,
    ket_pairs,
    quartets,
    owner,
    slots_vmem,
    slots,
    fetch,
    gathered,
    lines,
    columns,
    bra_tiles,
    ket_tiles,
    spread,
    product,
    weighted,
    keep,
    sib_out,
    sib_in,
    x_out,
    rel_in,
    x_in,
    z_out,
    z_in,
    part_send,
    part_recv,
    ring_send,
    ring_recv,
    sib_send,
    sib_recv,
    rel_send,
    rel_recv,
    x_send,
    x_recv,
    z_send,
    z_recv,
):
    row = lax.axis_index("bra")
    col = lax.axis_index("ket")
    y, deep = row // DEEP, row % DEEP
    core = col % 2
    zl = (col // 2) % SIDE
    xx = col // (2 * SIDE)

    def at_row(yy, dd):
        return lax.rem(yy + 2 * RING, RING) * DEEP + dd

    def at_col(x_at, z_at, core_at):
        return (lax.rem(x_at + SIDE, SIDE) * SIDE + z_at) * 2 + core_at

    up, down = at_row(y + 1, deep), at_row(y - 1, deep)
    partner = at_row(y, 1 - deep)
    sibling = at_col(xx, zl, 1 - core)
    x_up, x_down = at_col(xx + 1, zl, core), at_col(xx - 1, zl, core)

    def z_at(step):
        return lax.rem(zl + step, SIDE)

    peers = [(up, col), (down, col), (partner, col), (row, sibling), (row, x_up), (row, x_down)]
    peers += [(row, at_col(xx, z_at(step), core)) for step in range(1, SIDE)]
    barrier = pltpu.get_barrier_semaphore()
    for peer in peers:
        pl.semaphore_signal(barrier, inc=1, device_id=peer, device_id_type=MESH)
    own_slots = gathered.at[pl.ds(row * OWN, OWN)]
    sources = (density_hbm, ket_hbm, bra_hbm, centers_hbm, owner_hbm, quartets_hbm)
    places = (own_slots, ket_pairs, bra_pairs, centers, owner, quartets)
    fetches = [
        pltpu.make_async_copy(src, dst, fetch.at[n])
        for n, (src, dst) in enumerate(zip(sources, places))
    ]
    for copy in fetches:
        copy.start()
    fetches[0].wait()
    pl.semaphore_wait(barrier, len(peers))

    def remote(src, dst, send, recv, device):
        return pltpu.make_async_remote_copy(
            src_ref=src,
            dst_ref=dst,
            send_sem=send,
            recv_sem=recv,
            device_id=device,
            device_id_type=MESH,
        )

    to_partner = remote(own_slots, own_slots, part_send, part_recv, (partner, col))
    to_partner.start()

    def hop(family, way, m, arriving):
        sign = 1 - 2 * way
        dd = deep if family == 0 else 1 - deep
        back = m // OWN + arriving
        slot = at_row(y - sign * back, dd) * OWN + lax.rem(m + 2 * way, OWN)
        ref = gathered.at[pl.ds(slot, 1)]
        device = (up, col) if way == 0 else (down, col)
        return remote(
            ref, ref, ring_send.at[family, way, m], ring_recv.at[family, way, m], device
        )

    last = 3 * OWN + OWN // 2

    def first_sends(family):
        for m in range(OWN):
            for way in range(2):
                hop(family, way, m, 0).start()

    def forward(family, m):
        for way in range(2):
            hop(family, way, m - OWN, 1).wait_recv()
            hop(family, way, m, 0).start()

    first_sends(0)
    for copy in fetches[1:]:
        copy.wait()

    lane = lax.broadcasted_iota(jnp.int32, (8, BLOCK), 1)
    table = jnp.full((8, BLOCK), PAIRS, jnp.int32)
    for q in range(PAIRS):
        table = jnp.where(lane == ket_pairs[q], q, table)
    slots_vmem[...] = table
    to_slots = pltpu.make_async_copy(slots_vmem, slots, fetch.at[len(fetches)])
    to_slots.start()
    ket_tiles[PAIRS] = jnp.zeros((BLOCK, BLOCK), BF16)
    weighted[PAIRS] = jnp.zeros((BLOCK, BLOCK), F32)

    for block in range(NBLK):
        lines[block, 0:3] = centers[:, block * BLOCK : (block + 1) * BLOCK]
    for side, start in ((0, row * (NBLK // 16)), (1, col * (NBLK // 32))):
        line = lines[start]
        for axis in range(3):
            wide = jnp.broadcast_to(line[axis : axis + 1], (BLOCK, BLOCK))
            columns[side, axis] = wide.T

    def tile(side, block, ref, place):
        line = lines[block]
        rows = 32
        for part in range(BLOCK // rows):
            squared = jnp.full((rows, BLOCK), SOFTEN, F32)
            for axis in range(3):
                difference = columns[side, axis, pl.ds(part * rows, rows)] - line[axis : axis + 1]
                squared = squared + difference * difference
            ref[place, pl.ds(part * rows, rows)] = kernel_value(squared).astype(BF16)

    def ket_tile(q):
        tile(1, ket_pairs[q], ket_tiles, q)

    def bra_tile(p):
        tile(0, bra_pairs[p], bra_tiles, p)

    entry = lax.broadcasted_iota(jnp.int32, (PAIRS, quartets.shape[3]), 1)
    slot = lax.broadcasted_iota(jnp.int32, (PAIRS, quartets.shape[3]), 0)
    one, zero = jnp.float32(1.0), jnp.float32(0.0)
    bra_hot = jnp.where(
        (quartets[0, 0, 0:1] == slot) & (entry < count[0, 0]), one, zero
    ).astype(BF16)
    ket_hot = jnp.where(quartets[0, 0, 1:2] == slot, one, zero).astype(BF16)
    counts = lax.dot_general(
        ket_hot, bra_hot, (((1,), (1,)), ((), ())), preferred_element_type=F32
    ).astype(BF16)
    size = PAIRS * GROUP

    def iota(shape, axis):
        return lax.broadcasted_iota(jnp.int32, shape, axis)

    tall = jnp.where(iota((size, PAIRS), 0) // GROUP == iota((size, PAIRS), 1), one, zero)
    wide = jnp.where(iota((PAIRS, size), 1) // GROUP == iota((PAIRS, size), 0), one, zero)
    same = iota((size, size), 0) % GROUP == iota((size, size), 1) % GROUP
    rows = jnp.dot(tall.astype(BF16), counts, preferred_element_type=F32).astype(BF16)
    spread[...] = jnp.where(
        same, jnp.dot(rows, wide.astype(BF16), preferred_element_type=F32), zero
    ).astype(BF16)

    @pl.loop(OWN, last)
    def _(m):
        forward(0, m)
        for extra in range(3):
            bra_tile((m - OWN) * 3 + extra)

    to_partner.wait()
    first_sends(1)
    for p in (30, 31):
        bra_tile(p)
    for q in (0, 1):
        ket_tile(q)

    @pl.loop(OWN, last)
    def _(m):
        forward(1, m)
        for extra in range(3):
            ket_tile(2 + (m - OWN) * 3 + extra)

    to_slots.wait()

    @pl.loop(last - OWN, last)
    def _(m):
        for family in range(2):
            for way in range(2):
                hop(family, way, m, 1).wait_recv()

    @pl.loop(0, PAIRS // 4)
    def _(n):
        for extra in range(4):
            p = n * 4 + extra
            block = gathered[owner[0, bra_pairs[p]]]
            z = jnp.dot(bra_tiles[p], block, preferred_element_type=F32)
            product[p] = z.astype(BF16).astype(F32)

    @pl.loop(0, BLOCK // GROUP // 2)
    def _(n):
        base = pl.multiple_of(n * 2 * GROUP, 2 * GROUP)
        halves = [
            product[:, pl.ds(base + half * GROUP, GROUP), :]
            .reshape(PAIRS * GROUP, BLOCK)
            .astype(BF16)
            for half in range(2)
        ]
        both = jnp.dot(
            spread[...], jnp.concatenate(halves, axis=1), preferred_element_type=F32
        )
        for half in range(2):
            weighted[0:PAIRS, pl.ds(base + half * GROUP, GROUP), :] = both[
                :, half * BLOCK : (half + 1) * BLOCK
            ].reshape(PAIRS, GROUP, BLOCK)

    def image(j):
        q = slots[0, j]
        return jnp.dot(weighted[q].astype(BF16), ket_tiles[q], preferred_element_type=F32)

    def to_sibling(d):
        return remote(
            sib_out.at[d], sib_in.at[d], sib_send.at[d], sib_recv.at[d], (row, sibling)
        )

    def images(d):
        base = lax.rem(xx + d, SIDE) * 4 * SIDE

        @pl.loop(0, SIDE)
        def _(zz):
            for jj in range(2):
                sib_out[d, jj, zz] = image(base + zz * 4 + (1 - core) * 2 + jj).astype(BF16)

        to_sibling(d).start()

        @pl.loop(0, SIDE)
        def _(zz):
            for jj in range(2):
                keep[d, jj, zz] = image(base + zz * 4 + core * 2 + jj)

    def half_rows(half):
        return pl.ds(half * HALF, HALF)

    def chip_sum(d, jj, half):
        rows = half_rows(half)
        return keep[d, jj, :, rows] + sib_in[d, jj, :, rows].astype(F32)

    def relay(way, half):
        device = (row, x_up) if way == 0 else (row, x_down)
        return remote(
            x_out.at[half, 2, way],
            rel_in.at[half, way],
            rel_send.at[half, way],
            rel_recv.at[half, way],
            device,
        )

    def to_x(way, jj, half):
        device = (row, x_up) if way == 0 else (row, x_down)
        return remote(
            x_out.at[half, way, jj],
            x_in.at[half, way, jj],
            x_send.at[half, way, jj],
            x_recv.at[half, way, jj],
            device,
        )

    def to_z(step, half):
        return remote(
            z_out.at[half, step - 1],
            z_in.at[half, step - 1],
            z_send.at[half, step - 1],
            z_recv.at[half, step - 1],
            (row, at_col(xx, z_at(step), core)),
        )

    def direct(half):
        for way, d in ((0, 1), (1, 3)):
            x_out[half, way, 1 - way] = chip_sum(d, 1 - way, half).astype(BF16)
            to_x(way, 1 - way, half).start()

    def summed(half):
        for way, d in ((0, 1), (1, 3)):
            relay(way, half).wait_recv()
            x_out[half, way, way] = (
                chip_sum(d, way, half) + rel_in[half, way].astype(F32)
            ).astype(BF16)
            to_x(way, way, half).start()

    def own_sum(half):
        rows = half_rows(half)
        for jj in range(2):
            keep[0, jj, :, rows] = chip_sum(0, jj, half)

    def from_x(half):
        rows = half_rows(half)
        for jj in range(2):
            for way in (1 - jj, jj):
                to_x(way, jj, half).wait_recv()
                keep[0, jj, :, rows] = keep[0, jj, :, rows] + x_in[half, way, jj].astype(F32)
        for step in (2, 3, 1):
            for jj in range(2):
                z_out[half, step - 1, jj] = keep[0, jj, z_at(step), rows].astype(BF16)
            to_z(step, half).start()

    def finish(half):
        rows = half_rows(half)
        for step in (1, 3, 2):
            to_z(step, half).wait_recv()
        for jj in range(2):
            total = keep[0, jj, zl, rows]
            for step in range(1, SIDE):
                total = total + z_in[half, step - 1, jj].astype(F32)
            out[rows, jj * BLOCK : (jj + 1) * BLOCK] = total.astype(BF16)

    images(2)
    images(1)
    to_sibling(2).wait_recv()
    for half in range(2):
        for way in range(2):
            x_out[half, 2, way] = chip_sum(2, way, half).astype(BF16)
            relay(way, half).start()
    images(3)
    images(0)
    to_sibling(1).wait_recv()
    to_sibling(3).wait_recv()
    direct(0)
    summed(0)
    direct(1)
    summed(1)
    to_sibling(0).wait_recv()
    own_sum(0)
    own_sum(1)
    from_x(0)

    @pl.loop(0, last)
    def _(m):
        for family in range(2):
            for way in range(2):
                hop(family, way, m, 0).wait_send()

    from_x(1)
    finish(0)
    for d in range(SIDE):
        to_sibling(d).wait_send()
    for half in range(2):
        for way in range(2):
            relay(way, half).wait_send()
            for jj in range(2):
                to_x(way, jj, half).wait_send()
        for step in range(1, SIDE):
            to_z(step, half).wait_send()
    finish(1)


def local(
    basis_centers, bra_pairs, ket_pairs, quartets, quartet_counts, density_owner, density_store
):
    hbm = pl.BlockSpec(memory_space=pltpu.HBM)
    smem, i32 = pltpu.SMEM, jnp.int32
    block, half = (BLOCK, BLOCK), (HALF, BLOCK)
    dma = pltpu.SemaphoreType.DMA
    hops = 3 * OWN + OWN // 2
    return pl.pallas_call(
        body,
        out_shape=jax.ShapeDtypeStruct((BLOCK, 2 * BLOCK), BF16),
        in_specs=[hbm] * 4 + [pl.BlockSpec(memory_space=smem)] + [hbm] * 2,
        out_specs=pl.BlockSpec(memory_space=pltpu.VMEM),
        scratch_shapes=[
            pltpu.VMEM(basis_centers.shape, F32),
            smem(bra_pairs.shape, i32),
            smem(ket_pairs.shape, i32),
            pltpu.VMEM(quartets.shape, i32),
            smem(density_owner.shape, i32),
            pltpu.VMEM((8, BLOCK), i32),
            smem((8, BLOCK), i32),
            dma((7,)),
            pltpu.VMEM((NBLK,) + block, BF16),
            pltpu.VMEM((NBLK, 8, BLOCK), F32),
            pltpu.VMEM((2, 3) + block, F32),
            pltpu.VMEM((PAIRS,) + block, BF16),
            pltpu.VMEM((PAIRS + 1,) + block, BF16),
            pltpu.VMEM((PAIRS * GROUP, PAIRS * GROUP), BF16),
            pltpu.VMEM((PAIRS,) + block, F32),
            pltpu.VMEM((PAIRS + 1,) + block, F32),
            pltpu.VMEM((SIDE, 2, SIDE) + block, F32),
            pltpu.VMEM((SIDE, 2, SIDE) + block, BF16),
            pltpu.VMEM((SIDE, 2, SIDE) + block, BF16),
            pltpu.VMEM((2, 3, 2, SIDE) + half, BF16),
            pltpu.VMEM((2, 2, SIDE) + half, BF16),
            pltpu.VMEM((2, 2, 2, SIDE) + half, BF16),
            pltpu.VMEM((2, 3, 2) + half, BF16),
            pltpu.VMEM((2, 3, 2) + half, BF16),
            dma,
            dma,
            dma((2, 2, hops)),
            dma((2, 2, hops)),
            dma((SIDE,)),
            dma((SIDE,)),
            dma((2, 2)),
            dma((2, 2)),
            dma((2, 2, 2)),
            dma((2, 2, 2)),
            dma((2, 3)),
            dma((2, 3)),
        ],
        compiler_params=pltpu.CompilerParams(
            collective_id=0, has_side_effects=True, vmem_limit_bytes=56 * 2**20
        ),
        cost_estimate=pl.CostEstimate(
            flops=2 * 10**9, bytes_accessed=4 * 2**20, transcendentals=4 * 10**6
        ),
    )(
        basis_centers,
        bra_pairs,
        ket_pairs,
        quartets,
        quartet_counts,
        density_owner,
        density_store,
    )


def solution(mesh):
    return jax.shard_map(
        local,
        mesh=mesh,
        in_specs=(
            P(),
            P("bra"),
            P("ket"),
            P("bra", "ket", None, None),
            P("bra", "ket"),
            P("ket", None),
            P("bra", "ket", None),
        ),
        out_specs=P("bra", "ket"),
        check_vma=False,
    )
```

```python
import jax
import jax.numpy as jnp
from jax import lax
from jax.experimental import pallas as pl
from jax.experimental.pallas import tpu as pltpu
from jax.sharding import PartitionSpec as P

OMEGA = 0.11
SOFTEN = 0.25
BLOCK = 128
NBLK = 64
PAIRS = 32
RING = 8
DEEP = 2
SIDE = 4
OWN = 4
HALF = 64
GROUP = 8
MESH = pl.DeviceIdType.MESH
F32 = jnp.float32
BF16 = jnp.bfloat16

SLOPE = 0.6 * OMEGA
DECAY = -OMEGA * OMEGA * 1.4426950408889634
ERFC = (
    0.33856715,
    0.33711259,
    0.29264139,
    0.06933287,
    0.29272546,
    -0.65555156,
    0.41918066,
    -0.09400974,
)


def kernel_value(squared):
    inverse = lax.rsqrt(squared)
    divisor = 1.0 + SLOPE * (squared * inverse)
    t = pl.reciprocal(divisor, approx=True)
    t = t * (2.0 - divisor * t)
    poly = ERFC[-1] * t + ERFC[-2]
    for c in ERFC[-3::-1]:
        poly = poly * t + c
    return jnp.exp2(DECAY * squared) * (t * inverse) * poly


def body(
    centers_hbm,
    bra_hbm,
    ket_hbm,
    quartets_hbm,
    count,
    owner_hbm,
    density_hbm,
    out,
    centers,
    bra_pairs,
    ket_pairs,
    quartets,
    owner,
    slots_vmem,
    slots,
    sib_slots_vmem,
    sib_slots,
    places_vmem,
    places,
    fetch,
    gathered,
    lines,
    columns,
    bra_tiles,
    ket_tiles,
    sib_tiles,
    spread,
    product,
    weighted,
    w_low,
    w_high,
    sib_low,
    sib_high,
    keep,
    x_out,
    rel_in,
    x_in,
    z_out,
    z_in,
    part_send,
    part_recv,
    ring_send,
    ring_recv,
    sib_send,
    sib_recv,
    rel_send,
    rel_recv,
    x_send,
    x_recv,
    z_send,
    z_recv,
):
    row = lax.axis_index("bra")
    col = lax.axis_index("ket")
    y, deep = row // DEEP, row % DEEP
    core = col % 2
    zl = (col // 2) % SIDE
    xx = col // (2 * SIDE)
    w_own, w_sib = (w_low, w_high), (sib_low, sib_high)

    def at_row(yy, dd):
        return lax.rem(yy + 2 * RING, RING) * DEEP + dd

    def at_col(x_at, z_at, core_at):
        return (lax.rem(x_at + SIDE, SIDE) * SIDE + z_at) * 2 + core_at

    up, down = at_row(y + 1, deep), at_row(y - 1, deep)
    partner = at_row(y, 1 - deep)
    sibling = at_col(xx, zl, 1 - core)
    x_up, x_down = at_col(xx + 1, zl, core), at_col(xx - 1, zl, core)

    def z_at(step):
        return lax.rem(zl + step, SIDE)

    peers = [(up, col), (down, col), (partner, col), (row, sibling), (row, x_up), (row, x_down)]
    peers += [(row, at_col(xx, z_at(step), core)) for step in range(1, SIDE)]
    barrier = pltpu.get_barrier_semaphore()
    for peer in peers:
        pl.semaphore_signal(barrier, inc=1, device_id=peer, device_id_type=MESH)
    own_slots = gathered.at[pl.ds(row * OWN, OWN)]
    sources = (ket_hbm, bra_hbm, centers_hbm, owner_hbm, quartets_hbm, density_hbm)
    targets = (ket_pairs, bra_pairs, centers, owner, quartets, own_slots)
    fetches = [
        pltpu.make_async_copy(src, dst, fetch.at[n])
        for n, (src, dst) in enumerate(zip(sources, targets))
    ]
    for copy in fetches:
        copy.start()
    for tiles in (bra_tiles, ket_tiles, sib_tiles):
        tiles[PAIRS] = jnp.zeros((BLOCK, BLOCK), BF16)
    for part in w_own + w_sib:
        part[PAIRS] = jnp.zeros((HALF, BLOCK), BF16)
    pl.semaphore_wait(barrier, len(peers))

    def remote(src, dst, send, recv, device):
        return pltpu.make_async_remote_copy(
            src_ref=src,
            dst_ref=dst,
            send_sem=send,
            recv_sem=recv,
            device_id=device,
            device_id_type=MESH,
        )

    to_partner = remote(density_hbm, own_slots, part_send, part_recv, (partner, col))
    to_partner.start()

    def depth(family):
        return deep if family == 0 else 1 - deep

    def hop(family, way, m, arriving, first=False):
        sign = 1 - 2 * way
        back = m // OWN + arriving
        place = lax.rem(m + 2 * way, OWN)
        ref = gathered.at[pl.ds(at_row(y - sign * back, depth(family)) * OWN + place, 1)]
        src = density_hbm.at[pl.ds(place, 1)] if first else ref
        device = (up, col) if way == 0 else (down, col)
        return remote(
            src, ref, ring_send.at[family, way, m], ring_recv.at[family, way, m], device
        )

    last = 3 * OWN + OWN // 2

    def first_sends(family):
        for m in range(OWN):
            for way in range(2):
                hop(family, way, m, 0, family == 0).start()

    def arrive(family, m):
        for way in range(2):
            hop(family, way, m, 1).wait_recv()

    def forward(family, m):
        for way in range(2):
            hop(family, way, m - OWN, 1).wait_recv()
            hop(family, way, m, 0).start()

    first_sends(0)
    for copy in fetches[:-1]:
        copy.wait()

    lane = lax.broadcasted_iota(jnp.int32, (8, BLOCK), 1)
    ket_table = jnp.full((8, BLOCK), PAIRS, jnp.int32)
    bra_table = jnp.full((8, BLOCK), PAIRS, jnp.int32)
    for n in range(PAIRS):
        ket_table = jnp.where(lane == ket_pairs[n], n, ket_table)
        bra_table = jnp.where(lane == owner[0, bra_pairs[n]], n, bra_table)
    slots_vmem[...] = ket_table
    places_vmem[...] = bra_table
    to_slots = pltpu.make_async_copy(slots_vmem, slots, fetch.at[len(fetches)])
    to_slots.start()
    to_places = pltpu.make_async_copy(places_vmem, places, fetch.at[len(fetches) + 1])
    to_places.start()
    there = (row, sibling)
    table_swap = remote(slots_vmem, sib_slots_vmem, sib_send.at[0], sib_recv.at[0], there)
    table_swap.start()

    for block in range(NBLK):
        lines[block, 0:3] = centers[:, block * BLOCK : (block + 1) * BLOCK]
    for side, start in ((0, row * (NBLK // 16)), (1, col * (NBLK // 32))):
        line = lines[start]
        for axis in range(3):
            wide = jnp.broadcast_to(line[axis : axis + 1], (BLOCK, BLOCK))
            columns[side, axis] = wide.T

    def tile(side, block, ref, place):
        line = lines[block]
        rows = 32
        for part in range(BLOCK // rows):
            squared = jnp.full((rows, BLOCK), SOFTEN, F32)
            for axis in range(3):
                difference = columns[side, axis, pl.ds(part * rows, rows)] - line[axis : axis + 1]
                squared = squared + difference * difference
            ref[place, pl.ds(part * rows, rows)] = kernel_value(squared).astype(BF16)

    def ket_tile(q):
        tile(1, ket_pairs[q], ket_tiles, q)

    def bra_tile(p):
        tile(0, bra_pairs[p], bra_tiles, p)

    def iota(shape, axis):
        return lax.broadcasted_iota(jnp.int32, shape, axis)

    def hot(condition):
        return jnp.where(condition, jnp.float32(1.0), jnp.float32(0.0)).astype(BF16)

    long = (PAIRS, quartets.shape[3])
    bra_hot = hot((quartets[0, 0, 0:1] == iota(long, 0)) & (iota(long, 1) < count[0, 0]))
    ket_hot = hot(quartets[0, 0, 1:2] == iota(long, 0))
    counts = lax.dot_general(
        ket_hot, bra_hot, (((1,), (1,)), ((), ())), preferred_element_type=F32
    ).astype(BF16)
    size = PAIRS * GROUP
    by_slot = jnp.dot(
        counts, hot(bra_table[0:1] == iota((PAIRS, BLOCK), 0)), preferred_element_type=F32
    ).astype(BF16)
    tall = hot(iota((size, PAIRS), 0) // GROUP == iota((size, PAIRS), 1))
    rows_of = jnp.dot(tall, by_slot, preferred_element_type=F32).astype(BF16)
    same = iota((size, size), 0) % GROUP == iota((size, size), 1) % GROUP
    local_slot = iota((BLOCK, size), 1) // GROUP
    row_slot = (local_slot // OWN) * (OWN * DEEP) + local_slot % OWN
    for family in range(2):
        wide = hot(row_slot + depth(family) * OWN == iota((BLOCK, size), 0))
        spread[family] = jnp.where(
            same, jnp.dot(rows_of, wide, preferred_element_type=F32), jnp.float32(0.0)
        ).astype(BF16)

    def z_row(family, yy):
        at = lax.rem(yy + 2 * RING, RING)
        for extra in range(OWN):
            s = (at * DEEP + depth(family)) * OWN + extra
            z = jnp.dot(bra_tiles[places[0, s]], gathered[s], preferred_element_type=F32)
            product[family, at * OWN + extra] = z.astype(BF16).astype(F32)

    def w_part(family, n):
        base = pl.multiple_of(n * 2 * GROUP, 2 * GROUP)
        halves = [
            product[family, :, pl.ds(base + half * GROUP, GROUP), :]
            .reshape(size, BLOCK)
            .astype(BF16)
            for half in range(2)
        ]
        both = jnp.dot(
            spread[family], jnp.concatenate(halves, axis=1), preferred_element_type=F32
        )
        return jnp.concatenate(
            [
                both[:, half * BLOCK : (half + 1) * BLOCK].reshape(PAIRS, GROUP, BLOCK)
                for half in range(2)
            ],
            axis=1,
        )

    @pl.loop(OWN, 3 * OWN)
    def _(m):
        forward(0, m)
        for extra in range(4):
            bra_tile((m - OWN) * 4 + extra)
        ket_tile(m - OWN)

    @pl.loop(3 * OWN, last)
    def _(m):
        forward(0, m)
        for extra in range(5):
            ket_tile(8 + (m - 3 * OWN) * 5 + extra)

    to_partner.wait()
    first_sends(1)

    @pl.loop(0, 7)
    def _(n):
        for extra in range(2):
            ket_tile(18 + n * 2 + extra)

    swapped = ket_tiles.at[pl.ds(0, PAIRS)]
    tile_swap = remote(
        swapped, sib_tiles.at[pl.ds(0, PAIRS)], sib_send.at[1], sib_recv.at[1], there
    )
    tile_swap.start()
    to_places.wait()
    fetches[-1].wait()
    for m in range(last - OWN, last):
        arrive(0, m)

    @pl.loop(OWN, 2 * OWN)
    def _(m):
        forward(1, m)
        for extra in range(2):
            z_row(0, (m - OWN) * 2 + extra)

    @pl.loop(2 * OWN, 3 * OWN)
    def _(m):
        forward(1, m)
        for extra in range(2):
            n = (m - 2 * OWN) * 2 + extra
            weighted[:, pl.ds(n * 2 * GROUP, 2 * GROUP)] = w_part(0, n)

    forward(1, 3 * OWN)
    z_row(1, y)
    z_row(1, y - 1)
    forward(1, 3 * OWN + 1)
    z_row(1, y + 1)
    z_row(1, y - 2)
    z_row(1, y + 2)
    arrive(1, last - 4)
    arrive(1, last - 3)
    z_row(1, y - 3)
    z_row(1, y + 3)
    table_swap.wait()
    sib_to_slots = pltpu.make_async_copy(sib_slots_vmem, sib_slots, fetch.at[len(fetches) + 2])
    sib_to_slots.start()
    arrive(1, last - 2)
    arrive(1, last - 1)
    z_row(1, y + 4)

    def w_swap(half):
        return remote(
            w_own[half].at[pl.ds(0, PAIRS)],
            w_sib[half].at[pl.ds(0, PAIRS)],
            sib_send.at[2 + half],
            sib_recv.at[2 + half],
            there,
        )

    for half in range(2):

        @pl.loop(0, HALF // GROUP // 2)
        def _(n):
            at = pl.multiple_of(n * 2 * GROUP, 2 * GROUP)
            total = w_part(1, n + half * (HALF // GROUP // 2))
            total = total + weighted[:, pl.ds(at + half * HALF, 2 * GROUP)]
            w_own[half][0:PAIRS, pl.ds(at, 2 * GROUP)] = total.astype(BF16)

        w_swap(half).start()

    def image(d, zz, jj, half):
        j = (lax.rem(xx + d, SIDE) * SIDE + zz) * 4 + core * 2 + jj
        a, b = slots[0, j], sib_slots[0, j]
        left = jnp.concatenate([w_own[half][a], w_sib[half][b]], axis=1)
        right = jnp.concatenate([ket_tiles[a], sib_tiles[b]], axis=0)
        return jnp.dot(left, right, preferred_element_type=F32)

    def relay(way, half):
        device = (row, x_up) if way == 0 else (row, x_down)
        return remote(
            x_out.at[half, 2, way],
            rel_in.at[half, way],
            rel_send.at[half, way],
            rel_recv.at[half, way],
            device,
        )

    def to_x(way, jj, half):
        device = (row, x_up) if way == 0 else (row, x_down)
        return remote(
            x_out.at[half, way, jj],
            x_in.at[half, way, jj],
            x_send.at[half, way, jj],
            x_recv.at[half, way, jj],
            device,
        )

    def to_z(step, half):
        return remote(
            z_out.at[half, step - 1],
            z_in.at[half, step - 1],
            z_send.at[half, step - 1],
            z_recv.at[half, step - 1],
            (row, at_col(xx, z_at(step), core)),
        )

    def relays(half):
        for way in range(2):
            for zz in range(SIDE):
                x_out[half, 2, way, zz] = image(2, zz, way, half).astype(BF16)
            relay(way, half).start()

    def direct(half):
        for way, d in ((0, 1), (1, 3)):
            for zz in range(SIDE):
                x_out[half, way, 1 - way, zz] = image(d, zz, 1 - way, half).astype(BF16)
            to_x(way, 1 - way, half).start()

    def summed(half):
        for way, d in ((0, 1), (1, 3)):
            images = [image(d, zz, way, half) for zz in range(SIDE)]
            relay(way, half).wait_recv()
            for zz in range(SIDE):
                total = images[zz] + rel_in[half, way, zz].astype(F32)
                x_out[half, way, way, zz] = total.astype(BF16)
            to_x(way, way, half).start()

    def own_sum(half):
        for jj in range(2):
            for zz in range(SIDE):
                keep[half, jj, zz] = image(0, zz, jj, half)

    def from_x(half):
        for jj in range(2):
            for way in (1 - jj, jj):
                to_x(way, jj, half).wait_recv()
                keep[half, jj] = keep[half, jj] + x_in[half, way, jj].astype(F32)
        for step in (2, 3, 1):
            for jj in range(2):
                z_out[half, step - 1, jj] = keep[half, jj, z_at(step)].astype(BF16)
            to_z(step, half).start()

    def finish(half):
        for step in (1, 3, 2):
            to_z(step, half).wait_recv()
        rows = pl.ds(half * HALF, HALF)
        for jj in range(2):
            total = keep[half, jj, zl]
            for step in range(1, SIDE):
                total = total + z_in[half, step - 1, jj].astype(F32)
            out[rows, jj * BLOCK : (jj + 1) * BLOCK] = total.astype(BF16)

    to_slots.wait()
    sib_to_slots.wait()
    tile_swap.wait()
    w_swap(0).wait()
    relays(0)
    direct(0)
    w_swap(1).wait()
    relays(1)
    summed(0)
    direct(1)
    own_sum(0)
    summed(1)
    own_sum(1)
    from_x(0)

    @pl.loop(0, last)
    def _(m):
        for family in range(2):
            for way in range(2):
                hop(family, way, m, 0).wait_send()

    from_x(1)
    finish(0)
    for half in range(2):
        for way in range(2):
            relay(way, half).wait_send()
            for jj in range(2):
                to_x(way, jj, half).wait_send()
        for step in range(1, SIDE):
            to_z(step, half).wait_send()
    finish(1)


def local(
    basis_centers, bra_pairs, ket_pairs, quartets, quartet_counts, density_owner, density_store
):
    hbm = pl.BlockSpec(memory_space=pltpu.HBM)
    smem, i32 = pltpu.SMEM, jnp.int32
    block, half = (BLOCK, BLOCK), (HALF, BLOCK)
    dma = pltpu.SemaphoreType.DMA
    hops = 3 * OWN + OWN // 2
    return pl.pallas_call(
        body,
        out_shape=jax.ShapeDtypeStruct((BLOCK, 2 * BLOCK), BF16),
        in_specs=[hbm] * 4 + [pl.BlockSpec(memory_space=smem)] + [hbm] * 2,
        out_specs=pl.BlockSpec(memory_space=pltpu.VMEM),
        scratch_shapes=[
            pltpu.VMEM(basis_centers.shape, F32),
            smem(bra_pairs.shape, i32),
            smem(ket_pairs.shape, i32),
            pltpu.VMEM(quartets.shape, i32),
            smem(density_owner.shape, i32),
            pltpu.VMEM((8, BLOCK), i32),
            smem((8, BLOCK), i32),
            pltpu.VMEM((8, BLOCK), i32),
            smem((8, BLOCK), i32),
            pltpu.VMEM((8, BLOCK), i32),
            smem((8, BLOCK), i32),
            dma((9,)),
            pltpu.VMEM((NBLK,) + block, BF16),
            pltpu.VMEM((NBLK, 8, BLOCK), F32),
            pltpu.VMEM((2, 3) + block, F32),
            pltpu.VMEM((PAIRS + 1,) + block, BF16),
            pltpu.VMEM((PAIRS + 1,) + block, BF16),
            pltpu.VMEM((PAIRS + 1,) + block, BF16),
            pltpu.VMEM((2, PAIRS * GROUP, PAIRS * GROUP), BF16),
            pltpu.VMEM((2, PAIRS) + block, F32),
            pltpu.VMEM((PAIRS,) + block, F32),
            pltpu.VMEM((PAIRS + 1,) + half, BF16),
            pltpu.VMEM((PAIRS + 1,) + half, BF16),
            pltpu.VMEM((PAIRS + 1,) + half, BF16),
            pltpu.VMEM((PAIRS + 1,) + half, BF16),
            pltpu.VMEM((2, 2, SIDE) + half, F32),
            pltpu.VMEM((2, 3, 2, SIDE) + half, BF16),
            pltpu.VMEM((2, 2, SIDE) + half, BF16),
            pltpu.VMEM((2, 2, 2, SIDE) + half, BF16),
            pltpu.VMEM((2, 3, 2) + half, BF16),
            pltpu.VMEM((2, 3, 2) + half, BF16),
            dma,
            dma,
            dma((2, 2, hops)),
            dma((2, 2, hops)),
            dma((4,)),
            dma((4,)),
            dma((2, 2)),
            dma((2, 2)),
            dma((2, 2, 2)),
            dma((2, 2, 2)),
            dma((2, 3)),
            dma((2, 3)),
        ],
        compiler_params=pltpu.CompilerParams(
            collective_id=0, has_side_effects=True, vmem_limit_bytes=56 * 2**20
        ),
        cost_estimate=pl.CostEstimate(
            flops=2 * 10**9, bytes_accessed=4 * 2**20, transcendentals=4 * 10**6
        ),
    )(
        basis_centers,
        bra_pairs,
        ket_pairs,
        quartets,
        quartet_counts,
        density_owner,
        density_store,
    )


def solution(mesh):
    return jax.shard_map(
        local,
        mesh=mesh,
        in_specs=(
            P(),
            P("bra"),
            P("ket"),
            P("bra", "ket", None, None),
            P("bra", "ket"),
            P("ket", None),
            P("bra", "ket", None),
        ),
        out_specs=P("bra", "ket"),
        check_vma=False,
    )
```

```python
import jax
import jax.numpy as jnp
from jax import lax
from jax.experimental import pallas as pl
from jax.experimental.pallas import tpu as pltpu
from jax.sharding import PartitionSpec as P

OMEGA = 0.11
SOFTEN = 0.25
BLOCK = 128
NBLK = 64
PAIRS = 32
RING = 8
DEEP = 2
SIDE = 4
OWN = 4
HALF = 64
GROUP = 8
MESH = pl.DeviceIdType.MESH
F32 = jnp.float32
BF16 = jnp.bfloat16

SLOPE = 0.6 * OMEGA
DECAY = -OMEGA * OMEGA * 1.4426950408889634
ERFC = (
    0.33856715,
    0.33711259,
    0.29264139,
    0.06933287,
    0.29272546,
    -0.65555156,
    0.41918066,
    -0.09400974,
)


def kernel_value(squared):
    inverse = lax.rsqrt(squared)
    divisor = 1.0 + SLOPE * (squared * inverse)
    t = pl.reciprocal(divisor, approx=True)
    t = t * (2.0 - divisor * t)
    poly = ERFC[-1] * t + ERFC[-2]
    for c in ERFC[-3::-1]:
        poly = poly * t + c
    return jnp.exp2(DECAY * squared) * (t * inverse) * poly


def body(
    centers_hbm,
    bra_hbm,
    ket_hbm,
    quartets_hbm,
    count,
    owner_hbm,
    density_hbm,
    out,
    centers,
    bra_pairs,
    ket_pairs,
    quartets,
    owner,
    slots_vmem,
    slots,
    sib_slots_vmem,
    sib_slots,
    places_vmem,
    places,
    fetch,
    gathered,
    lines,
    columns,
    bra_tiles,
    ket_tiles,
    sib_tiles,
    spread,
    product,
    weighted,
    w_low,
    w_high,
    sib_low,
    sib_high,
    keep,
    x_out,
    rel_in,
    x_in,
    z_out,
    z_in,
    part_send,
    part_recv,
    ring_send,
    ring_recv,
    sib_send,
    sib_recv,
    rel_send,
    rel_recv,
    x_send,
    x_recv,
    z_send,
    z_recv,
):
    row = lax.axis_index("bra")
    col = lax.axis_index("ket")
    y, deep = row // DEEP, row % DEEP
    core = col % 2
    zl = (col // 2) % SIDE
    xx = col // (2 * SIDE)
    w_own, w_sib = (w_low, w_high), (sib_low, sib_high)

    def at_row(yy, dd):
        return lax.rem(yy + 2 * RING, RING) * DEEP + dd

    def at_col(x_at, z_at, core_at):
        return (lax.rem(x_at + SIDE, SIDE) * SIDE + z_at) * 2 + core_at

    up, down = at_row(y + 1, deep), at_row(y - 1, deep)
    partner = at_row(y, 1 - deep)
    sibling = at_col(xx, zl, 1 - core)
    x_up, x_down = at_col(xx + 1, zl, core), at_col(xx - 1, zl, core)

    def z_at(step):
        return lax.rem(zl + step, SIDE)

    peers = [(up, col), (down, col), (partner, col), (row, sibling), (row, x_up), (row, x_down)]
    peers += [(row, at_col(xx, z_at(step), core)) for step in range(1, SIDE)]
    barrier = pltpu.get_barrier_semaphore()
    for peer in peers:
        pl.semaphore_signal(barrier, inc=1, device_id=peer, device_id_type=MESH)
    own_slots = gathered.at[pl.ds(row * OWN, OWN)]
    sources = (ket_hbm, bra_hbm, centers_hbm, owner_hbm, quartets_hbm, density_hbm)
    targets = (ket_pairs, bra_pairs, centers, owner, quartets, own_slots)
    fetches = [
        pltpu.make_async_copy(src, dst, fetch.at[n])
        for n, (src, dst) in enumerate(zip(sources, targets))
    ]
    for copy in fetches:
        copy.start()
    for tiles in (bra_tiles, ket_tiles, sib_tiles):
        tiles[PAIRS] = jnp.zeros((BLOCK, BLOCK), BF16)
    for part in w_own + w_sib:
        part[PAIRS] = jnp.zeros((HALF, BLOCK), BF16)
    pl.semaphore_wait(barrier, len(peers))

    def remote(src, dst, send, recv, device):
        return pltpu.make_async_remote_copy(
            src_ref=src,
            dst_ref=dst,
            send_sem=send,
            recv_sem=recv,
            device_id=device,
            device_id_type=MESH,
        )

    def to_partner(place):
        return remote(
            density_hbm.at[pl.ds(place, 1)],
            gathered.at[pl.ds(row * OWN + place, 1)],
            part_send.at[place],
            part_recv.at[place],
            (partner, col),
        )

    for place in (0, 2, 1, 3):
        to_partner(place).start()

    def depth(family):
        return deep if family == 0 else 1 - deep

    def hop(family, way, m, arriving, first=False):
        sign = 1 - 2 * way
        back = m // OWN + arriving
        place = lax.rem(m + 2 * way, OWN)
        ref = gathered.at[pl.ds(at_row(y - sign * back, depth(family)) * OWN + place, 1)]
        src = density_hbm.at[pl.ds(place, 1)] if first else ref
        device = (up, col) if way == 0 else (down, col)
        return remote(
            src, ref, ring_send.at[family, way, m], ring_recv.at[family, way, m], device
        )

    last = 3 * OWN + OWN // 2

    def send_own(family, m):
        for way in range(2):
            hop(family, way, m, 0, family == 0).start()

    def arrive(family, m):
        for way in range(2):
            hop(family, way, m, 1).wait_recv()

    def forward(family, m):
        for way in range(2):
            hop(family, way, m - OWN, 1).wait_recv()
            hop(family, way, m, 0).start()

    for m in range(OWN):
        send_own(0, m)
    for copy in fetches[:-1]:
        copy.wait()

    lane = lax.broadcasted_iota(jnp.int32, (8, BLOCK), 1)
    ket_table = jnp.full((8, BLOCK), PAIRS, jnp.int32)
    bra_table = jnp.full((8, BLOCK), PAIRS, jnp.int32)
    for n in range(PAIRS):
        ket_table = jnp.where(lane == ket_pairs[n], n, ket_table)
        bra_table = jnp.where(lane == owner[0, bra_pairs[n]], n, bra_table)
    slots_vmem[...] = ket_table
    places_vmem[...] = bra_table
    to_slots = pltpu.make_async_copy(slots_vmem, slots, fetch.at[len(fetches)])
    to_slots.start()
    to_places = pltpu.make_async_copy(places_vmem, places, fetch.at[len(fetches) + 1])
    to_places.start()
    there = (row, sibling)
    table_swap = remote(slots_vmem, sib_slots_vmem, sib_send.at[0], sib_recv.at[0], there)
    table_swap.start()

    for block in range(NBLK):
        lines[block, 0:3] = centers[:, block * BLOCK : (block + 1) * BLOCK]
    for side, start in ((0, row * (NBLK // 16)), (1, col * (NBLK // 32))):
        line = lines[start]
        for axis in range(3):
            wide = jnp.broadcast_to(line[axis : axis + 1], (BLOCK, BLOCK))
            columns[side, axis] = wide.T

    def tile(side, block, ref, place):
        line = lines[block]
        rows = 32
        for part in range(BLOCK // rows):
            squared = jnp.full((rows, BLOCK), SOFTEN, F32)
            for axis in range(3):
                difference = columns[side, axis, pl.ds(part * rows, rows)] - line[axis : axis + 1]
                squared = squared + difference * difference
            ref[place, pl.ds(part * rows, rows)] = kernel_value(squared).astype(BF16)

    def ket_tile(q):
        tile(1, ket_pairs[q], ket_tiles, q)

    def bra_tile(p):
        tile(0, bra_pairs[p], bra_tiles, p)

    def iota(shape, axis):
        return lax.broadcasted_iota(jnp.int32, shape, axis)

    def hot(condition):
        return jnp.where(condition, jnp.float32(1.0), jnp.float32(0.0)).astype(BF16)

    long = (PAIRS, quartets.shape[3])
    bra_hot = hot((quartets[0, 0, 0:1] == iota(long, 0)) & (iota(long, 1) < count[0, 0]))
    ket_hot = hot(quartets[0, 0, 1:2] == iota(long, 0))
    counts = lax.dot_general(
        ket_hot, bra_hot, (((1,), (1,)), ((), ())), preferred_element_type=F32
    ).astype(BF16)
    size = PAIRS * GROUP
    by_slot = jnp.dot(
        counts, hot(bra_table[0:1] == iota((PAIRS, BLOCK), 0)), preferred_element_type=F32
    ).astype(BF16)
    tall = hot(iota((size, PAIRS), 0) // GROUP == iota((size, PAIRS), 1))
    rows_of = jnp.dot(tall, by_slot, preferred_element_type=F32).astype(BF16)
    same = iota((size, size), 0) % GROUP == iota((size, size), 1) % GROUP
    local_slot = iota((BLOCK, size), 1) // GROUP
    row_slot = (local_slot // OWN) * (OWN * DEEP) + local_slot % OWN
    for family in range(2):
        wide = hot(row_slot + depth(family) * OWN == iota((BLOCK, size), 0))
        spread[family] = jnp.where(
            same, jnp.dot(rows_of, wide, preferred_element_type=F32), jnp.float32(0.0)
        ).astype(BF16)

    def z_row(family, yy):
        at = lax.rem(yy + 2 * RING, RING)
        for extra in range(OWN):
            s = (at * DEEP + depth(family)) * OWN + extra
            z = jnp.dot(bra_tiles[places[0, s]], gathered[s], preferred_element_type=F32)
            product[family, at * OWN + extra] = z.astype(BF16).astype(F32)

    def w_part(family, n):
        base = pl.multiple_of(n * 2 * GROUP, 2 * GROUP)
        halves = [
            product[family, :, pl.ds(base + half * GROUP, GROUP), :]
            .reshape(size, BLOCK)
            .astype(BF16)
            for half in range(2)
        ]
        both = jnp.dot(
            spread[family], jnp.concatenate(halves, axis=1), preferred_element_type=F32
        )
        return jnp.concatenate(
            [
                both[:, half * BLOCK : (half + 1) * BLOCK].reshape(PAIRS, GROUP, BLOCK)
                for half in range(2)
            ],
            axis=1,
        )

    def swap_tiles(src, dst, first, total, index):
        return remote(
            src.at[pl.ds(first, total)],
            dst.at[pl.ds(first, total)],
            sib_send.at[index],
            sib_recv.at[index],
            there,
        )

    mine = core * (PAIRS // 2)
    bra_swap = swap_tiles(bra_tiles, bra_tiles, mine, PAIRS // 2, 1)
    ket_swap = swap_tiles(ket_tiles, sib_tiles, 0, PAIRS, 4)

    def ket_run(first, total):
        @pl.loop(first, first + total)
        def _(q):
            ket_tile(q)

    def w_first(first, total):
        @pl.loop(first, first + total)
        def _(n):
            weighted[:, pl.ds(n * 2 * GROUP, 2 * GROUP)] = w_part(0, n)

    @pl.loop(OWN, 2 * OWN)
    def _(m):
        forward(0, m)

        @pl.loop(0, 4)
        def _(n):
            bra_tile(mine + (m - OWN) * 4 + n)

    bra_swap.start()
    for m in range(OWN):
        forward(0, 2 * OWN + m)
        ket_run(m * 6, 3)
        if m < 2:
            to_partner(m).wait_recv()
            to_partner(m + 2).wait_recv()
        send_own(1, m)
        ket_run(m * 6 + 3, 3)
    for m in range(2):
        forward(1, OWN + m)
        ket_run(24 + m * 4, 2)
        forward(0, 3 * OWN + m)
        ket_run(26 + m * 4, 2)
    ket_swap.start()
    bra_swap.wait()
    to_places.wait()
    fetches[-1].wait()
    forward(1, OWN + 2)
    z_row(0, y)
    z_row(0, y - 1)
    forward(1, OWN + 3)
    z_row(0, y + 1)
    z_row(0, y - 2)
    forward(1, 2 * OWN)
    z_row(0, y + 2)
    arrive(0, last - 4)
    arrive(0, last - 3)
    z_row(0, y - 3)
    forward(1, 2 * OWN + 1)
    z_row(0, y + 3)
    arrive(0, last - 2)
    arrive(0, last - 1)
    z_row(0, y + 4)
    forward(1, 2 * OWN + 2)
    w_first(0, 3)
    forward(1, 2 * OWN + 3)
    w_first(3, 2)
    forward(1, 3 * OWN)
    w_first(5, 1)
    forward(1, 3 * OWN + 1)
    w_first(6, 2)
    for away in (0, 1, -1, 2, -2):
        z_row(1, y + away)
    arrive(1, last - 4)
    arrive(1, last - 3)
    z_row(1, y - 3)
    z_row(1, y + 3)
    table_swap.wait()
    sib_to_slots = pltpu.make_async_copy(sib_slots_vmem, sib_slots, fetch.at[len(fetches) + 2])
    sib_to_slots.start()
    arrive(1, last - 2)
    arrive(1, last - 1)
    z_row(1, y + 4)

    def w_swap(half):
        return remote(
            w_own[half].at[pl.ds(0, PAIRS)],
            w_sib[half].at[pl.ds(0, PAIRS)],
            sib_send.at[2 + half],
            sib_recv.at[2 + half],
            there,
        )

    for half in range(2):

        @pl.loop(0, HALF // GROUP // 2)
        def _(n):
            at = pl.multiple_of(n * 2 * GROUP, 2 * GROUP)
            total = w_part(1, n + half * (HALF // GROUP // 2))
            total = total + weighted[:, pl.ds(at + half * HALF, 2 * GROUP)]
            w_own[half][0:PAIRS, pl.ds(at, 2 * GROUP)] = total.astype(BF16)

        w_swap(half).start()

    def image(d, zz, jj, half):
        j = (lax.rem(xx + d, SIDE) * SIDE + zz) * 4 + core * 2 + jj
        a, b = slots[0, j], sib_slots[0, j]
        left = jnp.concatenate([w_own[half][a], w_sib[half][b]], axis=1)
        right = jnp.concatenate([ket_tiles[a], sib_tiles[b]], axis=0)
        return jnp.dot(left, right, preferred_element_type=F32)

    def relay(way, half):
        device = (row, x_up) if way == 0 else (row, x_down)
        return remote(
            x_out.at[half, 2, way],
            rel_in.at[half, way],
            rel_send.at[half, way],
            rel_recv.at[half, way],
            device,
        )

    def to_x(way, jj, half):
        device = (row, x_up) if way == 0 else (row, x_down)
        return remote(
            x_out.at[half, way, jj],
            x_in.at[half, way, jj],
            x_send.at[half, way, jj],
            x_recv.at[half, way, jj],
            device,
        )

    def to_z(step, half):
        return remote(
            z_out.at[half, step - 1],
            z_in.at[half, step - 1],
            z_send.at[half, step - 1],
            z_recv.at[half, step - 1],
            (row, at_col(xx, z_at(step), core)),
        )

    def relays(half):
        for way in range(2):
            for zz in range(SIDE):
                x_out[half, 2, way, zz] = image(2, zz, way, half).astype(BF16)
            relay(way, half).start()

    def direct(half):
        for way, d in ((0, 1), (1, 3)):
            for zz in range(SIDE):
                x_out[half, way, 1 - way, zz] = image(d, zz, 1 - way, half).astype(BF16)
            to_x(way, 1 - way, half).start()

    def summed(half):
        for way, d in ((0, 1), (1, 3)):
            images = [image(d, zz, way, half) for zz in range(SIDE)]
            relay(way, half).wait_recv()
            for zz in range(SIDE):
                total = images[zz] + rel_in[half, way, zz].astype(F32)
                x_out[half, way, way, zz] = total.astype(BF16)
            to_x(way, way, half).start()

    def own_sum(half):
        for jj in range(2):
            for zz in range(SIDE):
                keep[half, jj, zz] = image(0, zz, jj, half)

    def from_x(half):
        for jj in range(2):
            for way in (1 - jj, jj):
                to_x(way, jj, half).wait_recv()
                keep[half, jj] = keep[half, jj] + x_in[half, way, jj].astype(F32)
        for step in (2, 3, 1):
            for jj in range(2):
                z_out[half, step - 1, jj] = keep[half, jj, z_at(step)].astype(BF16)
            to_z(step, half).start()

    def finish(half):
        for step in (1, 3, 2):
            to_z(step, half).wait_recv()
        rows = pl.ds(half * HALF, HALF)
        for jj in range(2):
            total = keep[half, jj, zl]
            for step in range(1, SIDE):
                total = total + z_in[half, step - 1, jj].astype(F32)
            out[rows, jj * BLOCK : (jj + 1) * BLOCK] = total.astype(BF16)

    to_slots.wait()
    sib_to_slots.wait()
    ket_swap.wait()
    w_swap(0).wait()
    relays(0)
    direct(0)
    w_swap(1).wait()
    relays(1)
    summed(0)
    direct(1)
    own_sum(0)
    summed(1)
    own_sum(1)
    from_x(0)

    @pl.loop(0, last)
    def _(m):
        for family in range(2):
            for way in range(2):
                hop(family, way, m, 0).wait_send()

    for place in range(OWN):
        to_partner(place).wait_send()
    from_x(1)
    finish(0)
    for half in range(2):
        for way in range(2):
            relay(way, half).wait_send()
            for jj in range(2):
                to_x(way, jj, half).wait_send()
        for step in range(1, SIDE):
            to_z(step, half).wait_send()
    finish(1)


def local(
    basis_centers, bra_pairs, ket_pairs, quartets, quartet_counts, density_owner, density_store
):
    hbm = pl.BlockSpec(memory_space=pltpu.HBM)
    smem, i32 = pltpu.SMEM, jnp.int32
    block, half = (BLOCK, BLOCK), (HALF, BLOCK)
    dma = pltpu.SemaphoreType.DMA
    hops = 3 * OWN + OWN // 2
    return pl.pallas_call(
        body,
        out_shape=jax.ShapeDtypeStruct((BLOCK, 2 * BLOCK), BF16),
        in_specs=[hbm] * 4 + [pl.BlockSpec(memory_space=smem)] + [hbm] * 2,
        out_specs=pl.BlockSpec(memory_space=pltpu.VMEM),
        scratch_shapes=[
            pltpu.VMEM(basis_centers.shape, F32),
            smem(bra_pairs.shape, i32),
            smem(ket_pairs.shape, i32),
            pltpu.VMEM(quartets.shape, i32),
            smem(density_owner.shape, i32),
            pltpu.VMEM((8, BLOCK), i32),
            smem((8, BLOCK), i32),
            pltpu.VMEM((8, BLOCK), i32),
            smem((8, BLOCK), i32),
            pltpu.VMEM((8, BLOCK), i32),
            smem((8, BLOCK), i32),
            dma((9,)),
            pltpu.VMEM((NBLK,) + block, BF16),
            pltpu.VMEM((NBLK, 8, BLOCK), F32),
            pltpu.VMEM((2, 3) + block, F32),
            pltpu.VMEM((PAIRS + 1,) + block, BF16),
            pltpu.VMEM((PAIRS + 1,) + block, BF16),
            pltpu.VMEM((PAIRS + 1,) + block, BF16),
            pltpu.VMEM((2, PAIRS * GROUP, PAIRS * GROUP), BF16),
            pltpu.VMEM((2, PAIRS) + block, F32),
            pltpu.VMEM((PAIRS,) + block, F32),
            pltpu.VMEM((PAIRS + 1,) + half, BF16),
            pltpu.VMEM((PAIRS + 1,) + half, BF16),
            pltpu.VMEM((PAIRS + 1,) + half, BF16),
            pltpu.VMEM((PAIRS + 1,) + half, BF16),
            pltpu.VMEM((2, 2, SIDE) + half, F32),
            pltpu.VMEM((2, 3, 2, SIDE) + half, BF16),
            pltpu.VMEM((2, 2, SIDE) + half, BF16),
            pltpu.VMEM((2, 2, 2, SIDE) + half, BF16),
            pltpu.VMEM((2, 3, 2) + half, BF16),
            pltpu.VMEM((2, 3, 2) + half, BF16),
            dma((OWN,)),
            dma((OWN,)),
            dma((2, 2, hops)),
            dma((2, 2, hops)),
            dma((5,)),
            dma((5,)),
            dma((2, 2)),
            dma((2, 2)),
            dma((2, 2, 2)),
            dma((2, 2, 2)),
            dma((2, 3)),
            dma((2, 3)),
        ],
        compiler_params=pltpu.CompilerParams(
            collective_id=0, has_side_effects=True, vmem_limit_bytes=56 * 2**20
        ),
        cost_estimate=pl.CostEstimate(
            flops=2 * 10**9, bytes_accessed=4 * 2**20, transcendentals=4 * 10**6
        ),
    )(
        basis_centers,
        bra_pairs,
        ket_pairs,
        quartets,
        quartet_counts,
        density_owner,
        density_store,
    )


def solution(mesh):
    return jax.shard_map(
        local,
        mesh=mesh,
        in_specs=(
            P(),
            P("bra"),
            P("ket"),
            P("bra", "ket", None, None),
            P("bra", "ket"),
            P("ket", None),
            P("bra", "ket", None),
        ),
        out_specs=P("bra", "ket"),
        check_vma=False,
    )
```

```python
import jax
import jax.numpy as jnp
from jax import lax
from jax.experimental import pallas as pl
from jax.experimental.pallas import tpu as pltpu
from jax.sharding import PartitionSpec as P

OMEGA = 0.11
SOFTEN = 0.25
BLOCK = 128
NBLK = 64
PAIRS = 32
RING = 8
DEEP = 2
SIDE = 4
OWN = 4
HALF = 64
GROUP = 8
MESH = pl.DeviceIdType.MESH
F32 = jnp.float32
BF16 = jnp.bfloat16

SLOPE = 0.6 * OMEGA
DECAY = -OMEGA * OMEGA * 1.4426950408889634
ERFC = (
    0.33856715,
    0.33711259,
    0.29264139,
    0.06933287,
    0.29272546,
    -0.65555156,
    0.41918066,
    -0.09400974,
)


def kernel_value(squared):
    inverse = lax.rsqrt(squared)
    divisor = 1.0 + SLOPE * (squared * inverse)
    t = pl.reciprocal(divisor, approx=True)
    t = t * (2.0 - divisor * t)
    poly = ERFC[-1] * t + ERFC[-2]
    for c in ERFC[-3::-1]:
        poly = poly * t + c
    return jnp.exp2(DECAY * squared) * (t * inverse) * poly


def body(
    centers_hbm,
    bra_hbm,
    ket_hbm,
    quartets_hbm,
    count,
    owner_hbm,
    density_hbm,
    out,
    centers,
    bra_pairs,
    ket_pairs,
    quartets,
    owner,
    slots_vmem,
    slots,
    sib_slots_vmem,
    sib_slots,
    places_vmem,
    places,
    fetch,
    gathered,
    lines,
    columns,
    bra_tiles,
    ket_tiles,
    sib_tiles,
    spread,
    product,
    weighted,
    w_low,
    w_high,
    sib_low,
    sib_high,
    keep,
    x_out,
    rel_in,
    x_in,
    z_out,
    z_in,
    part_send,
    part_recv,
    ring_send,
    ring_recv,
    sib_send,
    sib_recv,
    rel_send,
    rel_recv,
    x_send,
    x_recv,
    z_send,
    z_recv,
):
    row = lax.axis_index("bra")
    col = lax.axis_index("ket")
    y, deep = row // DEEP, row % DEEP
    core = col % 2
    zl = (col // 2) % SIDE
    xx = col // (2 * SIDE)
    w_own, w_sib = (w_low, w_high), (sib_low, sib_high)

    def at_row(yy, dd):
        return lax.rem(yy + 2 * RING, RING) * DEEP + dd

    def at_col(x_at, z_at, core_at):
        return (lax.rem(x_at + SIDE, SIDE) * SIDE + z_at) * 2 + core_at

    up, down = at_row(y + 1, deep), at_row(y - 1, deep)
    partner = at_row(y, 1 - deep)
    sibling = at_col(xx, zl, 1 - core)
    x_up, x_down = at_col(xx + 1, zl, core), at_col(xx - 1, zl, core)

    def z_at(step):
        return lax.rem(zl + step, SIDE)

    peers = [(up, col), (down, col), (partner, col), (row, sibling), (row, x_up), (row, x_down)]
    peers += [(row, at_col(xx, z_at(step), core)) for step in range(1, SIDE)]
    barrier = pltpu.get_barrier_semaphore()
    for peer in peers:
        pl.semaphore_signal(barrier, inc=1, device_id=peer, device_id_type=MESH)
    own_slots = gathered.at[pl.ds(row * OWN, OWN)]
    sources = (ket_hbm, bra_hbm, centers_hbm, owner_hbm, quartets_hbm, density_hbm)
    targets = (ket_pairs, bra_pairs, centers, owner, quartets, own_slots)
    fetches = [
        pltpu.make_async_copy(src, dst, fetch.at[n])
        for n, (src, dst) in enumerate(zip(sources, targets))
    ]
    for copy in fetches:
        copy.start()
    for tiles in (bra_tiles, ket_tiles, sib_tiles):
        tiles[PAIRS] = jnp.zeros((BLOCK, BLOCK), BF16)
    for part in w_own + w_sib:
        part[PAIRS] = jnp.zeros((HALF, BLOCK), BF16)
    pl.semaphore_wait(barrier, len(peers))

    def remote(src, dst, send, recv, device):
        return pltpu.make_async_remote_copy(
            src_ref=src,
            dst_ref=dst,
            send_sem=send,
            recv_sem=recv,
            device_id=device,
            device_id_type=MESH,
        )

    def to_partner(place):
        return remote(
            density_hbm.at[pl.ds(place, 1)],
            gathered.at[pl.ds(row * OWN + place, 1)],
            part_send.at[place],
            part_recv.at[place],
            (partner, col),
        )

    for place in (0, 2, 1, 3):
        to_partner(place).start()

    def depth(family):
        return deep if family == 0 else 1 - deep

    def hop(family, way, m, arriving, first=False):
        sign = 1 - 2 * way
        back = m // OWN + arriving
        place = lax.rem(m + 2 * way, OWN)
        ref = gathered.at[pl.ds(at_row(y - sign * back, depth(family)) * OWN + place, 1)]
        src = density_hbm.at[pl.ds(place, 1)] if first else ref
        device = (up, col) if way == 0 else (down, col)
        return remote(
            src, ref, ring_send.at[family, way, m], ring_recv.at[family, way, m], device
        )

    last = 3 * OWN + OWN // 2

    def send_own(family, m):
        for way in range(2):
            hop(family, way, m, 0, family == 0).start()

    def arrive(family, m):
        for way in range(2):
            hop(family, way, m, 1).wait_recv()

    def forward(family, m):
        for way in range(2):
            hop(family, way, m - OWN, 1).wait_recv()
            hop(family, way, m, 0).start()

    for m in range(OWN):
        send_own(0, m)
    for copy in fetches[:-1]:
        copy.wait()

    lane = lax.broadcasted_iota(jnp.int32, (8, BLOCK), 1)
    ket_table = jnp.full((8, BLOCK), PAIRS, jnp.int32)
    bra_table = jnp.full((8, BLOCK), PAIRS, jnp.int32)
    for n in range(PAIRS):
        ket_table = jnp.where(lane == ket_pairs[n], n, ket_table)
        bra_table = jnp.where(lane == owner[0, bra_pairs[n]], n, bra_table)
    slots_vmem[...] = ket_table
    places_vmem[...] = bra_table
    to_slots = pltpu.make_async_copy(slots_vmem, slots, fetch.at[len(fetches)])
    to_slots.start()
    to_places = pltpu.make_async_copy(places_vmem, places, fetch.at[len(fetches) + 1])
    to_places.start()
    there = (row, sibling)
    table_swap = remote(slots_vmem, sib_slots_vmem, sib_send.at[0], sib_recv.at[0], there)
    table_swap.start()

    for block in range(NBLK):
        lines[block, 0:3] = centers[:, block * BLOCK : (block + 1) * BLOCK]
    for side, start in ((0, row * (NBLK // 16)), (1, col * (NBLK // 32))):
        line = lines[start]
        for axis in range(3):
            wide = jnp.broadcast_to(line[axis : axis + 1], (BLOCK, BLOCK))
            columns[side, axis] = wide.T

    def tile(side, block, ref, place):
        line = lines[block]
        rows = 32
        for part in range(BLOCK // rows):
            squared = jnp.full((rows, BLOCK), SOFTEN, F32)
            for axis in range(3):
                difference = columns[side, axis, pl.ds(part * rows, rows)] - line[axis : axis + 1]
                squared = squared + difference * difference
            ref[place, pl.ds(part * rows, rows)] = kernel_value(squared).astype(BF16)

    def ket_tile(q):
        tile(1, ket_pairs[q], ket_tiles, q)

    def bra_tile(p):
        tile(0, bra_pairs[p], bra_tiles, p)

    def iota(shape, axis):
        return lax.broadcasted_iota(jnp.int32, shape, axis)

    def hot(condition):
        return jnp.where(condition, jnp.float32(1.0), jnp.float32(0.0)).astype(BF16)

    long = (PAIRS, quartets.shape[3])
    bra_hot = hot((quartets[0, 0, 0:1] == iota(long, 0)) & (iota(long, 1) < count[0, 0]))
    ket_hot = hot(quartets[0, 0, 1:2] == iota(long, 0))
    counts = lax.dot_general(
        ket_hot, bra_hot, (((1,), (1,)), ((), ())), preferred_element_type=F32
    ).astype(BF16)
    size = PAIRS * GROUP
    by_slot = jnp.dot(
        counts, hot(bra_table[0:1] == iota((PAIRS, BLOCK), 0)), preferred_element_type=F32
    ).astype(BF16)
    tall = hot(iota((size, PAIRS), 0) // GROUP == iota((size, PAIRS), 1))
    rows_of = jnp.dot(tall, by_slot, preferred_element_type=F32).astype(BF16)
    same = iota((size, size), 0) % GROUP == iota((size, size), 1) % GROUP
    local_slot = iota((BLOCK, size), 1) // GROUP
    row_slot = (local_slot // OWN) * (OWN * DEEP) + local_slot % OWN
    for family in range(2):
        wide = hot(row_slot + depth(family) * OWN == iota((BLOCK, size), 0))
        spread[family] = jnp.where(
            same, jnp.dot(rows_of, wide, preferred_element_type=F32), jnp.float32(0.0)
        ).astype(BF16)

    def z_row(family, yy):
        at = lax.rem(yy + 2 * RING, RING)
        for extra in range(OWN):
            s = (at * DEEP + depth(family)) * OWN + extra
            z = jnp.dot(bra_tiles[places[0, s]], gathered[s], preferred_element_type=F32)
            product[family, at * OWN + extra] = z.astype(BF16).astype(F32)

    def w_part(family, n):
        base = pl.multiple_of(n * 2 * GROUP, 2 * GROUP)
        halves = [
            product[family, :, pl.ds(base + half * GROUP, GROUP), :]
            .reshape(size, BLOCK)
            .astype(BF16)
            for half in range(2)
        ]
        both = jnp.dot(
            spread[family], jnp.concatenate(halves, axis=1), preferred_element_type=F32
        )
        return jnp.concatenate(
            [
                both[:, half * BLOCK : (half + 1) * BLOCK].reshape(PAIRS, GROUP, BLOCK)
                for half in range(2)
            ],
            axis=1,
        )

    def swap_tiles(src, dst, first, total, index):
        return remote(
            src.at[pl.ds(first, total)],
            dst.at[pl.ds(first, total)],
            sib_send.at[index],
            sib_recv.at[index],
            there,
        )

    mine = core * (PAIRS // 2)
    bra_swap = swap_tiles(bra_tiles, bra_tiles, mine, PAIRS // 2, 1)
    ket_swap = swap_tiles(ket_tiles, sib_tiles, 0, PAIRS, 4)

    def ket_run(first, total):
        @pl.loop(first, first + total)
        def _(q):
            ket_tile(q)

    def w_first(first, total):
        @pl.loop(first, first + total)
        def _(n):
            weighted[:, pl.ds(n * 2 * GROUP, 2 * GROUP)] = w_part(0, n)

    @pl.loop(OWN, 2 * OWN)
    def _(m):
        forward(0, m)

        @pl.loop(0, 4)
        def _(n):
            bra_tile(mine + (m - OWN) * 4 + n)

    bra_swap.start()
    def send_partner(m):
        if m < 2:
            to_partner(m).wait_recv()
            to_partner(m + 2).wait_recv()
        send_own(1, m)

    @pl.when(deep == 0)
    def _():
        @pl.loop(2 * OWN, last)
        def _(m):
            forward(0, m)

            @pl.loop(0, 5)
            def _(n):
                ket_tile((m - 2 * OWN) * 5 + n)

        ket_run(30, 2)
        ket_swap.start()
        bra_swap.wait()
        to_places.wait()
        fetches[-1].wait()
        for away in (0, 1, -1, 2, -2):
            z_row(0, y + away)
        arrive(0, last - 4)
        arrive(0, last - 3)
        z_row(0, y - 3)
        z_row(0, y + 3)
        for m in range(OWN):
            send_partner(m)
        arrive(0, last - 2)
        arrive(0, last - 1)
        z_row(0, y + 4)
        for m in range(OWN):
            forward(1, OWN + m)
            w_first(2 * m, 2)
        forward(1, 2 * OWN)
        z_row(1, y)
        forward(1, 2 * OWN + 1)
        z_row(1, y + 1)
        forward(1, 2 * OWN + 2)
        z_row(1, y - 1)
        for m in range(2 * OWN + 3, last):
            forward(1, m)

    @pl.when(deep == 1)
    def _():
        for m in range(OWN):
            forward(0, 2 * OWN + m)
            ket_run(m * 6, 3)
            send_partner(m)
            ket_run(m * 6 + 3, 3)
        for m in range(2):
            forward(1, OWN + m)
            ket_run(24 + m * 4, 2)
            forward(0, 3 * OWN + m)
            ket_run(26 + m * 4, 2)
        ket_swap.start()
        bra_swap.wait()
        to_places.wait()
        fetches[-1].wait()
        forward(1, OWN + 2)
        z_row(0, y)
        z_row(0, y - 1)
        forward(1, OWN + 3)
        z_row(0, y + 1)
        z_row(0, y - 2)
        forward(1, 2 * OWN)
        z_row(0, y + 2)
        arrive(0, last - 4)
        arrive(0, last - 3)
        z_row(0, y - 3)
        forward(1, 2 * OWN + 1)
        z_row(0, y + 3)
        arrive(0, last - 2)
        arrive(0, last - 1)
        z_row(0, y + 4)
        forward(1, 2 * OWN + 2)
        w_first(0, 3)
        forward(1, 2 * OWN + 3)
        w_first(3, 2)
        forward(1, 3 * OWN)
        w_first(5, 1)
        forward(1, 3 * OWN + 1)
        w_first(6, 2)
        for away in (0, 1, -1):
            z_row(1, y + away)

    z_row(1, y + 2)
    z_row(1, y - 2)
    arrive(1, last - 4)
    arrive(1, last - 3)
    z_row(1, y - 3)
    z_row(1, y + 3)
    table_swap.wait()
    sib_to_slots = pltpu.make_async_copy(sib_slots_vmem, sib_slots, fetch.at[len(fetches) + 2])
    sib_to_slots.start()
    arrive(1, last - 2)
    arrive(1, last - 1)
    z_row(1, y + 4)

    def w_swap(half):
        return remote(
            w_own[half].at[pl.ds(0, PAIRS)],
            w_sib[half].at[pl.ds(0, PAIRS)],
            sib_send.at[2 + half],
            sib_recv.at[2 + half],
            there,
        )

    for half in range(2):

        @pl.loop(0, HALF // GROUP // 2)
        def _(n):
            at = pl.multiple_of(n * 2 * GROUP, 2 * GROUP)
            total = w_part(1, n + half * (HALF // GROUP // 2))
            total = total + weighted[:, pl.ds(at + half * HALF, 2 * GROUP)]
            w_own[half][0:PAIRS, pl.ds(at, 2 * GROUP)] = total.astype(BF16)

        w_swap(half).start()

    def image(d, zz, jj, half):
        j = (lax.rem(xx + d, SIDE) * SIDE + zz) * 4 + core * 2 + jj
        a, b = slots[0, j], sib_slots[0, j]
        left = jnp.concatenate([w_own[half][a], w_sib[half][b]], axis=1)
        right = jnp.concatenate([ket_tiles[a], sib_tiles[b]], axis=0)
        return jnp.dot(left, right, preferred_element_type=F32)

    def relay(way, half):
        device = (row, x_up) if way == 0 else (row, x_down)
        return remote(
            x_out.at[half, 2, way],
            rel_in.at[half, way],
            rel_send.at[half, way],
            rel_recv.at[half, way],
            device,
        )

    def to_x(way, jj, half):
        device = (row, x_up) if way == 0 else (row, x_down)
        return remote(
            x_out.at[half, way, jj],
            x_in.at[half, way, jj],
            x_send.at[half, way, jj],
            x_recv.at[half, way, jj],
            device,
        )

    def to_z(step, half):
        return remote(
            z_out.at[half, step - 1],
            z_in.at[half, step - 1],
            z_send.at[half, step - 1],
            z_recv.at[half, step - 1],
            (row, at_col(xx, z_at(step), core)),
        )

    def relays(half):
        for way in range(2):
            for zz in range(SIDE):
                x_out[half, 2, way, zz] = image(2, zz, way, half).astype(BF16)
            relay(way, half).start()

    def direct(half):
        for way, d in ((0, 1), (1, 3)):
            for zz in range(SIDE):
                x_out[half, way, 1 - way, zz] = image(d, zz, 1 - way, half).astype(BF16)
            to_x(way, 1 - way, half).start()

    def summed(half):
        for way, d in ((0, 1), (1, 3)):
            images = [image(d, zz, way, half) for zz in range(SIDE)]
            relay(way, half).wait_recv()
            for zz in range(SIDE):
                total = images[zz] + rel_in[half, way, zz].astype(F32)
                x_out[half, way, way, zz] = total.astype(BF16)
            to_x(way, way, half).start()

    def own_sum(half):
        for jj in range(2):
            for zz in range(SIDE):
                keep[half, jj, zz] = image(0, zz, jj, half)

    def from_x(half):
        for jj in range(2):
            for way in (1 - jj, jj):
                to_x(way, jj, half).wait_recv()
                keep[half, jj] = keep[half, jj] + x_in[half, way, jj].astype(F32)
        for step in (2, 3, 1):
            for jj in range(2):
                z_out[half, step - 1, jj] = keep[half, jj, z_at(step)].astype(BF16)
            to_z(step, half).start()

    def finish(half):
        for step in (1, 3, 2):
            to_z(step, half).wait_recv()
        rows = pl.ds(half * HALF, HALF)
        for jj in range(2):
            total = keep[half, jj, zl]
            for step in range(1, SIDE):
                total = total + z_in[half, step - 1, jj].astype(F32)
            out[rows, jj * BLOCK : (jj + 1) * BLOCK] = total.astype(BF16)

    to_slots.wait()
    sib_to_slots.wait()
    ket_swap.wait()
    w_swap(0).wait()
    relays(0)
    direct(0)
    w_swap(1).wait()
    relays(1)
    summed(0)
    direct(1)
    own_sum(0)
    summed(1)
    own_sum(1)
    from_x(0)

    @pl.loop(0, last)
    def _(m):
        for family in range(2):
            for way in range(2):
                hop(family, way, m, 0).wait_send()

    for place in range(OWN):
        to_partner(place).wait_send()
    from_x(1)
    finish(0)
    for half in range(2):
        for way in range(2):
            relay(way, half).wait_send()
            for jj in range(2):
                to_x(way, jj, half).wait_send()
        for step in range(1, SIDE):
            to_z(step, half).wait_send()
    finish(1)


def local(
    basis_centers, bra_pairs, ket_pairs, quartets, quartet_counts, density_owner, density_store
):
    hbm = pl.BlockSpec(memory_space=pltpu.HBM)
    smem, i32 = pltpu.SMEM, jnp.int32
    block, half = (BLOCK, BLOCK), (HALF, BLOCK)
    dma = pltpu.SemaphoreType.DMA
    hops = 3 * OWN + OWN // 2
    return pl.pallas_call(
        body,
        out_shape=jax.ShapeDtypeStruct((BLOCK, 2 * BLOCK), BF16),
        in_specs=[hbm] * 4 + [pl.BlockSpec(memory_space=smem)] + [hbm] * 2,
        out_specs=pl.BlockSpec(memory_space=pltpu.VMEM),
        scratch_shapes=[
            pltpu.VMEM(basis_centers.shape, F32),
            smem(bra_pairs.shape, i32),
            smem(ket_pairs.shape, i32),
            pltpu.VMEM(quartets.shape, i32),
            smem(density_owner.shape, i32),
            pltpu.VMEM((8, BLOCK), i32),
            smem((8, BLOCK), i32),
            pltpu.VMEM((8, BLOCK), i32),
            smem((8, BLOCK), i32),
            pltpu.VMEM((8, BLOCK), i32),
            smem((8, BLOCK), i32),
            dma((9,)),
            pltpu.VMEM((NBLK,) + block, BF16),
            pltpu.VMEM((NBLK, 8, BLOCK), F32),
            pltpu.VMEM((2, 3) + block, F32),
            pltpu.VMEM((PAIRS + 1,) + block, BF16),
            pltpu.VMEM((PAIRS + 1,) + block, BF16),
            pltpu.VMEM((PAIRS + 1,) + block, BF16),
            pltpu.VMEM((2, PAIRS * GROUP, PAIRS * GROUP), BF16),
            pltpu.VMEM((2, PAIRS) + block, F32),
            pltpu.VMEM((PAIRS,) + block, F32),
            pltpu.VMEM((PAIRS + 1,) + half, BF16),
            pltpu.VMEM((PAIRS + 1,) + half, BF16),
            pltpu.VMEM((PAIRS + 1,) + half, BF16),
            pltpu.VMEM((PAIRS + 1,) + half, BF16),
            pltpu.VMEM((2, 2, SIDE) + half, F32),
            pltpu.VMEM((2, 3, 2, SIDE) + half, BF16),
            pltpu.VMEM((2, 2, SIDE) + half, BF16),
            pltpu.VMEM((2, 2, 2, SIDE) + half, BF16),
            pltpu.VMEM((2, 3, 2) + half, BF16),
            pltpu.VMEM((2, 3, 2) + half, BF16),
            dma((OWN,)),
            dma((OWN,)),
            dma((2, 2, hops)),
            dma((2, 2, hops)),
            dma((5,)),
            dma((5,)),
            dma((2, 2)),
            dma((2, 2)),
            dma((2, 2, 2)),
            dma((2, 2, 2)),
            dma((2, 3)),
            dma((2, 3)),
        ],
        compiler_params=pltpu.CompilerParams(
            collective_id=0, has_side_effects=True, vmem_limit_bytes=56 * 2**20
        ),
        cost_estimate=pl.CostEstimate(
            flops=2 * 10**9, bytes_accessed=4 * 2**20, transcendentals=4 * 10**6
        ),
    )(
        basis_centers,
        bra_pairs,
        ket_pairs,
        quartets,
        quartet_counts,
        density_owner,
        density_store,
    )


def solution(mesh):
    return jax.shard_map(
        local,
        mesh=mesh,
        in_specs=(
            P(),
            P("bra"),
            P("ket"),
            P("bra", "ket", None, None),
            P("bra", "ket"),
            P("ket", None),
            P("bra", "ket", None),
        ),
        out_specs=P("bra", "ket"),
        check_vma=False,
    )
```

```python
import jax
import jax.numpy as jnp
from jax import lax
from jax.experimental import pallas as pl
from jax.experimental.pallas import tpu as pltpu
from jax.sharding import PartitionSpec as P

OMEGA = 0.11
SOFTEN = 0.25
BLOCK = 128
NBLK = 64
PAIRS = 32
RING = 8
DEEP = 2
SIDE = 4
OWN = 4
PARTS = ((0, 32), (32, 64), (96, 32))
GROUP = 8
SHIFT = 3
MESH = pl.DeviceIdType.MESH
F32 = jnp.float32
BF16 = jnp.bfloat16

SLOPE = 0.6 * OMEGA
DECAY = -OMEGA * OMEGA * 1.4426950408889634
ERFC = (
    0.33856715,
    0.33711259,
    0.29264139,
    0.06933287,
    0.29272546,
    -0.65555156,
    0.41918066,
    -0.09400974,
)


def kernel_value(squared):
    inverse = lax.rsqrt(squared)
    divisor = 1.0 + SLOPE * (squared * inverse)
    t = pl.reciprocal(divisor, approx=True)
    t = t * (2.0 - divisor * t)
    poly = ERFC[-1] * t + ERFC[-2]
    for c in ERFC[-3::-1]:
        poly = poly * t + c
    return jnp.exp2(DECAY * squared) * (t * inverse) * poly


def body(
    centers_hbm,
    bra_hbm,
    ket_hbm,
    quartets_hbm,
    count,
    owner_hbm,
    density_hbm,
    out,
    centers,
    bra_pairs,
    ket_pairs,
    quartets,
    owner,
    slots_vmem,
    slots,
    sib_slots_vmem,
    sib_slots,
    places_vmem,
    places,
    fetch,
    gathered,
    lines,
    columns,
    bra_tiles,
    ket_tiles,
    sib_tiles,
    spread,
    product,
    weighted,
    w_own,
    w_sib,
    keep,
    x_out,
    rel_in,
    x_in,
    z_out,
    z_in,
    part_send,
    part_recv,
    ring_send,
    ring_recv,
    sib_send,
    sib_recv,
    swap_send,
    swap_recv,
    rel_send,
    rel_recv,
    x_send,
    x_recv,
    z_send,
    z_recv,
):
    row = lax.axis_index("bra")
    col = lax.axis_index("ket")
    y, deep = row // DEEP, row % DEEP
    core = col % 2
    zl = (col // 2) % SIDE
    xx = col // (2 * SIDE)

    def at_row(yy, dd):
        return lax.rem(yy + 2 * RING, RING) * DEEP + dd

    def at_col(x_at, z_at, core_at):
        return (lax.rem(x_at + SIDE, SIDE) * SIDE + z_at) * 2 + core_at

    up, down = at_row(y + 1, deep), at_row(y - 1, deep)
    partner = at_row(y, 1 - deep)
    sibling = at_col(xx, zl, 1 - core)
    x_up, x_down = at_col(xx + 1, zl, core), at_col(xx - 1, zl, core)

    def z_at(step):
        return lax.rem(zl + step, SIDE)

    peers = [(up, col), (down, col), (partner, col), (row, sibling), (row, x_up), (row, x_down)]
    peers += [(row, at_col(xx, z_at(step), core)) for step in range(1, SIDE)]
    barrier = pltpu.get_barrier_semaphore()
    for peer in peers:
        pl.semaphore_signal(barrier, inc=1, device_id=peer, device_id_type=MESH)
    own_slots = gathered.at[pl.ds(row * OWN, OWN)]
    sources = (ket_hbm, bra_hbm, centers_hbm, owner_hbm, quartets_hbm, density_hbm)
    targets = (ket_pairs, bra_pairs, centers, owner, quartets, own_slots)
    fetches = [
        pltpu.make_async_copy(src, dst, fetch.at[n])
        for n, (src, dst) in enumerate(zip(sources, targets))
    ]
    for copy in fetches:
        copy.start()
    for tiles in (bra_tiles, ket_tiles, sib_tiles):
        tiles[PAIRS] = jnp.zeros((BLOCK, BLOCK), BF16)
    for part, (_, rows) in enumerate(PARTS):
        w_own[part][PAIRS] = jnp.zeros((rows, BLOCK), BF16)
        w_sib[part][PAIRS] = jnp.zeros((rows, BLOCK), BF16)
    pl.semaphore_wait(barrier, len(peers))

    def remote(src, dst, send, recv, device):
        return pltpu.make_async_remote_copy(
            src_ref=src,
            dst_ref=dst,
            send_sem=send,
            recv_sem=recv,
            device_id=device,
            device_id_type=MESH,
        )

    def to_partner(place):
        return remote(
            density_hbm.at[pl.ds(place, 1)],
            gathered.at[pl.ds(row * OWN + place, 1)],
            part_send.at[place],
            part_recv.at[place],
            (partner, col),
        )

    for place in (0, 2, 1, 3):
        to_partner(place).start()

    def depth(family):
        return deep if family == 0 else 1 - deep

    def hop(family, way, m, arriving, first=False):
        sign = 1 - 2 * way
        back = m // OWN + arriving
        place = lax.rem(m + 2 * way, OWN)
        ref = gathered.at[pl.ds(at_row(y - sign * back, depth(family)) * OWN + place, 1)]
        src = density_hbm.at[pl.ds(place, 1)] if first else ref
        device = (up, col) if way == 0 else (down, col)
        return remote(
            src, ref, ring_send.at[family, way, m], ring_recv.at[family, way, m], device
        )

    last = 3 * OWN + OWN // 2

    def send_own(family, m):
        for way in range(2):
            hop(family, way, m, 0, family == 0).start()

    def arrive(family, m):
        for way in range(2):
            hop(family, way, m, 1).wait_recv()

    def forward(family, m):
        for way in range(2):
            hop(family, way, m - OWN, 1).wait_recv()
            hop(family, way, m, 0).start()

    for m in range(OWN):
        send_own(0, m)
    for copy in fetches[:-1]:
        copy.wait()

    lane = lax.broadcasted_iota(jnp.int32, (8, BLOCK), 1)
    ket_table = jnp.full((8, BLOCK), PAIRS, jnp.int32)
    bra_table = jnp.full((8, BLOCK), PAIRS, jnp.int32)
    for n in range(PAIRS):
        ket_table = jnp.where(lane == ket_pairs[n], n, ket_table)
        bra_table = jnp.where(lane == owner[0, bra_pairs[n]], n, bra_table)
    slots_vmem[...] = ket_table
    places_vmem[...] = bra_table
    to_slots = pltpu.make_async_copy(slots_vmem, slots, fetch.at[len(fetches)])
    to_slots.start()
    to_places = pltpu.make_async_copy(places_vmem, places, fetch.at[len(fetches) + 1])
    to_places.start()
    there = (row, sibling)
    table_swap = remote(slots_vmem, sib_slots_vmem, sib_send.at[0], sib_recv.at[0], there)
    table_swap.start()

    for block in range(NBLK):
        lines[block, 0:3] = centers[:, block * BLOCK : (block + 1) * BLOCK]
    for side, start in ((0, row * (NBLK // 16)), (1, col * (NBLK // 32))):
        line = lines[start]
        for axis in range(3):
            wide = jnp.broadcast_to(line[axis : axis + 1], (BLOCK, BLOCK))
            columns[side, axis] = wide.T

    def tile(side, block, ref, place):
        line = lines[block]
        rows = 32
        for part in range(BLOCK // rows):
            squared = jnp.full((rows, BLOCK), SOFTEN, F32)
            for axis in range(3):
                difference = columns[side, axis, pl.ds(part * rows, rows)] - line[axis : axis + 1]
                squared = squared + difference * difference
            ref[place, pl.ds(part * rows, rows)] = kernel_value(squared).astype(BF16)

    def ket_tile(q):
        tile(1, ket_pairs[q], ket_tiles, q)

    def bra_tile(p):
        tile(0, bra_pairs[p], bra_tiles, p)

    def iota(shape, axis):
        return lax.broadcasted_iota(jnp.int32, shape, axis)

    def hot(condition):
        return jnp.where(condition, jnp.float32(1.0), jnp.float32(0.0)).astype(BF16)

    long = (PAIRS, quartets.shape[3])
    bra_hot = hot((quartets[0, 0, 0:1] == iota(long, 0)) & (iota(long, 1) < count[0, 0]))
    ket_hot = hot(quartets[0, 0, 1:2] == iota(long, 0))
    counts = lax.dot_general(
        ket_hot, bra_hot, (((1,), (1,)), ((), ())), preferred_element_type=F32
    ).astype(BF16)
    size = PAIRS * GROUP
    by_slot = jnp.dot(
        counts, hot(bra_table[0:1] == iota((PAIRS, BLOCK), 0)), preferred_element_type=F32
    ).astype(BF16)
    tall = hot(iota((size, PAIRS), 0) >> SHIFT == iota((size, PAIRS), 1))
    rows_of = jnp.dot(tall, by_slot, preferred_element_type=F32).astype(BF16)
    same = (iota((size, size), 0) ^ iota((size, size), 1)) & (GROUP - 1) == 0
    local_slot = iota((BLOCK, size), 1) >> SHIFT
    row_slot = (local_slot >> 2) * (OWN * DEEP) + (local_slot & (OWN - 1))
    for family in range(2):
        wide = hot(row_slot + depth(family) * OWN == iota((BLOCK, size), 0))
        spread[family] = jnp.where(
            same, jnp.dot(rows_of, wide, preferred_element_type=F32), jnp.float32(0.0)
        ).astype(BF16)

    def z_row(family, yy):
        at = lax.rem(yy + 2 * RING, RING)
        for extra in range(OWN):
            s = (at * DEEP + depth(family)) * OWN + extra
            z = jnp.dot(bra_tiles[places[0, s]], gathered[s], preferred_element_type=F32)
            product[family, at * OWN + extra] = z.astype(BF16).astype(F32)

    def w_part(family, n):
        base = pl.multiple_of(n * 2 * GROUP, 2 * GROUP)
        halves = [
            product[family, :, pl.ds(base + half * GROUP, GROUP), :]
            .reshape(size, BLOCK)
            .astype(BF16)
            for half in range(2)
        ]
        both = jnp.dot(
            spread[family], jnp.concatenate(halves, axis=1), preferred_element_type=F32
        )
        return jnp.concatenate(
            [
                both[:, half * BLOCK : (half + 1) * BLOCK].reshape(PAIRS, GROUP, BLOCK)
                for half in range(2)
            ],
            axis=1,
        )

    def swap_tiles(src, dst, first, total, index):
        return remote(
            src.at[pl.ds(first, total)],
            dst.at[pl.ds(first, total)],
            sib_send.at[index],
            sib_recv.at[index],
            there,
        )

    mine = core * (PAIRS // 2)
    bra_swap = swap_tiles(bra_tiles, bra_tiles, mine, PAIRS // 2, 1)
    ket_swap = swap_tiles(ket_tiles, sib_tiles, 0, PAIRS, 2)

    def ket_run(first, total):
        @pl.loop(first, first + total)
        def _(q):
            ket_tile(q)

    def w_first(first, total):
        @pl.loop(first, first + total)
        def _(n):
            weighted[:, pl.ds(n * 2 * GROUP, 2 * GROUP)] = w_part(0, n)

    @pl.loop(OWN, 2 * OWN)
    def _(m):
        forward(0, m)

        @pl.loop(0, 4)
        def _(n):
            bra_tile(mine + (m - OWN) * 4 + n)

    bra_swap.start()
    for m in range(OWN):
        forward(0, 2 * OWN + m)
        ket_run(m * 6, 3)
        if m < 2:
            to_partner(m).wait_recv()
            to_partner(m + 2).wait_recv()
        send_own(1, m)
        ket_run(m * 6 + 3, 3)
    for m in range(2):
        forward(1, OWN + m)
        ket_run(24 + m * 4, 2)
        forward(0, 3 * OWN + m)
        ket_run(26 + m * 4, 2)
    ket_swap.start()
    bra_swap.wait()
    to_places.wait()
    fetches[-1].wait()
    forward(1, OWN + 2)
    z_row(0, y)
    z_row(0, y - 1)
    forward(1, OWN + 3)
    z_row(0, y + 1)
    z_row(0, y - 2)
    forward(1, 2 * OWN)
    z_row(0, y + 2)
    arrive(0, last - 4)
    arrive(0, last - 3)
    z_row(0, y - 3)
    forward(1, 2 * OWN + 1)
    z_row(0, y + 3)
    arrive(0, last - 2)
    arrive(0, last - 1)
    z_row(0, y + 4)
    forward(1, 2 * OWN + 2)
    w_first(0, 3)
    forward(1, 2 * OWN + 3)
    w_first(3, 2)
    forward(1, 3 * OWN)
    w_first(5, 1)
    forward(1, 3 * OWN + 1)
    w_first(6, 2)
    for away in (0, 1, -1, 2, -2):
        z_row(1, y + away)
    arrive(1, last - 4)
    arrive(1, last - 3)
    z_row(1, y - 3)
    z_row(1, y + 3)
    table_swap.wait()
    sib_to_slots = pltpu.make_async_copy(sib_slots_vmem, sib_slots, fetch.at[len(fetches) + 2])
    sib_to_slots.start()
    arrive(1, last - 2)
    arrive(1, last - 1)
    z_row(1, y + 4)

    def w_swap(part):
        return remote(
            w_own[part].at[pl.ds(0, PAIRS)],
            w_sib[part].at[pl.ds(0, PAIRS)],
            swap_send.at[part],
            swap_recv.at[part],
            there,
        )

    for part, (start, rows) in enumerate(PARTS):

        @pl.loop(0, rows // (2 * GROUP))
        def _(n):
            at = pl.multiple_of(n * 2 * GROUP, 2 * GROUP)
            total = w_part(1, n + start // (2 * GROUP))
            total = total + weighted[:, pl.ds(at + start, 2 * GROUP)]
            w_own[part][0:PAIRS, pl.ds(at, 2 * GROUP)] = total.astype(BF16)

        w_swap(part).start()

    def image(d, zz, jj, part):
        j = (lax.rem(xx + d, SIDE) * SIDE + zz) * 4 + core * 2 + jj
        a, b = slots[0, j], sib_slots[0, j]
        left = jnp.concatenate([w_own[part][a], w_sib[part][b]], axis=1)
        right = jnp.concatenate([ket_tiles[a], sib_tiles[b]], axis=0)
        return jnp.dot(left, right, preferred_element_type=F32)

    def relay(way, part):
        device = (row, x_up) if way == 0 else (row, x_down)
        return remote(
            x_out[part].at[2, way],
            rel_in[part].at[way],
            rel_send.at[part, way],
            rel_recv.at[part, way],
            device,
        )

    def to_x(way, jj, part):
        device = (row, x_up) if way == 0 else (row, x_down)
        return remote(
            x_out[part].at[way, jj],
            x_in[part].at[way, jj],
            x_send.at[part, way, jj],
            x_recv.at[part, way, jj],
            device,
        )

    def to_z(step, part):
        return remote(
            z_out[part].at[step - 1],
            z_in[part].at[step - 1],
            z_send.at[part, step - 1],
            z_recv.at[part, step - 1],
            (row, at_col(xx, z_at(step), core)),
        )

    def relays(part):
        for way in range(2):
            for zz in range(SIDE):
                x_out[part][2, way, zz] = image(2, zz, way, part).astype(BF16)
            relay(way, part).start()

    def direct(part):
        for way, d in ((0, 1), (1, 3)):
            for zz in range(SIDE):
                x_out[part][way, 1 - way, zz] = image(d, zz, 1 - way, part).astype(BF16)
            to_x(way, 1 - way, part).start()

    def summed(part):
        for way, d in ((0, 1), (1, 3)):
            images = [image(d, zz, way, part) for zz in range(SIDE)]
            relay(way, part).wait_recv()
            for zz in range(SIDE):
                total = images[zz] + rel_in[part][way, zz].astype(F32)
                x_out[part][way, way, zz] = total.astype(BF16)
            to_x(way, way, part).start()

    def own_sum(part):
        for jj in range(2):
            for zz in range(SIDE):
                keep[part][jj, zz] = image(0, zz, jj, part)

    def from_x(part):
        for jj in range(2):
            for way in (1 - jj, jj):
                to_x(way, jj, part).wait_recv()
                keep[part][jj] = keep[part][jj] + x_in[part][way, jj].astype(F32)
        for step in (2, 3, 1):
            for jj in range(2):
                z_out[part][step - 1, jj] = keep[part][jj, z_at(step)].astype(BF16)
            to_z(step, part).start()

    def finish(part):
        for step in (1, 3, 2):
            to_z(step, part).wait_recv()
        start, rows = PARTS[part]
        for jj in range(2):
            total = keep[part][jj, zl]
            for step in range(1, SIDE):
                total = total + z_in[part][step - 1, jj].astype(F32)
            out[start : start + rows, jj * BLOCK : (jj + 1) * BLOCK] = total.astype(BF16)

    to_slots.wait()
    sib_to_slots.wait()
    ket_swap.wait()
    w_swap(0).wait()
    relays(0)
    direct(0)
    w_swap(1).wait()
    relays(1)
    summed(0)
    direct(1)
    w_swap(2).wait()
    relays(2)
    summed(1)
    direct(2)
    own_sum(0)
    from_x(0)
    summed(2)
    own_sum(1)
    own_sum(2)
    from_x(1)

    @pl.loop(0, last)
    def _(m):
        for family in range(2):
            for way in range(2):
                hop(family, way, m, 0).wait_send()

    for place in range(OWN):
        to_partner(place).wait_send()
    from_x(2)
    finish(0)
    finish(1)
    for part in range(len(PARTS)):
        for way in range(2):
            relay(way, part).wait_send()
            for jj in range(2):
                to_x(way, jj, part).wait_send()
        for step in range(1, SIDE):
            to_z(step, part).wait_send()
    finish(2)


def local(
    basis_centers, bra_pairs, ket_pairs, quartets, quartet_counts, density_owner, density_store
):
    hbm = pl.BlockSpec(memory_space=pltpu.HBM)
    smem, i32 = pltpu.SMEM, jnp.int32
    block, count = (BLOCK, BLOCK), len(PARTS)

    def parts(lead, kind=BF16):
        return [pltpu.VMEM(lead + (rows, BLOCK), kind) for _, rows in PARTS]

    dma = pltpu.SemaphoreType.DMA
    hops = 3 * OWN + OWN // 2
    return pl.pallas_call(
        body,
        out_shape=jax.ShapeDtypeStruct((BLOCK, 2 * BLOCK), BF16),
        in_specs=[hbm] * 4 + [pl.BlockSpec(memory_space=smem)] + [hbm] * 2,
        out_specs=pl.BlockSpec(memory_space=pltpu.VMEM),
        scratch_shapes=[
            pltpu.VMEM(basis_centers.shape, F32),
            smem(bra_pairs.shape, i32),
            smem(ket_pairs.shape, i32),
            pltpu.VMEM(quartets.shape, i32),
            smem(density_owner.shape, i32),
            pltpu.VMEM((8, BLOCK), i32),
            smem((8, BLOCK), i32),
            pltpu.VMEM((8, BLOCK), i32),
            smem((8, BLOCK), i32),
            pltpu.VMEM((8, BLOCK), i32),
            smem((8, BLOCK), i32),
            dma((9,)),
            pltpu.VMEM((NBLK,) + block, BF16),
            pltpu.VMEM((NBLK, 8, BLOCK), F32),
            pltpu.VMEM((2, 3) + block, F32),
            pltpu.VMEM((PAIRS + 1,) + block, BF16),
            pltpu.VMEM((PAIRS + 1,) + block, BF16),
            pltpu.VMEM((PAIRS + 1,) + block, BF16),
            pltpu.VMEM((2, PAIRS * GROUP, PAIRS * GROUP), BF16),
            pltpu.VMEM((2, PAIRS) + block, F32),
            pltpu.VMEM((PAIRS,) + block, F32),
            parts((PAIRS + 1,)),
            parts((PAIRS + 1,)),
            parts((2, SIDE), F32),
            parts((3, 2, SIDE)),
            parts((2, SIDE)),
            parts((2, 2, SIDE)),
            parts((3, 2)),
            parts((3, 2)),
            dma((OWN,)),
            dma((OWN,)),
            dma((2, 2, hops)),
            dma((2, 2, hops)),
            dma((3,)),
            dma((3,)),
            dma((count,)),
            dma((count,)),
            dma((count, 2)),
            dma((count, 2)),
            dma((count, 2, 2)),
            dma((count, 2, 2)),
            dma((count, 3)),
            dma((count, 3)),
        ],
        compiler_params=pltpu.CompilerParams(
            collective_id=0, has_side_effects=True, vmem_limit_bytes=56 * 2**20
        ),
        cost_estimate=pl.CostEstimate(
            flops=2 * 10**9, bytes_accessed=4 * 2**20, transcendentals=4 * 10**6
        ),
    )(
        basis_centers,
        bra_pairs,
        ket_pairs,
        quartets,
        quartet_counts,
        density_owner,
        density_store,
    )


def solution(mesh):
    return jax.shard_map(
        local,
        mesh=mesh,
        in_specs=(
            P(),
            P("bra"),
            P("ket"),
            P("bra", "ket", None, None),
            P("bra", "ket"),
            P("ket", None),
            P("bra", "ket", None),
        ),
        out_specs=P("bra", "ket"),
        check_vma=False,
    )
```

```python
import jax
import jax.numpy as jnp
from jax import lax
from jax.experimental import pallas as pl
from jax.experimental.pallas import tpu as pltpu
from jax.sharding import PartitionSpec as P

OMEGA = 0.11
SOFTEN = 0.25
BLOCK = 128
NBLK = 64
PAIRS = 32
RING = 8
DEEP = 2
SIDE = 4
OWN = 4
PARTS = ((0, 32), (32, 64), (96, 32))
GROUP = 8
SHIFT = 3
MESH = pl.DeviceIdType.MESH
F32 = jnp.float32
BF16 = jnp.bfloat16

SLOPE = 0.6 * OMEGA
DECAY = -OMEGA * OMEGA * 1.4426950408889634
ERFC = (
    0.33856715,
    0.33711259,
    0.29264139,
    0.06933287,
    0.29272546,
    -0.65555156,
    0.41918066,
    -0.09400974,
)


def kernel_value(squared):
    inverse = lax.rsqrt(squared)
    divisor = 1.0 + SLOPE * (squared * inverse)
    t = pl.reciprocal(divisor, approx=True)
    t = t * (2.0 - divisor * t)
    poly = ERFC[-1] * t + ERFC[-2]
    for c in ERFC[-3::-1]:
        poly = poly * t + c
    return jnp.exp2(DECAY * squared) * (t * inverse) * poly


def body(
    centers_hbm,
    bra_hbm,
    ket_hbm,
    quartets_hbm,
    count,
    owner_hbm,
    density_hbm,
    out,
    centers,
    bra_pairs,
    ket_pairs,
    quartets,
    owner,
    slots_vmem,
    slots,
    sib_slots_vmem,
    sib_slots,
    places_vmem,
    places,
    fetch,
    gathered,
    lines,
    columns,
    bra_tiles,
    ket_tiles,
    sib_tiles,
    spread,
    product,
    weighted,
    w_own,
    w_sib,
    keep,
    x_out,
    rel_in,
    x_in,
    z_out,
    z_in,
    part_send,
    part_recv,
    ring_send,
    ring_recv,
    sib_send,
    sib_recv,
    swap_send,
    swap_recv,
    share_send,
    share_recv,
    rel_send,
    rel_recv,
    x_send,
    x_recv,
    z_send,
    z_recv,
):
    row = lax.axis_index("bra")
    col = lax.axis_index("ket")
    y, deep = row // DEEP, row % DEEP
    core = col % 2
    zl = (col // 2) % SIDE
    xx = col // (2 * SIDE)

    def at_row(yy, dd):
        return lax.rem(yy + 2 * RING, RING) * DEEP + dd

    def at_col(x_at, z_at, core_at):
        return (lax.rem(x_at + SIDE, SIDE) * SIDE + z_at) * 2 + core_at

    up, down = at_row(y + 1, deep), at_row(y - 1, deep)
    partner = at_row(y, 1 - deep)
    sibling = at_col(xx, zl, 1 - core)
    x_up, x_down = at_col(xx + 1, zl, core), at_col(xx - 1, zl, core)

    def z_at(step):
        return lax.rem(zl + step, SIDE)

    peers = [(up, col), (down, col), (partner, col), (row, sibling), (row, x_up), (row, x_down)]
    peers += [(row, at_col(xx, z_at(step), core)) for step in range(1, SIDE)]
    peers += [(row, at_col(xx + 2, zl, core))]
    barrier = pltpu.get_barrier_semaphore()
    for peer in peers:
        pl.semaphore_signal(barrier, inc=1, device_id=peer, device_id_type=MESH)
    own_slots = gathered.at[pl.ds(row * OWN, OWN)]
    sources = (ket_hbm, bra_hbm, centers_hbm, owner_hbm, quartets_hbm, density_hbm)
    targets = (ket_pairs, bra_pairs, centers, owner, quartets, own_slots)
    fetches = [
        pltpu.make_async_copy(src, dst, fetch.at[n])
        for n, (src, dst) in enumerate(zip(sources, targets))
    ]
    for copy in fetches:
        copy.start()
    for tiles in (bra_tiles, ket_tiles, sib_tiles):
        tiles[PAIRS] = jnp.zeros((BLOCK, BLOCK), BF16)
    for part, (_, rows) in enumerate(PARTS):
        w_own[part][PAIRS] = jnp.zeros((rows, BLOCK), BF16)
        w_sib[part][PAIRS] = jnp.zeros((rows, BLOCK), BF16)
    pl.semaphore_wait(barrier, len(peers))

    def remote(src, dst, send, recv, device):
        return pltpu.make_async_remote_copy(
            src_ref=src,
            dst_ref=dst,
            send_sem=send,
            recv_sem=recv,
            device_id=device,
            device_id_type=MESH,
        )

    def to_partner(place):
        return remote(
            density_hbm.at[pl.ds(place, 1)],
            gathered.at[pl.ds(row * OWN + place, 1)],
            part_send.at[place],
            part_recv.at[place],
            (partner, col),
        )

    for place in (0, 2, 1, 3):
        to_partner(place).start()

    def depth(family):
        return deep if family == 0 else 1 - deep

    def hop(family, way, m, arriving, first=False):
        sign = 1 - 2 * way
        back = m // OWN + arriving
        place = lax.rem(m + 2 * way, OWN)
        ref = gathered.at[pl.ds(at_row(y - sign * back, depth(family)) * OWN + place, 1)]
        src = density_hbm.at[pl.ds(place, 1)] if first else ref
        device = (up, col) if way == 0 else (down, col)
        return remote(
            src, ref, ring_send.at[family, way, m], ring_recv.at[family, way, m], device
        )

    last = 3 * OWN + OWN // 2

    def send_own(family, m):
        for way in range(2):
            hop(family, way, m, 0, family == 0).start()

    def arrive(family, m):
        for way in range(2):
            hop(family, way, m, 1).wait_recv()

    def forward(family, m):
        for way in range(2):
            hop(family, way, m - OWN, 1).wait_recv()
            hop(family, way, m, 0).start()

    for m in range(OWN):
        send_own(0, m)
    for copy in fetches[:-1]:
        copy.wait()

    lane = lax.broadcasted_iota(jnp.int32, (8, BLOCK), 1)
    ket_table = jnp.full((8, BLOCK), PAIRS, jnp.int32)
    bra_table = jnp.full((8, BLOCK), PAIRS, jnp.int32)
    for n in range(PAIRS):
        ket_table = jnp.where(lane == ket_pairs[n], n, ket_table)
        bra_table = jnp.where(lane == owner[0, bra_pairs[n]], n, bra_table)
    slots_vmem[...] = ket_table
    places_vmem[...] = bra_table
    to_slots = pltpu.make_async_copy(slots_vmem, slots, fetch.at[len(fetches)])
    to_slots.start()
    to_places = pltpu.make_async_copy(places_vmem, places, fetch.at[len(fetches) + 1])
    to_places.start()
    there = (row, sibling)
    table_swap = remote(slots_vmem, sib_slots_vmem, sib_send.at[0], sib_recv.at[0], there)
    table_swap.start()

    for block in range(NBLK):
        lines[block, 0:3] = centers[:, block * BLOCK : (block + 1) * BLOCK]
    for side, start in ((0, row * (NBLK // 16)), (1, col * (NBLK // 32))):
        line = lines[start]
        for axis in range(3):
            wide = jnp.broadcast_to(line[axis : axis + 1], (BLOCK, BLOCK))
            columns[side, axis] = wide.T

    def tile(side, block, ref, place):
        line = lines[block]
        rows = 32
        for part in range(BLOCK // rows):
            squared = jnp.full((rows, BLOCK), SOFTEN, F32)
            for axis in range(3):
                difference = columns[side, axis, pl.ds(part * rows, rows)] - line[axis : axis + 1]
                squared = squared + difference * difference
            ref[place, pl.ds(part * rows, rows)] = kernel_value(squared).astype(BF16)

    def ket_tile(q):
        tile(1, ket_pairs[q], ket_tiles, q)

    def bra_tile(p):
        tile(0, bra_pairs[p], bra_tiles, p)

    def iota(shape, axis):
        return lax.broadcasted_iota(jnp.int32, shape, axis)

    def hot(condition):
        return jnp.where(condition, jnp.float32(1.0), jnp.float32(0.0)).astype(BF16)

    size = PAIRS * GROUP

    def count_pairs():
        long = (PAIRS, quartets.shape[3])
        bra_hot = hot((quartets[0, 0, 0:1] == iota(long, 0)) & (iota(long, 1) < count[0, 0]))
        ket_hot = hot(quartets[0, 0, 1:2] == iota(long, 0))
        return lax.dot_general(
            ket_hot, bra_hot, (((1,), (1,)), ((), ())), preferred_element_type=F32
        ).astype(BF16)

    def spread_rows(counts):
        by_slot = jnp.dot(
            counts, hot(bra_table[0:1] == iota((PAIRS, BLOCK), 0)), preferred_element_type=F32
        ).astype(BF16)
        tall = hot(iota((size, PAIRS), 0) >> SHIFT == iota((size, PAIRS), 1))
        return jnp.dot(tall, by_slot, preferred_element_type=F32).astype(BF16)

    def spread_family(rows_of, family):
        same = (iota((size, size), 0) ^ iota((size, size), 1)) & (GROUP - 1) == 0
        local_slot = iota((BLOCK, size), 1) >> SHIFT
        row_slot = (local_slot >> 2) * (OWN * DEEP) + (local_slot & (OWN - 1))
        wide = hot(row_slot + depth(family) * OWN == iota((BLOCK, size), 0))
        spread[family] = jnp.where(
            same, jnp.dot(rows_of, wide, preferred_element_type=F32), jnp.float32(0.0)
        ).astype(BF16)

    def z_row(family, yy):
        at = lax.rem(yy + 2 * RING, RING)
        for extra in range(OWN):
            s = (at * DEEP + depth(family)) * OWN + extra
            z = jnp.dot(bra_tiles[places[0, s]], gathered[s], preferred_element_type=F32)
            product[family, at * OWN + extra] = z.astype(BF16).astype(F32)

    def w_part(family, n):
        base = pl.multiple_of(n * 2 * GROUP, 2 * GROUP)
        halves = [
            product[family, :, pl.ds(base + half * GROUP, GROUP), :]
            .reshape(size, BLOCK)
            .astype(BF16)
            for half in range(2)
        ]
        both = jnp.dot(
            spread[family], jnp.concatenate(halves, axis=1), preferred_element_type=F32
        )
        return jnp.concatenate(
            [
                both[:, half * BLOCK : (half + 1) * BLOCK].reshape(PAIRS, GROUP, BLOCK)
                for half in range(2)
            ],
            axis=1,
        )

    def swap_tiles(src, dst, first, total, index):
        return remote(
            src.at[pl.ds(first, total)],
            dst.at[pl.ds(first, total)],
            sib_send.at[index],
            sib_recv.at[index],
            there,
        )

    share = PAIRS // (2 * SIDE)
    mine = core * (PAIRS // 2) + xx * share
    bra_swap = swap_tiles(bra_tiles, bra_tiles, core * (PAIRS // 2), PAIRS // 2, 1)
    ket_swap = swap_tiles(ket_tiles, sib_tiles, 0, PAIRS, 2)

    def bra_share(step):
        tiles = bra_tiles.at[pl.ds(mine, share)]
        return remote(
            tiles,
            tiles,
            share_send.at[step - 1],
            share_recv.at[step - 1],
            (row, at_col(xx + step, zl, core)),
        )

    def bra_shared(step):
        first = core * (PAIRS // 2) + lax.rem(xx - step + SIDE, SIDE) * share
        tiles = bra_tiles.at[pl.ds(first, share)]
        return remote(
            tiles,
            tiles,
            share_send.at[step - 1],
            share_recv.at[step - 1],
            (row, at_col(xx + step, zl, core)),
        )

    def ket_run(first, total):
        @pl.loop(first, first + total)
        def _(q):
            ket_tile(q)

    def w_first(first, total):
        @pl.loop(first, first + total)
        def _(n):
            weighted[:, pl.ds(n * 2 * GROUP, 2 * GROUP)] = w_part(0, n)

    @pl.loop(OWN, 2 * OWN)
    def _(m):
        forward(0, m)
        bra_tile(mine + m - OWN)

        @pl.loop(0, 2)
        def _(n):
            ket_tile((m - OWN) * 2 + n)

    for step in range(1, SIDE):
        bra_share(step).start()
    for m in range(OWN):
        forward(0, 2 * OWN + m)
        ket_run(8 + m * 3, 3)
        if m < 2:
            to_partner(m).wait_recv()
            to_partner(m + 2).wait_recv()
        send_own(1, m)
        if m == 0:
            counts = count_pairs()
        elif m == 1:
            rows_of = spread_rows(counts)
        else:
            spread_family(rows_of, m - 2)
    for m in range(2):
        forward(1, OWN + m)
        ket_run(20 + m * 6, 3)
        forward(0, 3 * OWN + m)
        if m == 0:
            for step in range(1, SIDE):
                bra_shared(step).wait_recv()
            bra_swap.start()
        ket_run(23 + m * 6, 3)
    ket_swap.start()
    bra_swap.wait()
    to_places.wait()
    fetches[-1].wait()
    forward(1, OWN + 2)
    z_row(0, y)
    z_row(0, y - 1)
    forward(1, OWN + 3)
    z_row(0, y + 1)
    z_row(0, y - 2)
    forward(1, 2 * OWN)
    z_row(0, y + 2)
    arrive(0, last - 4)
    arrive(0, last - 3)
    z_row(0, y - 3)
    forward(1, 2 * OWN + 1)
    z_row(0, y + 3)
    arrive(0, last - 2)
    arrive(0, last - 1)
    z_row(0, y + 4)
    forward(1, 2 * OWN + 2)
    w_first(0, 3)
    forward(1, 2 * OWN + 3)
    w_first(3, 2)
    forward(1, 3 * OWN)
    w_first(5, 1)
    forward(1, 3 * OWN + 1)
    w_first(6, 2)
    for away in (0, 1, -1, 2, -2):
        z_row(1, y + away)
    arrive(1, last - 4)
    arrive(1, last - 3)
    z_row(1, y - 3)
    z_row(1, y + 3)
    table_swap.wait()
    sib_to_slots = pltpu.make_async_copy(sib_slots_vmem, sib_slots, fetch.at[len(fetches) + 2])
    sib_to_slots.start()
    arrive(1, last - 2)
    arrive(1, last - 1)
    z_row(1, y + 4)

    def w_swap(part):
        return remote(
            w_own[part].at[pl.ds(0, PAIRS)],
            w_sib[part].at[pl.ds(0, PAIRS)],
            swap_send.at[part],
            swap_recv.at[part],
            there,
        )

    for part, (start, rows) in enumerate(PARTS):

        @pl.loop(0, rows // (2 * GROUP))
        def _(n):
            at = pl.multiple_of(n * 2 * GROUP, 2 * GROUP)
            total = w_part(1, n + start // (2 * GROUP))
            total = total + weighted[:, pl.ds(at + start, 2 * GROUP)]
            w_own[part][0:PAIRS, pl.ds(at, 2 * GROUP)] = total.astype(BF16)

        w_swap(part).start()

    def image(d, zz, jj, part):
        j = (lax.rem(xx + d, SIDE) * SIDE + zz) * 4 + core * 2 + jj
        a, b = slots[0, j], sib_slots[0, j]
        left = jnp.concatenate([w_own[part][a], w_sib[part][b]], axis=1)
        right = jnp.concatenate([ket_tiles[a], sib_tiles[b]], axis=0)
        return jnp.dot(left, right, preferred_element_type=F32)

    def relay(way, part):
        device = (row, x_up) if way == 0 else (row, x_down)
        return remote(
            x_out[part].at[2, way],
            rel_in[part].at[way],
            rel_send.at[part, way],
            rel_recv.at[part, way],
            device,
        )

    def to_x(way, jj, part):
        device = (row, x_up) if way == 0 else (row, x_down)
        return remote(
            x_out[part].at[way, jj],
            x_in[part].at[way, jj],
            x_send.at[part, way, jj],
            x_recv.at[part, way, jj],
            device,
        )

    def to_z(step, part):
        return remote(
            z_out[part].at[step - 1],
            z_in[part].at[step - 1],
            z_send.at[part, step - 1],
            z_recv.at[part, step - 1],
            (row, at_col(xx, z_at(step), core)),
        )

    def relays(part):
        for way in range(2):
            for zz in range(SIDE):
                x_out[part][2, way, zz] = image(2, zz, way, part).astype(BF16)
            relay(way, part).start()

    def direct(part):
        for way, d in ((0, 1), (1, 3)):
            for zz in range(SIDE):
                x_out[part][way, 1 - way, zz] = image(d, zz, 1 - way, part).astype(BF16)
            to_x(way, 1 - way, part).start()

    def summed(part):
        for way, d in ((0, 1), (1, 3)):
            images = [image(d, zz, way, part) for zz in range(SIDE)]
            relay(way, part).wait_recv()
            for zz in range(SIDE):
                total = images[zz] + rel_in[part][way, zz].astype(F32)
                x_out[part][way, way, zz] = total.astype(BF16)
            to_x(way, way, part).start()

    def own_sum(part):
        for jj in range(2):
            for zz in range(SIDE):
                keep[part][jj, zz] = image(0, zz, jj, part)

    def from_x(part):
        for jj in range(2):
            for way in (1 - jj, jj):
                to_x(way, jj, part).wait_recv()
                keep[part][jj] = keep[part][jj] + x_in[part][way, jj].astype(F32)
        for step in (2, 3, 1):
            for jj in range(2):
                z_out[part][step - 1, jj] = keep[part][jj, z_at(step)].astype(BF16)
            to_z(step, part).start()

    def finish(part):
        for step in (1, 3, 2):
            to_z(step, part).wait_recv()
        start, rows = PARTS[part]
        for jj in range(2):
            total = keep[part][jj, zl]
            for step in range(1, SIDE):
                total = total + z_in[part][step - 1, jj].astype(F32)
            out[start : start + rows, jj * BLOCK : (jj + 1) * BLOCK] = total.astype(BF16)

    to_slots.wait()
    sib_to_slots.wait()
    ket_swap.wait()
    w_swap(0).wait()
    relays(0)
    direct(0)
    w_swap(1).wait()
    relays(1)
    summed(0)
    direct(1)
    w_swap(2).wait()
    relays(2)
    summed(1)
    direct(2)
    own_sum(0)
    from_x(0)
    summed(2)
    own_sum(1)
    own_sum(2)
    from_x(1)

    @pl.loop(0, last)
    def _(m):
        for family in range(2):
            for way in range(2):
                hop(family, way, m, 0).wait_send()

    for place in range(OWN):
        to_partner(place).wait_send()
    for step in range(1, SIDE):
        bra_share(step).wait_send()
    from_x(2)
    finish(0)
    finish(1)
    for part in range(len(PARTS)):
        for way in range(2):
            relay(way, part).wait_send()
            for jj in range(2):
                to_x(way, jj, part).wait_send()
        for step in range(1, SIDE):
            to_z(step, part).wait_send()
    finish(2)


def local(
    basis_centers, bra_pairs, ket_pairs, quartets, quartet_counts, density_owner, density_store
):
    hbm = pl.BlockSpec(memory_space=pltpu.HBM)
    smem, i32 = pltpu.SMEM, jnp.int32
    block, count = (BLOCK, BLOCK), len(PARTS)

    def parts(lead, kind=BF16):
        return [pltpu.VMEM(lead + (rows, BLOCK), kind) for _, rows in PARTS]

    dma = pltpu.SemaphoreType.DMA
    hops = 3 * OWN + OWN // 2
    return pl.pallas_call(
        body,
        out_shape=jax.ShapeDtypeStruct((BLOCK, 2 * BLOCK), BF16),
        in_specs=[hbm] * 4 + [pl.BlockSpec(memory_space=smem)] + [hbm] * 2,
        out_specs=pl.BlockSpec(memory_space=pltpu.VMEM),
        scratch_shapes=[
            pltpu.VMEM(basis_centers.shape, F32),
            smem(bra_pairs.shape, i32),
            smem(ket_pairs.shape, i32),
            pltpu.VMEM(quartets.shape, i32),
            smem(density_owner.shape, i32),
            pltpu.VMEM((8, BLOCK), i32),
            smem((8, BLOCK), i32),
            pltpu.VMEM((8, BLOCK), i32),
            smem((8, BLOCK), i32),
            pltpu.VMEM((8, BLOCK), i32),
            smem((8, BLOCK), i32),
            dma((9,)),
            pltpu.VMEM((NBLK,) + block, BF16),
            pltpu.VMEM((NBLK, 8, BLOCK), F32),
            pltpu.VMEM((2, 3) + block, F32),
            pltpu.VMEM((PAIRS + 1,) + block, BF16),
            pltpu.VMEM((PAIRS + 1,) + block, BF16),
            pltpu.VMEM((PAIRS + 1,) + block, BF16),
            pltpu.VMEM((2, PAIRS * GROUP, PAIRS * GROUP), BF16),
            pltpu.VMEM((2, PAIRS) + block, F32),
            pltpu.VMEM((PAIRS,) + block, F32),
            parts((PAIRS + 1,)),
            parts((PAIRS + 1,)),
            parts((2, SIDE), F32),
            parts((3, 2, SIDE)),
            parts((2, SIDE)),
            parts((2, 2, SIDE)),
            parts((3, 2)),
            parts((3, 2)),
            dma((OWN,)),
            dma((OWN,)),
            dma((2, 2, hops)),
            dma((2, 2, hops)),
            dma((3,)),
            dma((3,)),
            dma((count,)),
            dma((count,)),
            dma((SIDE - 1,)),
            dma((SIDE - 1,)),
            dma((count, 2)),
            dma((count, 2)),
            dma((count, 2, 2)),
            dma((count, 2, 2)),
            dma((count, 3)),
            dma((count, 3)),
        ],
        compiler_params=pltpu.CompilerParams(
            collective_id=0, has_side_effects=True, vmem_limit_bytes=56 * 2**20
        ),
        cost_estimate=pl.CostEstimate(
            flops=2 * 10**9, bytes_accessed=4 * 2**20, transcendentals=4 * 10**6
        ),
    )(
        basis_centers,
        bra_pairs,
        ket_pairs,
        quartets,
        quartet_counts,
        density_owner,
        density_store,
    )


def solution(mesh):
    return jax.shard_map(
        local,
        mesh=mesh,
        in_specs=(
            P(),
            P("bra"),
            P("ket"),
            P("bra", "ket", None, None),
            P("bra", "ket"),
            P("ket", None),
            P("bra", "ket", None),
        ),
        out_specs=P("bra", "ket"),
        check_vma=False,
    )
```

```python
import jax
import jax.numpy as jnp
from jax import lax
from jax.experimental import pallas as pl
from jax.experimental.pallas import tpu as pltpu
from jax.sharding import PartitionSpec as P

OMEGA = 0.11
SOFTEN = 0.25
BLOCK = 128
NBLK = 64
PAIRS = 32
RING = 8
DEEP = 2
SIDE = 4
OWN = 4
PARTS = ((0, 32), (32, 64), (96, 32))
GROUP = 8
SHIFT = 3
MESH = pl.DeviceIdType.MESH
F32 = jnp.float32
BF16 = jnp.bfloat16

SLOPE = 0.6 * OMEGA
DECAY = -OMEGA * OMEGA * 1.4426950408889634
ERFC = (
    0.33856715,
    0.33711259,
    0.29264139,
    0.06933287,
    0.29272546,
    -0.65555156,
    0.41918066,
    -0.09400974,
)


def kernel_value(squared):
    inverse = lax.rsqrt(squared)
    divisor = 1.0 + SLOPE * (squared * inverse)
    t = pl.reciprocal(divisor, approx=True)
    t = t * (2.0 - divisor * t)
    poly = ERFC[-1] * t + ERFC[-2]
    for c in ERFC[-3::-1]:
        poly = poly * t + c
    return jnp.exp2(DECAY * squared) * (t * inverse) * poly


def body(
    centers_hbm,
    bra_hbm,
    ket_hbm,
    quartets_hbm,
    count,
    owner_hbm,
    density_hbm,
    out,
    centers,
    bra_pairs,
    ket_pairs,
    quartets,
    owner,
    slots_vmem,
    slots,
    sib_slots_vmem,
    sib_slots,
    places_vmem,
    places,
    fetch,
    gathered,
    lines,
    columns,
    bra_tiles,
    ket_tiles,
    sib_tiles,
    spread,
    product,
    weighted,
    w_own,
    w_sib,
    keep,
    x_out,
    rel_in,
    x_in,
    z_out,
    z_in,
    passing,
    side_send,
    side_recv,
    part_send,
    part_recv,
    ring_send,
    ring_recv,
    sib_send,
    sib_recv,
    swap_send,
    swap_recv,
    share_send,
    share_recv,
    rel_send,
    rel_recv,
    x_send,
    x_recv,
    z_send,
    z_recv,
):
    row = lax.axis_index("bra")
    col = lax.axis_index("ket")
    y, deep = row // DEEP, row % DEEP
    core = col % 2
    zl = (col // 2) % SIDE
    xx = col // (2 * SIDE)

    def at_row(yy, dd):
        return lax.rem(yy + 2 * RING, RING) * DEEP + dd

    def at_col(x_at, z_at, core_at):
        return (lax.rem(x_at + SIDE, SIDE) * SIDE + z_at) * 2 + core_at

    up, down = at_row(y + 1, deep), at_row(y - 1, deep)
    partner = at_row(y, 1 - deep)
    sibling = at_col(xx, zl, 1 - core)
    x_up, x_down = at_col(xx + 1, zl, core), at_col(xx - 1, zl, core)

    def z_at(step):
        return lax.rem(zl + step, SIDE)

    same_side = (row, at_col(xx, z_at(2), core))
    other_side = (partner, at_col(xx, z_at(2), core))
    peers = [(up, col), (down, col), other_side, (row, sibling), (row, x_up), (row, x_down)]
    peers += [(row, at_col(xx, z_at(step), core)) for step in range(1, SIDE)]
    peers += [(row, at_col(xx + 2, zl, core))]
    barrier = pltpu.get_barrier_semaphore()
    for peer in peers:
        pl.semaphore_signal(barrier, inc=1, device_id=peer, device_id_type=MESH)
    own_slots = gathered.at[pl.ds(row * OWN, OWN)]
    sources = (ket_hbm, bra_hbm, centers_hbm, owner_hbm, quartets_hbm, density_hbm)
    targets = (ket_pairs, bra_pairs, centers, owner, quartets, own_slots)
    fetches = [
        pltpu.make_async_copy(src, dst, fetch.at[n])
        for n, (src, dst) in enumerate(zip(sources, targets))
    ]
    for copy in fetches:
        copy.start()
    for tiles in (bra_tiles, ket_tiles, sib_tiles):
        tiles[PAIRS] = jnp.zeros((BLOCK, BLOCK), BF16)
    for part, (_, rows) in enumerate(PARTS):
        w_own[part][PAIRS] = jnp.zeros((rows, BLOCK), BF16)
        w_sib[part][PAIRS] = jnp.zeros((rows, BLOCK), BF16)
    pl.semaphore_wait(barrier, len(peers))

    def remote(src, dst, send, recv, device):
        return pltpu.make_async_remote_copy(
            src_ref=src,
            dst_ref=dst,
            send_sem=send,
            recv_sem=recv,
            device_id=device,
            device_id_type=MESH,
        )

    def to_side(place):
        return remote(
            density_hbm.at[pl.ds(place, 1)],
            passing.at[pl.ds(place, 1)],
            side_send.at[place],
            side_recv.at[place],
            same_side if place < 2 else other_side,
        )

    def pass_on(place):
        origin = row if place < 2 else partner
        return remote(
            passing.at[pl.ds(place, 1)],
            gathered.at[pl.ds(origin * OWN + place, 1)],
            part_send.at[place],
            part_recv.at[place],
            other_side if place < 2 else same_side,
        )

    def from_partner(place):
        ref = gathered.at[pl.ds(partner * OWN + place, 1)]
        device = other_side if place < 2 else same_side
        return remote(ref, ref, part_send.at[place], part_recv.at[place], device)

    for place in (0, 2, 1, 3):
        to_side(place).start()

    def depth(family):
        return deep if family == 0 else 1 - deep

    def hop(family, way, m, arriving, first=False):
        sign = 1 - 2 * way
        back = m // OWN + arriving
        place = lax.rem(m + 2 * way, OWN)
        ref = gathered.at[pl.ds(at_row(y - sign * back, depth(family)) * OWN + place, 1)]
        src = density_hbm.at[pl.ds(place, 1)] if first else ref
        device = (up, col) if way == 0 else (down, col)
        return remote(
            src, ref, ring_send.at[family, way, m], ring_recv.at[family, way, m], device
        )

    last = 3 * OWN + OWN // 2

    def send_own(family, m):
        for way in range(2):
            hop(family, way, m, 0, family == 0).start()

    def arrive(family, m):
        for way in range(2):
            hop(family, way, m, 1).wait_recv()

    def forward(family, m):
        for way in range(2):
            hop(family, way, m - OWN, 1).wait_recv()
            hop(family, way, m, 0).start()

    for m in range(OWN):
        send_own(0, m)
    for copy in fetches[:-1]:
        copy.wait()

    lane = lax.broadcasted_iota(jnp.int32, (8, BLOCK), 1)
    ket_table = jnp.full((8, BLOCK), PAIRS, jnp.int32)
    bra_table = jnp.full((8, BLOCK), PAIRS, jnp.int32)
    for n in range(PAIRS):
        ket_table = jnp.where(lane == ket_pairs[n], n, ket_table)
        bra_table = jnp.where(lane == owner[0, bra_pairs[n]], n, bra_table)
    slots_vmem[...] = ket_table
    places_vmem[...] = bra_table
    to_slots = pltpu.make_async_copy(slots_vmem, slots, fetch.at[len(fetches)])
    to_slots.start()
    to_places = pltpu.make_async_copy(places_vmem, places, fetch.at[len(fetches) + 1])
    to_places.start()
    there = (row, sibling)
    table_swap = remote(slots_vmem, sib_slots_vmem, sib_send.at[0], sib_recv.at[0], there)
    table_swap.start()

    for block in range(NBLK):
        lines[block, 0:3] = centers[:, block * BLOCK : (block + 1) * BLOCK]
    for side, start in ((0, row * (NBLK // 16)), (1, col * (NBLK // 32))):
        line = lines[start]
        for axis in range(3):
            wide = jnp.broadcast_to(line[axis : axis + 1], (BLOCK, BLOCK))
            columns[side, axis] = wide.T

    def tile(side, block, ref, place):
        line = lines[block]
        rows = 32
        for part in range(BLOCK // rows):
            squared = jnp.full((rows, BLOCK), SOFTEN, F32)
            for axis in range(3):
                difference = columns[side, axis, pl.ds(part * rows, rows)] - line[axis : axis + 1]
                squared = squared + difference * difference
            ref[place, pl.ds(part * rows, rows)] = kernel_value(squared).astype(BF16)

    def ket_tile(q):
        tile(1, ket_pairs[q], ket_tiles, q)

    def bra_tile(p):
        tile(0, bra_pairs[p], bra_tiles, p)

    def iota(shape, axis):
        return lax.broadcasted_iota(jnp.int32, shape, axis)

    def hot(condition):
        return jnp.where(condition, jnp.float32(1.0), jnp.float32(0.0)).astype(BF16)

    size = PAIRS * GROUP

    def count_pairs():
        long = (PAIRS, quartets.shape[3])
        bra_hot = hot((quartets[0, 0, 0:1] == iota(long, 0)) & (iota(long, 1) < count[0, 0]))
        ket_hot = hot(quartets[0, 0, 1:2] == iota(long, 0))
        return lax.dot_general(
            ket_hot, bra_hot, (((1,), (1,)), ((), ())), preferred_element_type=F32
        ).astype(BF16)

    def spread_rows(counts):
        by_slot = jnp.dot(
            counts, hot(bra_table[0:1] == iota((PAIRS, BLOCK), 0)), preferred_element_type=F32
        ).astype(BF16)
        tall = hot(iota((size, PAIRS), 0) >> SHIFT == iota((size, PAIRS), 1))
        return jnp.dot(tall, by_slot, preferred_element_type=F32).astype(BF16)

    def spread_family(rows_of, family):
        same = (iota((size, size), 0) ^ iota((size, size), 1)) & (GROUP - 1) == 0
        local_slot = iota((BLOCK, size), 1) >> SHIFT
        row_slot = (local_slot >> 2) * (OWN * DEEP) + (local_slot & (OWN - 1))
        wide = hot(row_slot + depth(family) * OWN == iota((BLOCK, size), 0))
        spread[family] = jnp.where(
            same, jnp.dot(rows_of, wide, preferred_element_type=F32), jnp.float32(0.0)
        ).astype(BF16)

    def z_row(family, yy):
        at = lax.rem(yy + 2 * RING, RING)
        for extra in range(OWN):
            s = (at * DEEP + depth(family)) * OWN + extra
            z = jnp.dot(bra_tiles[places[0, s]], gathered[s], preferred_element_type=F32)
            product[family, at * OWN + extra] = z.astype(BF16).astype(F32)

    def w_part(family, n):
        base = pl.multiple_of(n * 2 * GROUP, 2 * GROUP)
        halves = [
            product[family, :, pl.ds(base + half * GROUP, GROUP), :]
            .reshape(size, BLOCK)
            .astype(BF16)
            for half in range(2)
        ]
        both = jnp.dot(
            spread[family], jnp.concatenate(halves, axis=1), preferred_element_type=F32
        )
        return jnp.concatenate(
            [
                both[:, half * BLOCK : (half + 1) * BLOCK].reshape(PAIRS, GROUP, BLOCK)
                for half in range(2)
            ],
            axis=1,
        )

    def swap_tiles(src, dst, first, total, index):
        return remote(
            src.at[pl.ds(first, total)],
            dst.at[pl.ds(first, total)],
            sib_send.at[index],
            sib_recv.at[index],
            there,
        )

    share = PAIRS // (2 * SIDE)
    mine = core * (PAIRS // 2) + xx * share
    bra_swap = swap_tiles(bra_tiles, bra_tiles, core * (PAIRS // 2), PAIRS // 2, 1)
    ket_swap = swap_tiles(ket_tiles, sib_tiles, 0, PAIRS, 2)

    def bra_share(step):
        tiles = bra_tiles.at[pl.ds(mine, share)]
        return remote(
            tiles,
            tiles,
            share_send.at[step - 1],
            share_recv.at[step - 1],
            (row, at_col(xx + step, zl, core)),
        )

    def bra_shared(step):
        first = core * (PAIRS // 2) + lax.rem(xx - step + SIDE, SIDE) * share
        tiles = bra_tiles.at[pl.ds(first, share)]
        return remote(
            tiles,
            tiles,
            share_send.at[step - 1],
            share_recv.at[step - 1],
            (row, at_col(xx + step, zl, core)),
        )

    def ket_run(first, total):
        @pl.loop(first, first + total)
        def _(q):
            ket_tile(q)

    def w_first(first, total):
        @pl.loop(first, first + total)
        def _(n):
            weighted[:, pl.ds(n * 2 * GROUP, 2 * GROUP)] = w_part(0, n)

    for m in range(OWN):
        forward(0, OWN + m)
        if m < 2:
            for place in (m, m + 2):
                to_side(place).wait_recv()
                pass_on(place).start()
        bra_tile(mine + m)
        ket_run(2 * m, 2)

    for step in range(1, SIDE):
        bra_share(step).start()
    for m in range(OWN):
        forward(0, 2 * OWN + m)
        ket_run(8 + m * 3, 3)
        if m < 2:
            from_partner(m).wait_recv()
            from_partner(m + 2).wait_recv()
        send_own(1, m)
        if m == 0:
            counts = count_pairs()
        elif m == 1:
            rows_of = spread_rows(counts)
        else:
            spread_family(rows_of, m - 2)
    for m in range(2):
        forward(1, OWN + m)
        ket_run(20 + m * 6, 3)
        forward(0, 3 * OWN + m)
        if m == 0:
            for step in range(1, SIDE):
                bra_shared(step).wait_recv()
            bra_swap.start()
        ket_run(23 + m * 6, 3)
    ket_swap.start()
    bra_swap.wait()
    to_places.wait()
    fetches[-1].wait()
    forward(1, OWN + 2)
    z_row(0, y)
    z_row(0, y - 1)
    forward(1, OWN + 3)
    z_row(0, y + 1)
    z_row(0, y - 2)
    forward(1, 2 * OWN)
    z_row(0, y + 2)
    arrive(0, last - 4)
    arrive(0, last - 3)
    z_row(0, y - 3)
    forward(1, 2 * OWN + 1)
    z_row(0, y + 3)
    arrive(0, last - 2)
    arrive(0, last - 1)
    z_row(0, y + 4)
    forward(1, 2 * OWN + 2)
    w_first(0, 3)
    forward(1, 2 * OWN + 3)
    w_first(3, 2)
    forward(1, 3 * OWN)
    w_first(5, 1)
    forward(1, 3 * OWN + 1)
    w_first(6, 2)
    for away in (0, 1, -1, 2, -2):
        z_row(1, y + away)
    arrive(1, last - 4)
    arrive(1, last - 3)
    z_row(1, y - 3)
    z_row(1, y + 3)
    table_swap.wait()
    sib_to_slots = pltpu.make_async_copy(sib_slots_vmem, sib_slots, fetch.at[len(fetches) + 2])
    sib_to_slots.start()
    arrive(1, last - 2)
    arrive(1, last - 1)
    z_row(1, y + 4)

    def w_swap(part):
        return remote(
            w_own[part].at[pl.ds(0, PAIRS)],
            w_sib[part].at[pl.ds(0, PAIRS)],
            swap_send.at[part],
            swap_recv.at[part],
            there,
        )

    for part, (start, rows) in enumerate(PARTS):

        @pl.loop(0, rows // (2 * GROUP))
        def _(n):
            at = pl.multiple_of(n * 2 * GROUP, 2 * GROUP)
            total = w_part(1, n + start // (2 * GROUP))
            total = total + weighted[:, pl.ds(at + start, 2 * GROUP)]
            w_own[part][0:PAIRS, pl.ds(at, 2 * GROUP)] = total.astype(BF16)

        w_swap(part).start()

    def image(d, zz, jj, part):
        j = (lax.rem(xx + d, SIDE) * SIDE + zz) * 4 + core * 2 + jj
        a, b = slots[0, j], sib_slots[0, j]
        left = jnp.concatenate([w_own[part][a], w_sib[part][b]], axis=1)
        right = jnp.concatenate([ket_tiles[a], sib_tiles[b]], axis=0)
        return jnp.dot(left, right, preferred_element_type=F32)

    def relay(way, part):
        device = (row, x_up) if way == 0 else (row, x_down)
        return remote(
            x_out[part].at[2, way],
            rel_in[part].at[way],
            rel_send.at[part, way],
            rel_recv.at[part, way],
            device,
        )

    def to_x(way, jj, part):
        device = (row, x_up) if way == 0 else (row, x_down)
        return remote(
            x_out[part].at[way, jj],
            x_in[part].at[way, jj],
            x_send.at[part, way, jj],
            x_recv.at[part, way, jj],
            device,
        )

    def to_z(step, part):
        return remote(
            z_out[part].at[step - 1],
            z_in[part].at[step - 1],
            z_send.at[part, step - 1],
            z_recv.at[part, step - 1],
            (row, at_col(xx, z_at(step), core)),
        )

    def relays(part):
        for way in range(2):
            for zz in range(SIDE):
                x_out[part][2, way, zz] = image(2, zz, way, part).astype(BF16)
            relay(way, part).start()

    def direct(part):
        for way, d in ((0, 1), (1, 3)):
            for zz in range(SIDE):
                x_out[part][way, 1 - way, zz] = image(d, zz, 1 - way, part).astype(BF16)
            to_x(way, 1 - way, part).start()

    def summed(part):
        for way, d in ((0, 1), (1, 3)):
            images = [image(d, zz, way, part) for zz in range(SIDE)]
            relay(way, part).wait_recv()
            for zz in range(SIDE):
                total = images[zz] + rel_in[part][way, zz].astype(F32)
                x_out[part][way, way, zz] = total.astype(BF16)
            to_x(way, way, part).start()

    def own_sum(part):
        for jj in range(2):
            for zz in range(SIDE):
                keep[part][jj, zz] = image(0, zz, jj, part)

    def from_x(part):
        for jj in range(2):
            for way in (1 - jj, jj):
                to_x(way, jj, part).wait_recv()
                keep[part][jj] = keep[part][jj] + x_in[part][way, jj].astype(F32)
        for step in (2, 3, 1):
            for jj in range(2):
                z_out[part][step - 1, jj] = keep[part][jj, z_at(step)].astype(BF16)
            to_z(step, part).start()

    def finish(part):
        for step in (1, 3, 2):
            to_z(step, part).wait_recv()
        start, rows = PARTS[part]
        for jj in range(2):
            total = keep[part][jj, zl]
            for step in range(1, SIDE):
                total = total + z_in[part][step - 1, jj].astype(F32)
            out[start : start + rows, jj * BLOCK : (jj + 1) * BLOCK] = total.astype(BF16)

    to_slots.wait()
    sib_to_slots.wait()
    ket_swap.wait()
    w_swap(0).wait()
    relays(0)
    direct(0)
    w_swap(1).wait()
    relays(1)
    summed(0)
    direct(1)
    w_swap(2).wait()
    relays(2)
    summed(1)
    direct(2)
    own_sum(0)
    from_x(0)
    summed(2)
    own_sum(1)
    own_sum(2)
    from_x(1)

    @pl.loop(0, last)
    def _(m):
        for family in range(2):
            for way in range(2):
                hop(family, way, m, 0).wait_send()

    for place in range(OWN):
        to_side(place).wait_send()
        pass_on(place).wait_send()
    for step in range(1, SIDE):
        bra_share(step).wait_send()
    from_x(2)
    finish(0)
    finish(1)
    for part in range(len(PARTS)):
        for way in range(2):
            relay(way, part).wait_send()
            for jj in range(2):
                to_x(way, jj, part).wait_send()
        for step in range(1, SIDE):
            to_z(step, part).wait_send()
    finish(2)


def local(
    basis_centers, bra_pairs, ket_pairs, quartets, quartet_counts, density_owner, density_store
):
    hbm = pl.BlockSpec(memory_space=pltpu.HBM)
    smem, i32 = pltpu.SMEM, jnp.int32
    block, count = (BLOCK, BLOCK), len(PARTS)

    def parts(lead, kind=BF16):
        return [pltpu.VMEM(lead + (rows, BLOCK), kind) for _, rows in PARTS]

    dma = pltpu.SemaphoreType.DMA
    hops = 3 * OWN + OWN // 2
    return pl.pallas_call(
        body,
        out_shape=jax.ShapeDtypeStruct((BLOCK, 2 * BLOCK), BF16),
        in_specs=[hbm] * 4 + [pl.BlockSpec(memory_space=smem)] + [hbm] * 2,
        out_specs=pl.BlockSpec(memory_space=pltpu.VMEM),
        scratch_shapes=[
            pltpu.VMEM(basis_centers.shape, F32),
            smem(bra_pairs.shape, i32),
            smem(ket_pairs.shape, i32),
            pltpu.VMEM(quartets.shape, i32),
            smem(density_owner.shape, i32),
            pltpu.VMEM((8, BLOCK), i32),
            smem((8, BLOCK), i32),
            pltpu.VMEM((8, BLOCK), i32),
            smem((8, BLOCK), i32),
            pltpu.VMEM((8, BLOCK), i32),
            smem((8, BLOCK), i32),
            dma((9,)),
            pltpu.VMEM((NBLK,) + block, BF16),
            pltpu.VMEM((NBLK, 8, BLOCK), F32),
            pltpu.VMEM((2, 3) + block, F32),
            pltpu.VMEM((PAIRS + 1,) + block, BF16),
            pltpu.VMEM((PAIRS + 1,) + block, BF16),
            pltpu.VMEM((PAIRS + 1,) + block, BF16),
            pltpu.VMEM((2, PAIRS * GROUP, PAIRS * GROUP), BF16),
            pltpu.VMEM((2, PAIRS) + block, F32),
            pltpu.VMEM((PAIRS,) + block, F32),
            parts((PAIRS + 1,)),
            parts((PAIRS + 1,)),
            parts((2, SIDE), F32),
            parts((3, 2, SIDE)),
            parts((2, SIDE)),
            parts((2, 2, SIDE)),
            parts((3, 2)),
            parts((3, 2)),
            pltpu.VMEM((OWN,) + block, BF16),
            dma((OWN,)),
            dma((OWN,)),
            dma((OWN,)),
            dma((OWN,)),
            dma((2, 2, hops)),
            dma((2, 2, hops)),
            dma((3,)),
            dma((3,)),
            dma((count,)),
            dma((count,)),
            dma((SIDE - 1,)),
            dma((SIDE - 1,)),
            dma((count, 2)),
            dma((count, 2)),
            dma((count, 2, 2)),
            dma((count, 2, 2)),
            dma((count, 3)),
            dma((count, 3)),
        ],
        compiler_params=pltpu.CompilerParams(
            collective_id=0, has_side_effects=True, vmem_limit_bytes=56 * 2**20
        ),
        cost_estimate=pl.CostEstimate(
            flops=2 * 10**9, bytes_accessed=4 * 2**20, transcendentals=4 * 10**6
        ),
    )(
        basis_centers,
        bra_pairs,
        ket_pairs,
        quartets,
        quartet_counts,
        density_owner,
        density_store,
    )


def solution(mesh):
    return jax.shard_map(
        local,
        mesh=mesh,
        in_specs=(
            P(),
            P("bra"),
            P("ket"),
            P("bra", "ket", None, None),
            P("bra", "ket"),
            P("ket", None),
            P("bra", "ket", None),
        ),
        out_specs=P("bra", "ket"),
        check_vma=False,
    )
```

```python
import jax
import jax.numpy as jnp
from jax import lax
from jax.experimental import pallas as pl
from jax.experimental.pallas import tpu as pltpu
from jax.sharding import PartitionSpec as P

OMEGA = 0.11
SOFTEN = 0.25
BLOCK = 128
NBLK = 64
PAIRS = 32
RING = 8
DEEP = 2
SIDE = 4
OWN = 4
PIECE = 2
PER = OWN // PIECE
PARTS = ((0, 32), (32, 64), (96, 32))
GROUP = 8
SHIFT = 3
MESH = pl.DeviceIdType.MESH
F32 = jnp.float32
BF16 = jnp.bfloat16

SLOPE = 0.6 * OMEGA
DECAY = -OMEGA * OMEGA * 1.4426950408889634
ERFC = (
    0.33856715,
    0.33711259,
    0.29264139,
    0.06933287,
    0.29272546,
    -0.65555156,
    0.41918066,
    -0.09400974,
)


def kernel_value(squared):
    inverse = lax.rsqrt(squared)
    divisor = 1.0 + SLOPE * (squared * inverse)
    t = pl.reciprocal(divisor, approx=True)
    t = t * (2.0 - divisor * t)
    poly = ERFC[-1] * t + ERFC[-2]
    for c in ERFC[-3::-1]:
        poly = poly * t + c
    return jnp.exp2(DECAY * squared) * (t * inverse) * poly


def body(
    centers_hbm,
    bra_hbm,
    ket_hbm,
    quartets_hbm,
    count,
    owner_hbm,
    density_hbm,
    out,
    centers,
    bra_pairs,
    ket_pairs,
    quartets,
    owner,
    slots_vmem,
    slots,
    sib_slots_vmem,
    sib_slots,
    places_vmem,
    places,
    fetch,
    gathered,
    lines,
    columns,
    bra_tiles,
    ket_tiles,
    sib_tiles,
    spread,
    product,
    weighted,
    w_own,
    w_sib,
    keep,
    x_out,
    rel_in,
    x_in,
    z_out,
    z_in,
    passing,
    side_send,
    side_recv,
    part_send,
    part_recv,
    ring_send,
    ring_recv,
    sib_send,
    sib_recv,
    swap_send,
    swap_recv,
    share_send,
    share_recv,
    rel_send,
    rel_recv,
    x_send,
    x_recv,
    z_send,
    z_recv,
):
    row = lax.axis_index("bra")
    col = lax.axis_index("ket")
    y, deep = row // DEEP, row % DEEP
    core = col % 2
    zl = (col // 2) % SIDE
    xx = col // (2 * SIDE)

    def at_row(yy, dd):
        return lax.rem(yy + 2 * RING, RING) * DEEP + dd

    def at_col(x_at, z_at, core_at):
        return (lax.rem(x_at + SIDE, SIDE) * SIDE + z_at) * 2 + core_at

    up, down = at_row(y + 1, deep), at_row(y - 1, deep)
    partner = at_row(y, 1 - deep)
    sibling = at_col(xx, zl, 1 - core)
    x_up, x_down = at_col(xx + 1, zl, core), at_col(xx - 1, zl, core)

    def z_at(step):
        return lax.rem(zl + step, SIDE)

    same_side = (row, at_col(xx, z_at(2), core))
    other_side = (partner, at_col(xx, z_at(2), core))
    peers = [(up, col), (down, col), other_side, (row, sibling), (row, x_up), (row, x_down)]
    peers += [(row, at_col(xx, z_at(step), core)) for step in range(1, SIDE)]
    peers += [(row, at_col(xx + 2, zl, core))]
    barrier = pltpu.get_barrier_semaphore()
    for peer in peers:
        pl.semaphore_signal(barrier, inc=1, device_id=peer, device_id_type=MESH)
    own_slots = gathered.at[pl.ds(row * OWN, OWN)]
    sources = (ket_hbm, bra_hbm, centers_hbm, owner_hbm, quartets_hbm, density_hbm)
    targets = (ket_pairs, bra_pairs, centers, owner, quartets, own_slots)
    fetches = [
        pltpu.make_async_copy(src, dst, fetch.at[n])
        for n, (src, dst) in enumerate(zip(sources, targets))
    ]
    for copy in fetches:
        copy.start()
    for tiles in (bra_tiles, ket_tiles, sib_tiles):
        tiles[PAIRS] = jnp.zeros((BLOCK, BLOCK), BF16)
    for part, (_, rows) in enumerate(PARTS):
        w_own[part][PAIRS] = jnp.zeros((rows, BLOCK), BF16)
        w_sib[part][PAIRS] = jnp.zeros((rows, BLOCK), BF16)
    pl.semaphore_wait(barrier, len(peers))

    def remote(src, dst, send, recv, device):
        return pltpu.make_async_remote_copy(
            src_ref=src,
            dst_ref=dst,
            send_sem=send,
            recv_sem=recv,
            device_id=device,
            device_id_type=MESH,
        )

    def half_of(ref, base, side):
        return ref.at[pl.ds(base + side * PIECE, PIECE)]

    def to_side(side):
        return remote(
            half_of(density_hbm, 0, side),
            half_of(passing, 0, side),
            side_send.at[side],
            side_recv.at[side],
            other_side if side else same_side,
        )

    def pass_on(side):
        origin = partner if side else row
        return remote(
            half_of(passing, 0, side),
            half_of(gathered, origin * OWN, side),
            part_send.at[side],
            part_recv.at[side],
            same_side if side else other_side,
        )

    def from_partner(side):
        ref = half_of(gathered, partner * OWN, side)
        device = same_side if side else other_side
        return remote(ref, ref, part_send.at[side], part_recv.at[side], device)

    for side in range(2):
        to_side(side).start()

    def depth(family):
        return deep if family == 0 else 1 - deep

    def hop(family, way, m, arriving, first=False):
        sign = 1 - 2 * way
        back = m // PER + arriving
        place = lax.rem(m + way, PER) * PIECE
        ref = gathered.at[pl.ds(at_row(y - sign * back, depth(family)) * OWN + place, PIECE)]
        src = density_hbm.at[pl.ds(place, PIECE)] if first else ref
        device = (up, col) if way == 0 else (down, col)
        return remote(
            src, ref, ring_send.at[family, way, m], ring_recv.at[family, way, m], device
        )

    last = 3 * PER + PER // 2

    def send_own(family, m):
        for way in range(2):
            hop(family, way, m, 0, family == 0).start()

    def arrive(family, m):
        for way in range(2):
            hop(family, way, m, 1).wait_recv()

    def forward(family, m):
        for way in range(2):
            hop(family, way, m - PER, 1).wait_recv()
            hop(family, way, m, 0).start()

    for m in range(PER):
        send_own(0, m)
    for copy in fetches[:-1]:
        copy.wait()

    lane = lax.broadcasted_iota(jnp.int32, (8, BLOCK), 1)
    ket_table = jnp.full((8, BLOCK), PAIRS, jnp.int32)
    bra_table = jnp.full((8, BLOCK), PAIRS, jnp.int32)
    for n in range(PAIRS):
        ket_table = jnp.where(lane == ket_pairs[n], n, ket_table)
        bra_table = jnp.where(lane == owner[0, bra_pairs[n]], n, bra_table)
    slots_vmem[...] = ket_table
    places_vmem[...] = bra_table
    to_slots = pltpu.make_async_copy(slots_vmem, slots, fetch.at[len(fetches)])
    to_slots.start()
    to_places = pltpu.make_async_copy(places_vmem, places, fetch.at[len(fetches) + 1])
    to_places.start()
    there = (row, sibling)
    table_swap = remote(slots_vmem, sib_slots_vmem, sib_send.at[0], sib_recv.at[0], there)
    table_swap.start()

    for block in range(NBLK):
        lines[block, 0:3] = centers[:, block * BLOCK : (block + 1) * BLOCK]
    for side, start in ((0, row * (NBLK // 16)), (1, col * (NBLK // 32))):
        line = lines[start]
        for axis in range(3):
            wide = jnp.broadcast_to(line[axis : axis + 1], (BLOCK, BLOCK))
            columns[side, axis] = wide.T

    def tile(side, block, ref, place):
        line = lines[block]
        rows = 32
        for part in range(BLOCK // rows):
            squared = jnp.full((rows, BLOCK), SOFTEN, F32)
            for axis in range(3):
                difference = columns[side, axis, pl.ds(part * rows, rows)] - line[axis : axis + 1]
                squared = squared + difference * difference
            ref[place, pl.ds(part * rows, rows)] = kernel_value(squared).astype(BF16)

    def ket_tile(q):
        tile(1, ket_pairs[q], ket_tiles, q)

    def bra_tile(p):
        tile(0, bra_pairs[p], bra_tiles, p)

    def iota(shape, axis):
        return lax.broadcasted_iota(jnp.int32, shape, axis)

    def hot(condition):
        return jnp.where(condition, jnp.float32(1.0), jnp.float32(0.0)).astype(BF16)

    size = PAIRS * GROUP

    def count_pairs():
        long = (PAIRS, quartets.shape[3])
        bra_hot = hot((quartets[0, 0, 0:1] == iota(long, 0)) & (iota(long, 1) < count[0, 0]))
        ket_hot = hot(quartets[0, 0, 1:2] == iota(long, 0))
        return lax.dot_general(
            ket_hot, bra_hot, (((1,), (1,)), ((), ())), preferred_element_type=F32
        ).astype(BF16)

    def spread_rows(counts):
        by_slot = jnp.dot(
            counts, hot(bra_table[0:1] == iota((PAIRS, BLOCK), 0)), preferred_element_type=F32
        ).astype(BF16)
        tall = hot(iota((size, PAIRS), 0) >> SHIFT == iota((size, PAIRS), 1))
        return jnp.dot(tall, by_slot, preferred_element_type=F32).astype(BF16)

    def spread_family(rows_of, family):
        same = (iota((size, size), 0) ^ iota((size, size), 1)) & (GROUP - 1) == 0
        local_slot = iota((BLOCK, size), 1) >> SHIFT
        row_slot = (local_slot >> 2) * (OWN * DEEP) + (local_slot & (OWN - 1))
        wide = hot(row_slot + depth(family) * OWN == iota((BLOCK, size), 0))
        spread[family] = jnp.where(
            same, jnp.dot(rows_of, wide, preferred_element_type=F32), jnp.float32(0.0)
        ).astype(BF16)

    def z_row(family, yy):
        at = lax.rem(yy + 2 * RING, RING)
        for extra in range(OWN):
            s = (at * DEEP + depth(family)) * OWN + extra
            z = jnp.dot(bra_tiles[places[0, s]], gathered[s], preferred_element_type=F32)
            product[family, at * OWN + extra] = z.astype(BF16).astype(F32)

    def w_part(family, n):
        base = pl.multiple_of(n * 2 * GROUP, 2 * GROUP)
        halves = [
            product[family, :, pl.ds(base + half * GROUP, GROUP), :]
            .reshape(size, BLOCK)
            .astype(BF16)
            for half in range(2)
        ]
        both = jnp.dot(
            spread[family], jnp.concatenate(halves, axis=1), preferred_element_type=F32
        )
        return jnp.concatenate(
            [
                both[:, half * BLOCK : (half + 1) * BLOCK].reshape(PAIRS, GROUP, BLOCK)
                for half in range(2)
            ],
            axis=1,
        )

    def swap_tiles(src, dst, first, total, index):
        return remote(
            src.at[pl.ds(first, total)],
            dst.at[pl.ds(first, total)],
            sib_send.at[index],
            sib_recv.at[index],
            there,
        )

    share = PAIRS // (2 * SIDE)
    mine = core * (PAIRS // 2) + xx * share
    bra_swap = swap_tiles(bra_tiles, bra_tiles, core * (PAIRS // 2), PAIRS // 2, 1)
    ket_swap = swap_tiles(ket_tiles, sib_tiles, 0, PAIRS, 2)

    def bra_share(step):
        tiles = bra_tiles.at[pl.ds(mine, share)]
        return remote(
            tiles,
            tiles,
            share_send.at[step - 1],
            share_recv.at[step - 1],
            (row, at_col(xx + step, zl, core)),
        )

    def bra_shared(step):
        first = core * (PAIRS // 2) + lax.rem(xx - step + SIDE, SIDE) * share
        tiles = bra_tiles.at[pl.ds(first, share)]
        return remote(
            tiles,
            tiles,
            share_send.at[step - 1],
            share_recv.at[step - 1],
            (row, at_col(xx + step, zl, core)),
        )

    def ket_run(first, total):
        @pl.loop(first, first + total)
        def _(q):
            ket_tile(q)

    def w_first(first, total):
        @pl.loop(first, first + total)
        def _(n):
            weighted[:, pl.ds(n * 2 * GROUP, 2 * GROUP)] = w_part(0, n)

    for m in range(PER):
        forward(0, PER + m)
        bra_tile(mine + 2 * m)
        bra_tile(mine + 2 * m + 1)
        ket_run(4 * m, 2)
        to_side(m).wait_recv()
        pass_on(m).start()
        ket_run(4 * m + 2, 2)

    for step in range(1, SIDE):
        bra_share(step).start()
    for m in range(PER):
        forward(0, 2 * PER + m)
        ket_run(8 + m * 6, 3)
        if m == 0:
            from_partner(0).wait_recv()
            from_partner(1).wait_recv()
        send_own(1, m)
        if m == 0:
            counts = count_pairs()
            rows_of = spread_rows(counts)
            ket_run(11, 3)
        else:
            spread_family(rows_of, 0)
            ket_run(17, 3)
            spread_family(rows_of, 1)
    forward(1, PER)
    ket_run(20, 4)
    forward(0, 3 * PER)
    for step in range(1, SIDE):
        bra_shared(step).wait_recv()
    bra_swap.start()
    ket_run(24, 3)
    forward(1, PER + 1)
    ket_run(27, 5)
    ket_swap.start()
    bra_swap.wait()
    to_places.wait()
    fetches[-1].wait()
    z_row(0, y)
    z_row(0, y - 1)
    forward(1, 2 * PER)
    z_row(0, y + 1)
    z_row(0, y - 2)
    z_row(0, y + 2)
    arrive(0, 2 * PER + 1)
    z_row(0, y - 3)
    forward(1, 2 * PER + 1)
    z_row(0, y + 3)
    arrive(0, last - 1)
    z_row(0, y + 4)
    w_first(0, 3)
    forward(1, 3 * PER)
    w_first(3, 5)
    for away in (0, 1, -1, 2, -2):
        z_row(1, y + away)
    arrive(1, 2 * PER + 1)
    z_row(1, y - 3)
    z_row(1, y + 3)
    table_swap.wait()
    sib_to_slots = pltpu.make_async_copy(sib_slots_vmem, sib_slots, fetch.at[len(fetches) + 2])
    sib_to_slots.start()
    arrive(1, last - 1)
    z_row(1, y + 4)

    def w_swap(part):
        return remote(
            w_own[part].at[pl.ds(0, PAIRS)],
            w_sib[part].at[pl.ds(0, PAIRS)],
            swap_send.at[part],
            swap_recv.at[part],
            there,
        )

    for part, (start, rows) in enumerate(PARTS):

        @pl.loop(0, rows // (2 * GROUP))
        def _(n):
            at = pl.multiple_of(n * 2 * GROUP, 2 * GROUP)
            total = w_part(1, n + start // (2 * GROUP))
            total = total + weighted[:, pl.ds(at + start, 2 * GROUP)]
            w_own[part][0:PAIRS, pl.ds(at, 2 * GROUP)] = total.astype(BF16)

        w_swap(part).start()

    def image(d, zz, jj, part):
        j = (lax.rem(xx + d, SIDE) * SIDE + zz) * 4 + core * 2 + jj
        a, b = slots[0, j], sib_slots[0, j]
        left = jnp.concatenate([w_own[part][a], w_sib[part][b]], axis=1)
        right = jnp.concatenate([ket_tiles[a], sib_tiles[b]], axis=0)
        return jnp.dot(left, right, preferred_element_type=F32)

    def relay(way, part):
        device = (row, x_up) if way == 0 else (row, x_down)
        return remote(
            x_out[part].at[2, way],
            rel_in[part].at[way],
            rel_send.at[part, way],
            rel_recv.at[part, way],
            device,
        )

    def to_x(way, jj, part):
        device = (row, x_up) if way == 0 else (row, x_down)
        return remote(
            x_out[part].at[way, jj],
            x_in[part].at[way, jj],
            x_send.at[part, way, jj],
            x_recv.at[part, way, jj],
            device,
        )

    def to_z(step, part):
        return remote(
            z_out[part].at[step - 1],
            z_in[part].at[step - 1],
            z_send.at[part, step - 1],
            z_recv.at[part, step - 1],
            (row, at_col(xx, z_at(step), core)),
        )

    def relays(part):
        for way in range(2):
            for zz in range(SIDE):
                x_out[part][2, way, zz] = image(2, zz, way, part).astype(BF16)
            relay(way, part).start()

    def direct(part):
        for way, d in ((0, 1), (1, 3)):
            for zz in range(SIDE):
                x_out[part][way, 1 - way, zz] = image(d, zz, 1 - way, part).astype(BF16)
            to_x(way, 1 - way, part).start()

    def summed(part):
        for way, d in ((0, 1), (1, 3)):
            images = [image(d, zz, way, part) for zz in range(SIDE)]
            relay(way, part).wait_recv()
            for zz in range(SIDE):
                total = images[zz] + rel_in[part][way, zz].astype(F32)
                x_out[part][way, way, zz] = total.astype(BF16)
            to_x(way, way, part).start()

    def own_sum(part):
        for jj in range(2):
            for zz in range(SIDE):
                keep[part][jj, zz] = image(0, zz, jj, part)

    def from_x(part):
        for jj in range(2):
            for way in (1 - jj, jj):
                to_x(way, jj, part).wait_recv()
                keep[part][jj] = keep[part][jj] + x_in[part][way, jj].astype(F32)
        for step in (2, 3, 1):
            for jj in range(2):
                z_out[part][step - 1, jj] = keep[part][jj, z_at(step)].astype(BF16)
            to_z(step, part).start()

    def finish(part):
        for step in (1, 3, 2):
            to_z(step, part).wait_recv()
        start, rows = PARTS[part]
        for jj in range(2):
            total = keep[part][jj, zl]
            for step in range(1, SIDE):
                total = total + z_in[part][step - 1, jj].astype(F32)
            out[start : start + rows, jj * BLOCK : (jj + 1) * BLOCK] = total.astype(BF16)

    to_slots.wait()
    sib_to_slots.wait()
    ket_swap.wait()
    w_swap(0).wait()
    relays(0)
    direct(0)
    w_swap(1).wait()
    relays(1)
    summed(0)
    direct(1)
    w_swap(2).wait()
    relays(2)
    summed(1)
    direct(2)
    own_sum(0)
    from_x(0)
    summed(2)
    own_sum(1)
    own_sum(2)
    from_x(1)

    @pl.loop(0, last)
    def _(m):
        for family in range(2):
            for way in range(2):
                hop(family, way, m, 0).wait_send()

    for side in range(2):
        to_side(side).wait_send()
        pass_on(side).wait_send()
    for step in range(1, SIDE):
        bra_share(step).wait_send()
    from_x(2)
    finish(0)
    finish(1)
    for part in range(len(PARTS)):
        for way in range(2):
            relay(way, part).wait_send()
            for jj in range(2):
                to_x(way, jj, part).wait_send()
        for step in range(1, SIDE):
            to_z(step, part).wait_send()
    finish(2)


def local(
    basis_centers, bra_pairs, ket_pairs, quartets, quartet_counts, density_owner, density_store
):
    hbm = pl.BlockSpec(memory_space=pltpu.HBM)
    smem, i32 = pltpu.SMEM, jnp.int32
    block, count = (BLOCK, BLOCK), len(PARTS)

    def parts(lead, kind=BF16):
        return [pltpu.VMEM(lead + (rows, BLOCK), kind) for _, rows in PARTS]

    dma = pltpu.SemaphoreType.DMA
    hops = 3 * PER + PER // 2
    return pl.pallas_call(
        body,
        out_shape=jax.ShapeDtypeStruct((BLOCK, 2 * BLOCK), BF16),
        in_specs=[hbm] * 4 + [pl.BlockSpec(memory_space=smem)] + [hbm] * 2,
        out_specs=pl.BlockSpec(memory_space=pltpu.VMEM),
        scratch_shapes=[
            pltpu.VMEM(basis_centers.shape, F32),
            smem(bra_pairs.shape, i32),
            smem(ket_pairs.shape, i32),
            pltpu.VMEM(quartets.shape, i32),
            smem(density_owner.shape, i32),
            pltpu.VMEM((8, BLOCK), i32),
            smem((8, BLOCK), i32),
            pltpu.VMEM((8, BLOCK), i32),
            smem((8, BLOCK), i32),
            pltpu.VMEM((8, BLOCK), i32),
            smem((8, BLOCK), i32),
            dma((9,)),
            pltpu.VMEM((NBLK,) + block, BF16),
            pltpu.VMEM((NBLK, 8, BLOCK), F32),
            pltpu.VMEM((2, 3) + block, F32),
            pltpu.VMEM((PAIRS + 1,) + block, BF16),
            pltpu.VMEM((PAIRS + 1,) + block, BF16),
            pltpu.VMEM((PAIRS + 1,) + block, BF16),
            pltpu.VMEM((2, PAIRS * GROUP, PAIRS * GROUP), BF16),
            pltpu.VMEM((2, PAIRS) + block, F32),
            pltpu.VMEM((PAIRS,) + block, F32),
            parts((PAIRS + 1,)),
            parts((PAIRS + 1,)),
            parts((2, SIDE), F32),
            parts((3, 2, SIDE)),
            parts((2, SIDE)),
            parts((2, 2, SIDE)),
            parts((3, 2)),
            parts((3, 2)),
            pltpu.VMEM((OWN,) + block, BF16),
            dma((2,)),
            dma((2,)),
            dma((2,)),
            dma((2,)),
            dma((2, 2, hops)),
            dma((2, 2, hops)),
            dma((3,)),
            dma((3,)),
            dma((count,)),
            dma((count,)),
            dma((SIDE - 1,)),
            dma((SIDE - 1,)),
            dma((count, 2)),
            dma((count, 2)),
            dma((count, 2, 2)),
            dma((count, 2, 2)),
            dma((count, 3)),
            dma((count, 3)),
        ],
        compiler_params=pltpu.CompilerParams(
            collective_id=0, has_side_effects=True, vmem_limit_bytes=56 * 2**20
        ),
        cost_estimate=pl.CostEstimate(
            flops=2 * 10**9, bytes_accessed=4 * 2**20, transcendentals=4 * 10**6
        ),
    )(
        basis_centers,
        bra_pairs,
        ket_pairs,
        quartets,
        quartet_counts,
        density_owner,
        density_store,
    )


def solution(mesh):
    return jax.shard_map(
        local,
        mesh=mesh,
        in_specs=(
            P(),
            P("bra"),
            P("ket"),
            P("bra", "ket", None, None),
            P("bra", "ket"),
            P("ket", None),
            P("bra", "ket", None),
        ),
        out_specs=P("bra", "ket"),
        check_vma=False,
    )
```

```python
import jax
import jax.numpy as jnp
from jax import lax
from jax.experimental import pallas as pl
from jax.experimental.pallas import tpu as pltpu
from jax.sharding import PartitionSpec as P

OMEGA = 0.11
SOFTEN = 0.25
BLOCK = 128
NBLK = 64
PAIRS = 32
RING = 8
DEEP = 2
SIDE = 4
OWN = 4
PARTS = ((0, 32), (32, 64), (96, 32))
GROUP = 8
SHIFT = 3
MESH = pl.DeviceIdType.MESH
F32 = jnp.float32
BF16 = jnp.bfloat16

SLOPE = 0.6 * OMEGA
DECAY = -OMEGA * OMEGA * 1.4426950408889634
ERFC = (
    0.33856715,
    0.33711259,
    0.29264139,
    0.06933287,
    0.29272546,
    -0.65555156,
    0.41918066,
    -0.09400974,
)


def kernel_value(squared):
    inverse = lax.rsqrt(squared)
    divisor = 1.0 + SLOPE * (squared * inverse)
    t = pl.reciprocal(divisor, approx=True)
    t = t * (2.0 - divisor * t)
    poly = ERFC[-1] * t + ERFC[-2]
    for c in ERFC[-3::-1]:
        poly = poly * t + c
    return jnp.exp2(DECAY * squared) * (t * inverse) * poly


def body(
    centers_hbm,
    bra_hbm,
    ket_hbm,
    quartets_hbm,
    count,
    owner_hbm,
    density_hbm,
    out,
    centers,
    bra_pairs,
    ket_pairs,
    quartets,
    owner,
    slots_vmem,
    slots,
    sib_slots_vmem,
    sib_slots,
    places_vmem,
    places,
    fetch,
    gathered,
    lines,
    columns,
    bra_tiles,
    ket_tiles,
    sib_tiles,
    spread,
    product,
    weighted,
    w_own,
    w_sib,
    keep,
    x_out,
    rel_in,
    x_in,
    z_out,
    z_in,
    passing,
    side_send,
    side_recv,
    part_send,
    part_recv,
    ring_send,
    ring_recv,
    sib_send,
    sib_recv,
    swap_send,
    swap_recv,
    share_send,
    share_recv,
    rel_send,
    rel_recv,
    x_send,
    x_recv,
    z_send,
    z_recv,
):
    row = lax.axis_index("bra")
    col = lax.axis_index("ket")
    y, deep = row // DEEP, row % DEEP
    core = col % 2
    zl = (col // 2) % SIDE
    xx = col // (2 * SIDE)

    def at_row(yy, dd):
        return lax.rem(yy + 2 * RING, RING) * DEEP + dd

    def at_col(x_at, z_at, core_at):
        return (lax.rem(x_at + SIDE, SIDE) * SIDE + z_at) * 2 + core_at

    up, down = at_row(y + 1, deep), at_row(y - 1, deep)
    partner = at_row(y, 1 - deep)
    sibling = at_col(xx, zl, 1 - core)
    x_up, x_down = at_col(xx + 1, zl, core), at_col(xx - 1, zl, core)

    def z_at(step):
        return lax.rem(zl + step, SIDE)

    same_side = (row, at_col(xx, z_at(2), core))
    other_side = (partner, at_col(xx, z_at(2), core))
    peers = [(up, col), (down, col), other_side, (row, sibling), (row, x_up), (row, x_down)]
    peers += [(row, at_col(xx, z_at(step), core)) for step in range(1, SIDE)]
    peers += [(row, at_col(xx + 2, zl, core))]
    barrier = pltpu.get_barrier_semaphore()
    for peer in peers:
        pl.semaphore_signal(barrier, inc=1, device_id=peer, device_id_type=MESH)
    own_slots = gathered.at[pl.ds(row * OWN, OWN)]
    sources = (ket_hbm, bra_hbm, centers_hbm, owner_hbm, quartets_hbm, density_hbm)
    targets = (ket_pairs, bra_pairs, centers, owner, quartets, own_slots)
    fetches = [
        pltpu.make_async_copy(src, dst, fetch.at[n])
        for n, (src, dst) in enumerate(zip(sources, targets))
    ]
    for copy in fetches:
        copy.start()
    for tiles in (bra_tiles, ket_tiles, sib_tiles):
        tiles[PAIRS] = jnp.zeros((BLOCK, BLOCK), BF16)
    for part, (_, rows) in enumerate(PARTS):
        w_own[part][PAIRS] = jnp.zeros((rows, BLOCK), BF16)
        w_sib[part][PAIRS] = jnp.zeros((rows, BLOCK), BF16)
    pl.semaphore_wait(barrier, len(peers))

    def remote(src, dst, send, recv, device):
        return pltpu.make_async_remote_copy(
            src_ref=src,
            dst_ref=dst,
            send_sem=send,
            recv_sem=recv,
            device_id=device,
            device_id_type=MESH,
        )

    def to_side(place):
        return remote(
            density_hbm.at[pl.ds(place, 1)],
            passing.at[pl.ds(place, 1)],
            side_send.at[place],
            side_recv.at[place],
            same_side if place < 2 else other_side,
        )

    def pass_on(place):
        origin = row if place < 2 else partner
        return remote(
            passing.at[pl.ds(place, 1)],
            gathered.at[pl.ds(origin * OWN + place, 1)],
            part_send.at[place],
            part_recv.at[place],
            other_side if place < 2 else same_side,
        )

    def from_partner(place):
        ref = gathered.at[pl.ds(partner * OWN + place, 1)]
        device = other_side if place < 2 else same_side
        return remote(ref, ref, part_send.at[place], part_recv.at[place], device)

    for place in (0, 2, 1, 3):
        to_side(place).start()

    def depth(family):
        return deep if family == 0 else 1 - deep

    def hop(family, way, m, arriving, first=False):
        sign = 1 - 2 * way
        back = m // OWN + arriving
        place = lax.rem(m + 2 * way, OWN)
        ref = gathered.at[pl.ds(at_row(y - sign * back, depth(family)) * OWN + place, 1)]
        src = density_hbm.at[pl.ds(place, 1)] if first else ref
        device = (up, col) if way == 0 else (down, col)
        return remote(
            src, ref, ring_send.at[family, way, m], ring_recv.at[family, way, m], device
        )

    last = 3 * OWN + OWN // 2

    def send_own(family, m):
        for way in range(2):
            hop(family, way, m, 0, family == 0).start()

    def arrive(family, m):
        for way in range(2):
            hop(family, way, m, 1).wait_recv()

    def forward(family, m):
        for way in range(2):
            hop(family, way, m - OWN, 1).wait_recv()
            hop(family, way, m, 0).start()

    for m in range(OWN):
        send_own(0, m)
    for copy in fetches[:-1]:
        copy.wait()

    lane = lax.broadcasted_iota(jnp.int32, (8, BLOCK), 1)
    ket_table = jnp.full((8, BLOCK), PAIRS, jnp.int32)
    bra_table = jnp.full((8, BLOCK), PAIRS, jnp.int32)
    for n in range(PAIRS):
        ket_table = jnp.where(lane == ket_pairs[n], n, ket_table)
        bra_table = jnp.where(lane == owner[0, bra_pairs[n]], n, bra_table)
    slots_vmem[...] = ket_table
    places_vmem[...] = bra_table
    to_slots = pltpu.make_async_copy(slots_vmem, slots, fetch.at[len(fetches)])
    to_slots.start()
    to_places = pltpu.make_async_copy(places_vmem, places, fetch.at[len(fetches) + 1])
    to_places.start()
    there = (row, sibling)
    table_swap = remote(slots_vmem, sib_slots_vmem, sib_send.at[0], sib_recv.at[0], there)
    table_swap.start()

    for block in range(NBLK):
        lines[block, 0:3] = centers[:, block * BLOCK : (block + 1) * BLOCK]
    for side, start in ((0, row * (NBLK // 16)), (1, col * (NBLK // 32))):
        line = lines[start]
        for axis in range(3):
            wide = jnp.broadcast_to(line[axis : axis + 1], (BLOCK, BLOCK))
            columns[side, axis] = wide.T

    def tile(side, block, ref, place):
        line = lines[block]
        rows = 32
        for part in range(BLOCK // rows):
            squared = jnp.full((rows, BLOCK), SOFTEN, F32)
            for axis in range(3):
                difference = columns[side, axis, pl.ds(part * rows, rows)] - line[axis : axis + 1]
                squared = squared + difference * difference
            ref[place, pl.ds(part * rows, rows)] = kernel_value(squared).astype(BF16)

    def ket_tile(q):
        tile(1, ket_pairs[q], ket_tiles, q)

    def bra_tile(p):
        tile(0, bra_pairs[p], bra_tiles, p)

    def iota(shape, axis):
        return lax.broadcasted_iota(jnp.int32, shape, axis)

    def hot(condition):
        return jnp.where(condition, jnp.float32(1.0), jnp.float32(0.0)).astype(BF16)

    size = PAIRS * GROUP

    def count_pairs():
        long = (PAIRS, quartets.shape[3])
        bra_hot = hot((quartets[0, 0, 0:1] == iota(long, 0)) & (iota(long, 1) < count[0, 0]))
        ket_hot = hot(quartets[0, 0, 1:2] == iota(long, 0))
        return lax.dot_general(
            ket_hot, bra_hot, (((1,), (1,)), ((), ())), preferred_element_type=F32
        ).astype(BF16)

    def spread_rows(counts):
        by_slot = jnp.dot(
            counts, hot(bra_table[0:1] == iota((PAIRS, BLOCK), 0)), preferred_element_type=F32
        ).astype(BF16)
        tall = hot(iota((size, PAIRS), 0) >> SHIFT == iota((size, PAIRS), 1))
        return jnp.dot(tall, by_slot, preferred_element_type=F32).astype(BF16)

    def spread_family(rows_of, family):
        same = (iota((size, size), 0) ^ iota((size, size), 1)) & (GROUP - 1) == 0
        local_slot = iota((BLOCK, size), 1) >> SHIFT
        row_slot = (local_slot >> 2) * (OWN * DEEP) + (local_slot & (OWN - 1))
        wide = hot(row_slot + depth(family) * OWN == iota((BLOCK, size), 0))
        spread[family] = jnp.where(
            same, jnp.dot(rows_of, wide, preferred_element_type=F32), jnp.float32(0.0)
        ).astype(BF16)

    def z_row(family, yy):
        at = lax.rem(yy + 2 * RING, RING)
        for extra in range(OWN):
            s = (at * DEEP + depth(family)) * OWN + extra
            product[family, at * OWN + extra] = jnp.dot(
                bra_tiles[places[0, s]], gathered[s], preferred_element_type=F32
            )

    def w_part(family, n):
        base = pl.multiple_of(n * 2 * GROUP, 2 * GROUP)
        halves = [
            product[family, :, pl.ds(base + half * GROUP, GROUP), :]
            .reshape(size, BLOCK)
            .astype(BF16)
            for half in range(2)
        ]
        both = jnp.dot(
            spread[family], jnp.concatenate(halves, axis=1), preferred_element_type=F32
        )
        return jnp.concatenate(
            [
                both[:, half * BLOCK : (half + 1) * BLOCK].reshape(PAIRS, GROUP, BLOCK)
                for half in range(2)
            ],
            axis=1,
        )

    def swap_tiles(src, dst, first, total, index):
        return remote(
            src.at[pl.ds(first, total)],
            dst.at[pl.ds(first, total)],
            sib_send.at[index],
            sib_recv.at[index],
            there,
        )

    share = PAIRS // (2 * SIDE)
    mine = core * (PAIRS // 2) + xx * share
    bra_swap = swap_tiles(bra_tiles, bra_tiles, core * (PAIRS // 2), PAIRS // 2, 1)
    ket_swap = swap_tiles(ket_tiles, sib_tiles, 0, PAIRS, 2)

    def bra_share(step):
        tiles = bra_tiles.at[pl.ds(mine, share)]
        return remote(
            tiles,
            tiles,
            share_send.at[step - 1],
            share_recv.at[step - 1],
            (row, at_col(xx + step, zl, core)),
        )

    def bra_shared(step):
        first = core * (PAIRS // 2) + lax.rem(xx - step + SIDE, SIDE) * share
        tiles = bra_tiles.at[pl.ds(first, share)]
        return remote(
            tiles,
            tiles,
            share_send.at[step - 1],
            share_recv.at[step - 1],
            (row, at_col(xx + step, zl, core)),
        )

    def ket_run(first, total):
        @pl.loop(first, first + total)
        def _(q):
            ket_tile(q)

    def w_first(first, total):
        @pl.loop(first, first + total)
        def _(n):
            weighted[:, pl.ds(n * 2 * GROUP, 2 * GROUP)] = w_part(0, n)

    for m in range(OWN):
        forward(0, OWN + m)
        if m < 2:
            for place in (m, m + 2):
                to_side(place).wait_recv()
                pass_on(place).start()
        bra_tile(mine + m)
        ket_run(2 * m, 2)

    for step in range(1, SIDE):
        bra_share(step).start()
    for m in range(OWN):
        forward(0, 2 * OWN + m)
        ket_run(8 + m * 3, 3)
        if m < 2:
            from_partner(m).wait_recv()
            from_partner(m + 2).wait_recv()
        send_own(1, m)
        if m == 0:
            counts = count_pairs()
        elif m == 1:
            rows_of = spread_rows(counts)
        else:
            spread_family(rows_of, m - 2)
    for m in range(2):
        forward(1, OWN + m)
        ket_run(20 + m * 6, 3)
        forward(0, 3 * OWN + m)
        if m == 0:
            for step in range(1, SIDE):
                bra_shared(step).wait_recv()
            bra_swap.start()
        ket_run(23 + m * 6, 3)
    ket_swap.start()
    bra_swap.wait()
    to_places.wait()
    fetches[-1].wait()
    forward(1, OWN + 2)
    z_row(0, y)
    z_row(0, y - 1)
    forward(1, OWN + 3)
    z_row(0, y + 1)
    z_row(0, y - 2)
    forward(1, 2 * OWN)
    z_row(0, y + 2)
    arrive(0, last - 4)
    arrive(0, last - 3)
    z_row(0, y - 3)
    forward(1, 2 * OWN + 1)
    z_row(0, y + 3)
    arrive(0, last - 2)
    arrive(0, last - 1)
    z_row(0, y + 4)
    forward(1, 2 * OWN + 2)
    w_first(0, 3)
    forward(1, 2 * OWN + 3)
    w_first(3, 2)
    forward(1, 3 * OWN)
    w_first(5, 1)
    forward(1, 3 * OWN + 1)
    w_first(6, 2)
    for away in (0, 1, -1, 2, -2):
        z_row(1, y + away)
    arrive(1, last - 4)
    arrive(1, last - 3)
    z_row(1, y - 3)
    z_row(1, y + 3)
    table_swap.wait()
    sib_to_slots = pltpu.make_async_copy(sib_slots_vmem, sib_slots, fetch.at[len(fetches) + 2])
    sib_to_slots.start()
    arrive(1, last - 2)
    arrive(1, last - 1)
    z_row(1, y + 4)

    def w_swap(part):
        return remote(
            w_own[part].at[pl.ds(0, PAIRS)],
            w_sib[part].at[pl.ds(0, PAIRS)],
            swap_send.at[part],
            swap_recv.at[part],
            there,
        )

    def w_finish(part):
        start, rows = PARTS[part]

        @pl.loop(0, rows // (2 * GROUP))
        def _(n):
            at = pl.multiple_of(n * 2 * GROUP, 2 * GROUP)
            total = w_part(1, n + start // (2 * GROUP))
            total = total + weighted[:, pl.ds(at + start, 2 * GROUP)]
            w_own[part][0:PAIRS, pl.ds(at, 2 * GROUP)] = total.astype(BF16)

        w_swap(part).start()

    def image(d, zz, jj, part):
        j = (lax.rem(xx + d, SIDE) * SIDE + zz) * 4 + core * 2 + jj
        a, b = slots[0, j], sib_slots[0, j]
        left = jnp.concatenate([w_own[part][a], w_sib[part][b]], axis=1)
        right = jnp.concatenate([ket_tiles[a], sib_tiles[b]], axis=0)
        return jnp.dot(left, right, preferred_element_type=F32)

    def relay(way, part):
        device = (row, x_up) if way == 0 else (row, x_down)
        return remote(
            x_out[part].at[2, way],
            rel_in[part].at[way],
            rel_send.at[part, way],
            rel_recv.at[part, way],
            device,
        )

    def to_x(way, jj, part):
        device = (row, x_up) if way == 0 else (row, x_down)
        return remote(
            x_out[part].at[way, jj],
            x_in[part].at[way, jj],
            x_send.at[part, way, jj],
            x_recv.at[part, way, jj],
            device,
        )

    def to_z(step, part):
        return remote(
            z_out[part].at[step - 1],
            z_in[part].at[step - 1],
            z_send.at[part, step - 1],
            z_recv.at[part, step - 1],
            (row, at_col(xx, z_at(step), core)),
        )

    def relays(part):
        for way in range(2):
            for zz in range(SIDE):
                x_out[part][2, way, zz] = image(2, zz, way, part).astype(BF16)
            relay(way, part).start()

    def direct(part):
        for way, d in ((0, 1), (1, 3)):
            for zz in range(SIDE):
                x_out[part][way, 1 - way, zz] = image(d, zz, 1 - way, part).astype(BF16)
            to_x(way, 1 - way, part).start()

    def summed(part):
        for way, d in ((0, 1), (1, 3)):
            images = [image(d, zz, way, part) for zz in range(SIDE)]
            relay(way, part).wait_recv()
            for zz in range(SIDE):
                total = images[zz] + rel_in[part][way, zz].astype(F32)
                x_out[part][way, way, zz] = total.astype(BF16)
            to_x(way, way, part).start()

    def own_sum(part):
        for jj in range(2):
            for zz in range(SIDE):
                keep[part][jj, zz] = image(0, zz, jj, part)

    def from_x(part):
        for jj in range(2):
            for way in (1 - jj, jj):
                to_x(way, jj, part).wait_recv()
                keep[part][jj] = keep[part][jj] + x_in[part][way, jj].astype(F32)
        for step in (2, 3, 1):
            for jj in range(2):
                z_out[part][step - 1, jj] = keep[part][jj, z_at(step)].astype(BF16)
            to_z(step, part).start()

    def finish(part):
        for step in (1, 3, 2):
            to_z(step, part).wait_recv()
        start, rows = PARTS[part]
        for jj in range(2):
            total = keep[part][jj, zl]
            for step in range(1, SIDE):
                total = total + z_in[part][step - 1, jj].astype(F32)
            out[start : start + rows, jj * BLOCK : (jj + 1) * BLOCK] = total.astype(BF16)

    w_finish(0)
    w_finish(1)
    to_slots.wait()
    sib_to_slots.wait()
    ket_swap.wait()
    w_swap(0).wait()
    relays(0)
    direct(0)
    w_finish(2)
    w_swap(1).wait()
    relays(1)
    summed(0)
    direct(1)
    w_swap(2).wait()
    relays(2)
    summed(1)
    direct(2)
    own_sum(0)
    from_x(0)
    summed(2)
    own_sum(1)
    own_sum(2)
    from_x(1)

    @pl.loop(0, last)
    def _(m):
        for family in range(2):
            for way in range(2):
                hop(family, way, m, 0).wait_send()

    for place in range(OWN):
        to_side(place).wait_send()
        pass_on(place).wait_send()
    for step in range(1, SIDE):
        bra_share(step).wait_send()
    from_x(2)
    finish(0)
    finish(1)
    for part in range(len(PARTS)):
        for way in range(2):
            relay(way, part).wait_send()
            for jj in range(2):
                to_x(way, jj, part).wait_send()
        for step in range(1, SIDE):
            to_z(step, part).wait_send()
    finish(2)


def local(
    basis_centers, bra_pairs, ket_pairs, quartets, quartet_counts, density_owner, density_store
):
    hbm = pl.BlockSpec(memory_space=pltpu.HBM)
    smem, i32 = pltpu.SMEM, jnp.int32
    block, count = (BLOCK, BLOCK), len(PARTS)

    def parts(lead, kind=BF16):
        return [pltpu.VMEM(lead + (rows, BLOCK), kind) for _, rows in PARTS]

    dma = pltpu.SemaphoreType.DMA
    hops = 3 * OWN + OWN // 2
    return pl.pallas_call(
        body,
        out_shape=jax.ShapeDtypeStruct((BLOCK, 2 * BLOCK), BF16),
        in_specs=[hbm] * 4 + [pl.BlockSpec(memory_space=smem)] + [hbm] * 2,
        out_specs=pl.BlockSpec(memory_space=pltpu.VMEM),
        scratch_shapes=[
            pltpu.VMEM(basis_centers.shape, F32),
            smem(bra_pairs.shape, i32),
            smem(ket_pairs.shape, i32),
            pltpu.VMEM(quartets.shape, i32),
            smem(density_owner.shape, i32),
            pltpu.VMEM((8, BLOCK), i32),
            smem((8, BLOCK), i32),
            pltpu.VMEM((8, BLOCK), i32),
            smem((8, BLOCK), i32),
            pltpu.VMEM((8, BLOCK), i32),
            smem((8, BLOCK), i32),
            dma((9,)),
            pltpu.VMEM((NBLK,) + block, BF16),
            pltpu.VMEM((NBLK, 8, BLOCK), F32),
            pltpu.VMEM((2, 3) + block, F32),
            pltpu.VMEM((PAIRS + 1,) + block, BF16),
            pltpu.VMEM((PAIRS + 1,) + block, BF16),
            pltpu.VMEM((PAIRS + 1,) + block, BF16),
            pltpu.VMEM((2, PAIRS * GROUP, PAIRS * GROUP), BF16),
            pltpu.VMEM((2, PAIRS) + block, F32),
            pltpu.VMEM((PAIRS,) + block, F32),
            parts((PAIRS + 1,)),
            parts((PAIRS + 1,)),
            parts((2, SIDE), F32),
            parts((3, 2, SIDE)),
            parts((2, SIDE)),
            parts((2, 2, SIDE)),
            parts((3, 2)),
            parts((3, 2)),
            pltpu.VMEM((OWN,) + block, BF16),
            dma((OWN,)),
            dma((OWN,)),
            dma((OWN,)),
            dma((OWN,)),
            dma((2, 2, hops)),
            dma((2, 2, hops)),
            dma((3,)),
            dma((3,)),
            dma((count,)),
            dma((count,)),
            dma((SIDE - 1,)),
            dma((SIDE - 1,)),
            dma((count, 2)),
            dma((count, 2)),
            dma((count, 2, 2)),
            dma((count, 2, 2)),
            dma((count, 3)),
            dma((count, 3)),
        ],
        compiler_params=pltpu.CompilerParams(
            collective_id=0, has_side_effects=True, vmem_limit_bytes=56 * 2**20
        ),
        cost_estimate=pl.CostEstimate(
            flops=2 * 10**9, bytes_accessed=4 * 2**20, transcendentals=4 * 10**6
        ),
    )(
        basis_centers,
        bra_pairs,
        ket_pairs,
        quartets,
        quartet_counts,
        density_owner,
        density_store,
    )


def solution(mesh):
    return jax.shard_map(
        local,
        mesh=mesh,
        in_specs=(
            P(),
            P("bra"),
            P("ket"),
            P("bra", "ket", None, None),
            P("bra", "ket"),
            P("ket", None),
            P("bra", "ket", None),
        ),
        out_specs=P("bra", "ket"),
        check_vma=False,
    )
```

```python
import jax
import jax.numpy as jnp
from jax import lax
from jax.experimental import pallas as pl
from jax.experimental.pallas import tpu as pltpu
from jax.sharding import PartitionSpec as P

OMEGA = 0.11
SOFTEN = 0.25
BLOCK = 128
NBLK = 64
PAIRS = 32
RING = 8
DEEP = 2
SIDE = 4
OWN = 4
PARTS = ((0, 32), (32, 64), (96, 32))
GROUP = 8
SHIFT = 3
MESH = pl.DeviceIdType.MESH
F32 = jnp.float32
BF16 = jnp.bfloat16

SLOPE = 0.6 * OMEGA
DECAY = -OMEGA * OMEGA * 1.4426950408889634
ERFC = (
    0.33856715,
    0.33711259,
    0.29264139,
    0.06933287,
    0.29272546,
    -0.65555156,
    0.41918066,
    -0.09400974,
)


def kernel_value(squared):
    inverse = lax.rsqrt(squared)
    divisor = 1.0 + SLOPE * (squared * inverse)
    t = pl.reciprocal(divisor, approx=True)
    t = t * (2.0 - divisor * t)
    poly = ERFC[-1] * t + ERFC[-2]
    for c in ERFC[-3::-1]:
        poly = poly * t + c
    return jnp.exp2(DECAY * squared) * (t * inverse) * poly


def body(
    centers_hbm,
    bra_hbm,
    ket_hbm,
    quartets_hbm,
    count,
    owner_hbm,
    density_hbm,
    out,
    centers,
    bra_pairs,
    ket_pairs,
    quartets,
    owner,
    slots_vmem,
    slots,
    sib_slots_vmem,
    sib_slots,
    places_vmem,
    places,
    fetch,
    gathered,
    lines,
    columns,
    bra_tiles,
    ket_tiles,
    sib_tiles,
    spread,
    product,
    weighted,
    w_own,
    w_sib,
    keep,
    x_out,
    rel_in,
    x_in,
    z_out,
    z_in,
    joined,
    passing,
    side_send,
    side_recv,
    part_send,
    part_recv,
    ring_send,
    ring_recv,
    sib_send,
    sib_recv,
    swap_send,
    swap_recv,
    share_send,
    share_recv,
    rel_send,
    rel_recv,
    x_send,
    x_recv,
    z_send,
    z_recv,
):
    row = lax.axis_index("bra")
    col = lax.axis_index("ket")
    y, deep = row // DEEP, row % DEEP
    core = col % 2
    zl = (col // 2) % SIDE
    xx = col // (2 * SIDE)

    def at_row(yy, dd):
        return lax.rem(yy + 2 * RING, RING) * DEEP + dd

    def at_col(x_at, z_at, core_at):
        return (lax.rem(x_at + SIDE, SIDE) * SIDE + z_at) * 2 + core_at

    up, down = at_row(y + 1, deep), at_row(y - 1, deep)
    partner = at_row(y, 1 - deep)
    sibling = at_col(xx, zl, 1 - core)
    x_up, x_down = at_col(xx + 1, zl, core), at_col(xx - 1, zl, core)

    def z_at(step):
        return lax.rem(zl + step, SIDE)

    same_side = (row, at_col(xx, z_at(2), core))
    other_side = (partner, at_col(xx, z_at(2), core))
    peers = [(up, col), (down, col), (row, sibling), (row, x_up), (row, x_down)]
    peers += [(row, at_col(xx, z_at(step), core)) for step in range(1, SIDE)]
    peers += [(row, at_col(xx + 2, zl, core))]
    barrier = pltpu.get_barrier_semaphore()
    for peer in peers:
        pl.semaphore_signal(barrier, inc=1, device_id=peer, device_id_type=MESH)

    @pl.when(deep == 0)
    def _():
        pl.semaphore_signal(barrier, inc=1, device_id=other_side, device_id_type=MESH)

    own_slots = gathered.at[pl.ds(row * OWN, OWN)]
    sources = (ket_hbm, bra_hbm, centers_hbm, owner_hbm, quartets_hbm, density_hbm)
    targets = (ket_pairs, bra_pairs, centers, owner, quartets, own_slots)
    fetches = [
        pltpu.make_async_copy(src, dst, fetch.at[n])
        for n, (src, dst) in enumerate(zip(sources, targets))
    ]
    for copy in fetches:
        copy.start()
    for tiles in (bra_tiles, ket_tiles, sib_tiles):
        tiles[PAIRS] = jnp.zeros((BLOCK, BLOCK), BF16)
    for part, (_, rows) in enumerate(PARTS):
        w_own[part][PAIRS] = jnp.zeros((rows, BLOCK), BF16)
        w_sib[part][PAIRS] = jnp.zeros((rows, BLOCK), BF16)
    pl.semaphore_wait(barrier, len(peers) + deep)

    @pl.when(deep == 1)
    def _():
        pl.semaphore_signal(joined, inc=1, device_id=other_side, device_id_type=MESH)


    def remote(src, dst, send, recv, device):
        return pltpu.make_async_remote_copy(
            src_ref=src,
            dst_ref=dst,
            send_sem=send,
            recv_sem=recv,
            device_id=device,
            device_id_type=MESH,
        )

    def to_side(place):
        return remote(
            density_hbm.at[pl.ds(place, 1)],
            passing.at[pl.ds(place, 1)],
            side_send.at[place],
            side_recv.at[place],
            same_side if place < 2 else other_side,
        )

    def pass_on(place):
        origin = row if place < 2 else partner
        return remote(
            passing.at[pl.ds(place, 1)],
            gathered.at[pl.ds(origin * OWN + place, 1)],
            part_send.at[place],
            part_recv.at[place],
            other_side if place < 2 else same_side,
        )

    def from_partner(place):
        ref = gathered.at[pl.ds(partner * OWN + place, 1)]
        device = other_side if place < 2 else same_side
        return remote(ref, ref, part_send.at[place], part_recv.at[place], device)

    for place in (0, 1):
        to_side(place).start()

    @pl.when(deep == 1)
    def _():
        for place in (2, 3):
            to_side(place).start()

    def depth(family):
        return deep if family == 0 else 1 - deep

    def hop(family, way, m, arriving, first=False):
        sign = 1 - 2 * way
        back = m // OWN + arriving
        place = lax.rem(m + 2 * way, OWN)
        ref = gathered.at[pl.ds(at_row(y - sign * back, depth(family)) * OWN + place, 1)]
        src = density_hbm.at[pl.ds(place, 1)] if first else ref
        device = (up, col) if way == 0 else (down, col)
        return remote(
            src, ref, ring_send.at[family, way, m], ring_recv.at[family, way, m], device
        )

    last = 3 * OWN + OWN // 2

    def send_own(family, m):
        for way in range(2):
            hop(family, way, m, 0, family == 0).start()

    def arrive(family, m):
        for way in range(2):
            hop(family, way, m, 1).wait_recv()

    def forward(family, m):
        for way in range(2):
            hop(family, way, m - OWN, 1).wait_recv()
            hop(family, way, m, 0).start()

    for m in range(OWN):
        send_own(0, m)
    for copy in fetches[:-1]:
        copy.wait()

    lane = lax.broadcasted_iota(jnp.int32, (8, BLOCK), 1)
    ket_table = jnp.full((8, BLOCK), PAIRS, jnp.int32)
    bra_table = jnp.full((8, BLOCK), PAIRS, jnp.int32)
    for n in range(PAIRS):
        ket_table = jnp.where(lane == ket_pairs[n], n, ket_table)
        bra_table = jnp.where(lane == owner[0, bra_pairs[n]], n, bra_table)
    slots_vmem[...] = ket_table
    places_vmem[...] = bra_table
    to_slots = pltpu.make_async_copy(slots_vmem, slots, fetch.at[len(fetches)])
    to_slots.start()
    to_places = pltpu.make_async_copy(places_vmem, places, fetch.at[len(fetches) + 1])
    to_places.start()
    there = (row, sibling)
    table_swap = remote(slots_vmem, sib_slots_vmem, sib_send.at[0], sib_recv.at[0], there)
    table_swap.start()

    for block in range(NBLK):
        lines[block, 0:3] = centers[:, block * BLOCK : (block + 1) * BLOCK]
    for side, start in ((0, row * (NBLK // 16)), (1, col * (NBLK // 32))):
        line = lines[start]
        for axis in range(3):
            wide = jnp.broadcast_to(line[axis : axis + 1], (BLOCK, BLOCK))
            columns[side, axis] = wide.T

    def tile(side, block, ref, place):
        line = lines[block]
        rows = 32
        for part in range(BLOCK // rows):
            squared = jnp.full((rows, BLOCK), SOFTEN, F32)
            for axis in range(3):
                difference = columns[side, axis, pl.ds(part * rows, rows)] - line[axis : axis + 1]
                squared = squared + difference * difference
            ref[place, pl.ds(part * rows, rows)] = kernel_value(squared).astype(BF16)

    def ket_tile(q):
        tile(1, ket_pairs[q], ket_tiles, q)

    def bra_tile(p):
        tile(0, bra_pairs[p], bra_tiles, p)

    def iota(shape, axis):
        return lax.broadcasted_iota(jnp.int32, shape, axis)

    def hot(condition):
        return jnp.where(condition, jnp.float32(1.0), jnp.float32(0.0)).astype(BF16)

    size = PAIRS * GROUP

    def count_pairs():
        long = (PAIRS, quartets.shape[3])
        bra_hot = hot((quartets[0, 0, 0:1] == iota(long, 0)) & (iota(long, 1) < count[0, 0]))
        ket_hot = hot(quartets[0, 0, 1:2] == iota(long, 0))
        return lax.dot_general(
            ket_hot, bra_hot, (((1,), (1,)), ((), ())), preferred_element_type=F32
        ).astype(BF16)

    def spread_rows(counts):
        by_slot = jnp.dot(
            counts, hot(bra_table[0:1] == iota((PAIRS, BLOCK), 0)), preferred_element_type=F32
        ).astype(BF16)
        tall = hot(iota((size, PAIRS), 0) >> SHIFT == iota((size, PAIRS), 1))
        return jnp.dot(tall, by_slot, preferred_element_type=F32).astype(BF16)

    def spread_family(rows_of, family):
        same = (iota((size, size), 0) ^ iota((size, size), 1)) & (GROUP - 1) == 0
        local_slot = iota((BLOCK, size), 1) >> SHIFT
        row_slot = (local_slot >> 2) * (OWN * DEEP) + (local_slot & (OWN - 1))
        wide = hot(row_slot + depth(family) * OWN == iota((BLOCK, size), 0))
        spread[family] = jnp.where(
            same, jnp.dot(rows_of, wide, preferred_element_type=F32), jnp.float32(0.0)
        ).astype(BF16)

    def z_row(family, yy):
        at = lax.rem(yy + 2 * RING, RING)
        for extra in range(OWN):
            s = (at * DEEP + depth(family)) * OWN + extra
            product[family, at * OWN + extra] = jnp.dot(
                bra_tiles[places[0, s]], gathered[s], preferred_element_type=F32
            )

    def w_part(family, n):
        base = pl.multiple_of(n * 2 * GROUP, 2 * GROUP)
        halves = [
            product[family, :, pl.ds(base + half * GROUP, GROUP), :]
            .reshape(size, BLOCK)
            .astype(BF16)
            for half in range(2)
        ]
        both = jnp.dot(
            spread[family], jnp.concatenate(halves, axis=1), preferred_element_type=F32
        )
        return jnp.concatenate(
            [
                both[:, half * BLOCK : (half + 1) * BLOCK].reshape(PAIRS, GROUP, BLOCK)
                for half in range(2)
            ],
            axis=1,
        )

    def swap_tiles(src, dst, first, total, index):
        return remote(
            src.at[pl.ds(first, total)],
            dst.at[pl.ds(first, total)],
            sib_send.at[index],
            sib_recv.at[index],
            there,
        )

    share = PAIRS // (2 * SIDE)
    mine = core * (PAIRS // 2) + xx * share
    bra_swap = swap_tiles(bra_tiles, bra_tiles, core * (PAIRS // 2), PAIRS // 2, 1)
    ket_swap = swap_tiles(ket_tiles, sib_tiles, 0, PAIRS, 2)

    def bra_share(step):
        tiles = bra_tiles.at[pl.ds(mine, share)]
        return remote(
            tiles,
            tiles,
            share_send.at[step - 1],
            share_recv.at[step - 1],
            (row, at_col(xx + step, zl, core)),
        )

    def bra_shared(step):
        first = core * (PAIRS // 2) + lax.rem(xx - step + SIDE, SIDE) * share
        tiles = bra_tiles.at[pl.ds(first, share)]
        return remote(
            tiles,
            tiles,
            share_send.at[step - 1],
            share_recv.at[step - 1],
            (row, at_col(xx + step, zl, core)),
        )

    def ket_run(first, total):
        @pl.loop(first, first + total)
        def _(q):
            ket_tile(q)

    def w_first(first, total):
        @pl.loop(first, first + total)
        def _(n):
            weighted[:, pl.ds(n * 2 * GROUP, 2 * GROUP)] = w_part(0, n)

    for m in range(OWN):
        forward(0, OWN + m)
        if m < 2:

            @pl.when(deep == 1)
            def _():
                to_side(m).wait_recv()
                pass_on(m).start()

        else:
            to_side(m).wait_recv()
            pass_on(m).start()
        if m == 1:

            @pl.when(deep == 0)
            def _():
                pl.semaphore_wait(joined, 1)
                for place in (2, 3):
                    to_side(place).start()
                for place in (0, 1):
                    to_side(place).wait_recv()
                    pass_on(place).start()

        bra_tile(mine + m)
        ket_run(2 * m, 2)

    for step in range(1, SIDE):
        bra_share(step).start()
    for m in range(OWN):
        forward(0, 2 * OWN + m)
        ket_run(8 + m * 3, 3)
        if m < 2:
            from_partner(m).wait_recv()
            from_partner(m + 2).wait_recv()
        send_own(1, m)
        if m == 0:
            counts = count_pairs()
        elif m == 1:
            rows_of = spread_rows(counts)
        else:
            spread_family(rows_of, m - 2)
    for m in range(2):
        forward(1, OWN + m)
        ket_run(20 + m * 6, 3)
        forward(0, 3 * OWN + m)
        if m == 0:
            for step in range(1, SIDE):
                bra_shared(step).wait_recv()
            bra_swap.start()
        ket_run(23 + m * 6, 3)
    ket_swap.start()
    bra_swap.wait()
    to_places.wait()
    fetches[-1].wait()
    forward(1, OWN + 2)
    z_row(0, y)
    z_row(0, y - 1)
    forward(1, OWN + 3)
    z_row(0, y + 1)
    z_row(0, y - 2)
    forward(1, 2 * OWN)
    z_row(0, y + 2)
    arrive(0, last - 4)
    arrive(0, last - 3)
    z_row(0, y - 3)
    forward(1, 2 * OWN + 1)
    z_row(0, y + 3)
    arrive(0, last - 2)
    arrive(0, last - 1)
    z_row(0, y + 4)
    forward(1, 2 * OWN + 2)
    w_first(0, 3)
    forward(1, 2 * OWN + 3)
    w_first(3, 2)
    forward(1, 3 * OWN)
    w_first(5, 1)
    forward(1, 3 * OWN + 1)
    w_first(6, 2)
    for away in (0, 1, -1, 2, -2):
        z_row(1, y + away)
    arrive(1, last - 4)
    arrive(1, last - 3)
    z_row(1, y - 3)
    z_row(1, y + 3)
    table_swap.wait()
    sib_to_slots = pltpu.make_async_copy(sib_slots_vmem, sib_slots, fetch.at[len(fetches) + 2])
    sib_to_slots.start()
    arrive(1, last - 2)
    arrive(1, last - 1)
    z_row(1, y + 4)

    def w_swap(part):
        return remote(
            w_own[part].at[pl.ds(0, PAIRS)],
            w_sib[part].at[pl.ds(0, PAIRS)],
            swap_send.at[part],
            swap_recv.at[part],
            there,
        )

    def w_finish(part):
        start, rows = PARTS[part]

        @pl.loop(0, rows // (2 * GROUP))
        def _(n):
            at = pl.multiple_of(n * 2 * GROUP, 2 * GROUP)
            total = w_part(1, n + start // (2 * GROUP))
            total = total + weighted[:, pl.ds(at + start, 2 * GROUP)]
            w_own[part][0:PAIRS, pl.ds(at, 2 * GROUP)] = total.astype(BF16)

        w_swap(part).start()

    def image(d, zz, jj, part):
        j = (lax.rem(xx + d, SIDE) * SIDE + zz) * 4 + core * 2 + jj
        a, b = slots[0, j], sib_slots[0, j]
        left = jnp.concatenate([w_own[part][a], w_sib[part][b]], axis=1)
        right = jnp.concatenate([ket_tiles[a], sib_tiles[b]], axis=0)
        return jnp.dot(left, right, preferred_element_type=F32)

    def relay(way, part):
        device = (row, x_up) if way == 0 else (row, x_down)
        return remote(
            x_out[part].at[2, way],
            rel_in[part].at[way],
            rel_send.at[part, way],
            rel_recv.at[part, way],
            device,
        )

    def to_x(way, jj, part):
        device = (row, x_up) if way == 0 else (row, x_down)
        return remote(
            x_out[part].at[way, jj],
            x_in[part].at[way, jj],
            x_send.at[part, way, jj],
            x_recv.at[part, way, jj],
            device,
        )

    def to_z(step, part):
        return remote(
            z_out[part].at[step - 1],
            z_in[part].at[step - 1],
            z_send.at[part, step - 1],
            z_recv.at[part, step - 1],
            (row, at_col(xx, z_at(step), core)),
        )

    def relays(part):
        for way in range(2):
            for zz in range(SIDE):
                x_out[part][2, way, zz] = image(2, zz, way, part).astype(BF16)
            relay(way, part).start()

    def direct(part):
        for way, d in ((0, 1), (1, 3)):
            for zz in range(SIDE):
                x_out[part][way, 1 - way, zz] = image(d, zz, 1 - way, part).astype(BF16)
            to_x(way, 1 - way, part).start()

    def summed(part):
        for way, d in ((0, 1), (1, 3)):
            images = [image(d, zz, way, part) for zz in range(SIDE)]
            relay(way, part).wait_recv()
            for zz in range(SIDE):
                total = images[zz] + rel_in[part][way, zz].astype(F32)
                x_out[part][way, way, zz] = total.astype(BF16)
            to_x(way, way, part).start()

    def own_sum(part):
        for jj in range(2):
            for zz in range(SIDE):
                keep[part][jj, zz] = image(0, zz, jj, part)

    def from_x(part):
        for jj in range(2):
            for way in (1 - jj, jj):
                to_x(way, jj, part).wait_recv()
                keep[part][jj] = keep[part][jj] + x_in[part][way, jj].astype(F32)
        for step in (2, 3, 1):
            for jj in range(2):
                z_out[part][step - 1, jj] = keep[part][jj, z_at(step)].astype(BF16)
            to_z(step, part).start()

    def finish(part):
        for step in (1, 3, 2):
            to_z(step, part).wait_recv()
        start, rows = PARTS[part]
        for jj in range(2):
            total = keep[part][jj, zl]
            for step in range(1, SIDE):
                total = total + z_in[part][step - 1, jj].astype(F32)
            out[start : start + rows, jj * BLOCK : (jj + 1) * BLOCK] = total.astype(BF16)

    w_finish(0)
    w_finish(1)
    to_slots.wait()
    sib_to_slots.wait()
    ket_swap.wait()
    w_swap(0).wait()
    relays(0)
    direct(0)
    w_finish(2)
    w_swap(1).wait()
    relays(1)
    summed(0)
    direct(1)
    w_swap(2).wait()
    relays(2)
    summed(1)
    direct(2)
    own_sum(0)
    from_x(0)
    summed(2)
    own_sum(1)
    own_sum(2)
    from_x(1)

    @pl.loop(0, last)
    def _(m):
        for family in range(2):
            for way in range(2):
                hop(family, way, m, 0).wait_send()

    for place in range(OWN):
        to_side(place).wait_send()
        pass_on(place).wait_send()
    for step in range(1, SIDE):
        bra_share(step).wait_send()
    from_x(2)
    finish(0)
    finish(1)
    for part in range(len(PARTS)):
        for way in range(2):
            relay(way, part).wait_send()
            for jj in range(2):
                to_x(way, jj, part).wait_send()
        for step in range(1, SIDE):
            to_z(step, part).wait_send()
    finish(2)


def local(
    basis_centers, bra_pairs, ket_pairs, quartets, quartet_counts, density_owner, density_store
):
    hbm = pl.BlockSpec(memory_space=pltpu.HBM)
    smem, i32 = pltpu.SMEM, jnp.int32
    block, count = (BLOCK, BLOCK), len(PARTS)

    def parts(lead, kind=BF16):
        return [pltpu.VMEM(lead + (rows, BLOCK), kind) for _, rows in PARTS]

    dma = pltpu.SemaphoreType.DMA
    hops = 3 * OWN + OWN // 2
    return pl.pallas_call(
        body,
        out_shape=jax.ShapeDtypeStruct((BLOCK, 2 * BLOCK), BF16),
        in_specs=[hbm] * 4 + [pl.BlockSpec(memory_space=smem)] + [hbm] * 2,
        out_specs=pl.BlockSpec(memory_space=pltpu.VMEM),
        scratch_shapes=[
            pltpu.VMEM(basis_centers.shape, F32),
            smem(bra_pairs.shape, i32),
            smem(ket_pairs.shape, i32),
            pltpu.VMEM(quartets.shape, i32),
            smem(density_owner.shape, i32),
            pltpu.VMEM((8, BLOCK), i32),
            smem((8, BLOCK), i32),
            pltpu.VMEM((8, BLOCK), i32),
            smem((8, BLOCK), i32),
            pltpu.VMEM((8, BLOCK), i32),
            smem((8, BLOCK), i32),
            dma((9,)),
            pltpu.VMEM((NBLK,) + block, BF16),
            pltpu.VMEM((NBLK, 8, BLOCK), F32),
            pltpu.VMEM((2, 3) + block, F32),
            pltpu.VMEM((PAIRS + 1,) + block, BF16),
            pltpu.VMEM((PAIRS + 1,) + block, BF16),
            pltpu.VMEM((PAIRS + 1,) + block, BF16),
            pltpu.VMEM((2, PAIRS * GROUP, PAIRS * GROUP), BF16),
            pltpu.VMEM((2, PAIRS) + block, F32),
            pltpu.VMEM((PAIRS,) + block, F32),
            parts((PAIRS + 1,)),
            parts((PAIRS + 1,)),
            parts((2, SIDE), F32),
            parts((3, 2, SIDE)),
            parts((2, SIDE)),
            parts((2, 2, SIDE)),
            parts((3, 2)),
            parts((3, 2)),
            pltpu.SemaphoreType.REGULAR,
            pltpu.VMEM((OWN,) + block, BF16),
            dma((OWN,)),
            dma((OWN,)),
            dma((OWN,)),
            dma((OWN,)),
            dma((2, 2, hops)),
            dma((2, 2, hops)),
            dma((3,)),
            dma((3,)),
            dma((count,)),
            dma((count,)),
            dma((SIDE - 1,)),
            dma((SIDE - 1,)),
            dma((count, 2)),
            dma((count, 2)),
            dma((count, 2, 2)),
            dma((count, 2, 2)),
            dma((count, 3)),
            dma((count, 3)),
        ],
        compiler_params=pltpu.CompilerParams(
            collective_id=0, has_side_effects=True, vmem_limit_bytes=56 * 2**20
        ),
        cost_estimate=pl.CostEstimate(
            flops=2 * 10**9, bytes_accessed=4 * 2**20, transcendentals=4 * 10**6
        ),
    )(
        basis_centers,
        bra_pairs,
        ket_pairs,
        quartets,
        quartet_counts,
        density_owner,
        density_store,
    )


def solution(mesh):
    return jax.shard_map(
        local,
        mesh=mesh,
        in_specs=(
            P(),
            P("bra"),
            P("ket"),
            P("bra", "ket", None, None),
            P("bra", "ket"),
            P("ket", None),
            P("bra", "ket", None),
        ),
        out_specs=P("bra", "ket"),
        check_vma=False,
    )
```

```python
import jax
import jax.numpy as jnp
from jax import lax
from jax.experimental import pallas as pl
from jax.experimental.pallas import tpu as pltpu
from jax.sharding import PartitionSpec as P

OMEGA = 0.11
SOFTEN = 0.25
BLOCK = 128
NBLK = 64
PAIRS = 32
RING = 8
DEEP = 2
SIDE = 4
OWN = 4
PARTS = ((0, 32), (32, 64), (96, 32))
GROUP = 8
SHIFT = 3
MESH = pl.DeviceIdType.MESH
F32 = jnp.float32
BF16 = jnp.bfloat16

SLOPE = 0.6 * OMEGA
DECAY = -OMEGA * OMEGA * 1.4426950408889634
ERFC = (
    0.33856715,
    0.33711259,
    0.29264139,
    0.06933287,
    0.29272546,
    -0.65555156,
    0.41918066,
    -0.09400974,
)


def kernel_value(squared):
    inverse = lax.rsqrt(squared)
    divisor = 1.0 + SLOPE * (squared * inverse)
    t = pl.reciprocal(divisor, approx=True)
    t = t * (2.0 - divisor * t)
    poly = ERFC[-1] * t + ERFC[-2]
    for c in ERFC[-3::-1]:
        poly = poly * t + c
    return jnp.exp2(DECAY * squared) * (t * inverse) * poly


def body(
    centers_hbm,
    bra_hbm,
    ket_hbm,
    quartets_hbm,
    count,
    owner_hbm,
    density_hbm,
    out,
    centers,
    bra_pairs,
    ket_pairs,
    quartets,
    owner,
    slots_vmem,
    slots,
    sib_slots_vmem,
    sib_slots,
    places_vmem,
    places,
    fetch,
    gathered,
    lines,
    columns,
    bra_tiles,
    ket_tiles,
    sib_tiles,
    spread,
    product,
    weighted,
    w_own,
    w_sib,
    keep,
    x_out,
    rel_in,
    x_in,
    z_out,
    z_in,
    passing,
    side_send,
    side_recv,
    part_send,
    part_recv,
    ring_send,
    ring_recv,
    sib_send,
    sib_recv,
    swap_send,
    swap_recv,
    share_send,
    share_recv,
    rel_send,
    rel_recv,
    x_send,
    x_recv,
    z_send,
    z_recv,
):
    row = lax.axis_index("bra")
    col = lax.axis_index("ket")
    y, deep = row // DEEP, row % DEEP
    core = col % 2
    zl = (col // 2) % SIDE
    xx = col // (2 * SIDE)

    def at_row(yy, dd):
        return lax.rem(yy + 2 * RING, RING) * DEEP + dd

    def at_col(x_at, z_at, core_at):
        return (lax.rem(x_at + SIDE, SIDE) * SIDE + z_at) * 2 + core_at

    up, down = at_row(y + 1, deep), at_row(y - 1, deep)
    partner = at_row(y, 1 - deep)
    sibling = at_col(xx, zl, 1 - core)
    x_up, x_down = at_col(xx + 1, zl, core), at_col(xx - 1, zl, core)

    def z_at(step):
        return lax.rem(zl + step, SIDE)

    same_side = (row, at_col(xx, z_at(2), core))
    other_side = (partner, at_col(xx, z_at(2), core))
    peers = [(up, col), (down, col), other_side, (row, sibling), (row, x_up), (row, x_down)]
    peers += [(row, at_col(xx, z_at(step), core)) for step in range(1, SIDE)]
    peers += [(row, at_col(xx + 2, zl, core))]
    barrier = pltpu.get_barrier_semaphore()
    for peer in peers:
        pl.semaphore_signal(barrier, inc=1, device_id=peer, device_id_type=MESH)
    own_slots = gathered.at[pl.ds(row * OWN, OWN)]
    sources = (ket_hbm, bra_hbm, centers_hbm, owner_hbm, quartets_hbm, density_hbm)
    targets = (ket_pairs, bra_pairs, centers, owner, quartets, own_slots)
    fetches = [
        pltpu.make_async_copy(src, dst, fetch.at[n])
        for n, (src, dst) in enumerate(zip(sources, targets))
    ]
    for copy in fetches:
        copy.start()
    for tiles in (bra_tiles, ket_tiles, sib_tiles):
        tiles[PAIRS] = jnp.zeros((BLOCK, BLOCK), BF16)
    for part, (_, rows) in enumerate(PARTS):
        w_own[part][PAIRS] = jnp.zeros((rows, BLOCK), BF16)
        w_sib[part][PAIRS] = jnp.zeros((rows, BLOCK), BF16)
    pl.semaphore_wait(barrier, len(peers))

    def remote(src, dst, send, recv, device):
        return pltpu.make_async_remote_copy(
            src_ref=src,
            dst_ref=dst,
            send_sem=send,
            recv_sem=recv,
            device_id=device,
            device_id_type=MESH,
        )

    def to_side(place):
        return remote(
            density_hbm.at[pl.ds(place, 1)],
            passing.at[pl.ds(place, 1)],
            side_send.at[place],
            side_recv.at[place],
            same_side if place < 2 else other_side,
        )

    def pass_on(place):
        origin = row if place < 2 else partner
        return remote(
            passing.at[pl.ds(place, 1)],
            gathered.at[pl.ds(origin * OWN + place, 1)],
            part_send.at[place],
            part_recv.at[place],
            other_side if place < 2 else same_side,
        )

    def from_partner(place):
        ref = gathered.at[pl.ds(partner * OWN + place, 1)]
        device = other_side if place < 2 else same_side
        return remote(ref, ref, part_send.at[place], part_recv.at[place], device)

    for place in (0, 2, 1, 3):
        to_side(place).start()

    def depth(family):
        return deep if family == 0 else 1 - deep

    def hop(family, way, m, arriving, first=False):
        sign = 1 - 2 * way
        back = m // OWN + arriving
        place = lax.rem(m + 2 * way, OWN)
        ref = gathered.at[pl.ds(at_row(y - sign * back, depth(family)) * OWN + place, 1)]
        src = density_hbm.at[pl.ds(place, 1)] if first else ref
        device = (up, col) if way == 0 else (down, col)
        return remote(
            src, ref, ring_send.at[family, way, m], ring_recv.at[family, way, m], device
        )

    last = 3 * OWN + OWN // 2

    def send_own(family, m):
        for way in range(2):
            hop(family, way, m, 0, family == 0).start()

    def arrive(family, m):
        for way in range(2):
            hop(family, way, m, 1).wait_recv()

    def forward(family, m):
        for way in range(2):
            hop(family, way, m - OWN, 1).wait_recv()
            hop(family, way, m, 0).start()

    for m in range(OWN):
        send_own(0, m)
    for copy in fetches[:-1]:
        copy.wait()

    lane = lax.broadcasted_iota(jnp.int32, (8, BLOCK), 1)
    ket_table = jnp.full((8, BLOCK), PAIRS, jnp.int32)
    bra_table = jnp.full((8, BLOCK), PAIRS, jnp.int32)
    for n in range(PAIRS):
        ket_table = jnp.where(lane == ket_pairs[n], n, ket_table)
        bra_table = jnp.where(lane == owner[0, bra_pairs[n]], n, bra_table)
    slots_vmem[...] = ket_table
    places_vmem[...] = bra_table
    to_slots = pltpu.make_async_copy(slots_vmem, slots, fetch.at[len(fetches)])
    to_slots.start()
    to_places = pltpu.make_async_copy(places_vmem, places, fetch.at[len(fetches) + 1])
    to_places.start()
    there = (row, sibling)
    table_swap = remote(slots_vmem, sib_slots_vmem, sib_send.at[0], sib_recv.at[0], there)
    table_swap.start()

    for block in range(NBLK):
        lines[block, 0:3] = centers[:, block * BLOCK : (block + 1) * BLOCK]
    for side, start in ((0, row * (NBLK // 16)), (1, col * (NBLK // 32))):
        line = lines[start]
        for axis in range(3):
            wide = jnp.broadcast_to(line[axis : axis + 1], (BLOCK, BLOCK))
            columns[side, axis] = wide.T

    def tile(side, block, ref, place):
        line = lines[block]
        rows = 32
        for part in range(BLOCK // rows):
            squared = jnp.full((rows, BLOCK), SOFTEN, F32)
            for axis in range(3):
                difference = columns[side, axis, pl.ds(part * rows, rows)] - line[axis : axis + 1]
                squared = squared + difference * difference
            ref[place, pl.ds(part * rows, rows)] = kernel_value(squared).astype(BF16)

    def ket_tile(q):
        tile(1, ket_pairs[q], ket_tiles, q)

    def bra_tile(p):
        tile(0, bra_pairs[p], bra_tiles, p)

    def iota(shape, axis):
        return lax.broadcasted_iota(jnp.int32, shape, axis)

    def hot(condition):
        return jnp.where(condition, jnp.float32(1.0), jnp.float32(0.0)).astype(BF16)

    size = PAIRS * GROUP

    def count_pairs():
        long = (PAIRS, quartets.shape[3])
        bra_hot = hot((quartets[0, 0, 0:1] == iota(long, 0)) & (iota(long, 1) < count[0, 0]))
        ket_hot = hot(quartets[0, 0, 1:2] == iota(long, 0))
        return lax.dot_general(
            ket_hot, bra_hot, (((1,), (1,)), ((), ())), preferred_element_type=F32
        ).astype(BF16)

    def spread_rows(counts):
        by_slot = jnp.dot(
            counts, hot(bra_table[0:1] == iota((PAIRS, BLOCK), 0)), preferred_element_type=F32
        ).astype(BF16)
        tall = hot(iota((size, PAIRS), 0) >> SHIFT == iota((size, PAIRS), 1))
        return jnp.dot(tall, by_slot, preferred_element_type=F32).astype(BF16)

    def spread_family(rows_of, family):
        same = (iota((size, size), 0) ^ iota((size, size), 1)) & (GROUP - 1) == 0
        local_slot = iota((BLOCK, size), 1) >> SHIFT
        row_slot = (local_slot >> 2) * (OWN * DEEP) + (local_slot & (OWN - 1))
        wide = hot(row_slot + depth(family) * OWN == iota((BLOCK, size), 0))
        spread[family] = jnp.where(
            same, jnp.dot(rows_of, wide, preferred_element_type=F32), jnp.float32(0.0)
        ).astype(BF16)

    def z_row(family, yy):
        at = lax.rem(yy + 2 * RING, RING)
        for extra in range(OWN):
            s = (at * DEEP + depth(family)) * OWN + extra
            product[family, at * OWN + extra] = jnp.dot(
                bra_tiles[places[0, s]], gathered[s], preferred_element_type=F32
            )

    def w_part(family, n):
        base = pl.multiple_of(n * 2 * GROUP, 2 * GROUP)
        halves = [
            product[family, :, pl.ds(base + half * GROUP, GROUP), :]
            .reshape(size, BLOCK)
            .astype(BF16)
            for half in range(2)
        ]
        both = jnp.dot(
            spread[family], jnp.concatenate(halves, axis=1), preferred_element_type=F32
        )
        return jnp.concatenate(
            [
                both[:, half * BLOCK : (half + 1) * BLOCK].reshape(PAIRS, GROUP, BLOCK)
                for half in range(2)
            ],
            axis=1,
        )

    def swap_tiles(src, dst, first, total, index):
        return remote(
            src.at[pl.ds(first, total)],
            dst.at[pl.ds(first, total)],
            sib_send.at[index],
            sib_recv.at[index],
            there,
        )

    share = PAIRS // (2 * SIDE)
    mine = core * (PAIRS // 2) + xx * share
    bra_swap = swap_tiles(bra_tiles, bra_tiles, core * (PAIRS // 2), PAIRS // 2, 1)
    ket_swap = swap_tiles(ket_tiles, sib_tiles, 0, PAIRS, 2)

    def bra_share(step):
        tiles = bra_tiles.at[pl.ds(mine, share)]
        return remote(
            tiles,
            tiles,
            share_send.at[step - 1],
            share_recv.at[step - 1],
            (row, at_col(xx + step, zl, core)),
        )

    def bra_shared(step):
        first = core * (PAIRS // 2) + lax.rem(xx - step + SIDE, SIDE) * share
        tiles = bra_tiles.at[pl.ds(first, share)]
        return remote(
            tiles,
            tiles,
            share_send.at[step - 1],
            share_recv.at[step - 1],
            (row, at_col(xx + step, zl, core)),
        )

    def ket_run(first, total):
        @pl.loop(first, first + total)
        def _(q):
            ket_tile(q)

    def w_first(first, total):
        @pl.loop(first, first + total)
        def _(n):
            weighted[:, pl.ds(n * 2 * GROUP, 2 * GROUP)] = w_part(0, n)

    for m in range(OWN):
        forward(0, OWN + m)
        if m == 0:
            for place in (0, 2, 1, 3):
                to_side(place).wait_recv()
                pass_on(place).start()
        bra_tile(mine + m)
        if m == 0:
            ket_tile(0)
        else:
            ket_run(2 * m - 1, 2)

    for step in range(1, SIDE):
        bra_share(step).start()
    forward(0, 2 * OWN)
    ket_run(7, 3)
    forward(0, 2 * OWN + 1)
    counts = count_pairs()
    forward(0, 2 * OWN + 2)
    rows_of = spread_rows(counts)
    forward(0, 2 * OWN + 3)
    ket_run(10, 3)
    for m in range(OWN):
        if m < 2:
            from_partner(m).wait_recv()
            from_partner(m + 2).wait_recv()
        send_own(1, m)
        if m == 1:
            for step in range(1, SIDE):
                bra_shared(step).wait_recv()
            bra_swap.start()
        ket_run(13 + m * 3, 3)
    forward(0, 3 * OWN)
    ket_run(25, 3)
    forward(1, OWN)
    bra_swap.wait()
    to_places.wait()
    fetches[-1].wait()
    z_row(0, y)
    z_row(0, y - 1)
    forward(1, OWN + 1)
    z_row(0, y + 1)
    z_row(0, y - 2)
    forward(0, 3 * OWN + 1)
    z_row(0, y + 2)
    spread_family(rows_of, 0)
    forward(1, OWN + 2)
    ket_run(28, 2)
    spread_family(rows_of, 1)
    forward(1, OWN + 3)
    ket_run(30, 2)
    ket_swap.start()
    forward(1, 2 * OWN)
    arrive(0, last - 4)
    arrive(0, last - 3)
    z_row(0, y - 3)
    z_row(0, y + 3)
    forward(1, 2 * OWN + 1)
    arrive(0, last - 2)
    arrive(0, last - 1)
    z_row(0, y + 4)
    forward(1, 2 * OWN + 2)
    w_first(0, 2)
    forward(1, 2 * OWN + 3)
    w_first(2, 2)
    forward(1, 3 * OWN)
    w_first(4, 1)
    forward(1, 3 * OWN + 1)
    w_first(5, 3)
    for away in (0, 1, -1, 2, -2):
        z_row(1, y + away)
    arrive(1, last - 4)
    arrive(1, last - 3)
    z_row(1, y - 3)
    z_row(1, y + 3)
    table_swap.wait()
    sib_to_slots = pltpu.make_async_copy(sib_slots_vmem, sib_slots, fetch.at[len(fetches) + 2])
    sib_to_slots.start()
    arrive(1, last - 2)
    arrive(1, last - 1)
    z_row(1, y + 4)

    def w_swap(part):
        return remote(
            w_own[part].at[pl.ds(0, PAIRS)],
            w_sib[part].at[pl.ds(0, PAIRS)],
            swap_send.at[part],
            swap_recv.at[part],
            there,
        )

    def w_finish(part):
        start, rows = PARTS[part]

        @pl.loop(0, rows // (2 * GROUP))
        def _(n):
            at = pl.multiple_of(n * 2 * GROUP, 2 * GROUP)
            total = w_part(1, n + start // (2 * GROUP))
            total = total + weighted[:, pl.ds(at + start, 2 * GROUP)]
            w_own[part][0:PAIRS, pl.ds(at, 2 * GROUP)] = total.astype(BF16)

        w_swap(part).start()

    def image(d, zz, jj, part):
        j = (lax.rem(xx + d, SIDE) * SIDE + zz) * 4 + core * 2 + jj
        a, b = slots[0, j], sib_slots[0, j]
        left = jnp.concatenate([w_own[part][a], w_sib[part][b]], axis=1)
        right = jnp.concatenate([ket_tiles[a], sib_tiles[b]], axis=0)
        return jnp.dot(left, right, preferred_element_type=F32)

    def relay(way, part):
        device = (row, x_up) if way == 0 else (row, x_down)
        return remote(
            x_out[part].at[2, way],
            rel_in[part].at[way],
            rel_send.at[part, way],
            rel_recv.at[part, way],
            device,
        )

    def to_x(way, jj, part):
        device = (row, x_up) if way == 0 else (row, x_down)
        return remote(
            x_out[part].at[way, jj],
            x_in[part].at[way, jj],
            x_send.at[part, way, jj],
            x_recv.at[part, way, jj],
            device,
        )

    def to_z(step, part):
        return remote(
            z_out[part].at[step - 1],
            z_in[part].at[step - 1],
            z_send.at[part, step - 1],
            z_recv.at[part, step - 1],
            (row, at_col(xx, z_at(step), core)),
        )

    def relays(part):
        for way in range(2):
            for zz in range(SIDE):
                x_out[part][2, way, zz] = image(2, zz, way, part).astype(BF16)
            relay(way, part).start()

    def direct(part):
        for way, d in ((0, 1), (1, 3)):
            for zz in range(SIDE):
                x_out[part][way, 1 - way, zz] = image(d, zz, 1 - way, part).astype(BF16)
            to_x(way, 1 - way, part).start()

    def summed(part):
        for way, d in ((0, 1), (1, 3)):
            images = [image(d, zz, way, part) for zz in range(SIDE)]
            relay(way, part).wait_recv()
            for zz in range(SIDE):
                total = images[zz] + rel_in[part][way, zz].astype(F32)
                x_out[part][way, way, zz] = total.astype(BF16)
            to_x(way, way, part).start()

    def own_sum(part):
        for jj in range(2):
            for zz in range(SIDE):
                keep[part][jj, zz] = image(0, zz, jj, part)

    def from_x(part):
        for jj in range(2):
            for way in (1 - jj, jj):
                to_x(way, jj, part).wait_recv()
                keep[part][jj] = keep[part][jj] + x_in[part][way, jj].astype(F32)
        for step in (2, 3, 1):
            for jj in range(2):
                z_out[part][step - 1, jj] = keep[part][jj, z_at(step)].astype(BF16)
            to_z(step, part).start()

    def finish(part):
        for step in (1, 3, 2):
            to_z(step, part).wait_recv()
        start, rows = PARTS[part]
        for jj in range(2):
            total = keep[part][jj, zl]
            for step in range(1, SIDE):
                total = total + z_in[part][step - 1, jj].astype(F32)
            out[start : start + rows, jj * BLOCK : (jj + 1) * BLOCK] = total.astype(BF16)

    w_finish(0)
    w_finish(1)
    to_slots.wait()
    sib_to_slots.wait()
    ket_swap.wait()
    w_swap(0).wait()
    relays(0)
    direct(0)
    w_finish(2)
    w_swap(1).wait()
    relays(1)
    summed(0)
    direct(1)
    w_swap(2).wait()
    relays(2)
    summed(1)
    direct(2)
    own_sum(0)
    from_x(0)
    summed(2)
    own_sum(1)
    own_sum(2)
    from_x(1)

    @pl.loop(0, last)
    def _(m):
        for family in range(2):
            for way in range(2):
                hop(family, way, m, 0).wait_send()

    for place in range(OWN):
        to_side(place).wait_send()
        pass_on(place).wait_send()
    for step in range(1, SIDE):
        bra_share(step).wait_send()
    from_x(2)
    finish(0)
    finish(1)
    for part in range(len(PARTS)):
        for way in range(2):
            relay(way, part).wait_send()
            for jj in range(2):
                to_x(way, jj, part).wait_send()
        for step in range(1, SIDE):
            to_z(step, part).wait_send()
    finish(2)


def local(
    basis_centers, bra_pairs, ket_pairs, quartets, quartet_counts, density_owner, density_store
):
    hbm = pl.BlockSpec(memory_space=pltpu.HBM)
    smem, i32 = pltpu.SMEM, jnp.int32
    block, count = (BLOCK, BLOCK), len(PARTS)

    def parts(lead, kind=BF16):
        return [pltpu.VMEM(lead + (rows, BLOCK), kind) for _, rows in PARTS]

    dma = pltpu.SemaphoreType.DMA
    hops = 3 * OWN + OWN // 2
    return pl.pallas_call(
        body,
        out_shape=jax.ShapeDtypeStruct((BLOCK, 2 * BLOCK), BF16),
        in_specs=[hbm] * 4 + [pl.BlockSpec(memory_space=smem)] + [hbm] * 2,
        out_specs=pl.BlockSpec(memory_space=pltpu.VMEM),
        scratch_shapes=[
            pltpu.VMEM(basis_centers.shape, F32),
            smem(bra_pairs.shape, i32),
            smem(ket_pairs.shape, i32),
            pltpu.VMEM(quartets.shape, i32),
            smem(density_owner.shape, i32),
            pltpu.VMEM((8, BLOCK), i32),
            smem((8, BLOCK), i32),
            pltpu.VMEM((8, BLOCK), i32),
            smem((8, BLOCK), i32),
            pltpu.VMEM((8, BLOCK), i32),
            smem((8, BLOCK), i32),
            dma((9,)),
            pltpu.VMEM((NBLK,) + block, BF16),
            pltpu.VMEM((NBLK, 8, BLOCK), F32),
            pltpu.VMEM((2, 3) + block, F32),
            pltpu.VMEM((PAIRS + 1,) + block, BF16),
            pltpu.VMEM((PAIRS + 1,) + block, BF16),
            pltpu.VMEM((PAIRS + 1,) + block, BF16),
            pltpu.VMEM((2, PAIRS * GROUP, PAIRS * GROUP), BF16),
            pltpu.VMEM((2, PAIRS) + block, F32),
            pltpu.VMEM((PAIRS,) + block, F32),
            parts((PAIRS + 1,)),
            parts((PAIRS + 1,)),
            parts((2, SIDE), F32),
            parts((3, 2, SIDE)),
            parts((2, SIDE)),
            parts((2, 2, SIDE)),
            parts((3, 2)),
            parts((3, 2)),
            pltpu.VMEM((OWN,) + block, BF16),
            dma((OWN,)),
            dma((OWN,)),
            dma((OWN,)),
            dma((OWN,)),
            dma((2, 2, hops)),
            dma((2, 2, hops)),
            dma((3,)),
            dma((3,)),
            dma((count,)),
            dma((count,)),
            dma((SIDE - 1,)),
            dma((SIDE - 1,)),
            dma((count, 2)),
            dma((count, 2)),
            dma((count, 2, 2)),
            dma((count, 2, 2)),
            dma((count, 3)),
            dma((count, 3)),
        ],
        compiler_params=pltpu.CompilerParams(
            collective_id=0, has_side_effects=True, vmem_limit_bytes=56 * 2**20
        ),
        cost_estimate=pl.CostEstimate(
            flops=2 * 10**9, bytes_accessed=4 * 2**20, transcendentals=4 * 10**6
        ),
    )(
        basis_centers,
        bra_pairs,
        ket_pairs,
        quartets,
        quartet_counts,
        density_owner,
        density_store,
    )


def solution(mesh):
    return jax.shard_map(
        local,
        mesh=mesh,
        in_specs=(
            P(),
            P("bra"),
            P("ket"),
            P("bra", "ket", None, None),
            P("bra", "ket"),
            P("ket", None),
            P("bra", "ket", None),
        ),
        out_specs=P("bra", "ket"),
        check_vma=False,
    )
```

```python
import jax
import jax.numpy as jnp
from jax import lax
from jax.experimental import pallas as pl
from jax.experimental.pallas import tpu as pltpu
from jax.sharding import PartitionSpec as P

OMEGA = 0.11
SOFTEN = 0.25
BLOCK = 128
NBLK = 64
PAIRS = 32
RING = 8
DEEP = 2
SIDE = 4
OWN = 4
PARTS = ((0, 32), (32, 64), (96, 32))
GROUP = 8
SHIFT = 3
ORDER = (
    ((0, 0), (0, -1), (0, 1), (1, 0), (1, -1), (1, 1), (0, 2), (0, -2)),
    ((1, 2), (1, -2), (0, 3), (0, -3), (0, 4), (1, 3), (1, -3), (1, 4)),
)
MESH = pl.DeviceIdType.MESH
F32 = jnp.float32
BF16 = jnp.bfloat16

SLOPE = 0.6 * OMEGA
DECAY = -OMEGA * OMEGA * 1.4426950408889634
ERFC = (
    0.33856715,
    0.33711259,
    0.29264139,
    0.06933287,
    0.29272546,
    -0.65555156,
    0.41918066,
    -0.09400974,
)


def kernel_value(squared):
    inverse = lax.rsqrt(squared)
    divisor = 1.0 + SLOPE * (squared * inverse)
    t = pl.reciprocal(divisor, approx=True)
    t = t * (2.0 - divisor * t)
    poly = ERFC[-1] * t + ERFC[-2]
    for c in ERFC[-3::-1]:
        poly = poly * t + c
    return jnp.exp2(DECAY * squared) * (t * inverse) * poly


def body(
    centers_hbm,
    bra_hbm,
    ket_hbm,
    quartets_hbm,
    count,
    owner_hbm,
    density_hbm,
    out,
    centers,
    bra_pairs,
    ket_pairs,
    quartets,
    owner,
    slots_vmem,
    slots,
    sib_slots_vmem,
    sib_slots,
    places_vmem,
    places,
    fetch,
    gathered,
    lines,
    columns,
    bra_tiles,
    ket_tiles,
    sib_tiles,
    spread,
    product,
    weighted,
    w_own,
    w_sib,
    keep,
    x_out,
    rel_in,
    x_in,
    z_out,
    z_in,
    passing,
    side_send,
    side_recv,
    part_send,
    part_recv,
    ring_send,
    ring_recv,
    sib_send,
    sib_recv,
    swap_send,
    swap_recv,
    share_send,
    share_recv,
    rel_send,
    rel_recv,
    x_send,
    x_recv,
    z_send,
    z_recv,
):
    row = lax.axis_index("bra")
    col = lax.axis_index("ket")
    y, deep = row // DEEP, row % DEEP
    core = col % 2
    zl = (col // 2) % SIDE
    xx = col // (2 * SIDE)

    def at_row(yy, dd):
        return lax.rem(yy + 2 * RING, RING) * DEEP + dd

    def at_col(x_at, z_at, core_at):
        return (lax.rem(x_at + SIDE, SIDE) * SIDE + z_at) * 2 + core_at

    up, down = at_row(y + 1, deep), at_row(y - 1, deep)
    partner = at_row(y, 1 - deep)
    sibling = at_col(xx, zl, 1 - core)
    x_up, x_down = at_col(xx + 1, zl, core), at_col(xx - 1, zl, core)

    def z_at(step):
        return lax.rem(zl + step, SIDE)

    same_side = (row, at_col(xx, z_at(2), core))
    other_side = (partner, at_col(xx, z_at(2), core))
    peers = [(up, col), (down, col), other_side, (row, sibling), (row, x_up), (row, x_down)]
    peers += [(row, at_col(xx, z_at(step), core)) for step in range(1, SIDE)]
    peers += [(row, at_col(xx + 2, zl, core))]
    barrier = pltpu.get_barrier_semaphore()
    for peer in peers:
        pl.semaphore_signal(barrier, inc=1, device_id=peer, device_id_type=MESH)
    own_slots = gathered.at[pl.ds(row * OWN, OWN)]
    sources = (ket_hbm, bra_hbm, centers_hbm, owner_hbm, quartets_hbm, density_hbm)
    targets = (ket_pairs, bra_pairs, centers, owner, quartets, own_slots)
    fetches = [
        pltpu.make_async_copy(src, dst, fetch.at[n])
        for n, (src, dst) in enumerate(zip(sources, targets))
    ]
    for copy in fetches:
        copy.start()
    for tiles in (bra_tiles, ket_tiles, sib_tiles):
        tiles[PAIRS] = jnp.zeros((BLOCK, BLOCK), BF16)
    for part, (_, rows) in enumerate(PARTS):
        w_own[part][PAIRS] = jnp.zeros((rows, BLOCK), BF16)
        w_sib[part][PAIRS] = jnp.zeros((rows, BLOCK), BF16)
    pl.semaphore_wait(barrier, len(peers))

    def remote(src, dst, send, recv, device):
        return pltpu.make_async_remote_copy(
            src_ref=src,
            dst_ref=dst,
            send_sem=send,
            recv_sem=recv,
            device_id=device,
            device_id_type=MESH,
        )

    def to_side(place):
        return remote(
            density_hbm.at[pl.ds(place, 1)],
            passing.at[pl.ds(place, 1)],
            side_send.at[place],
            side_recv.at[place],
            same_side if place < 2 else other_side,
        )

    def pass_on(place):
        origin = row if place < 2 else partner
        return remote(
            passing.at[pl.ds(place, 1)],
            gathered.at[pl.ds(origin * OWN + place, 1)],
            part_send.at[place],
            part_recv.at[place],
            other_side if place < 2 else same_side,
        )

    def from_partner(place):
        ref = gathered.at[pl.ds(partner * OWN + place, 1)]
        device = other_side if place < 2 else same_side
        return remote(ref, ref, part_send.at[place], part_recv.at[place], device)

    for place in (0, 2, 1, 3):
        to_side(place).start()

    def depth(family):
        return deep if family == 0 else 1 - deep

    def hop(family, way, m, arriving, first=False):
        sign = 1 - 2 * way
        back = m // OWN + arriving
        place = lax.rem(m + 2 * way, OWN)
        ref = gathered.at[pl.ds(at_row(y - sign * back, depth(family)) * OWN + place, 1)]
        src = density_hbm.at[pl.ds(place, 1)] if first else ref
        device = (up, col) if way == 0 else (down, col)
        return remote(
            src, ref, ring_send.at[family, way, m], ring_recv.at[family, way, m], device
        )

    last = 3 * OWN + OWN // 2

    def send_own(family, m):
        for way in range(2):
            hop(family, way, m, 0, family == 0).start()

    def arrive(family, m):
        for way in range(2):
            hop(family, way, m, 1).wait_recv()

    def forward(family, m):
        for way in range(2):
            hop(family, way, m - OWN, 1).wait_recv()
            hop(family, way, m, 0).start()

    for m in range(OWN):
        send_own(0, m)
    for copy in fetches[:-1]:
        copy.wait()

    lane = lax.broadcasted_iota(jnp.int32, (8, BLOCK), 1)
    ket_table = jnp.full((8, BLOCK), PAIRS, jnp.int32)
    bra_table = jnp.full((8, BLOCK), PAIRS, jnp.int32)
    for n in range(PAIRS):
        ket_table = jnp.where(lane == ket_pairs[n], n, ket_table)
        bra_table = jnp.where(lane == owner[0, bra_pairs[n]], n, bra_table)
    slots_vmem[...] = ket_table
    places_vmem[...] = bra_table
    to_slots = pltpu.make_async_copy(slots_vmem, slots, fetch.at[len(fetches)])
    to_slots.start()
    to_places = pltpu.make_async_copy(places_vmem, places, fetch.at[len(fetches) + 1])
    to_places.start()
    there = (row, sibling)
    table_swap = remote(slots_vmem, sib_slots_vmem, sib_send.at[0], sib_recv.at[0], there)
    table_swap.start()

    for block in range(NBLK):
        lines[block, 0:3] = centers[:, block * BLOCK : (block + 1) * BLOCK]
    for side, start in ((0, row * (NBLK // 16)), (1, col * (NBLK // 32))):
        line = lines[start]
        for axis in range(3):
            wide = jnp.broadcast_to(line[axis : axis + 1], (BLOCK, BLOCK))
            columns[side, axis] = wide.T

    def tile(side, block, ref, place):
        line = lines[block]
        rows = 32
        for part in range(BLOCK // rows):
            squared = jnp.full((rows, BLOCK), SOFTEN, F32)
            for axis in range(3):
                difference = columns[side, axis, pl.ds(part * rows, rows)] - line[axis : axis + 1]
                squared = squared + difference * difference
            ref[place, pl.ds(part * rows, rows)] = kernel_value(squared).astype(BF16)

    def ket_tile(q):
        tile(1, ket_pairs[q], ket_tiles, q)

    def bra_tile(p):
        tile(0, bra_pairs[p], bra_tiles, p)

    def iota(shape, axis):
        return lax.broadcasted_iota(jnp.int32, shape, axis)

    def hot(condition):
        return jnp.where(condition, jnp.float32(1.0), jnp.float32(0.0)).astype(BF16)

    size = PAIRS * GROUP

    def count_pairs():
        long = (PAIRS, quartets.shape[3])
        bra_hot = hot((quartets[0, 0, 0:1] == iota(long, 0)) & (iota(long, 1) < count[0, 0]))
        ket_hot = hot(quartets[0, 0, 1:2] == iota(long, 0))
        return lax.dot_general(
            ket_hot, bra_hot, (((1,), (1,)), ((), ())), preferred_element_type=F32
        ).astype(BF16)

    def spread_rows(counts):
        by_slot = jnp.dot(
            counts, hot(bra_table[0:1] == iota((PAIRS, BLOCK), 0)), preferred_element_type=F32
        ).astype(BF16)
        tall = hot(iota((size, PAIRS), 0) >> SHIFT == iota((size, PAIRS), 1))
        return jnp.dot(tall, by_slot, preferred_element_type=F32).astype(BF16)

    def first_slot(group, place):
        family, away = ORDER[group][place]
        return at_row(y + away, depth(family)) * OWN

    def spread_group(rows_of, group):
        same = (iota((size, size), 0) ^ iota((size, size), 1)) & (GROUP - 1) == 0
        local_slot = iota((BLOCK, size), 1) >> SHIFT
        row_slot = local_slot & (OWN - 1)
        for place in range(len(ORDER[group])):
            here = local_slot >> 2 == place
            row_slot = row_slot + jnp.where(here, first_slot(group, place), 0)
        wide = hot(row_slot == iota((BLOCK, size), 0))
        spread[group] = jnp.where(
            same, jnp.dot(rows_of, wide, preferred_element_type=F32), jnp.float32(0.0)
        ).astype(BF16)

    def z_row(group, place):
        for extra in range(OWN):
            s = first_slot(group, place) + extra
            product[group, place * OWN + extra] = jnp.dot(
                bra_tiles[places[0, s]], gathered[s], preferred_element_type=F32
            )

    def w_part(group, n):
        base = pl.multiple_of(n * 2 * GROUP, 2 * GROUP)
        halves = [
            product[group, :, pl.ds(base + half * GROUP, GROUP), :]
            .reshape(size, BLOCK)
            .astype(BF16)
            for half in range(2)
        ]
        both = jnp.dot(
            spread[group], jnp.concatenate(halves, axis=1), preferred_element_type=F32
        )
        return jnp.concatenate(
            [
                both[:, half * BLOCK : (half + 1) * BLOCK].reshape(PAIRS, GROUP, BLOCK)
                for half in range(2)
            ],
            axis=1,
        )

    def swap_tiles(src, dst, first, total, index):
        return remote(
            src.at[pl.ds(first, total)],
            dst.at[pl.ds(first, total)],
            sib_send.at[index],
            sib_recv.at[index],
            there,
        )

    share = PAIRS // (2 * SIDE)
    mine = core * (PAIRS // 2) + xx * share
    bra_swap = swap_tiles(bra_tiles, bra_tiles, core * (PAIRS // 2), PAIRS // 2, 1)
    ket_swap = swap_tiles(ket_tiles, sib_tiles, 0, PAIRS, 2)

    def bra_share(step):
        tiles = bra_tiles.at[pl.ds(mine, share)]
        return remote(
            tiles,
            tiles,
            share_send.at[step - 1],
            share_recv.at[step - 1],
            (row, at_col(xx + step, zl, core)),
        )

    def bra_shared(step):
        first = core * (PAIRS // 2) + lax.rem(xx - step + SIDE, SIDE) * share
        tiles = bra_tiles.at[pl.ds(first, share)]
        return remote(
            tiles,
            tiles,
            share_send.at[step - 1],
            share_recv.at[step - 1],
            (row, at_col(xx + step, zl, core)),
        )

    def ket_run(first, total):
        @pl.loop(first, first + total)
        def _(q):
            ket_tile(q)

    def w_first(first, total):
        @pl.loop(first, first + total)
        def _(n):
            weighted[:, pl.ds(n * 2 * GROUP, 2 * GROUP)] = w_part(0, n)

    for m in range(OWN):
        forward(0, OWN + m)
        if m == 0:
            for place in (0, 2, 1, 3):
                to_side(place).wait_recv()
                pass_on(place).start()
        bra_tile(mine + m)
        if m == 0:
            ket_tile(0)
        else:
            ket_run(2 * m - 1, 2)

    for step in range(1, SIDE):
        bra_share(step).start()
    for m in range(OWN):
        if m < 2:
            from_partner(m).wait_recv()
            from_partner(m + 2).wait_recv()
        send_own(1, m)
        if m == 0:
            ket_run(7, 3)
        elif m == 1:
            counts = count_pairs()
        elif m == 2:
            rows_of = spread_rows(counts)
        else:
            ket_run(10, 3)
            for step in range(1, SIDE):
                bra_shared(step).wait_recv()
            bra_swap.start()
    forward(0, 2 * OWN)
    ket_run(13, 4)
    forward(0, 2 * OWN + 1)
    ket_run(17, 4)
    forward(1, OWN)
    ket_run(21, 4)
    forward(1, OWN + 1)
    bra_swap.wait()
    to_places.wait()
    fetches[-1].wait()
    z_row(0, 0)
    z_row(0, 1)
    forward(1, OWN + 2)
    z_row(0, 2)
    z_row(0, 3)
    forward(1, OWN + 3)
    spread_group(rows_of, 0)
    forward(0, 2 * OWN + 2)
    z_row(0, 4)
    z_row(0, 5)
    forward(0, 2 * OWN + 3)
    z_row(0, 6)
    z_row(0, 7)
    for m in range(OWN):
        forward(1, 2 * OWN + m)
        w_first(2 * m, 2)
    forward(0, 3 * OWN)
    ket_run(25, 3)
    forward(0, 3 * OWN + 1)
    ket_run(28, 3)
    forward(1, 3 * OWN)
    ket_run(31, 1)
    ket_swap.start()
    spread_group(rows_of, 1)
    forward(1, 3 * OWN + 1)
    z_row(1, 0)
    z_row(1, 1)
    arrive(0, last - 4)
    arrive(0, last - 3)
    z_row(1, 2)
    z_row(1, 3)
    arrive(0, last - 2)
    arrive(0, last - 1)
    z_row(1, 4)
    arrive(1, last - 4)
    arrive(1, last - 3)
    z_row(1, 5)
    z_row(1, 6)
    table_swap.wait()
    sib_to_slots = pltpu.make_async_copy(sib_slots_vmem, sib_slots, fetch.at[len(fetches) + 2])
    sib_to_slots.start()
    arrive(1, last - 2)
    arrive(1, last - 1)
    z_row(1, 7)

    def w_swap(part):
        return remote(
            w_own[part].at[pl.ds(0, PAIRS)],
            w_sib[part].at[pl.ds(0, PAIRS)],
            swap_send.at[part],
            swap_recv.at[part],
            there,
        )

    def w_finish(part):
        start, rows = PARTS[part]

        @pl.loop(0, rows // (2 * GROUP))
        def _(n):
            at = pl.multiple_of(n * 2 * GROUP, 2 * GROUP)
            total = w_part(1, n + start // (2 * GROUP))
            total = total + weighted[:, pl.ds(at + start, 2 * GROUP)]
            w_own[part][0:PAIRS, pl.ds(at, 2 * GROUP)] = total.astype(BF16)

        w_swap(part).start()

    def image(d, zz, jj, part):
        j = (lax.rem(xx + d, SIDE) * SIDE + zz) * 4 + core * 2 + jj
        a, b = slots[0, j], sib_slots[0, j]
        left = jnp.concatenate([w_own[part][a], w_sib[part][b]], axis=1)
        right = jnp.concatenate([ket_tiles[a], sib_tiles[b]], axis=0)
        return jnp.dot(left, right, preferred_element_type=F32)

    def relay(way, part):
        device = (row, x_up) if way == 0 else (row, x_down)
        return remote(
            x_out[part].at[2, way],
            rel_in[part].at[way],
            rel_send.at[part, way],
            rel_recv.at[part, way],
            device,
        )

    def to_x(way, jj, part):
        device = (row, x_up) if way == 0 else (row, x_down)
        return remote(
            x_out[part].at[way, jj],
            x_in[part].at[way, jj],
            x_send.at[part, way, jj],
            x_recv.at[part, way, jj],
            device,
        )

    def to_z(step, part):
        return remote(
            z_out[part].at[step - 1],
            z_in[part].at[step - 1],
            z_send.at[part, step - 1],
            z_recv.at[part, step - 1],
            (row, at_col(xx, z_at(step), core)),
        )

    def relays(part):
        for way in range(2):
            for zz in range(SIDE):
                x_out[part][2, way, zz] = image(2, zz, way, part).astype(BF16)
            relay(way, part).start()

    def direct(part):
        for way, d in ((0, 1), (1, 3)):
            for zz in range(SIDE):
                x_out[part][way, 1 - way, zz] = image(d, zz, 1 - way, part).astype(BF16)
            to_x(way, 1 - way, part).start()

    def summed(part):
        for way, d in ((0, 1), (1, 3)):
            images = [image(d, zz, way, part) for zz in range(SIDE)]
            relay(way, part).wait_recv()
            for zz in range(SIDE):
                total = images[zz] + rel_in[part][way, zz].astype(F32)
                x_out[part][way, way, zz] = total.astype(BF16)
            to_x(way, way, part).start()

    def own_sum(part):
        for jj in range(2):
            for zz in range(SIDE):
                keep[part][jj, zz] = image(0, zz, jj, part)

    def from_x(part):
        for jj in range(2):
            for way in (1 - jj, jj):
                to_x(way, jj, part).wait_recv()
                keep[part][jj] = keep[part][jj] + x_in[part][way, jj].astype(F32)
        for step in (2, 3, 1):
            for jj in range(2):
                z_out[part][step - 1, jj] = keep[part][jj, z_at(step)].astype(BF16)
            to_z(step, part).start()

    def finish(part):
        for step in (1, 3, 2):
            to_z(step, part).wait_recv()
        start, rows = PARTS[part]
        for jj in range(2):
            total = keep[part][jj, zl]
            for step in range(1, SIDE):
                total = total + z_in[part][step - 1, jj].astype(F32)
            out[start : start + rows, jj * BLOCK : (jj + 1) * BLOCK] = total.astype(BF16)

    w_finish(0)
    w_finish(1)
    to_slots.wait()
    sib_to_slots.wait()
    ket_swap.wait()
    w_swap(0).wait()
    relays(0)
    direct(0)
    w_finish(2)
    w_swap(1).wait()
    relays(1)
    summed(0)
    direct(1)
    w_swap(2).wait()
    relays(2)
    summed(1)
    direct(2)
    own_sum(0)
    from_x(0)
    summed(2)
    own_sum(1)
    own_sum(2)
    from_x(1)

    @pl.loop(0, last)
    def _(m):
        for family in range(2):
            for way in range(2):
                hop(family, way, m, 0).wait_send()

    for place in range(OWN):
        to_side(place).wait_send()
        pass_on(place).wait_send()
    for step in range(1, SIDE):
        bra_share(step).wait_send()
    from_x(2)
    finish(0)
    finish(1)
    for part in range(len(PARTS)):
        for way in range(2):
            relay(way, part).wait_send()
            for jj in range(2):
                to_x(way, jj, part).wait_send()
        for step in range(1, SIDE):
            to_z(step, part).wait_send()
    finish(2)


def local(
    basis_centers, bra_pairs, ket_pairs, quartets, quartet_counts, density_owner, density_store
):
    hbm = pl.BlockSpec(memory_space=pltpu.HBM)
    smem, i32 = pltpu.SMEM, jnp.int32
    block, count = (BLOCK, BLOCK), len(PARTS)

    def parts(lead, kind=BF16):
        return [pltpu.VMEM(lead + (rows, BLOCK), kind) for _, rows in PARTS]

    dma = pltpu.SemaphoreType.DMA
    hops = 3 * OWN + OWN // 2
    return pl.pallas_call(
        body,
        out_shape=jax.ShapeDtypeStruct((BLOCK, 2 * BLOCK), BF16),
        in_specs=[hbm] * 4 + [pl.BlockSpec(memory_space=smem)] + [hbm] * 2,
        out_specs=pl.BlockSpec(memory_space=pltpu.VMEM),
        scratch_shapes=[
            pltpu.VMEM(basis_centers.shape, F32),
            smem(bra_pairs.shape, i32),
            smem(ket_pairs.shape, i32),
            pltpu.VMEM(quartets.shape, i32),
            smem(density_owner.shape, i32),
            pltpu.VMEM((8, BLOCK), i32),
            smem((8, BLOCK), i32),
            pltpu.VMEM((8, BLOCK), i32),
            smem((8, BLOCK), i32),
            pltpu.VMEM((8, BLOCK), i32),
            smem((8, BLOCK), i32),
            dma((9,)),
            pltpu.VMEM((NBLK,) + block, BF16),
            pltpu.VMEM((NBLK, 8, BLOCK), F32),
            pltpu.VMEM((2, 3) + block, F32),
            pltpu.VMEM((PAIRS + 1,) + block, BF16),
            pltpu.VMEM((PAIRS + 1,) + block, BF16),
            pltpu.VMEM((PAIRS + 1,) + block, BF16),
            pltpu.VMEM((2, PAIRS * GROUP, PAIRS * GROUP), BF16),
            pltpu.VMEM((2, PAIRS) + block, F32),
            pltpu.VMEM((PAIRS,) + block, F32),
            parts((PAIRS + 1,)),
            parts((PAIRS + 1,)),
            parts((2, SIDE), F32),
            parts((3, 2, SIDE)),
            parts((2, SIDE)),
            parts((2, 2, SIDE)),
            parts((3, 2)),
            parts((3, 2)),
            pltpu.VMEM((OWN,) + block, BF16),
            dma((OWN,)),
            dma((OWN,)),
            dma((OWN,)),
            dma((OWN,)),
            dma((2, 2, hops)),
            dma((2, 2, hops)),
            dma((3,)),
            dma((3,)),
            dma((count,)),
            dma((count,)),
            dma((SIDE - 1,)),
            dma((SIDE - 1,)),
            dma((count, 2)),
            dma((count, 2)),
            dma((count, 2, 2)),
            dma((count, 2, 2)),
            dma((count, 3)),
            dma((count, 3)),
        ],
        compiler_params=pltpu.CompilerParams(
            collective_id=0, has_side_effects=True, vmem_limit_bytes=56 * 2**20
        ),
        cost_estimate=pl.CostEstimate(
            flops=2 * 10**9, bytes_accessed=4 * 2**20, transcendentals=4 * 10**6
        ),
    )(
        basis_centers,
        bra_pairs,
        ket_pairs,
        quartets,
        quartet_counts,
        density_owner,
        density_store,
    )


def solution(mesh):
    return jax.shard_map(
        local,
        mesh=mesh,
        in_specs=(
            P(),
            P("bra"),
            P("ket"),
            P("bra", "ket", None, None),
            P("bra", "ket"),
            P("ket", None),
            P("bra", "ket", None),
        ),
        out_specs=P("bra", "ket"),
        check_vma=False,
    )
```

```python
import jax
import jax.numpy as jnp
from jax import lax
from jax.experimental import pallas as pl
from jax.experimental.pallas import tpu as pltpu
from jax.sharding import PartitionSpec as P

OMEGA = 0.11
SOFTEN = 0.25
BLOCK = 128
NBLK = 64
PAIRS = 32
RING = 8
DEEP = 2
SIDE = 4
OWN = 4
PARTS = ((0, 32), (32, 64), (96, 32))
GROUP = 8
SHIFT = 3
ORDER = (
    ((0, 0), (0, -1), (0, 1), (1, 0), (1, -1), (1, 1), (0, 2), (0, -2)),
    ((1, 2), (1, -2), (0, 3), (0, -3), (0, 4), (1, 3), (1, -3), (1, 4)),
)
MESH = pl.DeviceIdType.MESH
F32 = jnp.float32
BF16 = jnp.bfloat16

SLOPE = 0.6 * OMEGA
DECAY = -OMEGA * OMEGA * 1.4426950408889634
ERFC = (
    0.33856715,
    0.33711259,
    0.29264139,
    0.06933287,
    0.29272546,
    -0.65555156,
    0.41918066,
    -0.09400974,
)


def kernel_value(squared):
    inverse = lax.rsqrt(squared)
    divisor = 1.0 + SLOPE * (squared * inverse)
    t = pl.reciprocal(divisor, approx=True)
    t = t * (2.0 - divisor * t)
    poly = ERFC[-1] * t + ERFC[-2]
    for c in ERFC[-3::-1]:
        poly = poly * t + c
    return jnp.exp2(DECAY * squared) * (t * inverse) * poly


def body(
    centers_hbm,
    bra_hbm,
    ket_hbm,
    quartets_hbm,
    count,
    owner_hbm,
    density_hbm,
    out,
    centers,
    bra_pairs,
    ket_pairs,
    quartets,
    owner,
    slots_vmem,
    slots,
    sib_slots_vmem,
    sib_slots,
    places_vmem,
    places,
    fetch,
    gathered,
    lines,
    columns,
    bra_tiles,
    ket_tiles,
    sib_tiles,
    spread,
    product,
    weighted,
    w_own,
    w_sib,
    keep,
    x_out,
    rel_in,
    x_in,
    z_out,
    z_in,
    passing,
    side_send,
    side_recv,
    part_send,
    part_recv,
    ring_send,
    ring_recv,
    sib_send,
    sib_recv,
    swap_send,
    swap_recv,
    share_send,
    share_recv,
    rel_send,
    rel_recv,
    x_send,
    x_recv,
    z_send,
    z_recv,
):
    row = lax.axis_index("bra")
    col = lax.axis_index("ket")
    y, deep = row // DEEP, row % DEEP
    core = col % 2
    zl = (col // 2) % SIDE
    xx = col // (2 * SIDE)

    def at_row(yy, dd):
        return lax.rem(yy + 2 * RING, RING) * DEEP + dd

    def at_col(x_at, z_at, core_at):
        return (lax.rem(x_at + SIDE, SIDE) * SIDE + z_at) * 2 + core_at

    up, down = at_row(y + 1, deep), at_row(y - 1, deep)
    partner = at_row(y, 1 - deep)
    sibling = at_col(xx, zl, 1 - core)
    x_up, x_down = at_col(xx + 1, zl, core), at_col(xx - 1, zl, core)

    def z_at(step):
        return lax.rem(zl + step, SIDE)

    same_side = (row, at_col(xx, z_at(2), core))
    other_side = (partner, at_col(xx, z_at(2), core))
    peers = [(up, col), (down, col), other_side, (row, sibling), (row, x_up), (row, x_down)]
    peers += [(row, at_col(xx, z_at(step), core)) for step in range(1, SIDE)]
    peers += [(row, at_col(xx + 2, zl, core))]
    barrier = pltpu.get_barrier_semaphore()
    for peer in peers:
        pl.semaphore_signal(barrier, inc=1, device_id=peer, device_id_type=MESH)
    own_slots = gathered.at[pl.ds(row * OWN, OWN)]
    sources = (ket_hbm, bra_hbm, centers_hbm, owner_hbm, quartets_hbm, density_hbm)
    targets = (ket_pairs, bra_pairs, centers, owner, quartets, own_slots)
    fetches = [
        pltpu.make_async_copy(src, dst, fetch.at[n])
        for n, (src, dst) in enumerate(zip(sources, targets))
    ]
    for copy in fetches:
        copy.start()
    for tiles in (bra_tiles, ket_tiles, sib_tiles):
        tiles[PAIRS] = jnp.zeros((BLOCK, BLOCK), BF16)
    for part, (_, rows) in enumerate(PARTS):
        w_own[part][PAIRS] = jnp.zeros((rows, BLOCK), BF16)
        w_sib[part][PAIRS] = jnp.zeros((rows, BLOCK), BF16)
    pl.semaphore_wait(barrier, len(peers))

    def remote(src, dst, send, recv, device):
        return pltpu.make_async_remote_copy(
            src_ref=src,
            dst_ref=dst,
            send_sem=send,
            recv_sem=recv,
            device_id=device,
            device_id_type=MESH,
        )

    def to_side(place):
        return remote(
            density_hbm.at[pl.ds(place, 1)],
            passing.at[pl.ds(place, 1)],
            side_send.at[place],
            side_recv.at[place],
            same_side if place < 2 else other_side,
        )

    def pass_on(place):
        origin = row if place < 2 else partner
        return remote(
            passing.at[pl.ds(place, 1)],
            gathered.at[pl.ds(origin * OWN + place, 1)],
            part_send.at[place],
            part_recv.at[place],
            other_side if place < 2 else same_side,
        )

    def from_partner(place):
        ref = gathered.at[pl.ds(partner * OWN + place, 1)]
        device = other_side if place < 2 else same_side
        return remote(ref, ref, part_send.at[place], part_recv.at[place], device)

    for place in (0, 2, 1, 3):
        to_side(place).start()

    def depth(family):
        return deep if family == 0 else 1 - deep

    def hop(family, way, m, arriving, first=False):
        sign = 1 - 2 * way
        back = m // OWN + arriving
        place = lax.rem(m + 2 * way, OWN)
        ref = gathered.at[pl.ds(at_row(y - sign * back, depth(family)) * OWN + place, 1)]
        src = density_hbm.at[pl.ds(place, 1)] if first else ref
        device = (up, col) if way == 0 else (down, col)
        return remote(
            src, ref, ring_send.at[family, way, m], ring_recv.at[family, way, m], device
        )

    last = 3 * OWN + OWN // 2

    def send_own(family, m):
        for way in range(2):
            hop(family, way, m, 0, family == 0).start()

    def arrive(family, m):
        for way in range(2):
            hop(family, way, m, 1).wait_recv()

    def forward(family, m):
        for way in range(2):
            hop(family, way, m - OWN, 1).wait_recv()
            hop(family, way, m, 0).start()

    for m in range(OWN):
        send_own(0, m)
    for copy in fetches[:-1]:
        copy.wait()

    lane = lax.broadcasted_iota(jnp.int32, (8, BLOCK), 1)
    ket_table = jnp.full((8, BLOCK), PAIRS, jnp.int32)
    bra_table = jnp.full((8, BLOCK), PAIRS, jnp.int32)
    for n in range(PAIRS):
        ket_table = jnp.where(lane == ket_pairs[n], n, ket_table)
        bra_table = jnp.where(lane == owner[0, bra_pairs[n]], n, bra_table)
    slots_vmem[...] = ket_table
    places_vmem[...] = bra_table
    to_slots = pltpu.make_async_copy(slots_vmem, slots, fetch.at[len(fetches)])
    to_slots.start()
    to_places = pltpu.make_async_copy(places_vmem, places, fetch.at[len(fetches) + 1])
    to_places.start()
    there = (row, sibling)
    table_swap = remote(slots_vmem, sib_slots_vmem, sib_send.at[0], sib_recv.at[0], there)
    table_swap.start()

    for block in range(NBLK):
        lines[block, 0:3] = centers[:, block * BLOCK : (block + 1) * BLOCK]
    for side, start in ((0, row * (NBLK // 16)), (1, col * (NBLK // 32))):
        line = lines[start]
        for axis in range(3):
            wide = jnp.broadcast_to(line[axis : axis + 1], (BLOCK, BLOCK))
            columns[side, axis] = wide.T

    def tile(side, block, ref, place):
        line = lines[block]
        rows = 32
        for part in range(BLOCK // rows):
            squared = jnp.full((rows, BLOCK), SOFTEN, F32)
            for axis in range(3):
                difference = columns[side, axis, pl.ds(part * rows, rows)] - line[axis : axis + 1]
                squared = squared + difference * difference
            ref[place, pl.ds(part * rows, rows)] = kernel_value(squared).astype(BF16)

    def ket_tile(q):
        tile(1, ket_pairs[q], ket_tiles, q)

    def bra_tile(p):
        tile(0, bra_pairs[p], bra_tiles, p)

    def iota(shape, axis):
        return lax.broadcasted_iota(jnp.int32, shape, axis)

    def hot(condition):
        return jnp.where(condition, jnp.float32(1.0), jnp.float32(0.0)).astype(BF16)

    size = PAIRS * GROUP

    def count_pairs():
        long = (PAIRS, quartets.shape[3])
        bra_hot = hot((quartets[0, 0, 0:1] == iota(long, 0)) & (iota(long, 1) < count[0, 0]))
        ket_hot = hot(quartets[0, 0, 1:2] == iota(long, 0))
        return lax.dot_general(
            ket_hot, bra_hot, (((1,), (1,)), ((), ())), preferred_element_type=F32
        ).astype(BF16)

    def spread_rows(counts):
        by_slot = jnp.dot(
            counts, hot(bra_table[0:1] == iota((PAIRS, BLOCK), 0)), preferred_element_type=F32
        ).astype(BF16)
        tall = hot(iota((size, PAIRS), 0) >> SHIFT == iota((size, PAIRS), 1))
        return jnp.dot(tall, by_slot, preferred_element_type=F32).astype(BF16)

    def first_slot(group, place):
        family, away = ORDER[group][place]
        return at_row(y + away, depth(family)) * OWN

    def spread_group(rows_of, group):
        same = (iota((size, size), 0) ^ iota((size, size), 1)) & (GROUP - 1) == 0
        local_slot = iota((BLOCK, size), 1) >> SHIFT
        row_slot = local_slot & (OWN - 1)
        for place in range(len(ORDER[group])):
            here = local_slot >> 2 == place
            row_slot = row_slot + jnp.where(here, first_slot(group, place), 0)
        wide = hot(row_slot == iota((BLOCK, size), 0))
        spread[group] = jnp.where(
            same, jnp.dot(rows_of, wide, preferred_element_type=F32), jnp.float32(0.0)
        ).astype(BF16)

    def z_row(group, place):
        for extra in range(OWN):
            s = first_slot(group, place) + extra
            product[group, place * OWN + extra] = jnp.dot(
                bra_tiles[places[0, s]], gathered[s], preferred_element_type=F32
            )

    def w_part(group, n):
        base = pl.multiple_of(n * 2 * GROUP, 2 * GROUP)
        halves = [
            product[group, :, pl.ds(base + half * GROUP, GROUP), :]
            .reshape(size, BLOCK)
            .astype(BF16)
            for half in range(2)
        ]
        both = jnp.dot(
            spread[group], jnp.concatenate(halves, axis=1), preferred_element_type=F32
        )
        return jnp.concatenate(
            [
                both[:, half * BLOCK : (half + 1) * BLOCK].reshape(PAIRS, GROUP, BLOCK)
                for half in range(2)
            ],
            axis=1,
        )

    def swap_tiles(src, dst, first, total, index):
        return remote(
            src.at[pl.ds(first, total)],
            dst.at[pl.ds(first, total)],
            sib_send.at[index],
            sib_recv.at[index],
            there,
        )

    share = PAIRS // (2 * SIDE)
    mine = core * (PAIRS // 2) + xx * share
    bra_swap = swap_tiles(bra_tiles, bra_tiles, core * (PAIRS // 2), PAIRS // 2, 1)
    ket_swap = swap_tiles(ket_tiles, sib_tiles, 0, PAIRS, 2)

    def bra_share(step):
        tiles = bra_tiles.at[pl.ds(mine, share)]
        return remote(
            tiles,
            tiles,
            share_send.at[step - 1],
            share_recv.at[step - 1],
            (row, at_col(xx + step, zl, core)),
        )

    def bra_shared(step):
        first = core * (PAIRS // 2) + lax.rem(xx - step + SIDE, SIDE) * share
        tiles = bra_tiles.at[pl.ds(first, share)]
        return remote(
            tiles,
            tiles,
            share_send.at[step - 1],
            share_recv.at[step - 1],
            (row, at_col(xx + step, zl, core)),
        )

    def ket_run(first, total):
        @pl.loop(first, first + total)
        def _(q):
            ket_tile(q)

    def w_first(first, total):
        @pl.loop(first, first + total)
        def _(n):
            weighted[:, pl.ds(n * 2 * GROUP, 2 * GROUP)] = w_part(0, n)

    for p in range(share):
        bra_tile(mine + p)
    for step in range(1, SIDE):
        bra_share(step).start()
    for m in range(OWN):
        forward(0, OWN + m)
        if m < 2:
            for place in (m, m + 2):
                to_side(place).wait_recv()
                pass_on(place).start()
            ket_run(2 * m, 2)
        else:
            ket_run(3 * m - 2, 3)

    for m in range(OWN):
        if m < 2:
            from_partner(m).wait_recv()
            from_partner(m + 2).wait_recv()
        send_own(1, m)
        if m == 0:
            ket_run(10, 3)
        elif m == 1:
            counts = count_pairs()
        elif m == 2:
            rows_of = spread_rows(counts)
        else:
            ket_run(13, 3)
    forward(0, 2 * OWN)
    ket_run(16, 3)
    forward(0, 2 * OWN + 1)
    ket_run(19, 3)
    forward(1, OWN)
    ket_run(22, 3)
    forward(1, OWN + 1)
    for step in range(1, SIDE):
        bra_shared(step).wait_recv()
    bra_swap.start()
    ket_run(25, 3)
    forward(1, OWN + 2)
    ket_run(28, 3)
    forward(1, OWN + 3)
    ket_run(31, 1)
    ket_swap.start()
    spread_group(rows_of, 0)
    forward(0, 2 * OWN + 2)
    bra_swap.wait()
    to_places.wait()
    fetches[-1].wait()
    z_row(0, 0)
    z_row(0, 1)
    forward(0, 2 * OWN + 3)
    z_row(0, 2)
    z_row(0, 3)
    forward(1, 2 * OWN)
    z_row(0, 4)
    z_row(0, 5)
    forward(1, 2 * OWN + 1)
    z_row(0, 6)
    z_row(0, 7)
    forward(1, 2 * OWN + 2)
    w_first(0, 2)
    forward(1, 2 * OWN + 3)
    w_first(2, 2)
    forward(0, 3 * OWN)
    w_first(4, 2)
    forward(0, 3 * OWN + 1)
    w_first(6, 2)
    forward(1, 3 * OWN)
    spread_group(rows_of, 1)
    forward(1, 3 * OWN + 1)
    z_row(1, 0)
    z_row(1, 1)
    arrive(0, last - 4)
    arrive(0, last - 3)
    z_row(1, 2)
    z_row(1, 3)
    arrive(0, last - 2)
    arrive(0, last - 1)
    z_row(1, 4)
    arrive(1, last - 4)
    arrive(1, last - 3)
    z_row(1, 5)
    z_row(1, 6)
    table_swap.wait()
    sib_to_slots = pltpu.make_async_copy(sib_slots_vmem, sib_slots, fetch.at[len(fetches) + 2])
    sib_to_slots.start()
    arrive(1, last - 2)
    arrive(1, last - 1)
    z_row(1, 7)

    def w_swap(part):
        return remote(
            w_own[part].at[pl.ds(0, PAIRS)],
            w_sib[part].at[pl.ds(0, PAIRS)],
            swap_send.at[part],
            swap_recv.at[part],
            there,
        )

    def w_finish(part):
        start, rows = PARTS[part]

        @pl.loop(0, rows // (2 * GROUP))
        def _(n):
            at = pl.multiple_of(n * 2 * GROUP, 2 * GROUP)
            total = w_part(1, n + start // (2 * GROUP))
            total = total + weighted[:, pl.ds(at + start, 2 * GROUP)]
            w_own[part][0:PAIRS, pl.ds(at, 2 * GROUP)] = total.astype(BF16)

        w_swap(part).start()

    def image(d, zz, jj, part):
        j = (lax.rem(xx + d, SIDE) * SIDE + zz) * 4 + core * 2 + jj
        a, b = slots[0, j], sib_slots[0, j]
        left = jnp.concatenate([w_own[part][a], w_sib[part][b]], axis=1)
        right = jnp.concatenate([ket_tiles[a], sib_tiles[b]], axis=0)
        return jnp.dot(left, right, preferred_element_type=F32)

    def relay(way, part):
        device = (row, x_up) if way == 0 else (row, x_down)
        return remote(
            x_out[part].at[2, way],
            rel_in[part].at[way],
            rel_send.at[part, way],
            rel_recv.at[part, way],
            device,
        )

    def to_x(way, jj, part):
        device = (row, x_up) if way == 0 else (row, x_down)
        return remote(
            x_out[part].at[way, jj],
            x_in[part].at[way, jj],
            x_send.at[part, way, jj],
            x_recv.at[part, way, jj],
            device,
        )

    def to_z(step, part):
        return remote(
            z_out[part].at[step - 1],
            z_in[part].at[step - 1],
            z_send.at[part, step - 1],
            z_recv.at[part, step - 1],
            (row, at_col(xx, z_at(step), core)),
        )

    def relays(part):
        for way in range(2):
            for zz in range(SIDE):
                x_out[part][2, way, zz] = image(2, zz, way, part).astype(BF16)
            relay(way, part).start()

    def direct(part):
        for way, d in ((0, 1), (1, 3)):
            for zz in range(SIDE):
                x_out[part][way, 1 - way, zz] = image(d, zz, 1 - way, part).astype(BF16)
            to_x(way, 1 - way, part).start()

    def summed(part):
        for way, d in ((0, 1), (1, 3)):
            images = [image(d, zz, way, part) for zz in range(SIDE)]
            relay(way, part).wait_recv()
            for zz in range(SIDE):
                total = images[zz] + rel_in[part][way, zz].astype(F32)
                x_out[part][way, way, zz] = total.astype(BF16)
            to_x(way, way, part).start()

    def own_sum(part):
        for jj in range(2):
            for zz in range(SIDE):
                keep[part][jj, zz] = image(0, zz, jj, part)

    def from_x(part):
        for jj in range(2):
            for way in (1 - jj, jj):
                to_x(way, jj, part).wait_recv()
                keep[part][jj] = keep[part][jj] + x_in[part][way, jj].astype(F32)
        for step in (2, 3, 1):
            for jj in range(2):
                z_out[part][step - 1, jj] = keep[part][jj, z_at(step)].astype(BF16)
            to_z(step, part).start()

    def finish(part):
        for step in (1, 3, 2):
            to_z(step, part).wait_recv()
        start, rows = PARTS[part]
        for jj in range(2):
            total = keep[part][jj, zl]
            for step in range(1, SIDE):
                total = total + z_in[part][step - 1, jj].astype(F32)
            out[start : start + rows, jj * BLOCK : (jj + 1) * BLOCK] = total.astype(BF16)

    w_finish(0)
    w_finish(1)
    to_slots.wait()
    sib_to_slots.wait()
    ket_swap.wait()
    w_swap(0).wait()
    relays(0)
    direct(0)
    w_finish(2)
    w_swap(1).wait()
    relays(1)
    summed(0)
    direct(1)
    w_swap(2).wait()
    relays(2)
    summed(1)
    direct(2)
    own_sum(0)
    from_x(0)
    summed(2)
    own_sum(1)
    own_sum(2)
    from_x(1)

    @pl.loop(0, last)
    def _(m):
        for family in range(2):
            for way in range(2):
                hop(family, way, m, 0).wait_send()

    for place in range(OWN):
        to_side(place).wait_send()
        pass_on(place).wait_send()
    for step in range(1, SIDE):
        bra_share(step).wait_send()
    from_x(2)
    finish(0)
    finish(1)
    for part in range(len(PARTS)):
        for way in range(2):
            relay(way, part).wait_send()
            for jj in range(2):
                to_x(way, jj, part).wait_send()
        for step in range(1, SIDE):
            to_z(step, part).wait_send()
    finish(2)


def local(
    basis_centers, bra_pairs, ket_pairs, quartets, quartet_counts, density_owner, density_store
):
    hbm = pl.BlockSpec(memory_space=pltpu.HBM)
    smem, i32 = pltpu.SMEM, jnp.int32
    block, count = (BLOCK, BLOCK), len(PARTS)

    def parts(lead, kind=BF16):
        return [pltpu.VMEM(lead + (rows, BLOCK), kind) for _, rows in PARTS]

    dma = pltpu.SemaphoreType.DMA
    hops = 3 * OWN + OWN // 2
    return pl.pallas_call(
        body,
        out_shape=jax.ShapeDtypeStruct((BLOCK, 2 * BLOCK), BF16),
        in_specs=[hbm] * 4 + [pl.BlockSpec(memory_space=smem)] + [hbm] * 2,
        out_specs=pl.BlockSpec(memory_space=pltpu.VMEM),
        scratch_shapes=[
            pltpu.VMEM(basis_centers.shape, F32),
            smem(bra_pairs.shape, i32),
            smem(ket_pairs.shape, i32),
            pltpu.VMEM(quartets.shape, i32),
            smem(density_owner.shape, i32),
            pltpu.VMEM((8, BLOCK), i32),
            smem((8, BLOCK), i32),
            pltpu.VMEM((8, BLOCK), i32),
            smem((8, BLOCK), i32),
            pltpu.VMEM((8, BLOCK), i32),
            smem((8, BLOCK), i32),
            dma((9,)),
            pltpu.VMEM((NBLK,) + block, BF16),
            pltpu.VMEM((NBLK, 8, BLOCK), F32),
            pltpu.VMEM((2, 3) + block, F32),
            pltpu.VMEM((PAIRS + 1,) + block, BF16),
            pltpu.VMEM((PAIRS + 1,) + block, BF16),
            pltpu.VMEM((PAIRS + 1,) + block, BF16),
            pltpu.VMEM((2, PAIRS * GROUP, PAIRS * GROUP), BF16),
            pltpu.VMEM((2, PAIRS) + block, F32),
            pltpu.VMEM((PAIRS,) + block, F32),
            parts((PAIRS + 1,)),
            parts((PAIRS + 1,)),
            parts((2, SIDE), F32),
            parts((3, 2, SIDE)),
            parts((2, SIDE)),
            parts((2, 2, SIDE)),
            parts((3, 2)),
            parts((3, 2)),
            pltpu.VMEM((OWN,) + block, BF16),
            dma((OWN,)),
            dma((OWN,)),
            dma((OWN,)),
            dma((OWN,)),
            dma((2, 2, hops)),
            dma((2, 2, hops)),
            dma((3,)),
            dma((3,)),
            dma((count,)),
            dma((count,)),
            dma((SIDE - 1,)),
            dma((SIDE - 1,)),
            dma((count, 2)),
            dma((count, 2)),
            dma((count, 2, 2)),
            dma((count, 2, 2)),
            dma((count, 3)),
            dma((count, 3)),
        ],
        compiler_params=pltpu.CompilerParams(
            collective_id=0, has_side_effects=True, vmem_limit_bytes=56 * 2**20
        ),
        cost_estimate=pl.CostEstimate(
            flops=2 * 10**9, bytes_accessed=4 * 2**20, transcendentals=4 * 10**6
        ),
    )(
        basis_centers,
        bra_pairs,
        ket_pairs,
        quartets,
        quartet_counts,
        density_owner,
        density_store,
    )


def solution(mesh):
    return jax.shard_map(
        local,
        mesh=mesh,
        in_specs=(
            P(),
            P("bra"),
            P("ket"),
            P("bra", "ket", None, None),
            P("bra", "ket"),
            P("ket", None),
            P("bra", "ket", None),
        ),
        out_specs=P("bra", "ket"),
        check_vma=False,
    )
```

```python
import jax
import jax.numpy as jnp
from jax import lax
from jax.experimental import pallas as pl
from jax.experimental.pallas import tpu as pltpu
from jax.sharding import PartitionSpec as P

OMEGA = 0.11
SOFTEN = 0.25
BLOCK = 128
NBLK = 64
PAIRS = 32
RING = 8
DEEP = 2
SIDE = 4
OWN = 4
PARTS = ((0, 32), (32, 64), (96, 32))
GROUP = 8
SHIFT = 3
ORDER = (
    ((0, 0), (0, -1), (0, 1), (1, 0), (1, -1), (1, 1), (0, 2), (0, -2)),
    ((1, 2), (1, -2), (0, 3), (0, -3), (0, 4), (1, 3), (1, -3), (1, 4)),
)
MESH = pl.DeviceIdType.MESH
F32 = jnp.float32
BF16 = jnp.bfloat16

SLOPE = 0.6 * OMEGA
DECAY = -OMEGA * OMEGA * 1.4426950408889634
ERFC = (
    0.33856715,
    0.33711259,
    0.29264139,
    0.06933287,
    0.29272546,
    -0.65555156,
    0.41918066,
    -0.09400974,
)


def kernel_value(squared):
    inverse = lax.rsqrt(squared)
    divisor = 1.0 + SLOPE * (squared * inverse)
    t = pl.reciprocal(divisor, approx=True)
    t = t * (2.0 - divisor * t)
    poly = ERFC[-1] * t + ERFC[-2]
    for c in ERFC[-3::-1]:
        poly = poly * t + c
    return jnp.exp2(DECAY * squared) * (t * inverse) * poly


def body(
    centers_hbm,
    bra_hbm,
    ket_hbm,
    quartets_hbm,
    count,
    owner_hbm,
    density_hbm,
    out,
    centers,
    bra_pairs,
    ket_pairs,
    quartets,
    owner,
    slots_vmem,
    slots,
    sib_slots_vmem,
    sib_slots,
    places_vmem,
    places,
    fetch,
    gathered,
    lines,
    columns,
    bra_tiles,
    ket_tiles,
    sib_tiles,
    spread,
    product,
    weighted,
    w_own,
    w_sib,
    keep,
    x_out,
    rel_in,
    x_in,
    z_out,
    z_in,
    passing,
    side_send,
    side_recv,
    part_send,
    part_recv,
    ring_send,
    ring_recv,
    sib_send,
    sib_recv,
    swap_send,
    swap_recv,
    rel_send,
    rel_recv,
    x_send,
    x_recv,
    z_send,
    z_recv,
):
    row = lax.axis_index("bra")
    col = lax.axis_index("ket")
    y, deep = row // DEEP, row % DEEP
    core = col % 2
    zl = (col // 2) % SIDE
    xx = col // (2 * SIDE)

    def at_row(yy, dd):
        return lax.rem(yy + 2 * RING, RING) * DEEP + dd

    def at_col(x_at, z_at, core_at):
        return (lax.rem(x_at + SIDE, SIDE) * SIDE + z_at) * 2 + core_at

    up, down = at_row(y + 1, deep), at_row(y - 1, deep)
    partner = at_row(y, 1 - deep)
    sibling = at_col(xx, zl, 1 - core)
    x_up, x_down = at_col(xx + 1, zl, core), at_col(xx - 1, zl, core)

    def z_at(step):
        return lax.rem(zl + step, SIDE)

    same_side = (row, at_col(xx, z_at(2), core))
    other_side = (partner, at_col(xx, z_at(2), core))
    peers = [(up, col), (down, col), other_side, (row, sibling), (row, x_up), (row, x_down)]
    peers += [(row, at_col(xx, z_at(step), core)) for step in range(1, SIDE)]
    barrier = pltpu.get_barrier_semaphore()
    for peer in peers:
        pl.semaphore_signal(barrier, inc=1, device_id=peer, device_id_type=MESH)
    own_slots = gathered.at[pl.ds(row * OWN, OWN)]
    sources = (ket_hbm, bra_hbm, centers_hbm, owner_hbm, quartets_hbm, density_hbm)
    targets = (ket_pairs, bra_pairs, centers, owner, quartets, own_slots)
    fetches = [
        pltpu.make_async_copy(src, dst, fetch.at[n])
        for n, (src, dst) in enumerate(zip(sources, targets))
    ]
    for copy in fetches:
        copy.start()
    for tiles in (bra_tiles, ket_tiles, sib_tiles):
        tiles[PAIRS] = jnp.zeros((BLOCK, BLOCK), BF16)
    for part, (_, rows) in enumerate(PARTS):
        w_own[part][PAIRS] = jnp.zeros((rows, BLOCK), BF16)
        w_sib[part][PAIRS] = jnp.zeros((rows, BLOCK), BF16)
    pl.semaphore_wait(barrier, len(peers))

    def remote(src, dst, send, recv, device):
        return pltpu.make_async_remote_copy(
            src_ref=src,
            dst_ref=dst,
            send_sem=send,
            recv_sem=recv,
            device_id=device,
            device_id_type=MESH,
        )

    def to_side(place):
        return remote(
            density_hbm.at[pl.ds(place, 1)],
            passing.at[pl.ds(place, 1)],
            side_send.at[place],
            side_recv.at[place],
            same_side if place < 2 else other_side,
        )

    def pass_on(place):
        origin = row if place < 2 else partner
        return remote(
            passing.at[pl.ds(place, 1)],
            gathered.at[pl.ds(origin * OWN + place, 1)],
            part_send.at[place],
            part_recv.at[place],
            other_side if place < 2 else same_side,
        )

    def from_partner(place):
        ref = gathered.at[pl.ds(partner * OWN + place, 1)]
        device = other_side if place < 2 else same_side
        return remote(ref, ref, part_send.at[place], part_recv.at[place], device)

    for place in (0, 2, 1, 3):
        to_side(place).start()

    def depth(family):
        return deep if family == 0 else 1 - deep

    def hop(family, way, m, arriving, first=False):
        sign = 1 - 2 * way
        back = m // OWN + arriving
        place = lax.rem(m + 2 * way, OWN)
        ref = gathered.at[pl.ds(at_row(y - sign * back, depth(family)) * OWN + place, 1)]
        src = density_hbm.at[pl.ds(place, 1)] if first else ref
        device = (up, col) if way == 0 else (down, col)
        return remote(
            src, ref, ring_send.at[family, way, m], ring_recv.at[family, way, m], device
        )

    last = 3 * OWN + OWN // 2

    def send_own(family, m):
        for way in range(2):
            hop(family, way, m, 0, family == 0).start()

    def arrive(family, m):
        for way in range(2):
            hop(family, way, m, 1).wait_recv()

    def forward(family, m):
        for way in range(2):
            hop(family, way, m - OWN, 1).wait_recv()
            hop(family, way, m, 0).start()

    for m in range(OWN):
        send_own(0, m)
    for copy in fetches[:-1]:
        copy.wait()

    lane = lax.broadcasted_iota(jnp.int32, (8, BLOCK), 1)
    ket_table = jnp.full((8, BLOCK), PAIRS, jnp.int32)
    bra_table = jnp.full((8, BLOCK), PAIRS, jnp.int32)
    for n in range(PAIRS):
        ket_table = jnp.where(lane == ket_pairs[n], n, ket_table)
        bra_table = jnp.where(lane == owner[0, bra_pairs[n]], n, bra_table)
    slots_vmem[...] = ket_table
    places_vmem[...] = bra_table
    to_slots = pltpu.make_async_copy(slots_vmem, slots, fetch.at[len(fetches)])
    to_slots.start()
    to_places = pltpu.make_async_copy(places_vmem, places, fetch.at[len(fetches) + 1])
    to_places.start()
    there = (row, sibling)
    table_swap = remote(slots_vmem, sib_slots_vmem, sib_send.at[0], sib_recv.at[0], there)
    table_swap.start()

    for block in range(NBLK):
        lines[block, 0:3] = centers[:, block * BLOCK : (block + 1) * BLOCK]
    for side, start in ((0, row * (NBLK // 16)), (1, col * (NBLK // 32))):
        line = lines[start]
        for axis in range(3):
            wide = jnp.broadcast_to(line[axis : axis + 1], (BLOCK, BLOCK))
            columns[side, axis] = wide.T

    def tile(side, block, ref, place):
        line = lines[block]
        rows = 32
        for part in range(BLOCK // rows):
            squared = jnp.full((rows, BLOCK), SOFTEN, F32)
            for axis in range(3):
                difference = columns[side, axis, pl.ds(part * rows, rows)] - line[axis : axis + 1]
                squared = squared + difference * difference
            ref[place, pl.ds(part * rows, rows)] = kernel_value(squared).astype(BF16)

    def ket_tile(q):
        tile(1, ket_pairs[q], ket_tiles, q)

    def bra_tile(p):
        tile(0, bra_pairs[p], bra_tiles, p)

    def iota(shape, axis):
        return lax.broadcasted_iota(jnp.int32, shape, axis)

    def hot(condition):
        return jnp.where(condition, jnp.float32(1.0), jnp.float32(0.0)).astype(BF16)

    size = PAIRS * GROUP

    def count_pairs():
        long = (PAIRS, quartets.shape[3])
        bra_hot = hot((quartets[0, 0, 0:1] == iota(long, 0)) & (iota(long, 1) < count[0, 0]))
        ket_hot = hot(quartets[0, 0, 1:2] == iota(long, 0))
        return lax.dot_general(
            ket_hot, bra_hot, (((1,), (1,)), ((), ())), preferred_element_type=F32
        ).astype(BF16)

    def spread_rows(counts):
        by_slot = jnp.dot(
            counts, hot(bra_table[0:1] == iota((PAIRS, BLOCK), 0)), preferred_element_type=F32
        ).astype(BF16)
        tall = hot(iota((size, PAIRS), 0) >> SHIFT == iota((size, PAIRS), 1))
        return jnp.dot(tall, by_slot, preferred_element_type=F32).astype(BF16)

    def first_slot(group, place):
        family, away = ORDER[group][place]
        return at_row(y + away, depth(family)) * OWN

    def spread_group(rows_of, group):
        same = (iota((size, size), 0) ^ iota((size, size), 1)) & (GROUP - 1) == 0
        local_slot = iota((BLOCK, size), 1) >> SHIFT
        row_slot = local_slot & (OWN - 1)
        for place in range(len(ORDER[group])):
            here = local_slot >> 2 == place
            row_slot = row_slot + jnp.where(here, first_slot(group, place), 0)
        wide = hot(row_slot == iota((BLOCK, size), 0))
        spread[group] = jnp.where(
            same, jnp.dot(rows_of, wide, preferred_element_type=F32), jnp.float32(0.0)
        ).astype(BF16)

    def z_row(group, place):
        for extra in range(OWN):
            s = first_slot(group, place) + extra
            product[group, place * OWN + extra] = jnp.dot(
                bra_tiles[places[0, s]], gathered[s], preferred_element_type=F32
            )

    def w_part(group, n):
        base = pl.multiple_of(n * 2 * GROUP, 2 * GROUP)
        halves = [
            product[group, :, pl.ds(base + half * GROUP, GROUP), :]
            .reshape(size, BLOCK)
            .astype(BF16)
            for half in range(2)
        ]
        both = jnp.dot(
            spread[group], jnp.concatenate(halves, axis=1), preferred_element_type=F32
        )
        return jnp.concatenate(
            [
                both[:, half * BLOCK : (half + 1) * BLOCK].reshape(PAIRS, GROUP, BLOCK)
                for half in range(2)
            ],
            axis=1,
        )

    def swap_tiles(src, dst, first, total, index):
        return remote(
            src.at[pl.ds(first, total)],
            dst.at[pl.ds(first, total)],
            sib_send.at[index],
            sib_recv.at[index],
            there,
        )

    mine = core * (PAIRS // 2)
    bra_swap = swap_tiles(bra_tiles, bra_tiles, mine, PAIRS // 2, 1)
    ket_swap = swap_tiles(ket_tiles, sib_tiles, 0, PAIRS, 2)

    def ket_run(first, total):
        @pl.loop(first, first + total)
        def _(q):
            ket_tile(q)

    def w_first(first, total):
        @pl.loop(first, first + total)
        def _(n):
            weighted[:, pl.ds(n * 2 * GROUP, 2 * GROUP)] = w_part(0, n)

    for m in range(OWN):
        forward(0, OWN + m)
        if m < 2:
            for place in (m, m + 2):
                to_side(place).wait_recv()
                pass_on(place).start()

        @pl.loop(0, 4)
        def _(n):
            bra_tile(mine + 4 * m + n)

    bra_swap.start()
    for m in range(OWN):
        if m < 2:
            from_partner(m).wait_recv()
            from_partner(m + 2).wait_recv()
        send_own(1, m)
        if m == 0:
            ket_run(0, 3)
        elif m == 1:
            counts = count_pairs()
        elif m == 2:
            rows_of = spread_rows(counts)
        else:
            spread_group(rows_of, 0)
    forward(0, 2 * OWN)
    ket_run(3, 2)
    spread_group(rows_of, 1)
    forward(0, 2 * OWN + 1)
    ket_run(5, 4)
    for m in range(OWN):
        forward(1, OWN + m)
        ket_run(9 + 5 * m, 5)
    forward(0, 2 * OWN + 2)
    ket_run(29, 3)
    ket_swap.start()
    bra_swap.wait()
    to_places.wait()
    fetches[-1].wait()
    forward(0, 2 * OWN + 3)
    z_row(0, 0)
    z_row(0, 1)
    forward(1, 2 * OWN)
    z_row(0, 2)
    z_row(0, 3)
    forward(1, 2 * OWN + 1)
    z_row(0, 4)
    z_row(0, 5)
    forward(1, 2 * OWN + 2)
    z_row(0, 6)
    z_row(0, 7)
    forward(1, 2 * OWN + 3)
    w_first(0, 2)
    forward(0, 3 * OWN)
    w_first(2, 2)
    forward(0, 3 * OWN + 1)
    w_first(4, 2)
    forward(1, 3 * OWN)
    w_first(6, 2)
    forward(1, 3 * OWN + 1)
    z_row(1, 0)
    z_row(1, 1)
    arrive(0, last - 4)
    arrive(0, last - 3)
    z_row(1, 2)
    z_row(1, 3)
    arrive(0, last - 2)
    arrive(0, last - 1)
    z_row(1, 4)
    arrive(1, last - 4)
    arrive(1, last - 3)
    z_row(1, 5)
    z_row(1, 6)
    table_swap.wait()
    sib_to_slots = pltpu.make_async_copy(sib_slots_vmem, sib_slots, fetch.at[len(fetches) + 2])
    sib_to_slots.start()
    arrive(1, last - 2)
    arrive(1, last - 1)
    z_row(1, 7)

    def w_swap(part):
        return remote(
            w_own[part].at[pl.ds(0, PAIRS)],
            w_sib[part].at[pl.ds(0, PAIRS)],
            swap_send.at[part],
            swap_recv.at[part],
            there,
        )

    def w_finish(part):
        start, rows = PARTS[part]

        @pl.loop(0, rows // (2 * GROUP))
        def _(n):
            at = pl.multiple_of(n * 2 * GROUP, 2 * GROUP)
            total = w_part(1, n + start // (2 * GROUP))
            total = total + weighted[:, pl.ds(at + start, 2 * GROUP)]
            w_own[part][0:PAIRS, pl.ds(at, 2 * GROUP)] = total.astype(BF16)

        w_swap(part).start()

    def image(d, zz, jj, part):
        j = (lax.rem(xx + d, SIDE) * SIDE + zz) * 4 + core * 2 + jj
        a, b = slots[0, j], sib_slots[0, j]
        left = jnp.concatenate([w_own[part][a], w_sib[part][b]], axis=1)
        right = jnp.concatenate([ket_tiles[a], sib_tiles[b]], axis=0)
        return jnp.dot(left, right, preferred_element_type=F32)

    def relay(way, part):
        device = (row, x_up) if way == 0 else (row, x_down)
        return remote(
            x_out[part].at[2, way],
            rel_in[part].at[way],
            rel_send.at[part, way],
            rel_recv.at[part, way],
            device,
        )

    def to_x(way, jj, part):
        device = (row, x_up) if way == 0 else (row, x_down)
        return remote(
            x_out[part].at[way, jj],
            x_in[part].at[way, jj],
            x_send.at[part, way, jj],
            x_recv.at[part, way, jj],
            device,
        )

    def to_z(step, part):
        return remote(
            z_out[part].at[step - 1],
            z_in[part].at[step - 1],
            z_send.at[part, step - 1],
            z_recv.at[part, step - 1],
            (row, at_col(xx, z_at(step), core)),
        )

    def relays(part):
        for way in range(2):
            for zz in range(SIDE):
                x_out[part][2, way, zz] = image(2, zz, way, part).astype(BF16)
            relay(way, part).start()

    def direct(part):
        for way, d in ((0, 1), (1, 3)):
            for zz in range(SIDE):
                x_out[part][way, 1 - way, zz] = image(d, zz, 1 - way, part).astype(BF16)
            to_x(way, 1 - way, part).start()

    def summed(part):
        for way, d in ((0, 1), (1, 3)):
            images = [image(d, zz, way, part) for zz in range(SIDE)]
            relay(way, part).wait_recv()
            for zz in range(SIDE):
                total = images[zz] + rel_in[part][way, zz].astype(F32)
                x_out[part][way, way, zz] = total.astype(BF16)
            to_x(way, way, part).start()

    def own_sum(part):
        for jj in range(2):
            for zz in range(SIDE):
                keep[part][jj, zz] = image(0, zz, jj, part)

    def from_x(part):
        for jj in range(2):
            for way in (1 - jj, jj):
                to_x(way, jj, part).wait_recv()
                keep[part][jj] = keep[part][jj] + x_in[part][way, jj].astype(F32)
        for step in (2, 3, 1):
            for jj in range(2):
                z_out[part][step - 1, jj] = keep[part][jj, z_at(step)].astype(BF16)
            to_z(step, part).start()

    def finish(part):
        for step in (1, 3, 2):
            to_z(step, part).wait_recv()
        start, rows = PARTS[part]
        for jj in range(2):
            total = keep[part][jj, zl]
            for step in range(1, SIDE):
                total = total + z_in[part][step - 1, jj].astype(F32)
            out[start : start + rows, jj * BLOCK : (jj + 1) * BLOCK] = total.astype(BF16)

    w_finish(0)
    w_finish(1)
    to_slots.wait()
    sib_to_slots.wait()
    ket_swap.wait()
    w_swap(0).wait()
    relays(0)
    direct(0)
    w_finish(2)
    w_swap(1).wait()
    relays(1)
    summed(0)
    direct(1)
    w_swap(2).wait()
    relays(2)
    summed(1)
    direct(2)
    own_sum(0)
    from_x(0)
    summed(2)
    own_sum(1)
    own_sum(2)
    from_x(1)

    @pl.loop(0, last)
    def _(m):
        for family in range(2):
            for way in range(2):
                hop(family, way, m, 0).wait_send()

    for place in range(OWN):
        to_side(place).wait_send()
        pass_on(place).wait_send()
    from_x(2)
    finish(0)
    finish(1)
    for part in range(len(PARTS)):
        for way in range(2):
            relay(way, part).wait_send()
            for jj in range(2):
                to_x(way, jj, part).wait_send()
        for step in range(1, SIDE):
            to_z(step, part).wait_send()
    finish(2)


def local(
    basis_centers, bra_pairs, ket_pairs, quartets, quartet_counts, density_owner, density_store
):
    hbm = pl.BlockSpec(memory_space=pltpu.HBM)
    smem, i32 = pltpu.SMEM, jnp.int32
    block, count = (BLOCK, BLOCK), len(PARTS)

    def parts(lead, kind=BF16):
        return [pltpu.VMEM(lead + (rows, BLOCK), kind) for _, rows in PARTS]

    dma = pltpu.SemaphoreType.DMA
    hops = 3 * OWN + OWN // 2
    return pl.pallas_call(
        body,
        out_shape=jax.ShapeDtypeStruct((BLOCK, 2 * BLOCK), BF16),
        in_specs=[hbm] * 4 + [pl.BlockSpec(memory_space=smem)] + [hbm] * 2,
        out_specs=pl.BlockSpec(memory_space=pltpu.VMEM),
        scratch_shapes=[
            pltpu.VMEM(basis_centers.shape, F32),
            smem(bra_pairs.shape, i32),
            smem(ket_pairs.shape, i32),
            pltpu.VMEM(quartets.shape, i32),
            smem(density_owner.shape, i32),
            pltpu.VMEM((8, BLOCK), i32),
            smem((8, BLOCK), i32),
            pltpu.VMEM((8, BLOCK), i32),
            smem((8, BLOCK), i32),
            pltpu.VMEM((8, BLOCK), i32),
            smem((8, BLOCK), i32),
            dma((9,)),
            pltpu.VMEM((NBLK,) + block, BF16),
            pltpu.VMEM((NBLK, 8, BLOCK), F32),
            pltpu.VMEM((2, 3) + block, F32),
            pltpu.VMEM((PAIRS + 1,) + block, BF16),
            pltpu.VMEM((PAIRS + 1,) + block, BF16),
            pltpu.VMEM((PAIRS + 1,) + block, BF16),
            pltpu.VMEM((2, PAIRS * GROUP, PAIRS * GROUP), BF16),
            pltpu.VMEM((2, PAIRS) + block, F32),
            pltpu.VMEM((PAIRS,) + block, F32),
            parts((PAIRS + 1,)),
            parts((PAIRS + 1,)),
            parts((2, SIDE), F32),
            parts((3, 2, SIDE)),
            parts((2, SIDE)),
            parts((2, 2, SIDE)),
            parts((3, 2)),
            parts((3, 2)),
            pltpu.VMEM((OWN,) + block, BF16),
            dma((OWN,)),
            dma((OWN,)),
            dma((OWN,)),
            dma((OWN,)),
            dma((2, 2, hops)),
            dma((2, 2, hops)),
            dma((3,)),
            dma((3,)),
            dma((count,)),
            dma((count,)),
            dma((count, 2)),
            dma((count, 2)),
            dma((count, 2, 2)),
            dma((count, 2, 2)),
            dma((count, 3)),
            dma((count, 3)),
        ],
        compiler_params=pltpu.CompilerParams(
            collective_id=0, has_side_effects=True, vmem_limit_bytes=56 * 2**20
        ),
        cost_estimate=pl.CostEstimate(
            flops=2 * 10**9, bytes_accessed=4 * 2**20, transcendentals=4 * 10**6
        ),
    )(
        basis_centers,
        bra_pairs,
        ket_pairs,
        quartets,
        quartet_counts,
        density_owner,
        density_store,
    )


def solution(mesh):
    return jax.shard_map(
        local,
        mesh=mesh,
        in_specs=(
            P(),
            P("bra"),
            P("ket"),
            P("bra", "ket", None, None),
            P("bra", "ket"),
            P("ket", None),
            P("bra", "ket", None),
        ),
        out_specs=P("bra", "ket"),
        check_vma=False,
    )
```

```python
import jax
import jax.numpy as jnp
from jax import lax
from jax.experimental import pallas as pl
from jax.experimental.pallas import tpu as pltpu
from jax.sharding import PartitionSpec as P

OMEGA = 0.11
SOFTEN = 0.25
BLOCK = 128
NBLK = 64
PAIRS = 32
RING = 8
DEEP = 2
SIDE = 4
OWN = 4
PARTS = ((0, 32), (32, 64), (96, 32))
GROUP = 8
SHIFT = 3
AWAY = (0, -1, 1, 2, -2, 3, -3, 4)
ORDER = (
    (tuple((0, away) for away in AWAY), tuple((1, away) for away in AWAY)),
    (
        ((0, 0), (0, -1), (0, 1), (1, 0), (1, -1), (1, 1), (0, 2), (0, -2)),
        ((1, 2), (1, -2), (0, 3), (0, -3), (0, 4), (1, 3), (1, -3), (1, 4)),
    ),
)
MESH = pl.DeviceIdType.MESH
F32 = jnp.float32
BF16 = jnp.bfloat16

SLOPE = 0.6 * OMEGA
DECAY = -OMEGA * OMEGA * 1.4426950408889634
ERFC = (
    0.33856715,
    0.33711259,
    0.29264139,
    0.06933287,
    0.29272546,
    -0.65555156,
    0.41918066,
    -0.09400974,
)


def kernel_value(squared):
    inverse = lax.rsqrt(squared)
    divisor = 1.0 + SLOPE * (squared * inverse)
    t = pl.reciprocal(divisor, approx=True)
    t = t * (2.0 - divisor * t)
    poly = ERFC[-1] * t + ERFC[-2]
    for c in ERFC[-3::-1]:
        poly = poly * t + c
    return jnp.exp2(DECAY * squared) * (t * inverse) * poly


def body(
    centers_hbm,
    bra_hbm,
    ket_hbm,
    quartets_hbm,
    count,
    owner_hbm,
    density_hbm,
    out,
    centers,
    bra_pairs,
    ket_pairs,
    quartets,
    owner,
    slots_vmem,
    slots,
    sib_slots_vmem,
    sib_slots,
    places_vmem,
    places,
    fetch,
    gathered,
    lines,
    columns,
    bra_tiles,
    ket_tiles,
    sib_tiles,
    spread,
    product,
    weighted,
    w_own,
    w_sib,
    keep,
    x_out,
    rel_in,
    x_in,
    z_out,
    z_in,
    joined,
    passing,
    side_send,
    side_recv,
    part_send,
    part_recv,
    ring_send,
    ring_recv,
    sib_send,
    sib_recv,
    swap_send,
    swap_recv,
    rel_send,
    rel_recv,
    x_send,
    x_recv,
    z_send,
    z_recv,
):
    row = lax.axis_index("bra")
    col = lax.axis_index("ket")
    y, deep = row // DEEP, row % DEEP
    core = col % 2
    zl = (col // 2) % SIDE
    xx = col // (2 * SIDE)

    def at_row(yy, dd):
        return lax.rem(yy + 2 * RING, RING) * DEEP + dd

    def at_col(x_at, z_at, core_at):
        return (lax.rem(x_at + SIDE, SIDE) * SIDE + z_at) * 2 + core_at

    up, down = at_row(y + 1, deep), at_row(y - 1, deep)
    partner = at_row(y, 1 - deep)
    sibling = at_col(xx, zl, 1 - core)
    x_up, x_down = at_col(xx + 1, zl, core), at_col(xx - 1, zl, core)

    def z_at(step):
        return lax.rem(zl + step, SIDE)

    same_side = (row, at_col(xx, z_at(2), core))
    other_side = (partner, at_col(xx, z_at(2), core))
    peers = [(up, col), (down, col), (row, sibling), (row, x_up), (row, x_down)]
    peers += [(row, at_col(xx, z_at(step), core)) for step in range(1, SIDE)]
    barrier = pltpu.get_barrier_semaphore()
    for peer in peers:
        pl.semaphore_signal(barrier, inc=1, device_id=peer, device_id_type=MESH)

    @pl.when(deep == 0)
    def _():
        pl.semaphore_signal(barrier, inc=1, device_id=other_side, device_id_type=MESH)

    own_slots = gathered.at[pl.ds(row * OWN, OWN)]
    sources = (ket_hbm, bra_hbm, centers_hbm, owner_hbm, quartets_hbm, density_hbm)
    targets = (ket_pairs, bra_pairs, centers, owner, quartets, own_slots)
    fetches = [
        pltpu.make_async_copy(src, dst, fetch.at[n])
        for n, (src, dst) in enumerate(zip(sources, targets))
    ]
    for copy in fetches:
        copy.start()
    for tiles in (bra_tiles, ket_tiles, sib_tiles):
        tiles[PAIRS] = jnp.zeros((BLOCK, BLOCK), BF16)
    for part, (_, rows) in enumerate(PARTS):
        w_own[part][PAIRS] = jnp.zeros((rows, BLOCK), BF16)
        w_sib[part][PAIRS] = jnp.zeros((rows, BLOCK), BF16)
    pl.semaphore_wait(barrier, len(peers) + deep)

    @pl.when(deep == 1)
    def _():
        pl.semaphore_signal(joined, inc=1, device_id=other_side, device_id_type=MESH)


    def remote(src, dst, send, recv, device):
        return pltpu.make_async_remote_copy(
            src_ref=src,
            dst_ref=dst,
            send_sem=send,
            recv_sem=recv,
            device_id=device,
            device_id_type=MESH,
        )

    def to_side(place):
        return remote(
            density_hbm.at[pl.ds(place, 1)],
            passing.at[pl.ds(place, 1)],
            side_send.at[place],
            side_recv.at[place],
            same_side if place < 2 else other_side,
        )

    def pass_on(place):
        origin = row if place < 2 else partner
        return remote(
            passing.at[pl.ds(place, 1)],
            gathered.at[pl.ds(origin * OWN + place, 1)],
            part_send.at[place],
            part_recv.at[place],
            other_side if place < 2 else same_side,
        )

    def from_partner(place):
        ref = gathered.at[pl.ds(partner * OWN + place, 1)]
        device = other_side if place < 2 else same_side
        return remote(ref, ref, part_send.at[place], part_recv.at[place], device)

    for place in (0, 1):
        to_side(place).start()

    @pl.when(deep == 1)
    def _():
        for place in (2, 3):
            to_side(place).start()

    def depth(family):
        return deep if family == 0 else 1 - deep

    def hop(family, way, m, arriving, first=False):
        sign = 1 - 2 * way
        back = m // OWN + arriving
        place = lax.rem(m + 2 * way, OWN)
        ref = gathered.at[pl.ds(at_row(y - sign * back, depth(family)) * OWN + place, 1)]
        src = density_hbm.at[pl.ds(place, 1)] if first else ref
        device = (up, col) if way == 0 else (down, col)
        return remote(
            src, ref, ring_send.at[family, way, m], ring_recv.at[family, way, m], device
        )

    last = 3 * OWN + OWN // 2

    def send_own(family, m):
        for way in range(2):
            hop(family, way, m, 0, family == 0).start()

    def arrive(family, m):
        for way in range(2):
            hop(family, way, m, 1).wait_recv()

    def forward(family, m):
        for way in range(2):
            hop(family, way, m - OWN, 1).wait_recv()
            hop(family, way, m, 0).start()

    for m in range(OWN):
        send_own(0, m)
    for copy in fetches[:-1]:
        copy.wait()

    lane = lax.broadcasted_iota(jnp.int32, (8, BLOCK), 1)
    ket_table = jnp.full((8, BLOCK), PAIRS, jnp.int32)
    bra_table = jnp.full((8, BLOCK), PAIRS, jnp.int32)
    for n in range(PAIRS):
        ket_table = jnp.where(lane == ket_pairs[n], n, ket_table)
        bra_table = jnp.where(lane == owner[0, bra_pairs[n]], n, bra_table)
    slots_vmem[...] = ket_table
    places_vmem[...] = bra_table
    to_slots = pltpu.make_async_copy(slots_vmem, slots, fetch.at[len(fetches)])
    to_slots.start()
    to_places = pltpu.make_async_copy(places_vmem, places, fetch.at[len(fetches) + 1])
    to_places.start()
    there = (row, sibling)
    table_swap = remote(slots_vmem, sib_slots_vmem, sib_send.at[0], sib_recv.at[0], there)
    table_swap.start()

    for block in range(NBLK):
        lines[block, 0:3] = centers[:, block * BLOCK : (block + 1) * BLOCK]
    for side, start in ((0, row * (NBLK // 16)), (1, col * (NBLK // 32))):
        line = lines[start]
        for axis in range(3):
            wide = jnp.broadcast_to(line[axis : axis + 1], (BLOCK, BLOCK))
            columns[side, axis] = wide.T

    def tile(side, block, ref, place):
        line = lines[block]
        rows = 32
        for part in range(BLOCK // rows):
            squared = jnp.full((rows, BLOCK), SOFTEN, F32)
            for axis in range(3):
                difference = columns[side, axis, pl.ds(part * rows, rows)] - line[axis : axis + 1]
                squared = squared + difference * difference
            ref[place, pl.ds(part * rows, rows)] = kernel_value(squared).astype(BF16)

    def ket_tile(q):
        tile(1, ket_pairs[q], ket_tiles, q)

    def bra_tile(p):
        tile(0, bra_pairs[p], bra_tiles, p)

    def iota(shape, axis):
        return lax.broadcasted_iota(jnp.int32, shape, axis)

    def hot(condition):
        return jnp.where(condition, jnp.float32(1.0), jnp.float32(0.0)).astype(BF16)

    size = PAIRS * GROUP

    def count_pairs():
        long = (PAIRS, quartets.shape[3])
        bra_hot = hot((quartets[0, 0, 0:1] == iota(long, 0)) & (iota(long, 1) < count[0, 0]))
        ket_hot = hot(quartets[0, 0, 1:2] == iota(long, 0))
        return lax.dot_general(
            ket_hot, bra_hot, (((1,), (1,)), ((), ())), preferred_element_type=F32
        ).astype(BF16)

    def spread_rows(counts):
        by_slot = jnp.dot(
            counts, hot(bra_table[0:1] == iota((PAIRS, BLOCK), 0)), preferred_element_type=F32
        ).astype(BF16)
        tall = hot(iota((size, PAIRS), 0) >> SHIFT == iota((size, PAIRS), 1))
        return jnp.dot(tall, by_slot, preferred_element_type=F32).astype(BF16)

    def first_slot(group, place):
        slots_at = [
            at_row(y + ORDER[plane][group][place][1], depth(ORDER[plane][group][place][0])) * OWN
            for plane in range(DEEP)
        ]
        return jnp.where(deep == 0, slots_at[0], slots_at[1])

    def spread_group(rows_of, group):
        same = (iota((size, size), 0) ^ iota((size, size), 1)) & (GROUP - 1) == 0
        local_slot = iota((BLOCK, size), 1) >> SHIFT
        row_slot = local_slot & (OWN - 1)
        for place in range(RING):
            here = local_slot >> 2 == place
            row_slot = row_slot + jnp.where(here, first_slot(group, place), 0)
        wide = hot(row_slot == iota((BLOCK, size), 0))
        spread[group] = jnp.where(
            same, jnp.dot(rows_of, wide, preferred_element_type=F32), jnp.float32(0.0)
        ).astype(BF16)

    def z_row(group, place):
        for extra in range(OWN):
            s = first_slot(group, place) + extra
            product[group, place * OWN + extra] = jnp.dot(
                bra_tiles[places[0, s]], gathered[s], preferred_element_type=F32
            )

    def w_part(group, n):
        base = pl.multiple_of(n * 2 * GROUP, 2 * GROUP)
        halves = [
            product[group, :, pl.ds(base + half * GROUP, GROUP), :]
            .reshape(size, BLOCK)
            .astype(BF16)
            for half in range(2)
        ]
        both = jnp.dot(
            spread[group], jnp.concatenate(halves, axis=1), preferred_element_type=F32
        )
        return jnp.concatenate(
            [
                both[:, half * BLOCK : (half + 1) * BLOCK].reshape(PAIRS, GROUP, BLOCK)
                for half in range(2)
            ],
            axis=1,
        )

    def swap_tiles(src, dst, first, total, index):
        return remote(
            src.at[pl.ds(first, total)],
            dst.at[pl.ds(first, total)],
            sib_send.at[index],
            sib_recv.at[index],
            there,
        )

    mine = core * (PAIRS // 2)
    bra_swap = swap_tiles(bra_tiles, bra_tiles, mine, PAIRS // 2, 1)
    ket_swap = swap_tiles(ket_tiles, sib_tiles, 0, PAIRS, 2)

    def ket_run(first, total):
        @pl.loop(first, first + total)
        def _(q):
            ket_tile(q)

    def w_first(first, total):
        @pl.loop(first, first + total)
        def _(n):
            weighted[:, pl.ds(n * 2 * GROUP, 2 * GROUP)] = w_part(0, n)

    def bra_run(m):
        @pl.loop(0, 4)
        def _(n):
            bra_tile(mine + 4 * m + n)

    def send_partner(m):
        if m < 2:
            from_partner(m).wait_recv()
            from_partner(m + 2).wait_recv()
        send_own(1, m)

    def relay_side(place):
        to_side(place).wait_recv()
        pass_on(place).start()

    def ready_for_rows():
        ket_swap.start()
        bra_swap.wait()
        to_places.wait()
        fetches[-1].wait()

    @pl.when(deep == 0)
    def _():
        for m in range(OWN):
            forward(0, OWN + m)
            bra_run(m)
        bra_swap.start()
        pl.semaphore_wait(joined, 1)
        for place in (2, 3):
            to_side(place).start()
        for place in range(OWN):
            relay_side(place)
        forward(0, 2 * OWN)
        ket_run(0, 5)
        forward(0, 2 * OWN + 1)
        ket_run(5, 5)
        forward(0, 2 * OWN + 2)
        ket_run(10, 5)
        forward(0, 2 * OWN + 3)
        ket_run(15, 5)
        forward(0, 3 * OWN)
        ket_run(20, 4)
        forward(0, 3 * OWN + 1)
        ket_run(24, 4)
        counts = count_pairs()
        send_partner(0)
        rows_of = spread_rows(counts)
        send_partner(1)
        spread_group(rows_of, 0)
        send_partner(2)
        spread_group(rows_of, 1)
        send_partner(3)
        ket_run(28, 4)
        ready_for_rows()
        for m in range(OWN):
            forward(1, OWN + m)
            if m == 2:
                arrive(0, last - 4)
                arrive(0, last - 3)
            if m == 3:
                arrive(0, last - 2)
                arrive(0, last - 1)
            z_row(0, 2 * m)
            z_row(0, 2 * m + 1)
        for m in range(OWN):
            forward(1, 2 * OWN + m)
            w_first(2 * m, 2)
        forward(1, 3 * OWN)
        z_row(1, 0)
        forward(1, 3 * OWN + 1)
        for place in range(1, 5):
            z_row(1, place)

    @pl.when(deep == 1)
    def _():
        for m in range(OWN):
            forward(0, OWN + m)
            if m < 2:
                relay_side(m)
            bra_run(m)
        bra_swap.start()
        for place in (2, 3):
            relay_side(place)
        for m in range(OWN):
            send_partner(m)
            if m == 0:
                ket_run(0, 3)
            elif m == 1:
                counts = count_pairs()
            elif m == 2:
                rows_of = spread_rows(counts)
            else:
                spread_group(rows_of, 0)
        forward(0, 2 * OWN)
        ket_run(3, 2)
        spread_group(rows_of, 1)
        forward(0, 2 * OWN + 1)
        ket_run(5, 4)
        for m in range(OWN):
            forward(1, OWN + m)
            ket_run(9 + 5 * m, 5)
        forward(0, 2 * OWN + 2)
        ket_run(29, 3)
        ready_for_rows()
        forward(0, 2 * OWN + 3)
        z_row(0, 0)
        z_row(0, 1)
        for m in range(3):
            forward(1, 2 * OWN + m)
            z_row(0, 2 * m + 2)
            z_row(0, 2 * m + 3)
        forward(1, 2 * OWN + 3)
        w_first(0, 2)
        forward(0, 3 * OWN)
        w_first(2, 2)
        forward(0, 3 * OWN + 1)
        w_first(4, 2)
        forward(1, 3 * OWN)
        w_first(6, 2)
        forward(1, 3 * OWN + 1)
        z_row(1, 0)
        z_row(1, 1)
        arrive(0, last - 4)
        arrive(0, last - 3)
        z_row(1, 2)
        z_row(1, 3)
        arrive(0, last - 2)
        arrive(0, last - 1)
        z_row(1, 4)

    arrive(1, last - 4)
    arrive(1, last - 3)
    z_row(1, 5)
    z_row(1, 6)
    table_swap.wait()
    sib_to_slots = pltpu.make_async_copy(sib_slots_vmem, sib_slots, fetch.at[len(fetches) + 2])
    sib_to_slots.start()
    arrive(1, last - 2)
    arrive(1, last - 1)
    z_row(1, 7)

    def w_swap(part):
        return remote(
            w_own[part].at[pl.ds(0, PAIRS)],
            w_sib[part].at[pl.ds(0, PAIRS)],
            swap_send.at[part],
            swap_recv.at[part],
            there,
        )

    def w_finish(part):
        start, rows = PARTS[part]

        @pl.loop(0, rows // (2 * GROUP))
        def _(n):
            at = pl.multiple_of(n * 2 * GROUP, 2 * GROUP)
            total = w_part(1, n + start // (2 * GROUP))
            total = total + weighted[:, pl.ds(at + start, 2 * GROUP)]
            w_own[part][0:PAIRS, pl.ds(at, 2 * GROUP)] = total.astype(BF16)

        w_swap(part).start()

    def image(d, zz, jj, part):
        j = (lax.rem(xx + d, SIDE) * SIDE + zz) * 4 + core * 2 + jj
        a, b = slots[0, j], sib_slots[0, j]
        left = jnp.concatenate([w_own[part][a], w_sib[part][b]], axis=1)
        right = jnp.concatenate([ket_tiles[a], sib_tiles[b]], axis=0)
        return jnp.dot(left, right, preferred_element_type=F32)

    def relay(way, part):
        device = (row, x_up) if way == 0 else (row, x_down)
        return remote(
            x_out[part].at[2, way],
            rel_in[part].at[way],
            rel_send.at[part, way],
            rel_recv.at[part, way],
            device,
        )

    def to_x(way, jj, part):
        device = (row, x_up) if way == 0 else (row, x_down)
        return remote(
            x_out[part].at[way, jj],
            x_in[part].at[way, jj],
            x_send.at[part, way, jj],
            x_recv.at[part, way, jj],
            device,
        )

    def to_z(step, part):
        return remote(
            z_out[part].at[step - 1],
            z_in[part].at[step - 1],
            z_send.at[part, step - 1],
            z_recv.at[part, step - 1],
            (row, at_col(xx, z_at(step), core)),
        )

    def relays(part):
        for way in range(2):
            for zz in range(SIDE):
                x_out[part][2, way, zz] = image(2, zz, way, part).astype(BF16)
            relay(way, part).start()

    def direct(part):
        for way, d in ((0, 1), (1, 3)):
            for zz in range(SIDE):
                x_out[part][way, 1 - way, zz] = image(d, zz, 1 - way, part).astype(BF16)
            to_x(way, 1 - way, part).start()

    def summed(part):
        for way, d in ((0, 1), (1, 3)):
            images = [image(d, zz, way, part) for zz in range(SIDE)]
            relay(way, part).wait_recv()
            for zz in range(SIDE):
                total = images[zz] + rel_in[part][way, zz].astype(F32)
                x_out[part][way, way, zz] = total.astype(BF16)
            to_x(way, way, part).start()

    def own_sum(part):
        for jj in range(2):
            for zz in range(SIDE):
                keep[part][jj, zz] = image(0, zz, jj, part)

    def from_x(part):
        for jj in range(2):
            for way in (1 - jj, jj):
                to_x(way, jj, part).wait_recv()
                keep[part][jj] = keep[part][jj] + x_in[part][way, jj].astype(F32)
        for step in (2, 3, 1):
            for jj in range(2):
                z_out[part][step - 1, jj] = keep[part][jj, z_at(step)].astype(BF16)
            to_z(step, part).start()

    def finish(part):
        for step in (1, 3, 2):
            to_z(step, part).wait_recv()
        start, rows = PARTS[part]
        for jj in range(2):
            total = keep[part][jj, zl]
            for step in range(1, SIDE):
                total = total + z_in[part][step - 1, jj].astype(F32)
            out[start : start + rows, jj * BLOCK : (jj + 1) * BLOCK] = total.astype(BF16)

    w_finish(0)
    w_finish(1)
    to_slots.wait()
    sib_to_slots.wait()
    ket_swap.wait()
    w_swap(0).wait()
    relays(0)
    direct(0)
    w_finish(2)
    w_swap(1).wait()
    relays(1)
    summed(0)
    direct(1)
    w_swap(2).wait()
    relays(2)
    summed(1)
    direct(2)
    own_sum(0)
    from_x(0)
    summed(2)
    own_sum(1)
    own_sum(2)
    from_x(1)

    @pl.loop(0, last)
    def _(m):
        for family in range(2):
            for way in range(2):
                hop(family, way, m, 0).wait_send()

    for place in range(OWN):
        to_side(place).wait_send()
        pass_on(place).wait_send()
    from_x(2)
    finish(0)
    finish(1)
    for part in range(len(PARTS)):
        for way in range(2):
            relay(way, part).wait_send()
            for jj in range(2):
                to_x(way, jj, part).wait_send()
        for step in range(1, SIDE):
            to_z(step, part).wait_send()
    finish(2)


def local(
    basis_centers, bra_pairs, ket_pairs, quartets, quartet_counts, density_owner, density_store
):
    hbm = pl.BlockSpec(memory_space=pltpu.HBM)
    smem, i32 = pltpu.SMEM, jnp.int32
    block, count = (BLOCK, BLOCK), len(PARTS)

    def parts(lead, kind=BF16):
        return [pltpu.VMEM(lead + (rows, BLOCK), kind) for _, rows in PARTS]

    dma = pltpu.SemaphoreType.DMA
    hops = 3 * OWN + OWN // 2
    return pl.pallas_call(
        body,
        out_shape=jax.ShapeDtypeStruct((BLOCK, 2 * BLOCK), BF16),
        in_specs=[hbm] * 4 + [pl.BlockSpec(memory_space=smem)] + [hbm] * 2,
        out_specs=pl.BlockSpec(memory_space=pltpu.VMEM),
        scratch_shapes=[
            pltpu.VMEM(basis_centers.shape, F32),
            smem(bra_pairs.shape, i32),
            smem(ket_pairs.shape, i32),
            pltpu.VMEM(quartets.shape, i32),
            smem(density_owner.shape, i32),
            pltpu.VMEM((8, BLOCK), i32),
            smem((8, BLOCK), i32),
            pltpu.VMEM((8, BLOCK), i32),
            smem((8, BLOCK), i32),
            pltpu.VMEM((8, BLOCK), i32),
            smem((8, BLOCK), i32),
            dma((9,)),
            pltpu.VMEM((NBLK,) + block, BF16),
            pltpu.VMEM((NBLK, 8, BLOCK), F32),
            pltpu.VMEM((2, 3) + block, F32),
            pltpu.VMEM((PAIRS + 1,) + block, BF16),
            pltpu.VMEM((PAIRS + 1,) + block, BF16),
            pltpu.VMEM((PAIRS + 1,) + block, BF16),
            pltpu.VMEM((2, PAIRS * GROUP, PAIRS * GROUP), BF16),
            pltpu.VMEM((2, PAIRS) + block, F32),
            pltpu.VMEM((PAIRS,) + block, F32),
            parts((PAIRS + 1,)),
            parts((PAIRS + 1,)),
            parts((2, SIDE), F32),
            parts((3, 2, SIDE)),
            parts((2, SIDE)),
            parts((2, 2, SIDE)),
            parts((3, 2)),
            parts((3, 2)),
            pltpu.SemaphoreType.REGULAR,
            pltpu.VMEM((OWN,) + block, BF16),
            dma((OWN,)),
            dma((OWN,)),
            dma((OWN,)),
            dma((OWN,)),
            dma((2, 2, hops)),
            dma((2, 2, hops)),
            dma((3,)),
            dma((3,)),
            dma((count,)),
            dma((count,)),
            dma((count, 2)),
            dma((count, 2)),
            dma((count, 2, 2)),
            dma((count, 2, 2)),
            dma((count, 3)),
            dma((count, 3)),
        ],
        compiler_params=pltpu.CompilerParams(
            collective_id=0, has_side_effects=True, vmem_limit_bytes=56 * 2**20
        ),
        cost_estimate=pl.CostEstimate(
            flops=2 * 10**9, bytes_accessed=4 * 2**20, transcendentals=4 * 10**6
        ),
    )(
        basis_centers,
        bra_pairs,
        ket_pairs,
        quartets,
        quartet_counts,
        density_owner,
        density_store,
    )


def solution(mesh):
    return jax.shard_map(
        local,
        mesh=mesh,
        in_specs=(
            P(),
            P("bra"),
            P("ket"),
            P("bra", "ket", None, None),
            P("bra", "ket"),
            P("ket", None),
            P("bra", "ket", None),
        ),
        out_specs=P("bra", "ket"),
        check_vma=False,
    )
```

```python
import jax
import jax.numpy as jnp
from jax import lax
from jax.experimental import pallas as pl
from jax.experimental.pallas import tpu as pltpu
from jax.sharding import PartitionSpec as P

OMEGA = 0.11
SOFTEN = 0.25
BLOCK = 128
NBLK = 64
PAIRS = 32
RING = 8
DEEP = 2
SIDE = 4
OWN = 4
PARTS = ((0, 32), (32, 64), (96, 32))
GROUP = 8
SHIFT = 3
MESH = pl.DeviceIdType.MESH
F32 = jnp.float32
BF16 = jnp.bfloat16

SLOPE = 0.6 * OMEGA
DECAY = -OMEGA * OMEGA * 1.4426950408889634
ERFC = (
    0.33856715,
    0.33711259,
    0.29264139,
    0.06933287,
    0.29272546,
    -0.65555156,
    0.41918066,
    -0.09400974,
)


def kernel_value(squared):
    inverse = lax.rsqrt(squared)
    divisor = 1.0 + SLOPE * (squared * inverse)
    t = pl.reciprocal(divisor, approx=True)
    t = t * (2.0 - divisor * t)
    poly = ERFC[-1] * t + ERFC[-2]
    for c in ERFC[-3::-1]:
        poly = poly * t + c
    return jnp.exp2(DECAY * squared) * (t * inverse) * poly


def body(
    centers_hbm,
    bra_hbm,
    ket_hbm,
    quartets_hbm,
    count,
    owner_hbm,
    density_hbm,
    out,
    centers,
    bra_pairs,
    ket_pairs,
    quartets,
    owner,
    slots_vmem,
    slots,
    sib_slots_vmem,
    sib_slots,
    places_vmem,
    places,
    fetch,
    gathered,
    lines,
    columns,
    bra_tiles,
    ket_tiles,
    sib_tiles,
    spread,
    product,
    weighted,
    w_own,
    w_sib,
    keep,
    x_out,
    rel_in,
    x_in,
    z_out,
    z_in,
    passing,
    side_send,
    side_recv,
    part_send,
    part_recv,
    ring_send,
    ring_recv,
    sib_send,
    sib_recv,
    swap_send,
    swap_recv,
    share_send,
    share_recv,
    rel_send,
    rel_recv,
    x_send,
    x_recv,
    z_send,
    z_recv,
):
    row = lax.axis_index("bra")
    col = lax.axis_index("ket")
    y, deep = row // DEEP, row % DEEP
    core = col % 2
    zl = (col // 2) % SIDE
    xx = col // (2 * SIDE)

    def at_row(yy, dd):
        return lax.rem(yy + 2 * RING, RING) * DEEP + dd

    def at_col(x_at, z_at, core_at):
        return (lax.rem(x_at + SIDE, SIDE) * SIDE + z_at) * 2 + core_at

    up, down = at_row(y + 1, deep), at_row(y - 1, deep)
    partner = at_row(y, 1 - deep)
    sibling = at_col(xx, zl, 1 - core)
    x_up, x_down = at_col(xx + 1, zl, core), at_col(xx - 1, zl, core)

    def z_at(step):
        return lax.rem(zl + step, SIDE)

    same_side = (row, at_col(xx, z_at(2), core))
    other_side = (partner, at_col(xx, z_at(2), core))
    peers = [(up, col), (down, col), other_side, (row, sibling), (row, x_up), (row, x_down)]
    peers += [(row, at_col(xx, z_at(step), core)) for step in range(1, SIDE)]
    peers += [(row, at_col(xx + 2, zl, core))]
    barrier = pltpu.get_barrier_semaphore()
    for peer in peers:
        pl.semaphore_signal(barrier, inc=1, device_id=peer, device_id_type=MESH)
    own_slots = gathered.at[pl.ds(row * OWN, OWN)]
    sources = (ket_hbm, bra_hbm, centers_hbm, owner_hbm, quartets_hbm, density_hbm)
    targets = (ket_pairs, bra_pairs, centers, owner, quartets, own_slots)
    fetches = [
        pltpu.make_async_copy(src, dst, fetch.at[n])
        for n, (src, dst) in enumerate(zip(sources, targets))
    ]
    for copy in fetches:
        copy.start()
    for tiles in (bra_tiles, ket_tiles, sib_tiles):
        tiles[PAIRS] = jnp.zeros((BLOCK, BLOCK), BF16)
    for part, (_, rows) in enumerate(PARTS):
        w_own[part][PAIRS] = jnp.zeros((rows, BLOCK), BF16)
        w_sib[part][PAIRS] = jnp.zeros((rows, BLOCK), BF16)
    pl.semaphore_wait(barrier, len(peers))

    def remote(src, dst, send, recv, device):
        return pltpu.make_async_remote_copy(
            src_ref=src,
            dst_ref=dst,
            send_sem=send,
            recv_sem=recv,
            device_id=device,
            device_id_type=MESH,
        )

    def to_side(place):
        return remote(
            density_hbm.at[pl.ds(place, 1)],
            passing.at[pl.ds(place, 1)],
            side_send.at[place],
            side_recv.at[place],
            same_side if place < 2 else other_side,
        )

    def pass_on(place):
        origin = row if place < 2 else partner
        return remote(
            passing.at[pl.ds(place, 1)],
            gathered.at[pl.ds(origin * OWN + place, 1)],
            part_send.at[place],
            part_recv.at[place],
            other_side if place < 2 else same_side,
        )

    def from_partner(place):
        ref = gathered.at[pl.ds(partner * OWN + place, 1)]
        device = other_side if place < 2 else same_side
        return remote(ref, ref, part_send.at[place], part_recv.at[place], device)

    for place in (0, 2, 1, 3):
        to_side(place).start()

    def depth(family):
        return deep if family == 0 else 1 - deep

    def hop(family, way, m, arriving, first=False):
        sign = 1 - 2 * way
        back = m // OWN + arriving
        place = lax.rem(m + 2 * way, OWN)
        ref = gathered.at[pl.ds(at_row(y - sign * back, depth(family)) * OWN + place, 1)]
        src = density_hbm.at[pl.ds(place, 1)] if first else ref
        device = (up, col) if way == 0 else (down, col)
        return remote(
            src, ref, ring_send.at[family, way, m], ring_recv.at[family, way, m], device
        )

    last = 3 * OWN + OWN // 2

    def send_own(family, m):
        for way in range(2):
            hop(family, way, m, 0, family == 0).start()

    def arrive(family, m):
        for way in range(2):
            hop(family, way, m, 1).wait_recv()

    def forward(family, m):
        for way in range(2):
            hop(family, way, m - OWN, 1).wait_recv()
            hop(family, way, m, 0).start()

    for m in range(OWN):
        send_own(0, m)
    for copy in fetches[:-1]:
        copy.wait()

    lane = lax.broadcasted_iota(jnp.int32, (8, BLOCK), 1)
    ket_table = jnp.full((8, BLOCK), PAIRS, jnp.int32)
    bra_table = jnp.full((8, BLOCK), PAIRS, jnp.int32)
    for n in range(PAIRS):
        ket_table = jnp.where(lane == ket_pairs[n], n, ket_table)
        bra_table = jnp.where(lane == owner[0, bra_pairs[n]], n, bra_table)
    slots_vmem[...] = ket_table
    places_vmem[...] = bra_table
    to_slots = pltpu.make_async_copy(slots_vmem, slots, fetch.at[len(fetches)])
    to_slots.start()
    to_places = pltpu.make_async_copy(places_vmem, places, fetch.at[len(fetches) + 1])
    to_places.start()
    there = (row, sibling)
    table_swap = remote(slots_vmem, sib_slots_vmem, sib_send.at[0], sib_recv.at[0], there)
    table_swap.start()

    for block in range(NBLK):
        lines[block, 0:3] = centers[:, block * BLOCK : (block + 1) * BLOCK]
    for side, start in ((0, row * (NBLK // 16)), (1, col * (NBLK // 32))):
        line = lines[start]
        for axis in range(3):
            wide = jnp.broadcast_to(line[axis : axis + 1], (BLOCK, BLOCK))
            columns[side, axis] = wide.T

    def tile(side, block, ref, place):
        line = lines[block]
        rows = 32
        for part in range(BLOCK // rows):
            squared = jnp.full((rows, BLOCK), SOFTEN, F32)
            for axis in range(3):
                difference = columns[side, axis, pl.ds(part * rows, rows)] - line[axis : axis + 1]
                squared = squared + difference * difference
            ref[place, pl.ds(part * rows, rows)] = kernel_value(squared).astype(BF16)

    def ket_tile(q):
        tile(1, ket_pairs[q], ket_tiles, q)

    def bra_tile(p):
        tile(0, bra_pairs[p], bra_tiles, p)

    def iota(shape, axis):
        return lax.broadcasted_iota(jnp.int32, shape, axis)

    def hot(condition):
        return jnp.where(condition, jnp.float32(1.0), jnp.float32(0.0)).astype(BF16)

    size = PAIRS * GROUP

    def count_pairs():
        long = (PAIRS, quartets.shape[3])
        bra_hot = hot((quartets[0, 0, 0:1] == iota(long, 0)) & (iota(long, 1) < count[0, 0]))
        ket_hot = hot(quartets[0, 0, 1:2] == iota(long, 0))
        return lax.dot_general(
            ket_hot, bra_hot, (((1,), (1,)), ((), ())), preferred_element_type=F32
        ).astype(BF16)

    def spread_rows(counts):
        by_slot = jnp.dot(
            counts, hot(bra_table[0:1] == iota((PAIRS, BLOCK), 0)), preferred_element_type=F32
        ).astype(BF16)
        tall = hot(iota((size, PAIRS), 0) >> SHIFT == iota((size, PAIRS), 1))
        return jnp.dot(tall, by_slot, preferred_element_type=F32).astype(BF16)

    def spread_family(rows_of, family):
        same = (iota((size, size), 0) ^ iota((size, size), 1)) & (GROUP - 1) == 0
        local_slot = iota((BLOCK, size), 1) >> SHIFT
        row_slot = (local_slot >> 2) * (OWN * DEEP) + (local_slot & (OWN - 1))
        wide = hot(row_slot + depth(family) * OWN == iota((BLOCK, size), 0))
        spread[family] = jnp.where(
            same, jnp.dot(rows_of, wide, preferred_element_type=F32), jnp.float32(0.0)
        ).astype(BF16)

    def z_row(family, yy):
        at = lax.rem(yy + 2 * RING, RING)
        for extra in range(OWN):
            s = (at * DEEP + depth(family)) * OWN + extra
            product[family, at * OWN + extra] = jnp.dot(
                bra_tiles[places[0, s]], gathered[s], preferred_element_type=F32
            )

    def w_part(family, n):
        base = pl.multiple_of(n * 2 * GROUP, 2 * GROUP)
        halves = [
            product[family, :, pl.ds(base + half * GROUP, GROUP), :]
            .reshape(size, BLOCK)
            .astype(BF16)
            for half in range(2)
        ]
        both = jnp.dot(
            spread[family], jnp.concatenate(halves, axis=1), preferred_element_type=F32
        )
        return jnp.concatenate(
            [
                both[:, half * BLOCK : (half + 1) * BLOCK].reshape(PAIRS, GROUP, BLOCK)
                for half in range(2)
            ],
            axis=1,
        )

    def swap_tiles(src, dst, first, total, index):
        return remote(
            src.at[pl.ds(first, total)],
            dst.at[pl.ds(first, total)],
            sib_send.at[index],
            sib_recv.at[index],
            there,
        )

    share = PAIRS // (2 * SIDE)
    mine = core * (PAIRS // 2) + xx * share
    bra_swap = swap_tiles(bra_tiles, bra_tiles, core * (PAIRS // 2), PAIRS // 2, 1)
    ket_swap = swap_tiles(ket_tiles, sib_tiles, 0, PAIRS, 2)

    def bra_share(step):
        tiles = bra_tiles.at[pl.ds(mine, share)]
        return remote(
            tiles,
            tiles,
            share_send.at[step - 1],
            share_recv.at[step - 1],
            (row, at_col(xx + step, zl, core)),
        )

    def bra_shared(step):
        first = core * (PAIRS // 2) + lax.rem(xx - step + SIDE, SIDE) * share
        tiles = bra_tiles.at[pl.ds(first, share)]
        return remote(
            tiles,
            tiles,
            share_send.at[step - 1],
            share_recv.at[step - 1],
            (row, at_col(xx + step, zl, core)),
        )

    def ket_run(first, total):
        @pl.loop(first, first + total)
        def _(q):
            ket_tile(q)

    def w_first(first, total):
        @pl.loop(first, first + total)
        def _(n):
            weighted[:, pl.ds(n * 2 * GROUP, 2 * GROUP)] = w_part(0, n)

    for p in range(share):
        bra_tile(mine + p)
    for step in range(1, SIDE):
        bra_share(step).start()
    for m in range(OWN):
        forward(0, OWN + m)
        if m < 2:
            for place in (m, m + 2):
                to_side(place).wait_recv()
                pass_on(place).start()
        ket_run(2 * m, 2)

    for m in range(OWN):
        forward(0, 2 * OWN + m)
        ket_run(8 + m * 3, 3)
        if m < 2:
            from_partner(m).wait_recv()
            from_partner(m + 2).wait_recv()
        send_own(1, m)
        if m == 0:
            counts = count_pairs()
        elif m == 1:
            rows_of = spread_rows(counts)
        else:
            spread_family(rows_of, m - 2)
    for m in range(2):
        forward(1, OWN + m)
        ket_run(20 + m * 6, 3)
        forward(0, 3 * OWN + m)
        if m == 0:
            for step in range(1, SIDE):
                bra_shared(step).wait_recv()
            bra_swap.start()
        ket_run(23 + m * 6, 3)
    ket_swap.start()
    bra_swap.wait()
    to_places.wait()
    fetches[-1].wait()
    forward(1, OWN + 2)
    z_row(0, y)
    z_row(0, y - 1)
    forward(1, OWN + 3)
    z_row(0, y + 1)
    z_row(0, y - 2)
    forward(1, 2 * OWN)
    z_row(0, y + 2)
    arrive(0, last - 4)
    arrive(0, last - 3)
    z_row(0, y - 3)
    forward(1, 2 * OWN + 1)
    z_row(0, y + 3)
    arrive(0, last - 2)
    arrive(0, last - 1)
    z_row(0, y + 4)
    forward(1, 2 * OWN + 2)
    w_first(0, 3)
    forward(1, 2 * OWN + 3)
    w_first(3, 2)
    forward(1, 3 * OWN)
    w_first(5, 1)
    forward(1, 3 * OWN + 1)
    w_first(6, 2)
    for away in (0, 1, -1, 2, -2):
        z_row(1, y + away)
    arrive(1, last - 4)
    arrive(1, last - 3)
    z_row(1, y - 3)
    z_row(1, y + 3)
    table_swap.wait()
    sib_to_slots = pltpu.make_async_copy(sib_slots_vmem, sib_slots, fetch.at[len(fetches) + 2])
    sib_to_slots.start()
    arrive(1, last - 2)
    arrive(1, last - 1)
    z_row(1, y + 4)

    def w_swap(part):
        return remote(
            w_own[part].at[pl.ds(0, PAIRS)],
            w_sib[part].at[pl.ds(0, PAIRS)],
            swap_send.at[part],
            swap_recv.at[part],
            there,
        )

    def w_finish(part):
        start, rows = PARTS[part]

        @pl.loop(0, rows // (2 * GROUP))
        def _(n):
            at = pl.multiple_of(n * 2 * GROUP, 2 * GROUP)
            total = w_part(1, n + start // (2 * GROUP))
            total = total + weighted[:, pl.ds(at + start, 2 * GROUP)]
            w_own[part][0:PAIRS, pl.ds(at, 2 * GROUP)] = total.astype(BF16)

        w_swap(part).start()

    def image(d, zz, jj, part):
        j = (lax.rem(xx + d, SIDE) * SIDE + zz) * 4 + core * 2 + jj
        a, b = slots[0, j], sib_slots[0, j]
        left = jnp.concatenate([w_own[part][a], w_sib[part][b]], axis=1)
        right = jnp.concatenate([ket_tiles[a], sib_tiles[b]], axis=0)
        return jnp.dot(left, right, preferred_element_type=F32)

    def relay(way, part):
        device = (row, x_up) if way == 0 else (row, x_down)
        return remote(
            x_out[part].at[2, way],
            rel_in[part].at[way],
            rel_send.at[part, way],
            rel_recv.at[part, way],
            device,
        )

    def to_x(way, jj, part):
        device = (row, x_up) if way == 0 else (row, x_down)
        return remote(
            x_out[part].at[way, jj],
            x_in[part].at[way, jj],
            x_send.at[part, way, jj],
            x_recv.at[part, way, jj],
            device,
        )

    def to_z(step, part):
        return remote(
            z_out[part].at[step - 1],
            z_in[part].at[step - 1],
            z_send.at[part, step - 1],
            z_recv.at[part, step - 1],
            (row, at_col(xx, z_at(step), core)),
        )

    def relays(part):
        for way in range(2):
            for zz in range(SIDE):
                x_out[part][2, way, zz] = image(2, zz, way, part).astype(BF16)
            relay(way, part).start()

    def direct(part):
        for way, d in ((0, 1), (1, 3)):
            for zz in range(SIDE):
                x_out[part][way, 1 - way, zz] = image(d, zz, 1 - way, part).astype(BF16)
            to_x(way, 1 - way, part).start()

    def summed(part):
        for way, d in ((0, 1), (1, 3)):
            images = [image(d, zz, way, part) for zz in range(SIDE)]
            relay(way, part).wait_recv()
            for zz in range(SIDE):
                total = images[zz] + rel_in[part][way, zz].astype(F32)
                x_out[part][way, way, zz] = total.astype(BF16)
            to_x(way, way, part).start()

    def own_sum(part):
        for jj in range(2):
            for zz in range(SIDE):
                keep[part][jj, zz] = image(0, zz, jj, part)

    def from_x(part):
        for jj in range(2):
            for way in (1 - jj, jj):
                to_x(way, jj, part).wait_recv()
                keep[part][jj] = keep[part][jj] + x_in[part][way, jj].astype(F32)
        for step in (2, 3, 1):
            for jj in range(2):
                z_out[part][step - 1, jj] = keep[part][jj, z_at(step)].astype(BF16)
            to_z(step, part).start()

    def finish(part):
        for step in (1, 3, 2):
            to_z(step, part).wait_recv()
        start, rows = PARTS[part]
        for jj in range(2):
            total = keep[part][jj, zl]
            for step in range(1, SIDE):
                total = total + z_in[part][step - 1, jj].astype(F32)
            out[start : start + rows, jj * BLOCK : (jj + 1) * BLOCK] = total

    w_finish(0)
    w_finish(1)
    to_slots.wait()
    sib_to_slots.wait()
    ket_swap.wait()
    w_swap(0).wait()
    relays(0)
    direct(0)
    w_finish(2)
    w_swap(1).wait()
    relays(1)
    summed(0)
    direct(1)
    w_swap(2).wait()
    relays(2)
    summed(1)
    direct(2)
    own_sum(0)
    from_x(0)
    summed(2)
    own_sum(1)
    own_sum(2)
    from_x(1)

    @pl.loop(0, last)
    def _(m):
        for family in range(2):
            for way in range(2):
                hop(family, way, m, 0).wait_send()

    for place in range(OWN):
        to_side(place).wait_send()
        pass_on(place).wait_send()
    for step in range(1, SIDE):
        bra_share(step).wait_send()
    from_x(2)
    finish(0)
    finish(1)
    for part in range(len(PARTS)):
        for way in range(2):
            relay(way, part).wait_send()
            for jj in range(2):
                to_x(way, jj, part).wait_send()
        for step in range(1, SIDE):
            to_z(step, part).wait_send()
    finish(2)


def local(
    basis_centers, bra_pairs, ket_pairs, quartets, quartet_counts, density_owner, density_store
):
    hbm = pl.BlockSpec(memory_space=pltpu.HBM)
    smem, i32 = pltpu.SMEM, jnp.int32
    block, count = (BLOCK, BLOCK), len(PARTS)

    def parts(lead, kind=BF16):
        return [pltpu.VMEM(lead + (rows, BLOCK), kind) for _, rows in PARTS]

    dma = pltpu.SemaphoreType.DMA
    hops = 3 * OWN + OWN // 2
    return pl.pallas_call(
        body,
        out_shape=jax.ShapeDtypeStruct((BLOCK, 2 * BLOCK), F32),
        in_specs=[hbm] * 4 + [pl.BlockSpec(memory_space=smem)] + [hbm] * 2,
        out_specs=pl.BlockSpec(memory_space=pltpu.VMEM),
        scratch_shapes=[
            pltpu.VMEM(basis_centers.shape, F32),
            smem(bra_pairs.shape, i32),
            smem(ket_pairs.shape, i32),
            pltpu.VMEM(quartets.shape, i32),
            smem(density_owner.shape, i32),
            pltpu.VMEM((8, BLOCK), i32),
            smem((8, BLOCK), i32),
            pltpu.VMEM((8, BLOCK), i32),
            smem((8, BLOCK), i32),
            pltpu.VMEM((8, BLOCK), i32),
            smem((8, BLOCK), i32),
            dma((9,)),
            pltpu.VMEM((NBLK,) + block, BF16),
            pltpu.VMEM((NBLK, 8, BLOCK), F32),
            pltpu.VMEM((2, 3) + block, F32),
            pltpu.VMEM((PAIRS + 1,) + block, BF16),
            pltpu.VMEM((PAIRS + 1,) + block, BF16),
            pltpu.VMEM((PAIRS + 1,) + block, BF16),
            pltpu.VMEM((2, PAIRS * GROUP, PAIRS * GROUP), BF16),
            pltpu.VMEM((2, PAIRS) + block, F32),
            pltpu.VMEM((PAIRS,) + block, F32),
            parts((PAIRS + 1,)),
            parts((PAIRS + 1,)),
            parts((2, SIDE), F32),
            parts((3, 2, SIDE)),
            parts((2, SIDE)),
            parts((2, 2, SIDE)),
            parts((3, 2)),
            parts((3, 2)),
            pltpu.VMEM((OWN,) + block, BF16),
            dma((OWN,)),
            dma((OWN,)),
            dma((OWN,)),
            dma((OWN,)),
            dma((2, 2, hops)),
            dma((2, 2, hops)),
            dma((3,)),
            dma((3,)),
            dma((count,)),
            dma((count,)),
            dma((SIDE - 1,)),
            dma((SIDE - 1,)),
            dma((count, 2)),
            dma((count, 2)),
            dma((count, 2, 2)),
            dma((count, 2, 2)),
            dma((count, 3)),
            dma((count, 3)),
        ],
        compiler_params=pltpu.CompilerParams(
            collective_id=0, has_side_effects=True, vmem_limit_bytes=56 * 2**20
        ),
        cost_estimate=pl.CostEstimate(
            flops=2 * 10**9, bytes_accessed=4 * 2**20, transcendentals=4 * 10**6
        ),
    )(
        basis_centers,
        bra_pairs,
        ket_pairs,
        quartets,
        quartet_counts,
        density_owner,
        density_store,
    ).astype(BF16)


def solution(mesh):
    return jax.shard_map(
        local,
        mesh=mesh,
        in_specs=(
            P(),
            P("bra"),
            P("ket"),
            P("bra", "ket", None, None),
            P("bra", "ket"),
            P("ket", None),
            P("bra", "ket", None),
        ),
        out_specs=P("bra", "ket"),
        check_vma=False,
    )
```

```python
import jax
import jax.numpy as jnp
from jax import lax
from jax.experimental import pallas as pl
from jax.experimental.pallas import tpu as pltpu
from jax.sharding import PartitionSpec as P

OMEGA = 0.11
SOFTEN = 0.25
BLOCK = 128
NBLK = 64
PAIRS = 32
RING = 8
DEEP = 2
SIDE = 4
OWN = 4
PARTS = ((0, 32), (32, 32), (64, 32), (96, 32))
ALONG_Z = 1
GROUP = 8
SHIFT = 3
MESH = pl.DeviceIdType.MESH
F32 = jnp.float32
BF16 = jnp.bfloat16

SLOPE = 0.6 * OMEGA
DECAY = -OMEGA * OMEGA * 1.4426950408889634
ERFC = (
    0.33856715,
    0.33711259,
    0.29264139,
    0.06933287,
    0.29272546,
    -0.65555156,
    0.41918066,
    -0.09400974,
)


def kernel_value(squared):
    inverse = lax.rsqrt(squared)
    divisor = 1.0 + SLOPE * (squared * inverse)
    t = pl.reciprocal(divisor, approx=True)
    t = t * (2.0 - divisor * t)
    poly = ERFC[-1] * t + ERFC[-2]
    for c in ERFC[-3::-1]:
        poly = poly * t + c
    return jnp.exp2(DECAY * squared) * (t * inverse) * poly


def body(
    centers_hbm,
    bra_hbm,
    ket_hbm,
    quartets_hbm,
    count,
    owner_hbm,
    density_hbm,
    out,
    centers,
    bra_pairs,
    ket_pairs,
    quartets,
    owner,
    slots_vmem,
    slots,
    sib_slots_vmem,
    sib_slots,
    places_vmem,
    places,
    fetch,
    gathered,
    lines,
    columns,
    bra_tiles,
    ket_tiles,
    sib_tiles,
    spread,
    product,
    weighted,
    w_own,
    w_sib,
    keep,
    x_out,
    rel_in,
    x_in,
    z_out,
    z_in,
    zf_out,
    zf_in,
    zf_keep,
    xf_out,
    xf_in,
    passing,
    side_send,
    side_recv,
    part_send,
    part_recv,
    ring_send,
    ring_recv,
    sib_send,
    sib_recv,
    swap_send,
    swap_recv,
    share_send,
    share_recv,
    rel_send,
    rel_recv,
    x_send,
    x_recv,
    z_send,
    z_recv,
    zf_send,
    zf_recv,
    xf_send,
    xf_recv,
):
    row = lax.axis_index("bra")
    col = lax.axis_index("ket")
    y, deep = row // DEEP, row % DEEP
    core = col % 2
    zl = (col // 2) % SIDE
    xx = col // (2 * SIDE)

    def at_row(yy, dd):
        return lax.rem(yy + 2 * RING, RING) * DEEP + dd

    def at_col(x_at, z_at, core_at):
        return (lax.rem(x_at + SIDE, SIDE) * SIDE + z_at) * 2 + core_at

    up, down = at_row(y + 1, deep), at_row(y - 1, deep)
    partner = at_row(y, 1 - deep)
    sibling = at_col(xx, zl, 1 - core)
    x_up, x_down = at_col(xx + 1, zl, core), at_col(xx - 1, zl, core)

    def z_at(step):
        return lax.rem(zl + step, SIDE)

    same_side = (row, at_col(xx, z_at(2), core))
    other_side = (partner, at_col(xx, z_at(2), core))
    peers = [(up, col), (down, col), other_side, (row, sibling), (row, x_up), (row, x_down)]
    peers += [(row, at_col(xx, z_at(step), core)) for step in range(1, SIDE)]
    peers += [(row, at_col(xx + 2, zl, core))]
    barrier = pltpu.get_barrier_semaphore()
    for peer in peers:
        pl.semaphore_signal(barrier, inc=1, device_id=peer, device_id_type=MESH)
    own_slots = gathered.at[pl.ds(row * OWN, OWN)]
    sources = (ket_hbm, bra_hbm, centers_hbm, owner_hbm, quartets_hbm, density_hbm)
    targets = (ket_pairs, bra_pairs, centers, owner, quartets, own_slots)
    fetches = [
        pltpu.make_async_copy(src, dst, fetch.at[n])
        for n, (src, dst) in enumerate(zip(sources, targets))
    ]
    for copy in fetches:
        copy.start()
    for tiles in (bra_tiles, ket_tiles, sib_tiles):
        tiles[PAIRS] = jnp.zeros((BLOCK, BLOCK), BF16)
    for part, (_, rows) in enumerate(PARTS):
        w_own[part][PAIRS] = jnp.zeros((rows, BLOCK), BF16)
        w_sib[part][PAIRS] = jnp.zeros((rows, BLOCK), BF16)
    pl.semaphore_wait(barrier, len(peers))

    def remote(src, dst, send, recv, device):
        return pltpu.make_async_remote_copy(
            src_ref=src,
            dst_ref=dst,
            send_sem=send,
            recv_sem=recv,
            device_id=device,
            device_id_type=MESH,
        )

    def to_side(place):
        return remote(
            density_hbm.at[pl.ds(place, 1)],
            passing.at[pl.ds(place, 1)],
            side_send.at[place],
            side_recv.at[place],
            same_side if place < 2 else other_side,
        )

    def pass_on(place):
        origin = row if place < 2 else partner
        return remote(
            passing.at[pl.ds(place, 1)],
            gathered.at[pl.ds(origin * OWN + place, 1)],
            part_send.at[place],
            part_recv.at[place],
            other_side if place < 2 else same_side,
        )

    def from_partner(place):
        ref = gathered.at[pl.ds(partner * OWN + place, 1)]
        device = other_side if place < 2 else same_side
        return remote(ref, ref, part_send.at[place], part_recv.at[place], device)

    for place in (0, 2, 1, 3):
        to_side(place).start()

    def depth(family):
        return deep if family == 0 else 1 - deep

    def hop(family, way, m, arriving, first=False):
        sign = 1 - 2 * way
        back = m // OWN + arriving
        place = lax.rem(m + 2 * way, OWN)
        ref = gathered.at[pl.ds(at_row(y - sign * back, depth(family)) * OWN + place, 1)]
        src = density_hbm.at[pl.ds(place, 1)] if first else ref
        device = (up, col) if way == 0 else (down, col)
        return remote(
            src, ref, ring_send.at[family, way, m], ring_recv.at[family, way, m], device
        )

    last = 3 * OWN + OWN // 2

    def send_own(family, m):
        for way in range(2):
            hop(family, way, m, 0, family == 0).start()

    def arrive(family, m):
        for way in range(2):
            hop(family, way, m, 1).wait_recv()

    def forward(family, m):
        for way in range(2):
            hop(family, way, m - OWN, 1).wait_recv()
            hop(family, way, m, 0).start()

    for m in range(OWN):
        send_own(0, m)
    for copy in fetches[:-1]:
        copy.wait()

    lane = lax.broadcasted_iota(jnp.int32, (8, BLOCK), 1)
    ket_table = jnp.full((8, BLOCK), PAIRS, jnp.int32)
    bra_table = jnp.full((8, BLOCK), PAIRS, jnp.int32)
    for n in range(PAIRS):
        ket_table = jnp.where(lane == ket_pairs[n], n, ket_table)
        bra_table = jnp.where(lane == owner[0, bra_pairs[n]], n, bra_table)
    slots_vmem[...] = ket_table
    places_vmem[...] = bra_table
    to_slots = pltpu.make_async_copy(slots_vmem, slots, fetch.at[len(fetches)])
    to_slots.start()
    to_places = pltpu.make_async_copy(places_vmem, places, fetch.at[len(fetches) + 1])
    to_places.start()
    there = (row, sibling)
    table_swap = remote(slots_vmem, sib_slots_vmem, sib_send.at[0], sib_recv.at[0], there)
    table_swap.start()

    for block in range(NBLK):
        lines[block, 0:3] = centers[:, block * BLOCK : (block + 1) * BLOCK]
    for side, start in ((0, row * (NBLK // 16)), (1, col * (NBLK // 32))):
        line = lines[start]
        for axis in range(3):
            wide = jnp.broadcast_to(line[axis : axis + 1], (BLOCK, BLOCK))
            columns[side, axis] = wide.T

    def tile(side, block, ref, place):
        line = lines[block]
        rows = 32
        for part in range(BLOCK // rows):
            squared = jnp.full((rows, BLOCK), SOFTEN, F32)
            for axis in range(3):
                difference = columns[side, axis, pl.ds(part * rows, rows)] - line[axis : axis + 1]
                squared = squared + difference * difference
            ref[place, pl.ds(part * rows, rows)] = kernel_value(squared).astype(BF16)

    def ket_tile(q):
        tile(1, ket_pairs[q], ket_tiles, q)

    def bra_tile(p):
        tile(0, bra_pairs[p], bra_tiles, p)

    def iota(shape, axis):
        return lax.broadcasted_iota(jnp.int32, shape, axis)

    def hot(condition):
        return jnp.where(condition, jnp.float32(1.0), jnp.float32(0.0)).astype(BF16)

    size = PAIRS * GROUP

    def count_pairs():
        long = (PAIRS, quartets.shape[3])
        bra_hot = hot((quartets[0, 0, 0:1] == iota(long, 0)) & (iota(long, 1) < count[0, 0]))
        ket_hot = hot(quartets[0, 0, 1:2] == iota(long, 0))
        return lax.dot_general(
            ket_hot, bra_hot, (((1,), (1,)), ((), ())), preferred_element_type=F32
        ).astype(BF16)

    def spread_rows(counts):
        by_slot = jnp.dot(
            counts, hot(bra_table[0:1] == iota((PAIRS, BLOCK), 0)), preferred_element_type=F32
        ).astype(BF16)
        tall = hot(iota((size, PAIRS), 0) >> SHIFT == iota((size, PAIRS), 1))
        return jnp.dot(tall, by_slot, preferred_element_type=F32).astype(BF16)

    def spread_family(rows_of, family):
        same = (iota((size, size), 0) ^ iota((size, size), 1)) & (GROUP - 1) == 0
        local_slot = iota((BLOCK, size), 1) >> SHIFT
        row_slot = (local_slot >> 2) * (OWN * DEEP) + (local_slot & (OWN - 1))
        wide = hot(row_slot + depth(family) * OWN == iota((BLOCK, size), 0))
        spread[family] = jnp.where(
            same, jnp.dot(rows_of, wide, preferred_element_type=F32), jnp.float32(0.0)
        ).astype(BF16)

    def z_row(family, yy):
        at = lax.rem(yy + 2 * RING, RING)
        for extra in range(OWN):
            s = (at * DEEP + depth(family)) * OWN + extra
            product[family, at * OWN + extra] = jnp.dot(
                bra_tiles[places[0, s]], gathered[s], preferred_element_type=F32
            )

    def w_part(family, n):
        base = pl.multiple_of(n * 2 * GROUP, 2 * GROUP)
        halves = [
            product[family, :, pl.ds(base + half * GROUP, GROUP), :]
            .reshape(size, BLOCK)
            .astype(BF16)
            for half in range(2)
        ]
        both = jnp.dot(
            spread[family], jnp.concatenate(halves, axis=1), preferred_element_type=F32
        )
        return jnp.concatenate(
            [
                both[:, half * BLOCK : (half + 1) * BLOCK].reshape(PAIRS, GROUP, BLOCK)
                for half in range(2)
            ],
            axis=1,
        )

    def swap_tiles(src, dst, first, total, index):
        return remote(
            src.at[pl.ds(first, total)],
            dst.at[pl.ds(first, total)],
            sib_send.at[index],
            sib_recv.at[index],
            there,
        )

    share = PAIRS // (2 * SIDE)
    mine = core * (PAIRS // 2) + xx * share
    bra_swap = swap_tiles(bra_tiles, bra_tiles, core * (PAIRS // 2), PAIRS // 2, 1)
    ket_swap = swap_tiles(ket_tiles, sib_tiles, 0, PAIRS, 2)

    def bra_share(step):
        tiles = bra_tiles.at[pl.ds(mine, share)]
        return remote(
            tiles,
            tiles,
            share_send.at[step - 1],
            share_recv.at[step - 1],
            (row, at_col(xx + step, zl, core)),
        )

    def bra_shared(step):
        first = core * (PAIRS // 2) + lax.rem(xx - step + SIDE, SIDE) * share
        tiles = bra_tiles.at[pl.ds(first, share)]
        return remote(
            tiles,
            tiles,
            share_send.at[step - 1],
            share_recv.at[step - 1],
            (row, at_col(xx + step, zl, core)),
        )

    def ket_run(first, total):
        @pl.loop(first, first + total)
        def _(q):
            ket_tile(q)

    def w_first(first, total):
        @pl.loop(first, first + total)
        def _(n):
            weighted[:, pl.ds(n * 2 * GROUP, 2 * GROUP)] = w_part(0, n)

    for p in range(share):
        bra_tile(mine + p)
    for step in range(1, SIDE):
        bra_share(step).start()
    for m in range(OWN):
        forward(0, OWN + m)
        if m < 2:
            for place in (m, m + 2):
                to_side(place).wait_recv()
                pass_on(place).start()
        ket_run(2 * m, 2)

    for m in range(OWN):
        forward(0, 2 * OWN + m)
        ket_run(8 + m * 3, 3)
        if m < 2:
            from_partner(m).wait_recv()
            from_partner(m + 2).wait_recv()
        send_own(1, m)
        if m == 0:
            counts = count_pairs()
        elif m == 1:
            rows_of = spread_rows(counts)
        else:
            spread_family(rows_of, m - 2)
    for m in range(2):
        forward(1, OWN + m)
        ket_run(20 + m * 6, 3)
        forward(0, 3 * OWN + m)
        if m == 0:
            for step in range(1, SIDE):
                bra_shared(step).wait_recv()
            bra_swap.start()
        ket_run(23 + m * 6, 3)
    ket_swap.start()
    bra_swap.wait()
    to_places.wait()
    fetches[-1].wait()
    forward(1, OWN + 2)
    z_row(0, y)
    z_row(0, y - 1)
    forward(1, OWN + 3)
    z_row(0, y + 1)
    z_row(0, y - 2)
    forward(1, 2 * OWN)
    z_row(0, y + 2)
    arrive(0, last - 4)
    arrive(0, last - 3)
    z_row(0, y - 3)
    forward(1, 2 * OWN + 1)
    z_row(0, y + 3)
    arrive(0, last - 2)
    arrive(0, last - 1)
    z_row(0, y + 4)
    forward(1, 2 * OWN + 2)
    w_first(0, 3)
    forward(1, 2 * OWN + 3)
    w_first(3, 2)
    forward(1, 3 * OWN)
    w_first(5, 1)
    forward(1, 3 * OWN + 1)
    w_first(6, 2)
    for away in (0, 1, -1, 2, -2):
        z_row(1, y + away)
    arrive(1, last - 4)
    arrive(1, last - 3)
    z_row(1, y - 3)
    z_row(1, y + 3)
    table_swap.wait()
    sib_to_slots = pltpu.make_async_copy(sib_slots_vmem, sib_slots, fetch.at[len(fetches) + 2])
    sib_to_slots.start()
    arrive(1, last - 2)
    arrive(1, last - 1)
    z_row(1, y + 4)

    def w_swap(part):
        return remote(
            w_own[part].at[pl.ds(0, PAIRS)],
            w_sib[part].at[pl.ds(0, PAIRS)],
            swap_send.at[part],
            swap_recv.at[part],
            there,
        )

    def w_finish(part):
        start, rows = PARTS[part]

        @pl.loop(0, rows // (2 * GROUP))
        def _(n):
            at = pl.multiple_of(n * 2 * GROUP, 2 * GROUP)
            total = w_part(1, n + start // (2 * GROUP))
            total = total + weighted[:, pl.ds(at + start, 2 * GROUP)]
            w_own[part][0:PAIRS, pl.ds(at, 2 * GROUP)] = total.astype(BF16)

        w_swap(part).start()

    def image(d, zz, jj, part):
        j = (lax.rem(xx + d, SIDE) * SIDE + zz) * 4 + core * 2 + jj
        a, b = slots[0, j], sib_slots[0, j]
        left = jnp.concatenate([w_own[part][a], w_sib[part][b]], axis=1)
        right = jnp.concatenate([ket_tiles[a], sib_tiles[b]], axis=0)
        return jnp.dot(left, right, preferred_element_type=F32)

    def relay(way, part):
        device = (row, x_up) if way == 0 else (row, x_down)
        return remote(
            x_out[part].at[2, way],
            rel_in[part].at[way],
            rel_send.at[part, way],
            rel_recv.at[part, way],
            device,
        )

    def to_x(way, jj, part):
        device = (row, x_up) if way == 0 else (row, x_down)
        return remote(
            x_out[part].at[way, jj],
            x_in[part].at[way, jj],
            x_send.at[part, way, jj],
            x_recv.at[part, way, jj],
            device,
        )

    def to_z(step, part):
        return remote(
            z_out[part].at[step - 1],
            z_in[part].at[step - 1],
            z_send.at[part, step - 1],
            z_recv.at[part, step - 1],
            (row, at_col(xx, z_at(step), core)),
        )

    def relays(part):
        for way in range(2):
            for zz in range(SIDE):
                x_out[part][2, way, zz] = image(2, zz, way, part).astype(BF16)
            relay(way, part).start()

    def direct(part):
        for way, d in ((0, 1), (1, 3)):
            for zz in range(SIDE):
                x_out[part][way, 1 - way, zz] = image(d, zz, 1 - way, part).astype(BF16)
            to_x(way, 1 - way, part).start()

    def summed(part):
        for way, d in ((0, 1), (1, 3)):
            images = [image(d, zz, way, part) for zz in range(SIDE)]
            relay(way, part).wait_recv()
            for zz in range(SIDE):
                total = images[zz] + rel_in[part][way, zz].astype(F32)
                x_out[part][way, way, zz] = total.astype(BF16)
            to_x(way, way, part).start()

    def own_sum(part):
        for jj in range(2):
            for zz in range(SIDE):
                keep[part][jj, zz] = image(0, zz, jj, part)

    def from_x(part):
        for jj in range(2):
            for way in (1 - jj, jj):
                to_x(way, jj, part).wait_recv()
                keep[part][jj] = keep[part][jj] + x_in[part][way, jj].astype(F32)
        for step in (2, 3, 1):
            for jj in range(2):
                z_out[part][step - 1, jj] = keep[part][jj, z_at(step)].astype(BF16)
            to_z(step, part).start()

    def finish(part):
        for step in (1, 3, 2):
            to_z(step, part).wait_recv()
        start, rows = PARTS[part]
        for jj in range(2):
            total = keep[part][jj, zl]
            for step in range(1, SIDE):
                total = total + z_in[part][step - 1, jj].astype(F32)
            out[start : start + rows, jj * BLOCK : (jj + 1) * BLOCK] = total.astype(BF16)

    def z_first(step):
        return remote(
            zf_out.at[step - 1],
            zf_in.at[step - 1],
            zf_send.at[step - 1],
            zf_recv.at[step - 1],
            (row, at_col(xx, z_at(step), core)),
        )

    def x_last(d):
        return remote(
            xf_out.at[d - 1],
            xf_in.at[d - 1],
            xf_send.at[d - 1],
            xf_recv.at[d - 1],
            (row, at_col(xx + d, zl, core)),
        )

    def z_first_images():
        for step in (2, 3, 1):
            for d in range(SIDE):
                for jj in range(2):
                    zf_out[step - 1, d, jj] = image(d, z_at(step), jj, ALONG_Z).astype(BF16)
            z_first(step).start()

    def z_first_own():
        for d in range(SIDE):
            for jj in range(2):
                zf_keep[d, jj] = image(d, zl, jj, ALONG_Z)

    def z_first_sum():
        for step in (1, 3, 2):
            z_first(step).wait_recv()
        for d in (2, 1, 3, 0):
            total = zf_keep[d]
            for step in range(1, SIDE):
                total = total + zf_in[step - 1, d].astype(F32)
            if d:
                xf_out[d - 1] = total.astype(BF16)
                x_last(d).start()
            else:
                zf_keep[0] = total

    def z_first_finish():
        for d in range(1, SIDE):
            x_last(d).wait_recv()
        start, rows = PARTS[ALONG_Z]
        for jj in range(2):
            total = zf_keep[0, jj]
            for d in range(1, SIDE):
                total = total + xf_in[d - 1, jj].astype(F32)
            out[start : start + rows, jj * BLOCK : (jj + 1) * BLOCK] = total.astype(BF16)

    w_finish(0)
    w_finish(1)
    to_slots.wait()
    sib_to_slots.wait()
    ket_swap.wait()
    w_swap(0).wait()
    relays(0)
    direct(0)
    w_finish(2)
    w_swap(1).wait()
    z_first_images()
    w_finish(3)
    w_swap(2).wait()
    relays(2)
    summed(0)
    direct(2)
    w_swap(3).wait()
    relays(3)
    summed(2)
    direct(3)
    own_sum(0)
    from_x(0)
    summed(3)
    own_sum(2)
    own_sum(3)
    z_first_own()
    from_x(2)

    @pl.loop(0, last)
    def _(m):
        for family in range(2):
            for way in range(2):
                hop(family, way, m, 0).wait_send()

    for place in range(OWN):
        to_side(place).wait_send()
        pass_on(place).wait_send()
    for step in range(1, SIDE):
        bra_share(step).wait_send()
    from_x(3)
    z_first_sum()
    finish(0)
    finish(2)
    for part in (0, 2, 3):
        for way in range(2):
            relay(way, part).wait_send()
            for jj in range(2):
                to_x(way, jj, part).wait_send()
        for step in range(1, SIDE):
            to_z(step, part).wait_send()
    for step in range(1, SIDE):
        z_first(step).wait_send()
        x_last(step).wait_send()
    finish(3)
    z_first_finish()


def local(
    basis_centers, bra_pairs, ket_pairs, quartets, quartet_counts, density_owner, density_store
):
    hbm = pl.BlockSpec(memory_space=pltpu.HBM)
    smem, i32 = pltpu.SMEM, jnp.int32
    block, count = (BLOCK, BLOCK), len(PARTS)
    quarter = (PARTS[ALONG_Z][1], BLOCK)

    def parts(lead, kind=BF16):
        return [pltpu.VMEM(lead + (rows, BLOCK), kind) for _, rows in PARTS]

    dma = pltpu.SemaphoreType.DMA
    hops = 3 * OWN + OWN // 2
    return pl.pallas_call(
        body,
        out_shape=jax.ShapeDtypeStruct((BLOCK, 2 * BLOCK), BF16),
        in_specs=[hbm] * 4 + [pl.BlockSpec(memory_space=smem)] + [hbm] * 2,
        out_specs=pl.BlockSpec(memory_space=pltpu.VMEM),
        scratch_shapes=[
            pltpu.VMEM(basis_centers.shape, F32),
            smem(bra_pairs.shape, i32),
            smem(ket_pairs.shape, i32),
            pltpu.VMEM(quartets.shape, i32),
            smem(density_owner.shape, i32),
            pltpu.VMEM((8, BLOCK), i32),
            smem((8, BLOCK), i32),
            pltpu.VMEM((8, BLOCK), i32),
            smem((8, BLOCK), i32),
            pltpu.VMEM((8, BLOCK), i32),
            smem((8, BLOCK), i32),
            dma((9,)),
            pltpu.VMEM((NBLK,) + block, BF16),
            pltpu.VMEM((NBLK, 8, BLOCK), F32),
            pltpu.VMEM((2, 3) + block, F32),
            pltpu.VMEM((PAIRS + 1,) + block, BF16),
            pltpu.VMEM((PAIRS + 1,) + block, BF16),
            pltpu.VMEM((PAIRS + 1,) + block, BF16),
            pltpu.VMEM((2, PAIRS * GROUP, PAIRS * GROUP), BF16),
            pltpu.VMEM((2, PAIRS) + block, F32),
            pltpu.VMEM((PAIRS,) + block, F32),
            parts((PAIRS + 1,)),
            parts((PAIRS + 1,)),
            parts((2, SIDE), F32),
            parts((3, 2, SIDE)),
            parts((2, SIDE)),
            parts((2, 2, SIDE)),
            parts((3, 2)),
            parts((3, 2)),
            pltpu.VMEM((3, SIDE, 2) + quarter, BF16),
            pltpu.VMEM((3, SIDE, 2) + quarter, BF16),
            pltpu.VMEM((SIDE, 2) + quarter, F32),
            pltpu.VMEM((3, 2) + quarter, BF16),
            pltpu.VMEM((3, 2) + quarter, BF16),
            pltpu.VMEM((OWN,) + block, BF16),
            dma((OWN,)),
            dma((OWN,)),
            dma((OWN,)),
            dma((OWN,)),
            dma((2, 2, hops)),
            dma((2, 2, hops)),
            dma((3,)),
            dma((3,)),
            dma((count,)),
            dma((count,)),
            dma((SIDE - 1,)),
            dma((SIDE - 1,)),
            dma((count, 2)),
            dma((count, 2)),
            dma((count, 2, 2)),
            dma((count, 2, 2)),
            dma((count, 3)),
            dma((count, 3)),
            dma((3,)),
            dma((3,)),
            dma((3,)),
            dma((3,)),
        ],
        compiler_params=pltpu.CompilerParams(
            collective_id=0, has_side_effects=True, vmem_limit_bytes=56 * 2**20
        ),
        cost_estimate=pl.CostEstimate(
            flops=2 * 10**9, bytes_accessed=4 * 2**20, transcendentals=4 * 10**6
        ),
    )(
        basis_centers,
        bra_pairs,
        ket_pairs,
        quartets,
        quartet_counts,
        density_owner,
        density_store,
    )


def solution(mesh):
    return jax.shard_map(
        local,
        mesh=mesh,
        in_specs=(
            P(),
            P("bra"),
            P("ket"),
            P("bra", "ket", None, None),
            P("bra", "ket"),
            P("ket", None),
            P("bra", "ket", None),
        ),
        out_specs=P("bra", "ket"),
        check_vma=False,
    )
```

```python
import jax
import jax.numpy as jnp
from jax import lax
from jax.experimental import pallas as pl
from jax.experimental.pallas import tpu as pltpu
from jax.sharding import PartitionSpec as P

OMEGA = 0.11
SOFTEN = 0.25
BLOCK = 128
NBLK = 64
PAIRS = 32
RING = 8
DEEP = 2
SIDE = 4
OWN = 4
PARTS = ((0, 32), (32, 32), (64, 32), (96, 32))
ALONG_Z = 1
GROUP = 8
SHIFT = 3
MESH = pl.DeviceIdType.MESH
F32 = jnp.float32
BF16 = jnp.bfloat16

SLOPE = 0.6 * OMEGA
DECAY = -OMEGA * OMEGA * 1.4426950408889634
ERFC = (
    0.33856715,
    0.33711259,
    0.29264139,
    0.06933287,
    0.29272546,
    -0.65555156,
    0.41918066,
    -0.09400974,
)


def kernel_value(squared):
    inverse = lax.rsqrt(squared)
    divisor = 1.0 + SLOPE * (squared * inverse)
    t = pl.reciprocal(divisor, approx=True)
    t = t * (2.0 - divisor * t)
    poly = ERFC[-1] * t + ERFC[-2]
    for c in ERFC[-3::-1]:
        poly = poly * t + c
    return jnp.exp2(DECAY * squared) * (t * inverse) * poly


def body(
    centers_hbm,
    bra_hbm,
    ket_hbm,
    quartets_hbm,
    count,
    owner_hbm,
    density_hbm,
    out,
    centers,
    bra_pairs,
    ket_pairs,
    quartets,
    owner,
    slots_vmem,
    slots,
    sib_slots_vmem,
    sib_slots,
    places_vmem,
    places,
    fetch,
    gathered,
    lines,
    columns,
    bra_tiles,
    ket_tiles,
    sib_tiles,
    spread,
    product,
    weighted,
    w_own,
    w_sib,
    keep,
    x_out,
    rel_in,
    x_in,
    z_out,
    z_in,
    zf_out,
    zf_in,
    zf_keep,
    xf_out,
    xf_in,
    passing,
    side_send,
    side_recv,
    part_send,
    part_recv,
    ring_send,
    ring_recv,
    sib_send,
    sib_recv,
    swap_send,
    swap_recv,
    share_send,
    share_recv,
    rel_send,
    rel_recv,
    x_send,
    x_recv,
    z_send,
    z_recv,
    zf_send,
    zf_recv,
    xf_send,
    xf_recv,
):
    row = lax.axis_index("bra")
    col = lax.axis_index("ket")
    y, deep = row // DEEP, row % DEEP
    core = col % 2
    zl = (col // 2) % SIDE
    xx = col // (2 * SIDE)

    def at_row(yy, dd):
        return lax.rem(yy + 2 * RING, RING) * DEEP + dd

    def at_col(x_at, z_at, core_at):
        return (lax.rem(x_at + SIDE, SIDE) * SIDE + z_at) * 2 + core_at

    up, down = at_row(y + 1, deep), at_row(y - 1, deep)
    partner = at_row(y, 1 - deep)
    sibling = at_col(xx, zl, 1 - core)
    x_up, x_down = at_col(xx + 1, zl, core), at_col(xx - 1, zl, core)

    def z_at(step):
        return lax.rem(zl + step, SIDE)

    same_side = (row, at_col(xx, z_at(2), core))
    other_side = (partner, at_col(xx, z_at(2), core))
    peers = [(up, col), (down, col), other_side, (row, sibling), (row, x_up), (row, x_down)]
    peers += [(row, at_col(xx, z_at(step), core)) for step in range(1, SIDE)]
    peers += [(row, at_col(xx + 2, zl, core))]
    barrier = pltpu.get_barrier_semaphore()
    for peer in peers:
        pl.semaphore_signal(barrier, inc=1, device_id=peer, device_id_type=MESH)
    own_slots = gathered.at[pl.ds(row * OWN, OWN)]
    sources = (ket_hbm, bra_hbm, centers_hbm, owner_hbm, quartets_hbm, density_hbm)
    targets = (ket_pairs, bra_pairs, centers, owner, quartets, own_slots)
    fetches = [
        pltpu.make_async_copy(src, dst, fetch.at[n])
        for n, (src, dst) in enumerate(zip(sources, targets))
    ]
    for copy in fetches:
        copy.start()
    for tiles in (bra_tiles, ket_tiles, sib_tiles):
        tiles[PAIRS] = jnp.zeros((BLOCK, BLOCK), BF16)
    for part, (_, rows) in enumerate(PARTS):
        w_own[part][PAIRS] = jnp.zeros((rows, BLOCK), BF16)
        w_sib[part][PAIRS] = jnp.zeros((rows, BLOCK), BF16)
    pl.semaphore_wait(barrier, len(peers))

    def remote(src, dst, send, recv, device):
        return pltpu.make_async_remote_copy(
            src_ref=src,
            dst_ref=dst,
            send_sem=send,
            recv_sem=recv,
            device_id=device,
            device_id_type=MESH,
        )

    def to_side(place):
        return remote(
            density_hbm.at[pl.ds(place, 1)],
            passing.at[pl.ds(place, 1)],
            side_send.at[place],
            side_recv.at[place],
            same_side if place < 2 else other_side,
        )

    def pass_on(place):
        origin = row if place < 2 else partner
        return remote(
            passing.at[pl.ds(place, 1)],
            gathered.at[pl.ds(origin * OWN + place, 1)],
            part_send.at[place],
            part_recv.at[place],
            other_side if place < 2 else same_side,
        )

    def from_partner(place):
        ref = gathered.at[pl.ds(partner * OWN + place, 1)]
        device = other_side if place < 2 else same_side
        return remote(ref, ref, part_send.at[place], part_recv.at[place], device)

    for place in (0, 2, 1, 3):
        to_side(place).start()

    def depth(family):
        return deep if family == 0 else 1 - deep

    def hop(family, way, m, arriving, first=False):
        sign = 1 - 2 * way
        back = m // OWN + arriving
        place = lax.rem(m + 2 * way, OWN)
        ref = gathered.at[pl.ds(at_row(y - sign * back, depth(family)) * OWN + place, 1)]
        src = density_hbm.at[pl.ds(place, 1)] if first else ref
        device = (up, col) if way == 0 else (down, col)
        return remote(
            src, ref, ring_send.at[family, way, m], ring_recv.at[family, way, m], device
        )

    last = 3 * OWN + OWN // 2

    def send_own(family, m):
        for way in range(2):
            hop(family, way, m, 0, family == 0).start()

    def arrive(family, m):
        for way in range(2):
            hop(family, way, m, 1).wait_recv()

    def forward(family, m):
        for way in range(2):
            hop(family, way, m - OWN, 1).wait_recv()
            hop(family, way, m, 0).start()

    for m in range(OWN):
        send_own(0, m)
    for copy in fetches[:-1]:
        copy.wait()

    lane = lax.broadcasted_iota(jnp.int32, (8, BLOCK), 1)
    ket_table = jnp.full((8, BLOCK), PAIRS, jnp.int32)
    bra_table = jnp.full((8, BLOCK), PAIRS, jnp.int32)
    for n in range(PAIRS):
        ket_table = jnp.where(lane == ket_pairs[n], n, ket_table)
        bra_table = jnp.where(lane == owner[0, bra_pairs[n]], n, bra_table)
    slots_vmem[...] = ket_table
    places_vmem[...] = bra_table
    to_slots = pltpu.make_async_copy(slots_vmem, slots, fetch.at[len(fetches)])
    to_slots.start()
    to_places = pltpu.make_async_copy(places_vmem, places, fetch.at[len(fetches) + 1])
    to_places.start()
    there = (row, sibling)
    table_swap = remote(slots_vmem, sib_slots_vmem, sib_send.at[0], sib_recv.at[0], there)
    table_swap.start()

    for block in range(NBLK):
        lines[block, 0:3] = centers[:, block * BLOCK : (block + 1) * BLOCK]
    for side, start in ((0, row * (NBLK // 16)), (1, col * (NBLK // 32))):
        line = lines[start]
        for axis in range(3):
            wide = jnp.broadcast_to(line[axis : axis + 1], (BLOCK, BLOCK))
            columns[side, axis] = wide.T

    def tile(side, block, ref, place):
        line = lines[block]
        rows = 32
        for part in range(BLOCK // rows):
            squared = jnp.full((rows, BLOCK), SOFTEN, F32)
            for axis in range(3):
                difference = columns[side, axis, pl.ds(part * rows, rows)] - line[axis : axis + 1]
                squared = squared + difference * difference
            ref[place, pl.ds(part * rows, rows)] = kernel_value(squared).astype(BF16)

    def ket_tile(q):
        tile(1, ket_pairs[q], ket_tiles, q)

    def bra_tile(p):
        tile(0, bra_pairs[p], bra_tiles, p)

    def iota(shape, axis):
        return lax.broadcasted_iota(jnp.int32, shape, axis)

    def hot(condition):
        return jnp.where(condition, jnp.float32(1.0), jnp.float32(0.0)).astype(BF16)

    size = PAIRS * GROUP

    def count_pairs():
        long = (PAIRS, quartets.shape[3])
        bra_hot = hot((quartets[0, 0, 0:1] == iota(long, 0)) & (iota(long, 1) < count[0, 0]))
        ket_hot = hot(quartets[0, 0, 1:2] == iota(long, 0))
        return lax.dot_general(
            ket_hot, bra_hot, (((1,), (1,)), ((), ())), preferred_element_type=F32
        ).astype(BF16)

    def spread_rows(counts):
        by_slot = jnp.dot(
            counts, hot(bra_table[0:1] == iota((PAIRS, BLOCK), 0)), preferred_element_type=F32
        ).astype(BF16)
        tall = hot(iota((size, PAIRS), 0) >> SHIFT == iota((size, PAIRS), 1))
        return jnp.dot(tall, by_slot, preferred_element_type=F32).astype(BF16)

    def spread_family(rows_of, family):
        same = (iota((size, size), 0) ^ iota((size, size), 1)) & (GROUP - 1) == 0
        local_slot = iota((BLOCK, size), 1) >> SHIFT
        row_slot = (local_slot >> 2) * (OWN * DEEP) + (local_slot & (OWN - 1))
        wide = hot(row_slot + depth(family) * OWN == iota((BLOCK, size), 0))
        spread[family] = jnp.where(
            same, jnp.dot(rows_of, wide, preferred_element_type=F32), jnp.float32(0.0)
        ).astype(BF16)

    def z_row(family, yy):
        at = lax.rem(yy + 2 * RING, RING)
        for extra in range(OWN):
            s = (at * DEEP + depth(family)) * OWN + extra
            product[family, at * OWN + extra] = jnp.dot(
                bra_tiles[places[0, s]], gathered[s], preferred_element_type=F32
            )

    def w_part(family, n):
        base = pl.multiple_of(n * 2 * GROUP, 2 * GROUP)
        halves = [
            product[family, :, pl.ds(base + half * GROUP, GROUP), :]
            .reshape(size, BLOCK)
            .astype(BF16)
            for half in range(2)
        ]
        both = jnp.dot(
            spread[family], jnp.concatenate(halves, axis=1), preferred_element_type=F32
        )
        return jnp.concatenate(
            [
                both[:, half * BLOCK : (half + 1) * BLOCK].reshape(PAIRS, GROUP, BLOCK)
                for half in range(2)
            ],
            axis=1,
        )

    def swap_tiles(src, dst, first, total, index):
        return remote(
            src.at[pl.ds(first, total)],
            dst.at[pl.ds(first, total)],
            sib_send.at[index],
            sib_recv.at[index],
            there,
        )

    share = PAIRS // (2 * SIDE)
    mine = core * (PAIRS // 2) + xx * share
    bra_swap = swap_tiles(bra_tiles, bra_tiles, core * (PAIRS // 2), PAIRS // 2, 1)
    ket_swap = swap_tiles(ket_tiles, sib_tiles, 0, PAIRS, 2)

    def bra_share(step):
        tiles = bra_tiles.at[pl.ds(mine, share)]
        return remote(
            tiles,
            tiles,
            share_send.at[step - 1],
            share_recv.at[step - 1],
            (row, at_col(xx + step, zl, core)),
        )

    def bra_shared(step):
        first = core * (PAIRS // 2) + lax.rem(xx - step + SIDE, SIDE) * share
        tiles = bra_tiles.at[pl.ds(first, share)]
        return remote(
            tiles,
            tiles,
            share_send.at[step - 1],
            share_recv.at[step - 1],
            (row, at_col(xx + step, zl, core)),
        )

    def ket_run(first, total):
        @pl.loop(first, first + total)
        def _(q):
            ket_tile(q)

    def w_first(first, total):
        @pl.loop(first, first + total)
        def _(n):
            weighted[:, pl.ds(n * 2 * GROUP, 2 * GROUP)] = w_part(0, n)

    for p in range(share):
        bra_tile(mine + p)
    for step in range(1, SIDE):
        bra_share(step).start()
    for m in range(OWN):
        forward(0, OWN + m)
        if m < 2:
            for place in (m, m + 2):
                to_side(place).wait_recv()
                pass_on(place).start()
        ket_run(2 * m, 2)

    for m in range(OWN):
        forward(0, 2 * OWN + m)
        ket_run(8 + m * 3, 3)
        if m < 2:
            from_partner(m).wait_recv()
            from_partner(m + 2).wait_recv()
        send_own(1, m)
        if m == 0:
            counts = count_pairs()
        elif m == 1:
            rows_of = spread_rows(counts)
        else:
            spread_family(rows_of, m - 2)
    for m in range(2):
        forward(1, OWN + m)
        ket_run(20 + m * 6, 3)
        forward(0, 3 * OWN + m)
        if m == 0:
            for step in range(1, SIDE):
                bra_shared(step).wait_recv()
            bra_swap.start()
        ket_run(23 + m * 6, 3)
    ket_swap.start()
    bra_swap.wait()
    to_places.wait()
    fetches[-1].wait()
    forward(1, OWN + 2)
    z_row(0, y)
    z_row(0, y - 1)
    forward(1, OWN + 3)
    z_row(0, y + 1)
    z_row(0, y - 2)
    forward(1, 2 * OWN)
    z_row(0, y + 2)
    arrive(0, last - 4)
    arrive(0, last - 3)
    z_row(0, y - 3)
    forward(1, 2 * OWN + 1)
    z_row(0, y + 3)
    arrive(0, last - 2)
    arrive(0, last - 1)
    z_row(0, y + 4)
    forward(1, 2 * OWN + 2)
    w_first(0, 3)
    forward(1, 2 * OWN + 3)
    w_first(3, 2)
    forward(1, 3 * OWN)
    w_first(5, 1)
    forward(1, 3 * OWN + 1)
    w_first(6, 2)
    for away in (0, 1, -1, 2, -2):
        z_row(1, y + away)
    arrive(1, last - 4)
    arrive(1, last - 3)
    z_row(1, y - 3)
    z_row(1, y + 3)
    table_swap.wait()
    sib_to_slots = pltpu.make_async_copy(sib_slots_vmem, sib_slots, fetch.at[len(fetches) + 2])
    sib_to_slots.start()
    arrive(1, last - 2)
    arrive(1, last - 1)
    z_row(1, y + 4)

    def w_swap(part):
        return remote(
            w_own[part].at[pl.ds(0, PAIRS)],
            w_sib[part].at[pl.ds(0, PAIRS)],
            swap_send.at[part],
            swap_recv.at[part],
            there,
        )

    def w_finish(part):
        start, rows = PARTS[part]

        @pl.loop(0, rows // (2 * GROUP))
        def _(n):
            at = pl.multiple_of(n * 2 * GROUP, 2 * GROUP)
            total = w_part(1, n + start // (2 * GROUP))
            total = total + weighted[:, pl.ds(at + start, 2 * GROUP)]
            w_own[part][0:PAIRS, pl.ds(at, 2 * GROUP)] = total.astype(BF16)

        w_swap(part).start()

    def image(d, zz, jj, part):
        j = (lax.rem(xx + d, SIDE) * SIDE + zz) * 4 + core * 2 + jj
        a, b = slots[0, j], sib_slots[0, j]
        left = jnp.concatenate([w_own[part][a], w_sib[part][b]], axis=1)
        right = jnp.concatenate([ket_tiles[a], sib_tiles[b]], axis=0)
        return jnp.dot(left, right, preferred_element_type=F32)

    def relay(way, part):
        device = (row, x_up) if way == 0 else (row, x_down)
        return remote(
            x_out[part].at[2, way],
            rel_in[part].at[way],
            rel_send.at[part, way],
            rel_recv.at[part, way],
            device,
        )

    def to_x(way, jj, part):
        device = (row, x_up) if way == 0 else (row, x_down)
        return remote(
            x_out[part].at[way, jj],
            x_in[part].at[way, jj],
            x_send.at[part, way, jj],
            x_recv.at[part, way, jj],
            device,
        )

    def to_z(step, part):
        return remote(
            z_out[part].at[step - 1],
            z_in[part].at[step - 1],
            z_send.at[part, step - 1],
            z_recv.at[part, step - 1],
            (row, at_col(xx, z_at(step), core)),
        )

    def relays(part):
        for way in range(2):
            for zz in range(SIDE):
                x_out[part][2, way, zz] = image(2, zz, way, part).astype(BF16)
            relay(way, part).start()

    def direct(part):
        for way, d in ((0, 1), (1, 3)):
            for zz in range(SIDE):
                x_out[part][way, 1 - way, zz] = image(d, zz, 1 - way, part).astype(BF16)
            to_x(way, 1 - way, part).start()

    def summed(part):
        for way, d in ((0, 1), (1, 3)):
            images = [image(d, zz, way, part) for zz in range(SIDE)]
            relay(way, part).wait_recv()
            for zz in range(SIDE):
                total = images[zz] + rel_in[part][way, zz].astype(F32)
                x_out[part][way, way, zz] = total.astype(BF16)
            to_x(way, way, part).start()

    def own_sum(part):
        for jj in range(2):
            for zz in range(SIDE):
                keep[part][jj, zz] = image(0, zz, jj, part)

    def from_x(part):
        for jj in range(2):
            for way in (1 - jj, jj):
                to_x(way, jj, part).wait_recv()
                keep[part][jj] = keep[part][jj] + x_in[part][way, jj].astype(F32)
        for step in (2, 3, 1):
            for jj in range(2):
                z_out[part][step - 1, jj] = keep[part][jj, z_at(step)].astype(BF16)
            to_z(step, part).start()

    def finish(part):
        for step in (1, 3, 2):
            to_z(step, part).wait_recv()
        start, rows = PARTS[part]
        for jj in range(2):
            total = keep[part][jj, zl]
            for step in range(1, SIDE):
                total = total + z_in[part][step - 1, jj].astype(F32)
            out[start : start + rows, jj * BLOCK : (jj + 1) * BLOCK] = total.astype(BF16)

    def z_first(step):
        return remote(
            zf_out.at[step - 1],
            zf_in.at[step - 1],
            zf_send.at[step - 1],
            zf_recv.at[step - 1],
            (row, at_col(xx, z_at(step), core)),
        )

    def x_last(d):
        return remote(
            xf_out.at[d - 1],
            xf_in.at[d - 1],
            xf_send.at[d - 1],
            xf_recv.at[d - 1],
            (row, at_col(xx + d, zl, core)),
        )

    def z_first_images(step):
        for d in range(SIDE):
            for jj in range(2):
                zf_out[step - 1, d, jj] = image(d, z_at(step), jj, ALONG_Z).astype(BF16)
        z_first(step).start()

    def z_first_own():
        for d in range(SIDE):
            for jj in range(2):
                zf_keep[d, jj] = image(d, zl, jj, ALONG_Z)

    def z_first_sum():
        for step in (1, 3, 2):
            z_first(step).wait_recv()
        for d in (2, 1, 3, 0):
            total = zf_keep[d]
            for step in range(1, SIDE):
                total = total + zf_in[step - 1, d].astype(F32)
            if d:
                xf_out[d - 1] = total.astype(BF16)
                x_last(d).start()
            else:
                zf_keep[0] = total

    def z_first_finish():
        for d in range(1, SIDE):
            x_last(d).wait_recv()
        start, rows = PARTS[ALONG_Z]
        for jj in range(2):
            total = zf_keep[0, jj]
            for d in range(1, SIDE):
                total = total + xf_in[d - 1, jj].astype(F32)
            out[start : start + rows, jj * BLOCK : (jj + 1) * BLOCK] = total.astype(BF16)

    for part in range(len(PARTS)):
        w_finish(part)
    to_slots.wait()
    sib_to_slots.wait()
    ket_swap.wait()
    w_swap(0).wait()
    relays(0)
    direct(0)
    w_swap(1).wait()
    z_first_images(2)
    w_swap(2).wait()
    relays(2)
    summed(0)
    z_first_images(3)
    direct(2)
    z_first_images(1)
    w_swap(3).wait()
    relays(3)
    summed(2)
    direct(3)
    own_sum(0)
    from_x(0)
    summed(3)
    own_sum(2)
    own_sum(3)
    z_first_own()
    from_x(2)

    @pl.loop(0, last)
    def _(m):
        for family in range(2):
            for way in range(2):
                hop(family, way, m, 0).wait_send()

    for place in range(OWN):
        to_side(place).wait_send()
        pass_on(place).wait_send()
    for step in range(1, SIDE):
        bra_share(step).wait_send()
    from_x(3)
    z_first_sum()
    finish(0)
    finish(2)
    for part in (0, 2, 3):
        for way in range(2):
            relay(way, part).wait_send()
            for jj in range(2):
                to_x(way, jj, part).wait_send()
        for step in range(1, SIDE):
            to_z(step, part).wait_send()
    for step in range(1, SIDE):
        z_first(step).wait_send()
        x_last(step).wait_send()
    finish(3)
    z_first_finish()


def local(
    basis_centers, bra_pairs, ket_pairs, quartets, quartet_counts, density_owner, density_store
):
    hbm = pl.BlockSpec(memory_space=pltpu.HBM)
    smem, i32 = pltpu.SMEM, jnp.int32
    block, count = (BLOCK, BLOCK), len(PARTS)
    quarter = (PARTS[ALONG_Z][1], BLOCK)

    def parts(lead, kind=BF16):
        return [pltpu.VMEM(lead + (rows, BLOCK), kind) for _, rows in PARTS]

    dma = pltpu.SemaphoreType.DMA
    hops = 3 * OWN + OWN // 2
    return pl.pallas_call(
        body,
        out_shape=jax.ShapeDtypeStruct((BLOCK, 2 * BLOCK), BF16),
        in_specs=[hbm] * 4 + [pl.BlockSpec(memory_space=smem)] + [hbm] * 2,
        out_specs=pl.BlockSpec(memory_space=pltpu.VMEM),
        scratch_shapes=[
            pltpu.VMEM(basis_centers.shape, F32),
            smem(bra_pairs.shape, i32),
            smem(ket_pairs.shape, i32),
            pltpu.VMEM(quartets.shape, i32),
            smem(density_owner.shape, i32),
            pltpu.VMEM((8, BLOCK), i32),
            smem((8, BLOCK), i32),
            pltpu.VMEM((8, BLOCK), i32),
            smem((8, BLOCK), i32),
            pltpu.VMEM((8, BLOCK), i32),
            smem((8, BLOCK), i32),
            dma((9,)),
            pltpu.VMEM((NBLK,) + block, BF16),
            pltpu.VMEM((NBLK, 8, BLOCK), F32),
            pltpu.VMEM((2, 3) + block, F32),
            pltpu.VMEM((PAIRS + 1,) + block, BF16),
            pltpu.VMEM((PAIRS + 1,) + block, BF16),
            pltpu.VMEM((PAIRS + 1,) + block, BF16),
            pltpu.VMEM((2, PAIRS * GROUP, PAIRS * GROUP), BF16),
            pltpu.VMEM((2, PAIRS) + block, F32),
            pltpu.VMEM((PAIRS,) + block, F32),
            parts((PAIRS + 1,)),
            parts((PAIRS + 1,)),
            parts((2, SIDE), F32),
            parts((3, 2, SIDE)),
            parts((2, SIDE)),
            parts((2, 2, SIDE)),
            parts((3, 2)),
            parts((3, 2)),
            pltpu.VMEM((3, SIDE, 2) + quarter, BF16),
            pltpu.VMEM((3, SIDE, 2) + quarter, BF16),
            pltpu.VMEM((SIDE, 2) + quarter, F32),
            pltpu.VMEM((3, 2) + quarter, BF16),
            pltpu.VMEM((3, 2) + quarter, BF16),
            pltpu.VMEM((OWN,) + block, BF16),
            dma((OWN,)),
            dma((OWN,)),
            dma((OWN,)),
            dma((OWN,)),
            dma((2, 2, hops)),
            dma((2, 2, hops)),
            dma((3,)),
            dma((3,)),
            dma((count,)),
            dma((count,)),
            dma((SIDE - 1,)),
            dma((SIDE - 1,)),
            dma((count, 2)),
            dma((count, 2)),
            dma((count, 2, 2)),
            dma((count, 2, 2)),
            dma((count, 3)),
            dma((count, 3)),
            dma((3,)),
            dma((3,)),
            dma((3,)),
            dma((3,)),
        ],
        compiler_params=pltpu.CompilerParams(
            collective_id=0, has_side_effects=True, vmem_limit_bytes=56 * 2**20
        ),
        cost_estimate=pl.CostEstimate(
            flops=2 * 10**9, bytes_accessed=4 * 2**20, transcendentals=4 * 10**6
        ),
    )(
        basis_centers,
        bra_pairs,
        ket_pairs,
        quartets,
        quartet_counts,
        density_owner,
        density_store,
    )


def solution(mesh):
    return jax.shard_map(
        local,
        mesh=mesh,
        in_specs=(
            P(),
            P("bra"),
            P("ket"),
            P("bra", "ket", None, None),
            P("bra", "ket"),
            P("ket", None),
            P("bra", "ket", None),
        ),
        out_specs=P("bra", "ket"),
        check_vma=False,
    )
```

```python
import jax
import jax.numpy as jnp
from jax import lax
from jax.experimental import pallas as pl
from jax.experimental.pallas import tpu as pltpu
from jax.sharding import PartitionSpec as P

OMEGA = 0.11
SOFTEN = 0.25
BLOCK = 128
NBLK = 64
PAIRS = 32
RING = 8
DEEP = 2
SIDE = 4
OWN = 4
PARTS = ((0, 32), (32, 32), (64, 32), (96, 32))
ALONG_Z = 1
GROUP = 8
SHIFT = 3
MESH = pl.DeviceIdType.MESH
F32 = jnp.float32
BF16 = jnp.bfloat16

SLOPE = 0.6 * OMEGA
DECAY = -OMEGA * OMEGA * 1.4426950408889634
ERFC = (
    0.33856715,
    0.33711259,
    0.29264139,
    0.06933287,
    0.29272546,
    -0.65555156,
    0.41918066,
    -0.09400974,
)


def kernel_value(squared):
    inverse = lax.rsqrt(squared)
    divisor = 1.0 + SLOPE * (squared * inverse)
    t = pl.reciprocal(divisor, approx=True)
    t = t * (2.0 - divisor * t)
    poly = ERFC[-1] * t + ERFC[-2]
    for c in ERFC[-3::-1]:
        poly = poly * t + c
    return jnp.exp2(DECAY * squared) * (t * inverse) * poly


def body(
    centers_hbm,
    bra_hbm,
    ket_hbm,
    quartets_hbm,
    count,
    owner_hbm,
    density_hbm,
    out,
    centers,
    bra_pairs,
    ket_pairs,
    quartets,
    owner,
    slots_vmem,
    slots,
    sib_slots_vmem,
    sib_slots,
    places_vmem,
    places,
    fetch,
    gathered,
    lines,
    columns,
    bra_tiles,
    ket_tiles,
    sib_tiles,
    spread,
    product,
    weighted,
    w_own,
    w_sib,
    keep,
    x_out,
    rel_in,
    x_in,
    z_out,
    z_in,
    zf_out,
    zf_in,
    zf_keep,
    xf_out,
    xf_in,
    passing,
    side_send,
    side_recv,
    part_send,
    part_recv,
    ring_send,
    ring_recv,
    sib_send,
    sib_recv,
    swap_send,
    swap_recv,
    share_send,
    share_recv,
    rel_send,
    rel_recv,
    x_send,
    x_recv,
    z_send,
    z_recv,
    zf_send,
    zf_recv,
    xf_send,
    xf_recv,
):
    row = lax.axis_index("bra")
    col = lax.axis_index("ket")
    y, deep = row // DEEP, row % DEEP
    core = col % 2
    zl = (col // 2) % SIDE
    xx = col // (2 * SIDE)

    def at_row(yy, dd):
        return lax.rem(yy + 2 * RING, RING) * DEEP + dd

    def at_col(x_at, z_at, core_at):
        return (lax.rem(x_at + SIDE, SIDE) * SIDE + z_at) * 2 + core_at

    up, down = at_row(y + 1, deep), at_row(y - 1, deep)
    partner = at_row(y, 1 - deep)
    sibling = at_col(xx, zl, 1 - core)
    x_up, x_down = at_col(xx + 1, zl, core), at_col(xx - 1, zl, core)

    def z_at(step):
        return lax.rem(zl + step, SIDE)

    same_side = (row, at_col(xx, z_at(2), core))
    other_side = (partner, at_col(xx, z_at(2), core))
    peers = [(up, col), (down, col), other_side, (row, sibling), (row, x_up), (row, x_down)]
    peers += [(row, at_col(xx, z_at(step), core)) for step in range(1, SIDE)]
    peers += [(row, at_col(xx + 2, zl, core))]
    peers += [(at_row(y + 2, deep), col), (at_row(y - 2, deep), col)]
    barrier = pltpu.get_barrier_semaphore()
    for peer in peers:
        pl.semaphore_signal(barrier, inc=1, device_id=peer, device_id_type=MESH)
    own_slots = gathered.at[pl.ds(row * OWN, OWN)]
    sources = (ket_hbm, bra_hbm, centers_hbm, owner_hbm, quartets_hbm, density_hbm)
    targets = (ket_pairs, bra_pairs, centers, owner, quartets, own_slots)
    fetches = [
        pltpu.make_async_copy(src, dst, fetch.at[n])
        for n, (src, dst) in enumerate(zip(sources, targets))
    ]
    for copy in fetches:
        copy.start()
    for tiles in (bra_tiles, ket_tiles, sib_tiles):
        tiles[PAIRS] = jnp.zeros((BLOCK, BLOCK), BF16)
    for part, (_, rows) in enumerate(PARTS):
        w_own[part][PAIRS] = jnp.zeros((rows, BLOCK), BF16)
        w_sib[part][PAIRS] = jnp.zeros((rows, BLOCK), BF16)
    pl.semaphore_wait(barrier, len(peers))

    def remote(src, dst, send, recv, device):
        return pltpu.make_async_remote_copy(
            src_ref=src,
            dst_ref=dst,
            send_sem=send,
            recv_sem=recv,
            device_id=device,
            device_id_type=MESH,
        )

    def to_side(place):
        return remote(
            density_hbm.at[pl.ds(place, 1)],
            passing.at[pl.ds(place, 1)],
            side_send.at[place],
            side_recv.at[place],
            same_side if place < 2 else other_side,
        )

    def pass_on(place):
        origin = row if place < 2 else partner
        return remote(
            passing.at[pl.ds(place, 1)],
            gathered.at[pl.ds(origin * OWN + place, 1)],
            part_send.at[place],
            part_recv.at[place],
            other_side if place < 2 else same_side,
        )

    def from_partner(place):
        ref = gathered.at[pl.ds(partner * OWN + place, 1)]
        device = other_side if place < 2 else same_side
        return remote(ref, ref, part_send.at[place], part_recv.at[place], device)

    for place in (0, 2, 1, 3):
        to_side(place).start()

    def depth(family):
        return deep if family == 0 else 1 - deep

    def hop(family, way, m, arriving, first=False):
        sign = 1 - 2 * way
        back = m // OWN + arriving
        place = lax.rem(m + 2 * way, OWN)
        ref = gathered.at[pl.ds(at_row(y - sign * back, depth(family)) * OWN + place, 1)]
        src = density_hbm.at[pl.ds(place, 1)] if first else ref
        device = (up, col) if way == 0 else (down, col)
        return remote(
            src, ref, ring_send.at[family, way, m], ring_recv.at[family, way, m], device
        )

    last = 3 * OWN + OWN // 2

    def send_own(family, m):
        for way in range(2):
            hop(family, way, m, 0, family == 0).start()

    def arrive(family, m):
        for way in range(2):
            hop(family, way, m, 1).wait_recv()

    def send_far(part):
        m = 3 * OWN + part
        for way in range(2):
            sign = 1 - 2 * way
            slot = at_row(y - 2 * sign, depth(1)) * OWN + (m + 2 * way) % OWN
            ref = gathered.at[pl.ds(slot, 1)]
            remote(
                ref,
                ref,
                ring_send.at[1, way, m],
                ring_recv.at[1, way, m],
                (at_row(y + 2 * sign, deep), col),
            ).start()

    def forward(family, m):
        for way in range(2):
            hop(family, way, m - OWN, 1).wait_recv()
            hop(family, way, m, 0).start()

    for m in range(OWN):
        send_own(0, m)
    for copy in fetches[:-1]:
        copy.wait()

    lane = lax.broadcasted_iota(jnp.int32, (8, BLOCK), 1)
    ket_table = jnp.full((8, BLOCK), PAIRS, jnp.int32)
    bra_table = jnp.full((8, BLOCK), PAIRS, jnp.int32)
    for n in range(PAIRS):
        ket_table = jnp.where(lane == ket_pairs[n], n, ket_table)
        bra_table = jnp.where(lane == owner[0, bra_pairs[n]], n, bra_table)
    slots_vmem[...] = ket_table
    places_vmem[...] = bra_table
    to_slots = pltpu.make_async_copy(slots_vmem, slots, fetch.at[len(fetches)])
    to_slots.start()
    to_places = pltpu.make_async_copy(places_vmem, places, fetch.at[len(fetches) + 1])
    to_places.start()
    there = (row, sibling)
    table_swap = remote(slots_vmem, sib_slots_vmem, sib_send.at[0], sib_recv.at[0], there)
    table_swap.start()

    for block in range(NBLK):
        lines[block, 0:3] = centers[:, block * BLOCK : (block + 1) * BLOCK]
    for side, start in ((0, row * (NBLK // 16)), (1, col * (NBLK // 32))):
        line = lines[start]
        for axis in range(3):
            wide = jnp.broadcast_to(line[axis : axis + 1], (BLOCK, BLOCK))
            columns[side, axis] = wide.T

    def tile(side, block, ref, place):
        line = lines[block]
        rows = 32
        for part in range(BLOCK // rows):
            squared = jnp.full((rows, BLOCK), SOFTEN, F32)
            for axis in range(3):
                difference = columns[side, axis, pl.ds(part * rows, rows)] - line[axis : axis + 1]
                squared = squared + difference * difference
            ref[place, pl.ds(part * rows, rows)] = kernel_value(squared).astype(BF16)

    def ket_tile(q):
        tile(1, ket_pairs[q], ket_tiles, q)

    def bra_tile(p):
        tile(0, bra_pairs[p], bra_tiles, p)

    def iota(shape, axis):
        return lax.broadcasted_iota(jnp.int32, shape, axis)

    def hot(condition):
        return jnp.where(condition, jnp.float32(1.0), jnp.float32(0.0)).astype(BF16)

    size = PAIRS * GROUP

    def count_pairs():
        long = (PAIRS, quartets.shape[3])
        bra_hot = hot((quartets[0, 0, 0:1] == iota(long, 0)) & (iota(long, 1) < count[0, 0]))
        ket_hot = hot(quartets[0, 0, 1:2] == iota(long, 0))
        return lax.dot_general(
            ket_hot, bra_hot, (((1,), (1,)), ((), ())), preferred_element_type=F32
        ).astype(BF16)

    def spread_rows(counts):
        by_slot = jnp.dot(
            counts, hot(bra_table[0:1] == iota((PAIRS, BLOCK), 0)), preferred_element_type=F32
        ).astype(BF16)
        tall = hot(iota((size, PAIRS), 0) >> SHIFT == iota((size, PAIRS), 1))
        return jnp.dot(tall, by_slot, preferred_element_type=F32).astype(BF16)

    def spread_family(rows_of, family):
        same = (iota((size, size), 0) ^ iota((size, size), 1)) & (GROUP - 1) == 0
        local_slot = iota((BLOCK, size), 1) >> SHIFT
        row_slot = (local_slot >> 2) * (OWN * DEEP) + (local_slot & (OWN - 1))
        wide = hot(row_slot + depth(family) * OWN == iota((BLOCK, size), 0))
        spread[family] = jnp.where(
            same, jnp.dot(rows_of, wide, preferred_element_type=F32), jnp.float32(0.0)
        ).astype(BF16)

    def z_row(family, yy):
        at = lax.rem(yy + 2 * RING, RING)
        for extra in range(OWN):
            s = (at * DEEP + depth(family)) * OWN + extra
            product[family, at * OWN + extra] = jnp.dot(
                bra_tiles[places[0, s]], gathered[s], preferred_element_type=F32
            )

    def w_part(family, n):
        base = pl.multiple_of(n * 2 * GROUP, 2 * GROUP)
        halves = [
            product[family, :, pl.ds(base + half * GROUP, GROUP), :]
            .reshape(size, BLOCK)
            .astype(BF16)
            for half in range(2)
        ]
        both = jnp.dot(
            spread[family], jnp.concatenate(halves, axis=1), preferred_element_type=F32
        )
        return jnp.concatenate(
            [
                both[:, half * BLOCK : (half + 1) * BLOCK].reshape(PAIRS, GROUP, BLOCK)
                for half in range(2)
            ],
            axis=1,
        )

    def swap_tiles(src, dst, first, total, index):
        return remote(
            src.at[pl.ds(first, total)],
            dst.at[pl.ds(first, total)],
            sib_send.at[index],
            sib_recv.at[index],
            there,
        )

    share = PAIRS // (2 * SIDE)
    mine = core * (PAIRS // 2) + xx * share
    bra_swap = swap_tiles(bra_tiles, bra_tiles, core * (PAIRS // 2), PAIRS // 2, 1)
    ket_swap = swap_tiles(ket_tiles, sib_tiles, 0, PAIRS, 2)

    def bra_share(step):
        tiles = bra_tiles.at[pl.ds(mine, share)]
        return remote(
            tiles,
            tiles,
            share_send.at[step - 1],
            share_recv.at[step - 1],
            (row, at_col(xx + step, zl, core)),
        )

    def bra_shared(step):
        first = core * (PAIRS // 2) + lax.rem(xx - step + SIDE, SIDE) * share
        tiles = bra_tiles.at[pl.ds(first, share)]
        return remote(
            tiles,
            tiles,
            share_send.at[step - 1],
            share_recv.at[step - 1],
            (row, at_col(xx + step, zl, core)),
        )

    def ket_run(first, total):
        @pl.loop(first, first + total)
        def _(q):
            ket_tile(q)

    def w_first(first, total):
        @pl.loop(first, first + total)
        def _(n):
            weighted[:, pl.ds(n * 2 * GROUP, 2 * GROUP)] = w_part(0, n)

    for p in range(share):
        bra_tile(mine + p)
    for step in range(1, SIDE):
        bra_share(step).start()
    for m in range(OWN):
        forward(0, OWN + m)
        if m < 2:
            for place in (m, m + 2):
                to_side(place).wait_recv()
                pass_on(place).start()
        ket_run(2 * m, 2)

    for m in range(OWN):
        forward(0, 2 * OWN + m)
        ket_run(8 + m * 3, 3)
        if m < 2:
            from_partner(m).wait_recv()
            from_partner(m + 2).wait_recv()
        send_own(1, m)
        if m == 0:
            counts = count_pairs()
        elif m == 1:
            rows_of = spread_rows(counts)
        else:
            spread_family(rows_of, m - 2)
    for m in range(2):
        forward(1, OWN + m)
        ket_run(20 + m * 6, 3)
        forward(0, 3 * OWN + m)
        if m == 0:
            for step in range(1, SIDE):
                bra_shared(step).wait_recv()
            bra_swap.start()
        ket_run(23 + m * 6, 3)
    ket_swap.start()
    bra_swap.wait()
    to_places.wait()
    fetches[-1].wait()
    forward(1, OWN + 2)
    z_row(0, y)
    z_row(0, y - 1)
    forward(1, OWN + 3)
    z_row(0, y + 1)
    z_row(0, y - 2)
    forward(1, 2 * OWN)
    send_far(0)
    z_row(0, y + 2)
    arrive(0, last - 4)
    arrive(0, last - 3)
    z_row(0, y - 3)
    forward(1, 2 * OWN + 1)
    send_far(1)
    z_row(0, y + 3)
    arrive(0, last - 2)
    arrive(0, last - 1)
    z_row(0, y + 4)
    forward(1, 2 * OWN + 2)
    w_first(0, 3)
    forward(1, 2 * OWN + 3)
    w_first(3, 2)
    w_first(5, 3)
    for away in (0, 1, -1, 2, -2):
        z_row(1, y + away)
    for m in range(2 * OWN, 3 * OWN):
        arrive(1, m)
    z_row(1, y - 3)
    z_row(1, y + 3)
    table_swap.wait()
    sib_to_slots = pltpu.make_async_copy(sib_slots_vmem, sib_slots, fetch.at[len(fetches) + 2])
    sib_to_slots.start()
    arrive(1, last - 2)
    arrive(1, last - 1)
    z_row(1, y + 4)

    def w_swap(part):
        return remote(
            w_own[part].at[pl.ds(0, PAIRS)],
            w_sib[part].at[pl.ds(0, PAIRS)],
            swap_send.at[part],
            swap_recv.at[part],
            there,
        )

    def w_finish(part):
        start, rows = PARTS[part]

        @pl.loop(0, rows // (2 * GROUP))
        def _(n):
            at = pl.multiple_of(n * 2 * GROUP, 2 * GROUP)
            total = w_part(1, n + start // (2 * GROUP))
            total = total + weighted[:, pl.ds(at + start, 2 * GROUP)]
            w_own[part][0:PAIRS, pl.ds(at, 2 * GROUP)] = total.astype(BF16)

        w_swap(part).start()

    def image(d, zz, jj, part):
        j = (lax.rem(xx + d, SIDE) * SIDE + zz) * 4 + core * 2 + jj
        a, b = slots[0, j], sib_slots[0, j]
        left = jnp.concatenate([w_own[part][a], w_sib[part][b]], axis=1)
        right = jnp.concatenate([ket_tiles[a], sib_tiles[b]], axis=0)
        return jnp.dot(left, right, preferred_element_type=F32)

    def relay(way, part):
        device = (row, x_up) if way == 0 else (row, x_down)
        return remote(
            x_out[part].at[2, way],
            rel_in[part].at[way],
            rel_send.at[part, way],
            rel_recv.at[part, way],
            device,
        )

    def to_x(way, jj, part):
        device = (row, x_up) if way == 0 else (row, x_down)
        return remote(
            x_out[part].at[way, jj],
            x_in[part].at[way, jj],
            x_send.at[part, way, jj],
            x_recv.at[part, way, jj],
            device,
        )

    def to_z(step, part):
        return remote(
            z_out[part].at[step - 1],
            z_in[part].at[step - 1],
            z_send.at[part, step - 1],
            z_recv.at[part, step - 1],
            (row, at_col(xx, z_at(step), core)),
        )

    def relays(part):
        for way in range(2):
            for zz in range(SIDE):
                x_out[part][2, way, zz] = image(2, zz, way, part).astype(BF16)
            relay(way, part).start()

    def direct(part):
        for way, d in ((0, 1), (1, 3)):
            for zz in range(SIDE):
                x_out[part][way, 1 - way, zz] = image(d, zz, 1 - way, part).astype(BF16)
            to_x(way, 1 - way, part).start()

    def summed(part):
        for way, d in ((0, 1), (1, 3)):
            images = [image(d, zz, way, part) for zz in range(SIDE)]
            relay(way, part).wait_recv()
            for zz in range(SIDE):
                total = images[zz] + rel_in[part][way, zz].astype(F32)
                x_out[part][way, way, zz] = total.astype(BF16)
            to_x(way, way, part).start()

    def own_sum(part):
        for jj in range(2):
            for zz in range(SIDE):
                keep[part][jj, zz] = image(0, zz, jj, part)

    def from_x(part):
        for jj in range(2):
            for way in (1 - jj, jj):
                to_x(way, jj, part).wait_recv()
                keep[part][jj] = keep[part][jj] + x_in[part][way, jj].astype(F32)
        for step in (2, 3, 1):
            for jj in range(2):
                z_out[part][step - 1, jj] = keep[part][jj, z_at(step)].astype(BF16)
            to_z(step, part).start()

    def finish(part):
        for step in (1, 3, 2):
            to_z(step, part).wait_recv()
        start, rows = PARTS[part]
        for jj in range(2):
            total = keep[part][jj, zl]
            for step in range(1, SIDE):
                total = total + z_in[part][step - 1, jj].astype(F32)
            out[start : start + rows, jj * BLOCK : (jj + 1) * BLOCK] = total.astype(BF16)

    def z_first(step):
        return remote(
            zf_out.at[step - 1],
            zf_in.at[step - 1],
            zf_send.at[step - 1],
            zf_recv.at[step - 1],
            (row, at_col(xx, z_at(step), core)),
        )

    def x_last(d):
        return remote(
            xf_out.at[d - 1],
            xf_in.at[d - 1],
            xf_send.at[d - 1],
            xf_recv.at[d - 1],
            (row, at_col(xx + d, zl, core)),
        )

    def z_first_images():
        for step in (2, 3, 1):
            for d in range(SIDE):
                for jj in range(2):
                    zf_out[step - 1, d, jj] = image(d, z_at(step), jj, ALONG_Z).astype(BF16)
            z_first(step).start()

    def z_first_own():
        for d in range(SIDE):
            for jj in range(2):
                zf_keep[d, jj] = image(d, zl, jj, ALONG_Z)

    def z_first_sum():
        for step in (1, 3, 2):
            z_first(step).wait_recv()
        for d in (2, 1, 3, 0):
            total = zf_keep[d]
            for step in range(1, SIDE):
                total = total + zf_in[step - 1, d].astype(F32)
            if d:
                xf_out[d - 1] = total.astype(BF16)
                x_last(d).start()
            else:
                zf_keep[0] = total

    def z_first_finish():
        for d in range(1, SIDE):
            x_last(d).wait_recv()
        start, rows = PARTS[ALONG_Z]
        for jj in range(2):
            total = zf_keep[0, jj]
            for d in range(1, SIDE):
                total = total + xf_in[d - 1, jj].astype(F32)
            out[start : start + rows, jj * BLOCK : (jj + 1) * BLOCK] = total.astype(BF16)

    w_finish(0)
    w_finish(1)
    to_slots.wait()
    sib_to_slots.wait()
    ket_swap.wait()
    w_swap(0).wait()
    relays(0)
    direct(0)
    w_finish(2)
    w_swap(1).wait()
    z_first_images()
    w_finish(3)
    w_swap(2).wait()
    relays(2)
    summed(0)
    direct(2)
    w_swap(3).wait()
    relays(3)
    summed(2)
    direct(3)
    own_sum(0)
    from_x(0)
    summed(3)
    own_sum(2)
    own_sum(3)
    z_first_own()
    from_x(2)

    @pl.loop(0, last)
    def _(m):
        for family in range(2):
            for way in range(2):
                hop(family, way, m, 0).wait_send()

    for place in range(OWN):
        to_side(place).wait_send()
        pass_on(place).wait_send()
    for step in range(1, SIDE):
        bra_share(step).wait_send()
    from_x(3)
    z_first_sum()
    finish(0)
    finish(2)
    for part in (0, 2, 3):
        for way in range(2):
            relay(way, part).wait_send()
            for jj in range(2):
                to_x(way, jj, part).wait_send()
        for step in range(1, SIDE):
            to_z(step, part).wait_send()
    for step in range(1, SIDE):
        z_first(step).wait_send()
        x_last(step).wait_send()
    finish(3)
    z_first_finish()


def local(
    basis_centers, bra_pairs, ket_pairs, quartets, quartet_counts, density_owner, density_store
):
    hbm = pl.BlockSpec(memory_space=pltpu.HBM)
    smem, i32 = pltpu.SMEM, jnp.int32
    block, count = (BLOCK, BLOCK), len(PARTS)
    quarter = (PARTS[ALONG_Z][1], BLOCK)

    def parts(lead, kind=BF16):
        return [pltpu.VMEM(lead + (rows, BLOCK), kind) for _, rows in PARTS]

    dma = pltpu.SemaphoreType.DMA
    hops = 3 * OWN + OWN // 2
    return pl.pallas_call(
        body,
        out_shape=jax.ShapeDtypeStruct((BLOCK, 2 * BLOCK), BF16),
        in_specs=[hbm] * 4 + [pl.BlockSpec(memory_space=smem)] + [hbm] * 2,
        out_specs=pl.BlockSpec(memory_space=pltpu.VMEM),
        scratch_shapes=[
            pltpu.VMEM(basis_centers.shape, F32),
            smem(bra_pairs.shape, i32),
            smem(ket_pairs.shape, i32),
            pltpu.VMEM(quartets.shape, i32),
            smem(density_owner.shape, i32),
            pltpu.VMEM((8, BLOCK), i32),
            smem((8, BLOCK), i32),
            pltpu.VMEM((8, BLOCK), i32),
            smem((8, BLOCK), i32),
            pltpu.VMEM((8, BLOCK), i32),
            smem((8, BLOCK), i32),
            dma((9,)),
            pltpu.VMEM((NBLK,) + block, BF16),
            pltpu.VMEM((NBLK, 8, BLOCK), F32),
            pltpu.VMEM((2, 3) + block, F32),
            pltpu.VMEM((PAIRS + 1,) + block, BF16),
            pltpu.VMEM((PAIRS + 1,) + block, BF16),
            pltpu.VMEM((PAIRS + 1,) + block, BF16),
            pltpu.VMEM((2, PAIRS * GROUP, PAIRS * GROUP), BF16),
            pltpu.VMEM((2, PAIRS) + block, F32),
            pltpu.VMEM((PAIRS,) + block, F32),
            parts((PAIRS + 1,)),
            parts((PAIRS + 1,)),
            parts((2, SIDE), F32),
            parts((3, 2, SIDE)),
            parts((2, SIDE)),
            parts((2, 2, SIDE)),
            parts((3, 2)),
            parts((3, 2)),
            pltpu.VMEM((3, SIDE, 2) + quarter, BF16),
            pltpu.VMEM((3, SIDE, 2) + quarter, BF16),
            pltpu.VMEM((SIDE, 2) + quarter, F32),
            pltpu.VMEM((3, 2) + quarter, BF16),
            pltpu.VMEM((3, 2) + quarter, BF16),
            pltpu.VMEM((OWN,) + block, BF16),
            dma((OWN,)),
            dma((OWN,)),
            dma((OWN,)),
            dma((OWN,)),
            dma((2, 2, hops)),
            dma((2, 2, hops)),
            dma((3,)),
            dma((3,)),
            dma((count,)),
            dma((count,)),
            dma((SIDE - 1,)),
            dma((SIDE - 1,)),
            dma((count, 2)),
            dma((count, 2)),
            dma((count, 2, 2)),
            dma((count, 2, 2)),
            dma((count, 3)),
            dma((count, 3)),
            dma((3,)),
            dma((3,)),
            dma((3,)),
            dma((3,)),
        ],
        compiler_params=pltpu.CompilerParams(
            collective_id=0, has_side_effects=True, vmem_limit_bytes=56 * 2**20
        ),
        cost_estimate=pl.CostEstimate(
            flops=2 * 10**9, bytes_accessed=4 * 2**20, transcendentals=4 * 10**6
        ),
    )(
        basis_centers,
        bra_pairs,
        ket_pairs,
        quartets,
        quartet_counts,
        density_owner,
        density_store,
    )


def solution(mesh):
    return jax.shard_map(
        local,
        mesh=mesh,
        in_specs=(
            P(),
            P("bra"),
            P("ket"),
            P("bra", "ket", None, None),
            P("bra", "ket"),
            P("ket", None),
            P("bra", "ket", None),
        ),
        out_specs=P("bra", "ket"),
        check_vma=False,
    )
```

```python
import jax
import jax.numpy as jnp
from jax import lax
from jax.experimental import pallas as pl
from jax.experimental.pallas import tpu as pltpu
from jax.sharding import PartitionSpec as P

OMEGA = 0.11
SOFTEN = 0.25
BLOCK = 128
NBLK = 64
PAIRS = 32
RING = 8
DEEP = 2
SIDE = 4
OWN = 4
PARTS = ((0, 32), (32, 32), (64, 32), (96, 32))
ALONG_Z = 1
GROUP = 8
SHIFT = 3
MESH = pl.DeviceIdType.MESH
F32 = jnp.float32
BF16 = jnp.bfloat16

SLOPE = 0.6 * OMEGA
DECAY = -OMEGA * OMEGA * 1.4426950408889634
ERFC = (
    0.33856715,
    0.33711259,
    0.29264139,
    0.06933287,
    0.29272546,
    -0.65555156,
    0.41918066,
    -0.09400974,
)


def kernel_value(squared):
    inverse = lax.rsqrt(squared)
    divisor = 1.0 + SLOPE * (squared * inverse)
    t = pl.reciprocal(divisor, approx=True)
    t = t * (2.0 - divisor * t)
    poly = ERFC[-1] * t + ERFC[-2]
    for c in ERFC[-3::-1]:
        poly = poly * t + c
    return jnp.exp2(DECAY * squared) * (t * inverse) * poly


def body(
    centers_hbm,
    bra_hbm,
    ket_hbm,
    quartets_hbm,
    count,
    owner_hbm,
    density_hbm,
    out,
    centers,
    bra_pairs,
    ket_pairs,
    quartets,
    owner,
    slots_vmem,
    slots,
    sib_slots_vmem,
    sib_slots,
    places_vmem,
    places,
    fetch,
    gathered,
    lines,
    columns,
    bra_tiles,
    ket_tiles,
    sib_tiles,
    spread,
    product,
    weighted,
    w_own,
    w_sib,
    keep,
    x_out,
    rel_in,
    x_in,
    z_out,
    z_in,
    zf_out,
    zf_in,
    zf_keep,
    xf_out,
    xf_in,
    passing,
    side_send,
    side_recv,
    part_send,
    part_recv,
    far_passing,
    far_send,
    far_recv,
    ring_send,
    ring_recv,
    sib_send,
    sib_recv,
    swap_send,
    swap_recv,
    share_send,
    share_recv,
    rel_send,
    rel_recv,
    x_send,
    x_recv,
    z_send,
    z_recv,
    zf_send,
    zf_recv,
    xf_send,
    xf_recv,
):
    row = lax.axis_index("bra")
    col = lax.axis_index("ket")
    y, deep = row // DEEP, row % DEEP
    core = col % 2
    zl = (col // 2) % SIDE
    xx = col // (2 * SIDE)

    def at_row(yy, dd):
        return lax.rem(yy + 2 * RING, RING) * DEEP + dd

    def at_col(x_at, z_at, core_at):
        return (lax.rem(x_at + SIDE, SIDE) * SIDE + z_at) * 2 + core_at

    up, down = at_row(y + 1, deep), at_row(y - 1, deep)
    partner = at_row(y, 1 - deep)
    sibling = at_col(xx, zl, 1 - core)
    x_up, x_down = at_col(xx + 1, zl, core), at_col(xx - 1, zl, core)

    def z_at(step):
        return lax.rem(zl + step, SIDE)

    same_side = (row, at_col(xx, z_at(2), core))
    other_side = (partner, at_col(xx, z_at(2), core))
    peers = [(up, col), (down, col), other_side, (row, sibling), (row, x_up), (row, x_down)]
    peers += [(row, at_col(xx, z_at(step), core)) for step in range(1, SIDE)]
    peers += [(row, at_col(xx + 2, zl, core))]
    barrier = pltpu.get_barrier_semaphore()
    for peer in peers:
        pl.semaphore_signal(barrier, inc=1, device_id=peer, device_id_type=MESH)
    own_slots = gathered.at[pl.ds(row * OWN, OWN)]
    sources = (ket_hbm, bra_hbm, centers_hbm, owner_hbm, quartets_hbm, density_hbm)
    targets = (ket_pairs, bra_pairs, centers, owner, quartets, own_slots)
    fetches = [
        pltpu.make_async_copy(src, dst, fetch.at[n])
        for n, (src, dst) in enumerate(zip(sources, targets))
    ]
    for copy in fetches:
        copy.start()
    for tiles in (bra_tiles, ket_tiles, sib_tiles):
        tiles[PAIRS] = jnp.zeros((BLOCK, BLOCK), BF16)
    for part, (_, rows) in enumerate(PARTS):
        w_own[part][PAIRS] = jnp.zeros((rows, BLOCK), BF16)
        w_sib[part][PAIRS] = jnp.zeros((rows, BLOCK), BF16)
    pl.semaphore_wait(barrier, len(peers))

    def remote(src, dst, send, recv, device):
        return pltpu.make_async_remote_copy(
            src_ref=src,
            dst_ref=dst,
            send_sem=send,
            recv_sem=recv,
            device_id=device,
            device_id_type=MESH,
        )

    def to_side(place):
        return remote(
            density_hbm.at[pl.ds(place, 1)],
            passing.at[pl.ds(place, 1)],
            side_send.at[place],
            side_recv.at[place],
            same_side if place < 2 else other_side,
        )

    def pass_on(place):
        origin = row if place < 2 else partner
        return remote(
            passing.at[pl.ds(place, 1)],
            gathered.at[pl.ds(origin * OWN + place, 1)],
            part_send.at[place],
            part_recv.at[place],
            other_side if place < 2 else same_side,
        )

    def from_partner(place):
        ref = gathered.at[pl.ds(partner * OWN + place, 1)]
        device = other_side if place < 2 else same_side
        return remote(ref, ref, part_send.at[place], part_recv.at[place], device)

    for place in (0, 2, 1, 3):
        to_side(place).start()

    def far_ref(origin_row, place):
        return gathered.at[pl.ds(origin_row * OWN + place, 1)]

    def far_side(place):
        return remote(
            far_ref(at_row(y + 4, deep), place),
            far_passing.at[pl.ds(place, 1)],
            far_send.at[0, place],
            far_recv.at[0, place],
            same_side if place < 2 else other_side,
        )

    def far_on(place):
        ref = far_ref(at_row(y + 4, deep if place < 2 else 1 - deep), place)
        return remote(
            far_passing.at[pl.ds(place, 1)],
            ref,
            far_send.at[1, place],
            far_recv.at[1, place],
            other_side if place < 2 else same_side,
        )

    def far_from(place):
        ref = far_ref(at_row(y + 4, 1 - deep), place)
        device = other_side if place < 2 else same_side
        return remote(ref, ref, far_send.at[1, place], far_recv.at[1, place], device)

    def depth(family):
        return deep if family == 0 else 1 - deep

    def hop(family, way, m, arriving, first=False):
        sign = 1 - 2 * way
        back = m // OWN + arriving
        place = lax.rem(m + 2 * way, OWN)
        ref = gathered.at[pl.ds(at_row(y - sign * back, depth(family)) * OWN + place, 1)]
        src = density_hbm.at[pl.ds(place, 1)] if first else ref
        device = (up, col) if way == 0 else (down, col)
        return remote(
            src, ref, ring_send.at[family, way, m], ring_recv.at[family, way, m], device
        )

    last = 3 * OWN + OWN // 2

    def send_own(family, m):
        for way in range(2):
            hop(family, way, m, 0, family == 0).start()

    def arrive(family, m):
        for way in range(2):
            hop(family, way, m, 1).wait_recv()

    def forward(family, m):
        for way in range(2):
            hop(family, way, m - OWN, 1).wait_recv()
            hop(family, way, m, 0).start()

    for m in range(OWN):
        send_own(0, m)
    for copy in fetches[:-1]:
        copy.wait()

    lane = lax.broadcasted_iota(jnp.int32, (8, BLOCK), 1)
    ket_table = jnp.full((8, BLOCK), PAIRS, jnp.int32)
    bra_table = jnp.full((8, BLOCK), PAIRS, jnp.int32)
    for n in range(PAIRS):
        ket_table = jnp.where(lane == ket_pairs[n], n, ket_table)
        bra_table = jnp.where(lane == owner[0, bra_pairs[n]], n, bra_table)
    slots_vmem[...] = ket_table
    places_vmem[...] = bra_table
    to_slots = pltpu.make_async_copy(slots_vmem, slots, fetch.at[len(fetches)])
    to_slots.start()
    to_places = pltpu.make_async_copy(places_vmem, places, fetch.at[len(fetches) + 1])
    to_places.start()
    there = (row, sibling)
    table_swap = remote(slots_vmem, sib_slots_vmem, sib_send.at[0], sib_recv.at[0], there)
    table_swap.start()

    for block in range(NBLK):
        lines[block, 0:3] = centers[:, block * BLOCK : (block + 1) * BLOCK]
    for side, start in ((0, row * (NBLK // 16)), (1, col * (NBLK // 32))):
        line = lines[start]
        for axis in range(3):
            wide = jnp.broadcast_to(line[axis : axis + 1], (BLOCK, BLOCK))
            columns[side, axis] = wide.T

    def tile(side, block, ref, place):
        line = lines[block]
        rows = 32
        for part in range(BLOCK // rows):
            squared = jnp.full((rows, BLOCK), SOFTEN, F32)
            for axis in range(3):
                difference = columns[side, axis, pl.ds(part * rows, rows)] - line[axis : axis + 1]
                squared = squared + difference * difference
            ref[place, pl.ds(part * rows, rows)] = kernel_value(squared).astype(BF16)

    def ket_tile(q):
        tile(1, ket_pairs[q], ket_tiles, q)

    def bra_tile(p):
        tile(0, bra_pairs[p], bra_tiles, p)

    def iota(shape, axis):
        return lax.broadcasted_iota(jnp.int32, shape, axis)

    def hot(condition):
        return jnp.where(condition, jnp.float32(1.0), jnp.float32(0.0)).astype(BF16)

    size = PAIRS * GROUP

    def count_pairs():
        long = (PAIRS, quartets.shape[3])
        bra_hot = hot((quartets[0, 0, 0:1] == iota(long, 0)) & (iota(long, 1) < count[0, 0]))
        ket_hot = hot(quartets[0, 0, 1:2] == iota(long, 0))
        return lax.dot_general(
            ket_hot, bra_hot, (((1,), (1,)), ((), ())), preferred_element_type=F32
        ).astype(BF16)

    def spread_rows(counts):
        by_slot = jnp.dot(
            counts, hot(bra_table[0:1] == iota((PAIRS, BLOCK), 0)), preferred_element_type=F32
        ).astype(BF16)
        tall = hot(iota((size, PAIRS), 0) >> SHIFT == iota((size, PAIRS), 1))
        return jnp.dot(tall, by_slot, preferred_element_type=F32).astype(BF16)

    def spread_family(rows_of, family):
        same = (iota((size, size), 0) ^ iota((size, size), 1)) & (GROUP - 1) == 0
        local_slot = iota((BLOCK, size), 1) >> SHIFT
        row_slot = (local_slot >> 2) * (OWN * DEEP) + (local_slot & (OWN - 1))
        wide = hot(row_slot + depth(family) * OWN == iota((BLOCK, size), 0))
        spread[family] = jnp.where(
            same, jnp.dot(rows_of, wide, preferred_element_type=F32), jnp.float32(0.0)
        ).astype(BF16)

    def z_row(family, yy):
        at = lax.rem(yy + 2 * RING, RING)
        for extra in range(OWN):
            s = (at * DEEP + depth(family)) * OWN + extra
            product[family, at * OWN + extra] = jnp.dot(
                bra_tiles[places[0, s]], gathered[s], preferred_element_type=F32
            )

    def w_part(family, n):
        base = pl.multiple_of(n * 2 * GROUP, 2 * GROUP)
        halves = [
            product[family, :, pl.ds(base + half * GROUP, GROUP), :]
            .reshape(size, BLOCK)
            .astype(BF16)
            for half in range(2)
        ]
        both = jnp.dot(
            spread[family], jnp.concatenate(halves, axis=1), preferred_element_type=F32
        )
        return jnp.concatenate(
            [
                both[:, half * BLOCK : (half + 1) * BLOCK].reshape(PAIRS, GROUP, BLOCK)
                for half in range(2)
            ],
            axis=1,
        )

    def swap_tiles(src, dst, first, total, index):
        return remote(
            src.at[pl.ds(first, total)],
            dst.at[pl.ds(first, total)],
            sib_send.at[index],
            sib_recv.at[index],
            there,
        )

    share = PAIRS // (2 * SIDE)
    mine = core * (PAIRS // 2) + xx * share
    bra_swap = swap_tiles(bra_tiles, bra_tiles, core * (PAIRS // 2), PAIRS // 2, 1)
    ket_swap = swap_tiles(ket_tiles, sib_tiles, 0, PAIRS, 2)

    def bra_share(step):
        tiles = bra_tiles.at[pl.ds(mine, share)]
        return remote(
            tiles,
            tiles,
            share_send.at[step - 1],
            share_recv.at[step - 1],
            (row, at_col(xx + step, zl, core)),
        )

    def bra_shared(step):
        first = core * (PAIRS // 2) + lax.rem(xx - step + SIDE, SIDE) * share
        tiles = bra_tiles.at[pl.ds(first, share)]
        return remote(
            tiles,
            tiles,
            share_send.at[step - 1],
            share_recv.at[step - 1],
            (row, at_col(xx + step, zl, core)),
        )

    def ket_run(first, total):
        @pl.loop(first, first + total)
        def _(q):
            ket_tile(q)

    def w_first(first, total):
        @pl.loop(first, first + total)
        def _(n):
            weighted[:, pl.ds(n * 2 * GROUP, 2 * GROUP)] = w_part(0, n)

    for p in range(share):
        bra_tile(mine + p)
    for step in range(1, SIDE):
        bra_share(step).start()
    for m in range(OWN):
        forward(0, OWN + m)
        if m < 2:
            for place in (m, m + 2):
                to_side(place).wait_recv()
                pass_on(place).start()
        ket_run(2 * m, 2)

    for m in range(OWN):
        forward(0, 2 * OWN + m)
        ket_run(8 + m * 3, 3)
    for m in range(2):
        forward(0, 3 * OWN + m)
        ket_run(20 + 2 * m, 2)
    for m in range(OWN):
        if m < 2:
            from_partner(m).wait_recv()
            from_partner(m + 2).wait_recv()
        send_own(1, m)
        if m == 0:
            counts = count_pairs()
        elif m == 1:
            rows_of = spread_rows(counts)
        else:
            spread_family(rows_of, m - 2)
            arrive(0, 3 * OWN + m - 2)
            for place in (m - 2, m):
                far_side(place).start()
    for step in range(1, SIDE):
        bra_shared(step).wait_recv()
    bra_swap.start()
    forward(1, OWN)
    ket_run(24, 4)
    forward(1, OWN + 1)
    ket_run(28, 4)
    ket_swap.start()
    bra_swap.wait()
    to_places.wait()
    fetches[-1].wait()
    forward(1, OWN + 2)
    z_row(0, y)
    z_row(0, y - 1)
    forward(1, OWN + 3)
    z_row(0, y + 1)
    z_row(0, y - 2)
    for m in range(2):
        forward(1, 2 * OWN + m)
        for place in (m, m + 2):
            far_side(place).wait_recv()
            far_on(place).start()
        z_row(0, y + 2 + 2 * m)
    arrive(0, last - 4)
    arrive(0, last - 3)
    forward(1, 2 * OWN + 2)
    z_row(0, y - 3)
    z_row(0, y + 3)
    forward(1, 2 * OWN + 3)
    w_first(0, 8)
    for away in (0, 1, -1, 2, -2):
        z_row(1, y + away)
    for m in range(2 * OWN, 3 * OWN):
        arrive(1, m)
    z_row(1, y - 3)
    z_row(1, y + 3)
    table_swap.wait()
    sib_to_slots = pltpu.make_async_copy(sib_slots_vmem, sib_slots, fetch.at[len(fetches) + 2])
    sib_to_slots.start()
    for place in range(OWN):
        far_from(place).wait_recv()
    z_row(1, y + 4)

    def w_swap(part):
        return remote(
            w_own[part].at[pl.ds(0, PAIRS)],
            w_sib[part].at[pl.ds(0, PAIRS)],
            swap_send.at[part],
            swap_recv.at[part],
            there,
        )

    def w_finish(part):
        start, rows = PARTS[part]

        @pl.loop(0, rows // (2 * GROUP))
        def _(n):
            at = pl.multiple_of(n * 2 * GROUP, 2 * GROUP)
            total = w_part(1, n + start // (2 * GROUP))
            total = total + weighted[:, pl.ds(at + start, 2 * GROUP)]
            w_own[part][0:PAIRS, pl.ds(at, 2 * GROUP)] = total.astype(BF16)

        w_swap(part).start()

    def image(d, zz, jj, part):
        j = (lax.rem(xx + d, SIDE) * SIDE + zz) * 4 + core * 2 + jj
        a, b = slots[0, j], sib_slots[0, j]
        left = jnp.concatenate([w_own[part][a], w_sib[part][b]], axis=1)
        right = jnp.concatenate([ket_tiles[a], sib_tiles[b]], axis=0)
        return jnp.dot(left, right, preferred_element_type=F32)

    def relay(way, part):
        device = (row, x_up) if way == 0 else (row, x_down)
        return remote(
            x_out[part].at[2, way],
            rel_in[part].at[way],
            rel_send.at[part, way],
            rel_recv.at[part, way],
            device,
        )

    def to_x(way, jj, part):
        device = (row, x_up) if way == 0 else (row, x_down)
        return remote(
            x_out[part].at[way, jj],
            x_in[part].at[way, jj],
            x_send.at[part, way, jj],
            x_recv.at[part, way, jj],
            device,
        )

    def to_z(step, part):
        return remote(
            z_out[part].at[step - 1],
            z_in[part].at[step - 1],
            z_send.at[part, step - 1],
            z_recv.at[part, step - 1],
            (row, at_col(xx, z_at(step), core)),
        )

    def relays(part):
        for way in range(2):
            for zz in range(SIDE):
                x_out[part][2, way, zz] = image(2, zz, way, part).astype(BF16)
            relay(way, part).start()

    def direct(part):
        for way, d in ((0, 1), (1, 3)):
            for zz in range(SIDE):
                x_out[part][way, 1 - way, zz] = image(d, zz, 1 - way, part).astype(BF16)
            to_x(way, 1 - way, part).start()

    def summed(part):
        for way, d in ((0, 1), (1, 3)):
            images = [image(d, zz, way, part) for zz in range(SIDE)]
            relay(way, part).wait_recv()
            for zz in range(SIDE):
                total = images[zz] + rel_in[part][way, zz].astype(F32)
                x_out[part][way, way, zz] = total.astype(BF16)
            to_x(way, way, part).start()

    def own_sum(part):
        for jj in range(2):
            for zz in range(SIDE):
                keep[part][jj, zz] = image(0, zz, jj, part)

    def from_x(part):
        for jj in range(2):
            for way in (1 - jj, jj):
                to_x(way, jj, part).wait_recv()
                keep[part][jj] = keep[part][jj] + x_in[part][way, jj].astype(F32)
        for step in (2, 3, 1):
            for jj in range(2):
                z_out[part][step - 1, jj] = keep[part][jj, z_at(step)].astype(BF16)
            to_z(step, part).start()

    def finish(part):
        for step in (1, 3, 2):
            to_z(step, part).wait_recv()
        start, rows = PARTS[part]
        for jj in range(2):
            total = keep[part][jj, zl]
            for step in range(1, SIDE):
                total = total + z_in[part][step - 1, jj].astype(F32)
            out[start : start + rows, jj * BLOCK : (jj + 1) * BLOCK] = total.astype(BF16)

    def z_first(step):
        return remote(
            zf_out.at[step - 1],
            zf_in.at[step - 1],
            zf_send.at[step - 1],
            zf_recv.at[step - 1],
            (row, at_col(xx, z_at(step), core)),
        )

    def x_last(d):
        return remote(
            xf_out.at[d - 1],
            xf_in.at[d - 1],
            xf_send.at[d - 1],
            xf_recv.at[d - 1],
            (row, at_col(xx + d, zl, core)),
        )

    def z_first_images():
        for step in (2, 3, 1):
            for d in range(SIDE):
                for jj in range(2):
                    zf_out[step - 1, d, jj] = image(d, z_at(step), jj, ALONG_Z).astype(BF16)
            z_first(step).start()

    def z_first_own():
        for d in range(SIDE):
            for jj in range(2):
                zf_keep[d, jj] = image(d, zl, jj, ALONG_Z)

    def z_first_sum():
        for step in (1, 3, 2):
            z_first(step).wait_recv()
        for d in (2, 1, 3, 0):
            total = zf_keep[d]
            for step in range(1, SIDE):
                total = total + zf_in[step - 1, d].astype(F32)
            if d:
                xf_out[d - 1] = total.astype(BF16)
                x_last(d).start()
            else:
                zf_keep[0] = total

    def z_first_finish():
        for d in range(1, SIDE):
            x_last(d).wait_recv()
        start, rows = PARTS[ALONG_Z]
        for jj in range(2):
            total = zf_keep[0, jj]
            for d in range(1, SIDE):
                total = total + xf_in[d - 1, jj].astype(F32)
            out[start : start + rows, jj * BLOCK : (jj + 1) * BLOCK] = total.astype(BF16)

    w_finish(0)
    w_finish(1)
    to_slots.wait()
    sib_to_slots.wait()
    ket_swap.wait()
    w_swap(0).wait()
    relays(0)
    direct(0)
    w_finish(2)
    w_swap(1).wait()
    z_first_images()
    w_finish(3)
    w_swap(2).wait()
    relays(2)
    summed(0)
    direct(2)
    w_swap(3).wait()
    relays(3)
    summed(2)
    direct(3)
    own_sum(0)
    from_x(0)
    summed(3)
    own_sum(2)
    own_sum(3)
    z_first_own()
    from_x(2)

    @pl.loop(0, 3 * OWN)
    def _(m):
        for family in range(2):
            for way in range(2):
                hop(family, way, m, 0).wait_send()

    for m in range(3 * OWN, last):
        for way in range(2):
            hop(0, way, m, 0).wait_send()
    for place in range(OWN):
        far_side(place).wait_send()
        far_on(place).wait_send()
        to_side(place).wait_send()
        pass_on(place).wait_send()
    for step in range(1, SIDE):
        bra_share(step).wait_send()
    from_x(3)
    z_first_sum()
    finish(0)
    finish(2)
    for part in (0, 2, 3):
        for way in range(2):
            relay(way, part).wait_send()
            for jj in range(2):
                to_x(way, jj, part).wait_send()
        for step in range(1, SIDE):
            to_z(step, part).wait_send()
    for step in range(1, SIDE):
        z_first(step).wait_send()
        x_last(step).wait_send()
    finish(3)
    z_first_finish()


def local(
    basis_centers, bra_pairs, ket_pairs, quartets, quartet_counts, density_owner, density_store
):
    hbm = pl.BlockSpec(memory_space=pltpu.HBM)
    smem, i32 = pltpu.SMEM, jnp.int32
    block, count = (BLOCK, BLOCK), len(PARTS)
    quarter = (PARTS[ALONG_Z][1], BLOCK)

    def parts(lead, kind=BF16):
        return [pltpu.VMEM(lead + (rows, BLOCK), kind) for _, rows in PARTS]

    dma = pltpu.SemaphoreType.DMA
    hops = 3 * OWN + OWN // 2
    return pl.pallas_call(
        body,
        out_shape=jax.ShapeDtypeStruct((BLOCK, 2 * BLOCK), BF16),
        in_specs=[hbm] * 4 + [pl.BlockSpec(memory_space=smem)] + [hbm] * 2,
        out_specs=pl.BlockSpec(memory_space=pltpu.VMEM),
        scratch_shapes=[
            pltpu.VMEM(basis_centers.shape, F32),
            smem(bra_pairs.shape, i32),
            smem(ket_pairs.shape, i32),
            pltpu.VMEM(quartets.shape, i32),
            smem(density_owner.shape, i32),
            pltpu.VMEM((8, BLOCK), i32),
            smem((8, BLOCK), i32),
            pltpu.VMEM((8, BLOCK), i32),
            smem((8, BLOCK), i32),
            pltpu.VMEM((8, BLOCK), i32),
            smem((8, BLOCK), i32),
            dma((9,)),
            pltpu.VMEM((NBLK,) + block, BF16),
            pltpu.VMEM((NBLK, 8, BLOCK), F32),
            pltpu.VMEM((2, 3) + block, F32),
            pltpu.VMEM((PAIRS + 1,) + block, BF16),
            pltpu.VMEM((PAIRS + 1,) + block, BF16),
            pltpu.VMEM((PAIRS + 1,) + block, BF16),
            pltpu.VMEM((2, PAIRS * GROUP, PAIRS * GROUP), BF16),
            pltpu.VMEM((2, PAIRS) + block, F32),
            pltpu.VMEM((PAIRS,) + block, F32),
            parts((PAIRS + 1,)),
            parts((PAIRS + 1,)),
            parts((2, SIDE), F32),
            parts((3, 2, SIDE)),
            parts((2, SIDE)),
            parts((2, 2, SIDE)),
            parts((3, 2)),
            parts((3, 2)),
            pltpu.VMEM((3, SIDE, 2) + quarter, BF16),
            pltpu.VMEM((3, SIDE, 2) + quarter, BF16),
            pltpu.VMEM((SIDE, 2) + quarter, F32),
            pltpu.VMEM((3, 2) + quarter, BF16),
            pltpu.VMEM((3, 2) + quarter, BF16),
            pltpu.VMEM((OWN,) + block, BF16),
            dma((OWN,)),
            dma((OWN,)),
            dma((OWN,)),
            dma((OWN,)),
            pltpu.VMEM((OWN,) + block, BF16),
            dma((2, OWN)),
            dma((2, OWN)),
            dma((2, 2, hops)),
            dma((2, 2, hops)),
            dma((3,)),
            dma((3,)),
            dma((count,)),
            dma((count,)),
            dma((SIDE - 1,)),
            dma((SIDE - 1,)),
            dma((count, 2)),
            dma((count, 2)),
            dma((count, 2, 2)),
            dma((count, 2, 2)),
            dma((count, 3)),
            dma((count, 3)),
            dma((3,)),
            dma((3,)),
            dma((3,)),
            dma((3,)),
        ],
        compiler_params=pltpu.CompilerParams(
            collective_id=0, has_side_effects=True, vmem_limit_bytes=56 * 2**20
        ),
        cost_estimate=pl.CostEstimate(
            flops=2 * 10**9, bytes_accessed=4 * 2**20, transcendentals=4 * 10**6
        ),
    )(
        basis_centers,
        bra_pairs,
        ket_pairs,
        quartets,
        quartet_counts,
        density_owner,
        density_store,
    )


def solution(mesh):
    return jax.shard_map(
        local,
        mesh=mesh,
        in_specs=(
            P(),
            P("bra"),
            P("ket"),
            P("bra", "ket", None, None),
            P("bra", "ket"),
            P("ket", None),
            P("bra", "ket", None),
        ),
        out_specs=P("bra", "ket"),
        check_vma=False,
    )
```

```python
import jax
import jax.numpy as jnp
from jax import lax
from jax.experimental import pallas as pl
from jax.experimental.pallas import tpu as pltpu
from jax.sharding import PartitionSpec as P

OMEGA = 0.11
SOFTEN = 0.25
BLOCK = 128
NBLK = 64
PAIRS = 32
RING = 8
DEEP = 2
SIDE = 4
OWN = 4
PARTS = ((0, 32), (32, 32), (64, 48), (112, 16))
ALONG_Z = 1
GROUP = 8
SHIFT = 3
MESH = pl.DeviceIdType.MESH
F32 = jnp.float32
BF16 = jnp.bfloat16

SLOPE = 0.6 * OMEGA
DECAY = -OMEGA * OMEGA * 1.4426950408889634
ERFC = (
    0.33856715,
    0.33711259,
    0.29264139,
    0.06933287,
    0.29272546,
    -0.65555156,
    0.41918066,
    -0.09400974,
)


def kernel_value(squared):
    inverse = lax.rsqrt(squared)
    divisor = 1.0 + SLOPE * (squared * inverse)
    t = pl.reciprocal(divisor, approx=True)
    t = t * (2.0 - divisor * t)
    poly = ERFC[-1] * t + ERFC[-2]
    for c in ERFC[-3::-1]:
        poly = poly * t + c
    return jnp.exp2(DECAY * squared) * (t * inverse) * poly


def body(
    centers_hbm,
    bra_hbm,
    ket_hbm,
    quartets_hbm,
    count,
    owner_hbm,
    density_hbm,
    out,
    centers,
    bra_pairs,
    ket_pairs,
    quartets,
    owner,
    slots_vmem,
    slots,
    sib_slots_vmem,
    sib_slots,
    places_vmem,
    places,
    fetch,
    gathered,
    lines,
    columns,
    bra_tiles,
    ket_tiles,
    sib_tiles,
    spread,
    product,
    weighted,
    w_own,
    w_sib,
    keep,
    x_out,
    rel_in,
    x_in,
    z_out,
    z_in,
    zf_out,
    zf_in,
    zf_keep,
    xf_out,
    xf_in,
    passing,
    side_send,
    side_recv,
    part_send,
    part_recv,
    ring_send,
    ring_recv,
    sib_send,
    sib_recv,
    swap_send,
    swap_recv,
    share_send,
    share_recv,
    rel_send,
    rel_recv,
    x_send,
    x_recv,
    z_send,
    z_recv,
    zf_send,
    zf_recv,
    xf_send,
    xf_recv,
):
    row = lax.axis_index("bra")
    col = lax.axis_index("ket")
    y, deep = row // DEEP, row % DEEP
    core = col % 2
    zl = (col // 2) % SIDE
    xx = col // (2 * SIDE)

    def at_row(yy, dd):
        return lax.rem(yy + 2 * RING, RING) * DEEP + dd

    def at_col(x_at, z_at, core_at):
        return (lax.rem(x_at + SIDE, SIDE) * SIDE + z_at) * 2 + core_at

    up, down = at_row(y + 1, deep), at_row(y - 1, deep)
    partner = at_row(y, 1 - deep)
    sibling = at_col(xx, zl, 1 - core)
    x_up, x_down = at_col(xx + 1, zl, core), at_col(xx - 1, zl, core)

    def z_at(step):
        return lax.rem(zl + step, SIDE)

    same_side = (row, at_col(xx, z_at(2), core))
    other_side = (partner, at_col(xx, z_at(2), core))
    peers = [(up, col), (down, col), other_side, (row, sibling), (row, x_up), (row, x_down)]
    peers += [(row, at_col(xx, z_at(step), core)) for step in range(1, SIDE)]
    peers += [(row, at_col(xx + 2, zl, core))]
    barrier = pltpu.get_barrier_semaphore()
    for peer in peers:
        pl.semaphore_signal(barrier, inc=1, device_id=peer, device_id_type=MESH)
    own_slots = gathered.at[pl.ds(row * OWN, OWN)]
    sources = (ket_hbm, bra_hbm, centers_hbm, owner_hbm, quartets_hbm, density_hbm)
    targets = (ket_pairs, bra_pairs, centers, owner, quartets, own_slots)
    fetches = [
        pltpu.make_async_copy(src, dst, fetch.at[n])
        for n, (src, dst) in enumerate(zip(sources, targets))
    ]
    for copy in fetches:
        copy.start()
    for tiles in (bra_tiles, ket_tiles, sib_tiles):
        tiles[PAIRS] = jnp.zeros((BLOCK, BLOCK), BF16)
    for part, (_, rows) in enumerate(PARTS):
        w_own[part][PAIRS] = jnp.zeros((rows, BLOCK), BF16)
        w_sib[part][PAIRS] = jnp.zeros((rows, BLOCK), BF16)
    pl.semaphore_wait(barrier, len(peers))

    def remote(src, dst, send, recv, device):
        return pltpu.make_async_remote_copy(
            src_ref=src,
            dst_ref=dst,
            send_sem=send,
            recv_sem=recv,
            device_id=device,
            device_id_type=MESH,
        )

    def to_side(place):
        return remote(
            density_hbm.at[pl.ds(place, 1)],
            passing.at[pl.ds(place, 1)],
            side_send.at[place],
            side_recv.at[place],
            same_side if place < 2 else other_side,
        )

    def pass_on(place):
        origin = row if place < 2 else partner
        return remote(
            passing.at[pl.ds(place, 1)],
            gathered.at[pl.ds(origin * OWN + place, 1)],
            part_send.at[place],
            part_recv.at[place],
            other_side if place < 2 else same_side,
        )

    def from_partner(place):
        ref = gathered.at[pl.ds(partner * OWN + place, 1)]
        device = other_side if place < 2 else same_side
        return remote(ref, ref, part_send.at[place], part_recv.at[place], device)

    for place in (0, 2, 1, 3):
        to_side(place).start()

    def depth(family):
        return deep if family == 0 else 1 - deep

    def hop(family, way, m, arriving, first=False):
        sign = 1 - 2 * way
        back = m // OWN + arriving
        place = lax.rem(m + 2 * way, OWN)
        ref = gathered.at[pl.ds(at_row(y - sign * back, depth(family)) * OWN + place, 1)]
        src = density_hbm.at[pl.ds(place, 1)] if first else ref
        device = (up, col) if way == 0 else (down, col)
        return remote(
            src, ref, ring_send.at[family, way, m], ring_recv.at[family, way, m], device
        )

    last = 3 * OWN + OWN // 2

    def send_own(family, m):
        for way in range(2):
            hop(family, way, m, 0, family == 0).start()

    def arrive(family, m):
        for way in range(2):
            hop(family, way, m, 1).wait_recv()

    def forward(family, m):
        for way in range(2):
            hop(family, way, m - OWN, 1).wait_recv()
            hop(family, way, m, 0).start()

    for m in range(OWN):
        send_own(0, m)
    for copy in fetches[:-1]:
        copy.wait()

    lane = lax.broadcasted_iota(jnp.int32, (8, BLOCK), 1)
    ket_table = jnp.full((8, BLOCK), PAIRS, jnp.int32)
    bra_table = jnp.full((8, BLOCK), PAIRS, jnp.int32)
    for n in range(PAIRS):
        ket_table = jnp.where(lane == ket_pairs[n], n, ket_table)
        bra_table = jnp.where(lane == owner[0, bra_pairs[n]], n, bra_table)
    slots_vmem[...] = ket_table
    places_vmem[...] = bra_table
    to_slots = pltpu.make_async_copy(slots_vmem, slots, fetch.at[len(fetches)])
    to_slots.start()
    to_places = pltpu.make_async_copy(places_vmem, places, fetch.at[len(fetches) + 1])
    to_places.start()
    there = (row, sibling)
    table_swap = remote(slots_vmem, sib_slots_vmem, sib_send.at[0], sib_recv.at[0], there)
    table_swap.start()

    for block in range(NBLK):
        lines[block, 0:3] = centers[:, block * BLOCK : (block + 1) * BLOCK]
    for side, start in ((0, row * (NBLK // 16)), (1, col * (NBLK // 32))):
        line = lines[start]
        for axis in range(3):
            wide = jnp.broadcast_to(line[axis : axis + 1], (BLOCK, BLOCK))
            columns[side, axis] = wide.T

    def tile(side, block, ref, place):
        line = lines[block]
        rows = 32
        for part in range(BLOCK // rows):
            squared = jnp.full((rows, BLOCK), SOFTEN, F32)
            for axis in range(3):
                difference = columns[side, axis, pl.ds(part * rows, rows)] - line[axis : axis + 1]
                squared = squared + difference * difference
            ref[place, pl.ds(part * rows, rows)] = kernel_value(squared).astype(BF16)

    def ket_tile(q):
        tile(1, ket_pairs[q], ket_tiles, q)

    def bra_tile(p):
        tile(0, bra_pairs[p], bra_tiles, p)

    def iota(shape, axis):
        return lax.broadcasted_iota(jnp.int32, shape, axis)

    def hot(condition):
        return jnp.where(condition, jnp.float32(1.0), jnp.float32(0.0)).astype(BF16)

    size = PAIRS * GROUP

    def count_pairs():
        long = (PAIRS, quartets.shape[3])
        bra_hot = hot((quartets[0, 0, 0:1] == iota(long, 0)) & (iota(long, 1) < count[0, 0]))
        ket_hot = hot(quartets[0, 0, 1:2] == iota(long, 0))
        return lax.dot_general(
            ket_hot, bra_hot, (((1,), (1,)), ((), ())), preferred_element_type=F32
        ).astype(BF16)

    def spread_rows(counts):
        by_slot = jnp.dot(
            counts, hot(bra_table[0:1] == iota((PAIRS, BLOCK), 0)), preferred_element_type=F32
        ).astype(BF16)
        tall = hot(iota((size, PAIRS), 0) >> SHIFT == iota((size, PAIRS), 1))
        return jnp.dot(tall, by_slot, preferred_element_type=F32).astype(BF16)

    def spread_family(rows_of, family):
        same = (iota((size, size), 0) ^ iota((size, size), 1)) & (GROUP - 1) == 0
        local_slot = iota((BLOCK, size), 1) >> SHIFT
        row_slot = (local_slot >> 2) * (OWN * DEEP) + (local_slot & (OWN - 1))
        wide = hot(row_slot + depth(family) * OWN == iota((BLOCK, size), 0))
        spread[family] = jnp.where(
            same, jnp.dot(rows_of, wide, preferred_element_type=F32), jnp.float32(0.0)
        ).astype(BF16)

    def z_row(family, yy):
        at = lax.rem(yy + 2 * RING, RING)
        for extra in range(OWN):
            s = (at * DEEP + depth(family)) * OWN + extra
            product[family, at * OWN + extra] = jnp.dot(
                bra_tiles[places[0, s]], gathered[s], preferred_element_type=F32
            )

    def w_part(family, n):
        base = pl.multiple_of(n * 2 * GROUP, 2 * GROUP)
        halves = [
            product[family, :, pl.ds(base + half * GROUP, GROUP), :]
            .reshape(size, BLOCK)
            .astype(BF16)
            for half in range(2)
        ]
        both = jnp.dot(
            spread[family], jnp.concatenate(halves, axis=1), preferred_element_type=F32
        )
        return jnp.concatenate(
            [
                both[:, half * BLOCK : (half + 1) * BLOCK].reshape(PAIRS, GROUP, BLOCK)
                for half in range(2)
            ],
            axis=1,
        )

    def swap_tiles(src, dst, first, total, index):
        return remote(
            src.at[pl.ds(first, total)],
            dst.at[pl.ds(first, total)],
            sib_send.at[index],
            sib_recv.at[index],
            there,
        )

    share = PAIRS // (2 * SIDE)
    mine = core * (PAIRS // 2) + xx * share
    bra_swap = swap_tiles(bra_tiles, bra_tiles, core * (PAIRS // 2), PAIRS // 2, 1)
    ket_swap = swap_tiles(ket_tiles, sib_tiles, 0, PAIRS, 2)

    def bra_share(step):
        tiles = bra_tiles.at[pl.ds(mine, share)]
        return remote(
            tiles,
            tiles,
            share_send.at[step - 1],
            share_recv.at[step - 1],
            (row, at_col(xx + step, zl, core)),
        )

    def bra_shared(step):
        first = core * (PAIRS // 2) + lax.rem(xx - step + SIDE, SIDE) * share
        tiles = bra_tiles.at[pl.ds(first, share)]
        return remote(
            tiles,
            tiles,
            share_send.at[step - 1],
            share_recv.at[step - 1],
            (row, at_col(xx + step, zl, core)),
        )

    def ket_run(first, total):
        @pl.loop(first, first + total)
        def _(q):
            ket_tile(q)

    def w_first(first, total):
        @pl.loop(first, first + total)
        def _(n):
            weighted[:, pl.ds(n * 2 * GROUP, 2 * GROUP)] = w_part(0, n)

    for p in range(share):
        bra_tile(mine + p)
    for step in range(1, SIDE):
        bra_share(step).start()
    for m in range(OWN):
        forward(0, OWN + m)
        if m < 2:
            for place in (m, m + 2):
                to_side(place).wait_recv()
                pass_on(place).start()
        ket_run(2 * m, 2)

    for m in range(OWN):
        forward(0, 2 * OWN + m)
        ket_run(8 + m * 3, 3)
        if m < 2:
            from_partner(m).wait_recv()
            from_partner(m + 2).wait_recv()
        send_own(1, m)
        if m == 0:
            counts = count_pairs()
        elif m == 1:
            rows_of = spread_rows(counts)
        else:
            spread_family(rows_of, m - 2)
    for m in range(2):
        forward(1, OWN + m)
        ket_run(20 + m * 6, 3)
        forward(0, 3 * OWN + m)
        if m == 0:
            for step in range(1, SIDE):
                bra_shared(step).wait_recv()
            bra_swap.start()
        ket_run(23 + m * 6, 3)
    ket_swap.start()
    bra_swap.wait()
    to_places.wait()
    fetches[-1].wait()
    forward(1, OWN + 2)
    z_row(0, y)
    z_row(0, y - 1)
    forward(1, OWN + 3)
    z_row(0, y + 1)
    z_row(0, y - 2)
    forward(1, 2 * OWN)
    z_row(0, y + 2)
    arrive(0, last - 4)
    arrive(0, last - 3)
    z_row(0, y - 3)
    forward(1, 2 * OWN + 1)
    z_row(0, y + 3)
    arrive(0, last - 2)
    arrive(0, last - 1)
    z_row(0, y + 4)
    forward(1, 2 * OWN + 2)
    w_first(0, 3)
    forward(1, 2 * OWN + 3)
    w_first(3, 2)
    forward(1, 3 * OWN)
    w_first(5, 1)
    forward(1, 3 * OWN + 1)
    w_first(6, 2)
    for away in (0, 1, -1, 2, -2):
        z_row(1, y + away)
    arrive(1, last - 4)
    arrive(1, last - 3)
    z_row(1, y - 3)
    z_row(1, y + 3)
    table_swap.wait()
    sib_to_slots = pltpu.make_async_copy(sib_slots_vmem, sib_slots, fetch.at[len(fetches) + 2])
    sib_to_slots.start()
    arrive(1, last - 2)
    arrive(1, last - 1)
    z_row(1, y + 4)

    def w_swap(part):
        return remote(
            w_own[part].at[pl.ds(0, PAIRS)],
            w_sib[part].at[pl.ds(0, PAIRS)],
            swap_send.at[part],
            swap_recv.at[part],
            there,
        )

    def w_finish(part):
        start, rows = PARTS[part]

        @pl.loop(0, rows // (2 * GROUP))
        def _(n):
            at = pl.multiple_of(n * 2 * GROUP, 2 * GROUP)
            total = w_part(1, n + start // (2 * GROUP))
            total = total + weighted[:, pl.ds(at + start, 2 * GROUP)]
            w_own[part][0:PAIRS, pl.ds(at, 2 * GROUP)] = total.astype(BF16)

        w_swap(part).start()

    def image(d, zz, jj, part):
        j = (lax.rem(xx + d, SIDE) * SIDE + zz) * 4 + core * 2 + jj
        a, b = slots[0, j], sib_slots[0, j]
        left = jnp.concatenate([w_own[part][a], w_sib[part][b]], axis=1)
        right = jnp.concatenate([ket_tiles[a], sib_tiles[b]], axis=0)
        return jnp.dot(left, right, preferred_element_type=F32)

    def relay(way, part):
        device = (row, x_up) if way == 0 else (row, x_down)
        return remote(
            x_out[part].at[2, way],
            rel_in[part].at[way],
            rel_send.at[part, way],
            rel_recv.at[part, way],
            device,
        )

    def to_x(way, jj, part):
        device = (row, x_up) if way == 0 else (row, x_down)
        return remote(
            x_out[part].at[way, jj],
            x_in[part].at[way, jj],
            x_send.at[part, way, jj],
            x_recv.at[part, way, jj],
            device,
        )

    def to_z(step, part):
        return remote(
            z_out[part].at[step - 1],
            z_in[part].at[step - 1],
            z_send.at[part, step - 1],
            z_recv.at[part, step - 1],
            (row, at_col(xx, z_at(step), core)),
        )

    def relays(part):
        for way in range(2):
            for zz in range(SIDE):
                x_out[part][2, way, zz] = image(2, zz, way, part).astype(BF16)
            relay(way, part).start()

    def direct(part):
        for way, d in ((0, 1), (1, 3)):
            for zz in range(SIDE):
                x_out[part][way, 1 - way, zz] = image(d, zz, 1 - way, part).astype(BF16)
            to_x(way, 1 - way, part).start()

    def summed(part):
        for way, d in ((0, 1), (1, 3)):
            images = [image(d, zz, way, part) for zz in range(SIDE)]
            relay(way, part).wait_recv()
            for zz in range(SIDE):
                total = images[zz] + rel_in[part][way, zz].astype(F32)
                x_out[part][way, way, zz] = total.astype(BF16)
            to_x(way, way, part).start()

    def own_sum(part):
        for jj in range(2):
            for zz in range(SIDE):
                keep[part][jj, zz] = image(0, zz, jj, part)

    def from_x(part):
        for jj in range(2):
            for way in (1 - jj, jj):
                to_x(way, jj, part).wait_recv()
                keep[part][jj] = keep[part][jj] + x_in[part][way, jj].astype(F32)
        for step in (2, 3, 1):
            for jj in range(2):
                z_out[part][step - 1, jj] = keep[part][jj, z_at(step)].astype(BF16)
            to_z(step, part).start()

    def finish(part):
        for step in (1, 3, 2):
            to_z(step, part).wait_recv()
        start, rows = PARTS[part]
        for jj in range(2):
            total = keep[part][jj, zl]
            for step in range(1, SIDE):
                total = total + z_in[part][step - 1, jj].astype(F32)
            out[start : start + rows, jj * BLOCK : (jj + 1) * BLOCK] = total.astype(BF16)

    def z_first(step):
        return remote(
            zf_out.at[step - 1],
            zf_in.at[step - 1],
            zf_send.at[step - 1],
            zf_recv.at[step - 1],
            (row, at_col(xx, z_at(step), core)),
        )

    def x_last(d):
        return remote(
            xf_out.at[d - 1],
            xf_in.at[d - 1],
            xf_send.at[d - 1],
            xf_recv.at[d - 1],
            (row, at_col(xx + d, zl, core)),
        )

    def z_first_images():
        for step in (2, 3, 1):
            for d in range(SIDE):
                for jj in range(2):
                    zf_out[step - 1, d, jj] = image(d, z_at(step), jj, ALONG_Z).astype(BF16)
            z_first(step).start()

    def z_first_own():
        for d in range(SIDE):
            for jj in range(2):
                zf_keep[d, jj] = image(d, zl, jj, ALONG_Z)

    def z_first_sum():
        for step in (1, 3, 2):
            z_first(step).wait_recv()
        for d in (2, 1, 3, 0):
            total = zf_keep[d]
            for step in range(1, SIDE):
                total = total + zf_in[step - 1, d].astype(F32)
            if d:
                xf_out[d - 1] = total.astype(BF16)
                x_last(d).start()
            else:
                zf_keep[0] = total

    def z_first_finish():
        for d in range(1, SIDE):
            x_last(d).wait_recv()
        start, rows = PARTS[ALONG_Z]
        for jj in range(2):
            total = zf_keep[0, jj]
            for d in range(1, SIDE):
                total = total + xf_in[d - 1, jj].astype(F32)
            out[start : start + rows, jj * BLOCK : (jj + 1) * BLOCK] = total.astype(BF16)

    w_finish(0)
    w_finish(1)
    to_slots.wait()
    sib_to_slots.wait()
    ket_swap.wait()
    w_swap(0).wait()
    relays(0)
    direct(0)
    w_finish(2)
    w_swap(1).wait()
    z_first_images()
    w_finish(3)
    w_swap(2).wait()
    relays(2)
    summed(0)
    direct(2)
    w_swap(3).wait()
    relays(3)
    summed(2)
    direct(3)
    own_sum(0)
    from_x(0)
    summed(3)
    own_sum(2)
    own_sum(3)
    z_first_own()
    from_x(2)

    @pl.loop(0, last)
    def _(m):
        for family in range(2):
            for way in range(2):
                hop(family, way, m, 0).wait_send()

    for place in range(OWN):
        to_side(place).wait_send()
        pass_on(place).wait_send()
    for step in range(1, SIDE):
        bra_share(step).wait_send()
    from_x(3)
    z_first_sum()
    finish(0)
    finish(2)
    for part in (0, 2, 3):
        for way in range(2):
            relay(way, part).wait_send()
            for jj in range(2):
                to_x(way, jj, part).wait_send()
        for step in range(1, SIDE):
            to_z(step, part).wait_send()
    for step in range(1, SIDE):
        z_first(step).wait_send()
        x_last(step).wait_send()
    finish(3)
    z_first_finish()


def local(
    basis_centers, bra_pairs, ket_pairs, quartets, quartet_counts, density_owner, density_store
):
    hbm = pl.BlockSpec(memory_space=pltpu.HBM)
    smem, i32 = pltpu.SMEM, jnp.int32
    block, count = (BLOCK, BLOCK), len(PARTS)
    quarter = (PARTS[ALONG_Z][1], BLOCK)

    def parts(lead, kind=BF16):
        return [pltpu.VMEM(lead + (rows, BLOCK), kind) for _, rows in PARTS]

    dma = pltpu.SemaphoreType.DMA
    hops = 3 * OWN + OWN // 2
    return pl.pallas_call(
        body,
        out_shape=jax.ShapeDtypeStruct((BLOCK, 2 * BLOCK), BF16),
        in_specs=[hbm] * 4 + [pl.BlockSpec(memory_space=smem)] + [hbm] * 2,
        out_specs=pl.BlockSpec(memory_space=pltpu.VMEM),
        scratch_shapes=[
            pltpu.VMEM(basis_centers.shape, F32),
            smem(bra_pairs.shape, i32),
            smem(ket_pairs.shape, i32),
            pltpu.VMEM(quartets.shape, i32),
            smem(density_owner.shape, i32),
            pltpu.VMEM((8, BLOCK), i32),
            smem((8, BLOCK), i32),
            pltpu.VMEM((8, BLOCK), i32),
            smem((8, BLOCK), i32),
            pltpu.VMEM((8, BLOCK), i32),
            smem((8, BLOCK), i32),
            dma((9,)),
            pltpu.VMEM((NBLK,) + block, BF16),
            pltpu.VMEM((NBLK, 8, BLOCK), F32),
            pltpu.VMEM((2, 3) + block, F32),
            pltpu.VMEM((PAIRS + 1,) + block, BF16),
            pltpu.VMEM((PAIRS + 1,) + block, BF16),
            pltpu.VMEM((PAIRS + 1,) + block, BF16),
            pltpu.VMEM((2, PAIRS * GROUP, PAIRS * GROUP), BF16),
            pltpu.VMEM((2, PAIRS) + block, F32),
            pltpu.VMEM((PAIRS,) + block, F32),
            parts((PAIRS + 1,)),
            parts((PAIRS + 1,)),
            parts((2, SIDE), F32),
            parts((3, 2, SIDE)),
            parts((2, SIDE)),
            parts((2, 2, SIDE)),
            parts((3, 2)),
            parts((3, 2)),
            pltpu.VMEM((3, SIDE, 2) + quarter, BF16),
            pltpu.VMEM((3, SIDE, 2) + quarter, BF16),
            pltpu.VMEM((SIDE, 2) + quarter, F32),
            pltpu.VMEM((3, 2) + quarter, BF16),
            pltpu.VMEM((3, 2) + quarter, BF16),
            pltpu.VMEM((OWN,) + block, BF16),
            dma((OWN,)),
            dma((OWN,)),
            dma((OWN,)),
            dma((OWN,)),
            dma((2, 2, hops)),
            dma((2, 2, hops)),
            dma((3,)),
            dma((3,)),
            dma((count,)),
            dma((count,)),
            dma((SIDE - 1,)),
            dma((SIDE - 1,)),
            dma((count, 2)),
            dma((count, 2)),
            dma((count, 2, 2)),
            dma((count, 2, 2)),
            dma((count, 3)),
            dma((count, 3)),
            dma((3,)),
            dma((3,)),
            dma((3,)),
            dma((3,)),
        ],
        compiler_params=pltpu.CompilerParams(
            collective_id=0, has_side_effects=True, vmem_limit_bytes=56 * 2**20
        ),
        cost_estimate=pl.CostEstimate(
            flops=2 * 10**9, bytes_accessed=4 * 2**20, transcendentals=4 * 10**6
        ),
    )(
        basis_centers,
        bra_pairs,
        ket_pairs,
        quartets,
        quartet_counts,
        density_owner,
        density_store,
    )


def solution(mesh):
    return jax.shard_map(
        local,
        mesh=mesh,
        in_specs=(
            P(),
            P("bra"),
            P("ket"),
            P("bra", "ket", None, None),
            P("bra", "ket"),
            P("ket", None),
            P("bra", "ket", None),
        ),
        out_specs=P("bra", "ket"),
        check_vma=False,
    )
```

```python
import jax
import jax.numpy as jnp
from jax import lax
from jax.experimental import pallas as pl
from jax.experimental.pallas import tpu as pltpu
from jax.sharding import PartitionSpec as P

OMEGA = 0.11
SOFTEN = 0.25
BLOCK = 128
NBLK = 64
PAIRS = 32
RING = 8
DEEP = 2
SIDE = 4
OWN = 4
PARTS = ((0, 32), (32, 16), (48, 48), (96, 32))
ALONG_Z = 1
GROUP = 8
SHIFT = 3
MESH = pl.DeviceIdType.MESH
F32 = jnp.float32
BF16 = jnp.bfloat16

SLOPE = 0.6 * OMEGA
DECAY = -OMEGA * OMEGA * 1.4426950408889634
ERFC = (
    0.33856715,
    0.33711259,
    0.29264139,
    0.06933287,
    0.29272546,
    -0.65555156,
    0.41918066,
    -0.09400974,
)


def kernel_value(squared):
    inverse = lax.rsqrt(squared)
    divisor = 1.0 + SLOPE * (squared * inverse)
    t = pl.reciprocal(divisor, approx=True)
    t = t * (2.0 - divisor * t)
    poly = ERFC[-1] * t + ERFC[-2]
    for c in ERFC[-3::-1]:
        poly = poly * t + c
    return jnp.exp2(DECAY * squared) * (t * inverse) * poly


def body(
    centers_hbm,
    bra_hbm,
    ket_hbm,
    quartets_hbm,
    count,
    owner_hbm,
    density_hbm,
    out,
    centers,
    bra_pairs,
    ket_pairs,
    quartets,
    owner,
    slots_vmem,
    slots,
    sib_slots_vmem,
    sib_slots,
    places_vmem,
    places,
    fetch,
    gathered,
    lines,
    columns,
    bra_tiles,
    ket_tiles,
    sib_tiles,
    spread,
    product,
    weighted,
    w_own,
    w_sib,
    keep,
    x_out,
    rel_in,
    x_in,
    z_out,
    z_in,
    zf_out,
    zf_in,
    zf_keep,
    xf_out,
    xf_in,
    passing,
    side_send,
    side_recv,
    part_send,
    part_recv,
    ring_send,
    ring_recv,
    sib_send,
    sib_recv,
    swap_send,
    swap_recv,
    share_send,
    share_recv,
    rel_send,
    rel_recv,
    x_send,
    x_recv,
    z_send,
    z_recv,
    zf_send,
    zf_recv,
    xf_send,
    xf_recv,
):
    row = lax.axis_index("bra")
    col = lax.axis_index("ket")
    y, deep = row // DEEP, row % DEEP
    core = col % 2
    zl = (col // 2) % SIDE
    xx = col // (2 * SIDE)

    def at_row(yy, dd):
        return lax.rem(yy + 2 * RING, RING) * DEEP + dd

    def at_col(x_at, z_at, core_at):
        return (lax.rem(x_at + SIDE, SIDE) * SIDE + z_at) * 2 + core_at

    up, down = at_row(y + 1, deep), at_row(y - 1, deep)
    partner = at_row(y, 1 - deep)
    sibling = at_col(xx, zl, 1 - core)
    x_up, x_down = at_col(xx + 1, zl, core), at_col(xx - 1, zl, core)

    def z_at(step):
        return lax.rem(zl + step, SIDE)

    same_side = (row, at_col(xx, z_at(2), core))
    other_side = (partner, at_col(xx, z_at(2), core))
    peers = [(up, col), (down, col), other_side, (row, sibling), (row, x_up), (row, x_down)]
    peers += [(row, at_col(xx, z_at(step), core)) for step in range(1, SIDE)]
    peers += [(row, at_col(xx + 2, zl, core))]
    barrier = pltpu.get_barrier_semaphore()
    for peer in peers:
        pl.semaphore_signal(barrier, inc=1, device_id=peer, device_id_type=MESH)
    own_slots = gathered.at[pl.ds(row * OWN, OWN)]
    sources = (ket_hbm, bra_hbm, centers_hbm, owner_hbm, quartets_hbm, density_hbm)
    targets = (ket_pairs, bra_pairs, centers, owner, quartets, own_slots)
    fetches = [
        pltpu.make_async_copy(src, dst, fetch.at[n])
        for n, (src, dst) in enumerate(zip(sources, targets))
    ]
    for copy in fetches:
        copy.start()
    for tiles in (bra_tiles, ket_tiles, sib_tiles):
        tiles[PAIRS] = jnp.zeros((BLOCK, BLOCK), BF16)
    for part, (_, rows) in enumerate(PARTS):
        w_own[part][PAIRS] = jnp.zeros((rows, BLOCK), BF16)
        w_sib[part][PAIRS] = jnp.zeros((rows, BLOCK), BF16)
    pl.semaphore_wait(barrier, len(peers))

    def remote(src, dst, send, recv, device):
        return pltpu.make_async_remote_copy(
            src_ref=src,
            dst_ref=dst,
            send_sem=send,
            recv_sem=recv,
            device_id=device,
            device_id_type=MESH,
        )

    def to_side(place):
        return remote(
            density_hbm.at[pl.ds(place, 1)],
            passing.at[pl.ds(place, 1)],
            side_send.at[place],
            side_recv.at[place],
            same_side if place < 2 else other_side,
        )

    def pass_on(place):
        origin = row if place < 2 else partner
        return remote(
            passing.at[pl.ds(place, 1)],
            gathered.at[pl.ds(origin * OWN + place, 1)],
            part_send.at[place],
            part_recv.at[place],
            other_side if place < 2 else same_side,
        )

    def from_partner(place):
        ref = gathered.at[pl.ds(partner * OWN + place, 1)]
        device = other_side if place < 2 else same_side
        return remote(ref, ref, part_send.at[place], part_recv.at[place], device)

    for place in (0, 2, 1, 3):
        to_side(place).start()

    def depth(family):
        return deep if family == 0 else 1 - deep

    def hop(family, way, m, arriving, first=False):
        sign = 1 - 2 * way
        back = m // OWN + arriving
        place = lax.rem(m + 2 * way, OWN)
        ref = gathered.at[pl.ds(at_row(y - sign * back, depth(family)) * OWN + place, 1)]
        src = density_hbm.at[pl.ds(place, 1)] if first else ref
        device = (up, col) if way == 0 else (down, col)
        return remote(
            src, ref, ring_send.at[family, way, m], ring_recv.at[family, way, m], device
        )

    last = 3 * OWN + OWN // 2

    def send_own(family, m):
        for way in range(2):
            hop(family, way, m, 0, family == 0).start()

    def arrive(family, m):
        for way in range(2):
            hop(family, way, m, 1).wait_recv()

    def forward(family, m):
        for way in range(2):
            hop(family, way, m - OWN, 1).wait_recv()
            hop(family, way, m, 0).start()

    for m in range(OWN):
        send_own(0, m)
    for copy in fetches[:-1]:
        copy.wait()

    lane = lax.broadcasted_iota(jnp.int32, (8, BLOCK), 1)
    ket_table = jnp.full((8, BLOCK), PAIRS, jnp.int32)
    bra_table = jnp.full((8, BLOCK), PAIRS, jnp.int32)
    for n in range(PAIRS):
        ket_table = jnp.where(lane == ket_pairs[n], n, ket_table)
        bra_table = jnp.where(lane == owner[0, bra_pairs[n]], n, bra_table)
    slots_vmem[...] = ket_table
    places_vmem[...] = bra_table
    to_slots = pltpu.make_async_copy(slots_vmem, slots, fetch.at[len(fetches)])
    to_slots.start()
    to_places = pltpu.make_async_copy(places_vmem, places, fetch.at[len(fetches) + 1])
    to_places.start()
    there = (row, sibling)
    table_swap = remote(slots_vmem, sib_slots_vmem, sib_send.at[0], sib_recv.at[0], there)
    table_swap.start()

    for block in range(NBLK):
        lines[block, 0:3] = centers[:, block * BLOCK : (block + 1) * BLOCK]
    for side, start in ((0, row * (NBLK // 16)), (1, col * (NBLK // 32))):
        line = lines[start]
        for axis in range(3):
            wide = jnp.broadcast_to(line[axis : axis + 1], (BLOCK, BLOCK))
            columns[side, axis] = wide.T

    def tile(side, block, ref, place):
        line = lines[block]
        rows = 32
        for part in range(BLOCK // rows):
            squared = jnp.full((rows, BLOCK), SOFTEN, F32)
            for axis in range(3):
                difference = columns[side, axis, pl.ds(part * rows, rows)] - line[axis : axis + 1]
                squared = squared + difference * difference
            ref[place, pl.ds(part * rows, rows)] = kernel_value(squared).astype(BF16)

    def ket_tile(q):
        tile(1, ket_pairs[q], ket_tiles, q)

    def bra_tile(p):
        tile(0, bra_pairs[p], bra_tiles, p)

    def iota(shape, axis):
        return lax.broadcasted_iota(jnp.int32, shape, axis)

    def hot(condition):
        return jnp.where(condition, jnp.float32(1.0), jnp.float32(0.0)).astype(BF16)

    size = PAIRS * GROUP

    def count_pairs():
        long = (PAIRS, quartets.shape[3])
        bra_hot = hot((quartets[0, 0, 0:1] == iota(long, 0)) & (iota(long, 1) < count[0, 0]))
        ket_hot = hot(quartets[0, 0, 1:2] == iota(long, 0))
        return lax.dot_general(
            ket_hot, bra_hot, (((1,), (1,)), ((), ())), preferred_element_type=F32
        ).astype(BF16)

    def spread_rows(counts):
        by_slot = jnp.dot(
            counts, hot(bra_table[0:1] == iota((PAIRS, BLOCK), 0)), preferred_element_type=F32
        ).astype(BF16)
        tall = hot(iota((size, PAIRS), 0) >> SHIFT == iota((size, PAIRS), 1))
        return jnp.dot(tall, by_slot, preferred_element_type=F32).astype(BF16)

    def spread_family(rows_of, family):
        same = (iota((size, size), 0) ^ iota((size, size), 1)) & (GROUP - 1) == 0
        local_slot = iota((BLOCK, size), 1) >> SHIFT
        row_slot = (local_slot >> 2) * (OWN * DEEP) + (local_slot & (OWN - 1))
        wide = hot(row_slot + depth(family) * OWN == iota((BLOCK, size), 0))
        spread[family] = jnp.where(
            same, jnp.dot(rows_of, wide, preferred_element_type=F32), jnp.float32(0.0)
        ).astype(BF16)

    def z_row(family, yy):
        at = lax.rem(yy + 2 * RING, RING)
        for extra in range(OWN):
            s = (at * DEEP + depth(family)) * OWN + extra
            product[family, at * OWN + extra] = jnp.dot(
                bra_tiles[places[0, s]], gathered[s], preferred_element_type=F32
            )

    def w_part(family, n):
        base = pl.multiple_of(n * 2 * GROUP, 2 * GROUP)
        halves = [
            product[family, :, pl.ds(base + half * GROUP, GROUP), :]
            .reshape(size, BLOCK)
            .astype(BF16)
            for half in range(2)
        ]
        both = jnp.dot(
            spread[family], jnp.concatenate(halves, axis=1), preferred_element_type=F32
        )
        return jnp.concatenate(
            [
                both[:, half * BLOCK : (half + 1) * BLOCK].reshape(PAIRS, GROUP, BLOCK)
                for half in range(2)
            ],
            axis=1,
        )

    def swap_tiles(src, dst, first, total, index):
        return remote(
            src.at[pl.ds(first, total)],
            dst.at[pl.ds(first, total)],
            sib_send.at[index],
            sib_recv.at[index],
            there,
        )

    share = PAIRS // (2 * SIDE)
    mine = core * (PAIRS // 2) + xx * share
    bra_swap = swap_tiles(bra_tiles, bra_tiles, core * (PAIRS // 2), PAIRS // 2, 1)
    ket_swap = swap_tiles(ket_tiles, sib_tiles, 0, PAIRS, 2)

    def bra_share(step):
        tiles = bra_tiles.at[pl.ds(mine, share)]
        return remote(
            tiles,
            tiles,
            share_send.at[step - 1],
            share_recv.at[step - 1],
            (row, at_col(xx + step, zl, core)),
        )

    def bra_shared(step):
        first = core * (PAIRS // 2) + lax.rem(xx - step + SIDE, SIDE) * share
        tiles = bra_tiles.at[pl.ds(first, share)]
        return remote(
            tiles,
            tiles,
            share_send.at[step - 1],
            share_recv.at[step - 1],
            (row, at_col(xx + step, zl, core)),
        )

    def ket_run(first, total):
        @pl.loop(first, first + total)
        def _(q):
            ket_tile(q)

    def w_first(first, total):
        @pl.loop(first, first + total)
        def _(n):
            weighted[:, pl.ds(n * 2 * GROUP, 2 * GROUP)] = w_part(0, n)

    for p in range(share):
        bra_tile(mine + p)
    for step in range(1, SIDE):
        bra_share(step).start()
    for m in range(OWN):
        forward(0, OWN + m)
        if m < 2:
            for place in (m, m + 2):
                to_side(place).wait_recv()
                pass_on(place).start()
        ket_run(2 * m, 2)

    for m in range(OWN):
        forward(0, 2 * OWN + m)
        ket_run(8 + m * 3, 3)
        if m < 2:
            from_partner(m).wait_recv()
            from_partner(m + 2).wait_recv()
        send_own(1, m)
        if m == 0:
            counts = count_pairs()
        elif m == 1:
            rows_of = spread_rows(counts)
        else:
            spread_family(rows_of, m - 2)
    for m in range(2):
        forward(1, OWN + m)
        ket_run(20 + m * 6, 3)
        forward(0, 3 * OWN + m)
        if m == 0:
            for step in range(1, SIDE):
                bra_shared(step).wait_recv()
            bra_swap.start()
        ket_run(23 + m * 6, 3)
    ket_swap.start()
    bra_swap.wait()
    to_places.wait()
    fetches[-1].wait()
    forward(1, OWN + 2)
    z_row(0, y)
    z_row(0, y - 1)
    forward(1, OWN + 3)
    z_row(0, y + 1)
    z_row(0, y - 2)
    forward(1, 2 * OWN)
    z_row(0, y + 2)
    arrive(0, last - 4)
    arrive(0, last - 3)
    z_row(0, y - 3)
    forward(1, 2 * OWN + 1)
    z_row(0, y + 3)
    arrive(0, last - 2)
    arrive(0, last - 1)
    z_row(0, y + 4)
    forward(1, 2 * OWN + 2)
    w_first(0, 3)
    forward(1, 2 * OWN + 3)
    w_first(3, 2)
    forward(1, 3 * OWN)
    w_first(5, 1)
    forward(1, 3 * OWN + 1)
    w_first(6, 2)
    for away in (0, 1, -1, 2, -2):
        z_row(1, y + away)
    arrive(1, last - 4)
    arrive(1, last - 3)
    z_row(1, y - 3)
    z_row(1, y + 3)
    table_swap.wait()
    sib_to_slots = pltpu.make_async_copy(sib_slots_vmem, sib_slots, fetch.at[len(fetches) + 2])
    sib_to_slots.start()
    arrive(1, last - 2)
    arrive(1, last - 1)
    z_row(1, y + 4)

    def w_swap(part):
        return remote(
            w_own[part].at[pl.ds(0, PAIRS)],
            w_sib[part].at[pl.ds(0, PAIRS)],
            swap_send.at[part],
            swap_recv.at[part],
            there,
        )

    def w_finish(part):
        start, rows = PARTS[part]

        @pl.loop(0, rows // (2 * GROUP))
        def _(n):
            at = pl.multiple_of(n * 2 * GROUP, 2 * GROUP)
            total = w_part(1, n + start // (2 * GROUP))
            total = total + weighted[:, pl.ds(at + start, 2 * GROUP)]
            w_own[part][0:PAIRS, pl.ds(at, 2 * GROUP)] = total.astype(BF16)

        w_swap(part).start()

    def image(d, zz, jj, part):
        j = (lax.rem(xx + d, SIDE) * SIDE + zz) * 4 + core * 2 + jj
        a, b = slots[0, j], sib_slots[0, j]
        left = jnp.concatenate([w_own[part][a], w_sib[part][b]], axis=1)
        right = jnp.concatenate([ket_tiles[a], sib_tiles[b]], axis=0)
        return jnp.dot(left, right, preferred_element_type=F32)

    def relay(way, part):
        device = (row, x_up) if way == 0 else (row, x_down)
        return remote(
            x_out[part].at[2, way],
            rel_in[part].at[way],
            rel_send.at[part, way],
            rel_recv.at[part, way],
            device,
        )

    def to_x(way, jj, part):
        device = (row, x_up) if way == 0 else (row, x_down)
        return remote(
            x_out[part].at[way, jj],
            x_in[part].at[way, jj],
            x_send.at[part, way, jj],
            x_recv.at[part, way, jj],
            device,
        )

    def to_z(step, part):
        return remote(
            z_out[part].at[step - 1],
            z_in[part].at[step - 1],
            z_send.at[part, step - 1],
            z_recv.at[part, step - 1],
            (row, at_col(xx, z_at(step), core)),
        )

    def relays(part):
        for way in range(2):
            for zz in range(SIDE):
                x_out[part][2, way, zz] = image(2, zz, way, part).astype(BF16)
            relay(way, part).start()

    def direct(part):
        for way, d in ((0, 1), (1, 3)):
            for zz in range(SIDE):
                x_out[part][way, 1 - way, zz] = image(d, zz, 1 - way, part).astype(BF16)
            to_x(way, 1 - way, part).start()

    def summed(part):
        for way, d in ((0, 1), (1, 3)):
            images = [image(d, zz, way, part) for zz in range(SIDE)]
            relay(way, part).wait_recv()
            for zz in range(SIDE):
                total = images[zz] + rel_in[part][way, zz].astype(F32)
                x_out[part][way, way, zz] = total.astype(BF16)
            to_x(way, way, part).start()

    def own_sum(part):
        for jj in range(2):
            for zz in range(SIDE):
                keep[part][jj, zz] = image(0, zz, jj, part)

    def from_x(part):
        for jj in range(2):
            for way in (1 - jj, jj):
                to_x(way, jj, part).wait_recv()
                keep[part][jj] = keep[part][jj] + x_in[part][way, jj].astype(F32)
        for step in (2, 3, 1):
            for jj in range(2):
                z_out[part][step - 1, jj] = keep[part][jj, z_at(step)].astype(BF16)
            to_z(step, part).start()

    def finish(part):
        for step in (1, 3, 2):
            to_z(step, part).wait_recv()
        start, rows = PARTS[part]
        for jj in range(2):
            total = keep[part][jj, zl]
            for step in range(1, SIDE):
                total = total + z_in[part][step - 1, jj].astype(F32)
            out[start : start + rows, jj * BLOCK : (jj + 1) * BLOCK] = total.astype(BF16)

    def z_first(step):
        return remote(
            zf_out.at[step - 1],
            zf_in.at[step - 1],
            zf_send.at[step - 1],
            zf_recv.at[step - 1],
            (row, at_col(xx, z_at(step), core)),
        )

    def x_last(d):
        return remote(
            xf_out.at[d - 1],
            xf_in.at[d - 1],
            xf_send.at[d - 1],
            xf_recv.at[d - 1],
            (row, at_col(xx + d, zl, core)),
        )

    def z_first_images():
        for step in (2, 3, 1):
            for d in range(SIDE):
                for jj in range(2):
                    zf_out[step - 1, d, jj] = image(d, z_at(step), jj, ALONG_Z).astype(BF16)
            z_first(step).start()

    def z_first_own():
        for d in range(SIDE):
            for jj in range(2):
                zf_keep[d, jj] = image(d, zl, jj, ALONG_Z)

    def z_first_sum():
        for step in (1, 3, 2):
            z_first(step).wait_recv()
        for d in (2, 1, 3, 0):
            total = zf_keep[d]
            for step in range(1, SIDE):
                total = total + zf_in[step - 1, d].astype(F32)
            if d:
                xf_out[d - 1] = total.astype(BF16)
                x_last(d).start()
            else:
                zf_keep[0] = total

    def z_first_finish():
        for d in range(1, SIDE):
            x_last(d).wait_recv()
        start, rows = PARTS[ALONG_Z]
        for jj in range(2):
            total = zf_keep[0, jj]
            for d in range(1, SIDE):
                total = total + xf_in[d - 1, jj].astype(F32)
            out[start : start + rows, jj * BLOCK : (jj + 1) * BLOCK] = total.astype(BF16)

    w_finish(0)
    w_finish(1)
    to_slots.wait()
    sib_to_slots.wait()
    ket_swap.wait()
    w_swap(0).wait()
    relays(0)
    direct(0)
    w_finish(2)
    w_swap(1).wait()
    z_first_images()
    w_finish(3)
    w_swap(2).wait()
    relays(2)
    summed(0)
    direct(2)
    w_swap(3).wait()
    relays(3)
    summed(2)
    direct(3)
    own_sum(0)
    from_x(0)
    summed(3)
    own_sum(2)
    own_sum(3)
    z_first_own()
    from_x(2)

    @pl.loop(0, last)
    def _(m):
        for family in range(2):
            for way in range(2):
                hop(family, way, m, 0).wait_send()

    for place in range(OWN):
        to_side(place).wait_send()
        pass_on(place).wait_send()
    for step in range(1, SIDE):
        bra_share(step).wait_send()
    from_x(3)
    z_first_sum()
    finish(0)
    finish(2)
    for part in (0, 2, 3):
        for way in range(2):
            relay(way, part).wait_send()
            for jj in range(2):
                to_x(way, jj, part).wait_send()
        for step in range(1, SIDE):
            to_z(step, part).wait_send()
    for step in range(1, SIDE):
        z_first(step).wait_send()
        x_last(step).wait_send()
    finish(3)
    z_first_finish()


def local(
    basis_centers, bra_pairs, ket_pairs, quartets, quartet_counts, density_owner, density_store
):
    hbm = pl.BlockSpec(memory_space=pltpu.HBM)
    smem, i32 = pltpu.SMEM, jnp.int32
    block, count = (BLOCK, BLOCK), len(PARTS)
    quarter = (PARTS[ALONG_Z][1], BLOCK)

    def parts(lead, kind=BF16):
        return [pltpu.VMEM(lead + (rows, BLOCK), kind) for _, rows in PARTS]

    dma = pltpu.SemaphoreType.DMA
    hops = 3 * OWN + OWN // 2
    return pl.pallas_call(
        body,
        out_shape=jax.ShapeDtypeStruct((BLOCK, 2 * BLOCK), BF16),
        in_specs=[hbm] * 4 + [pl.BlockSpec(memory_space=smem)] + [hbm] * 2,
        out_specs=pl.BlockSpec(memory_space=pltpu.VMEM),
        scratch_shapes=[
            pltpu.VMEM(basis_centers.shape, F32),
            smem(bra_pairs.shape, i32),
            smem(ket_pairs.shape, i32),
            pltpu.VMEM(quartets.shape, i32),
            smem(density_owner.shape, i32),
            pltpu.VMEM((8, BLOCK), i32),
            smem((8, BLOCK), i32),
            pltpu.VMEM((8, BLOCK), i32),
            smem((8, BLOCK), i32),
            pltpu.VMEM((8, BLOCK), i32),
            smem((8, BLOCK), i32),
            dma((9,)),
            pltpu.VMEM((NBLK,) + block, BF16),
            pltpu.VMEM((NBLK, 8, BLOCK), F32),
            pltpu.VMEM((2, 3) + block, F32),
            pltpu.VMEM((PAIRS + 1,) + block, BF16),
            pltpu.VMEM((PAIRS + 1,) + block, BF16),
            pltpu.VMEM((PAIRS + 1,) + block, BF16),
            pltpu.VMEM((2, PAIRS * GROUP, PAIRS * GROUP), BF16),
            pltpu.VMEM((2, PAIRS) + block, F32),
            pltpu.VMEM((PAIRS,) + block, F32),
            parts((PAIRS + 1,)),
            parts((PAIRS + 1,)),
            parts((2, SIDE), F32),
            parts((3, 2, SIDE)),
            parts((2, SIDE)),
            parts((2, 2, SIDE)),
            parts((3, 2)),
            parts((3, 2)),
            pltpu.VMEM((3, SIDE, 2) + quarter, BF16),
            pltpu.VMEM((3, SIDE, 2) + quarter, BF16),
            pltpu.VMEM((SIDE, 2) + quarter, F32),
            pltpu.VMEM((3, 2) + quarter, BF16),
            pltpu.VMEM((3, 2) + quarter, BF16),
            pltpu.VMEM((OWN,) + block, BF16),
            dma((OWN,)),
            dma((OWN,)),
            dma((OWN,)),
            dma((OWN,)),
            dma((2, 2, hops)),
            dma((2, 2, hops)),
            dma((3,)),
            dma((3,)),
            dma((count,)),
            dma((count,)),
            dma((SIDE - 1,)),
            dma((SIDE - 1,)),
            dma((count, 2)),
            dma((count, 2)),
            dma((count, 2, 2)),
            dma((count, 2, 2)),
            dma((count, 3)),
            dma((count, 3)),
            dma((3,)),
            dma((3,)),
            dma((3,)),
            dma((3,)),
        ],
        compiler_params=pltpu.CompilerParams(
            collective_id=0, has_side_effects=True, vmem_limit_bytes=56 * 2**20
        ),
        cost_estimate=pl.CostEstimate(
            flops=2 * 10**9, bytes_accessed=4 * 2**20, transcendentals=4 * 10**6
        ),
    )(
        basis_centers,
        bra_pairs,
        ket_pairs,
        quartets,
        quartet_counts,
        density_owner,
        density_store,
    )


def solution(mesh):
    return jax.shard_map(
        local,
        mesh=mesh,
        in_specs=(
            P(),
            P("bra"),
            P("ket"),
            P("bra", "ket", None, None),
            P("bra", "ket"),
            P("ket", None),
            P("bra", "ket", None),
        ),
        out_specs=P("bra", "ket"),
        check_vma=False,
    )
```
